32 devices in a mesh: ctx: 4 (over z), shard: 8 (over y, x, core).
Axes of the slice: x: 2, y: 2, z: 4, core: 2. Of those that a mesh axis runs over, the one named last changes fastest.
Arguments:
- tokens: bfloat16 [8, 1024, 1024], P('shard', 'ctx'), may hold values from -6 to 6
- segments: int32 [8, 1024], P('shard', 'ctx'), may hold values from 0 to 254, as said below
- valid: int32 [8, 1024], P('shard', 'ctx'), may hold values from 0 to 1, as said below
- routes: int32 [8, 1024, 2], P('shard', 'ctx'), may hold values from 0 to 7, all different within a row; in each aligned block of 256 rows (0 to 255, 256 to 511, ..., all dimensions but the last counted through in order) at most 80 rows name the same one
- teacher: bfloat16 [8, 1024, 1024], P('shard', 'ctx'), may hold values from -6 to 6
- norm_attn: bfloat16 [1024], P(('ctx', 'shard')), may hold values from 0.5 to 1.5
- w_query: bfloat16 [1024, 1024], P(('ctx', 'shard')), may hold values from -0.1875 to 0.1875
- w_key: bfloat16 [1024, 1024], P(('ctx', 'shard')), may hold values from -0.1875 to 0.1875
- w_value: bfloat16 [1024, 1024], P(('ctx', 'shard')), may hold values from -0.1875 to 0.1875
- output_weight: bfloat16 [1024, 1024], P(('ctx', 'shard')), may hold values from -1.5 to 1.5
- rel_bias: bfloat16 [512], P(('ctx', 'shard')), may hold values from -4 to 4
- norm_ffn: bfloat16 [1024], P(('ctx', 'shard')), may hold values from 0.5 to 1.5
- w_router: bfloat16 [1024, 8], P(('ctx', 'shard')), may hold values from -0.125 to 0.125
- w_gate: bfloat16 [8, 1024, 2816], P('shard'), may hold values from -0.1875 to 0.1875
- w_up: bfloat16 [8, 1024, 2816], P('shard'), may hold values from -0.1875 to 0.1875
- w_down: bfloat16 [8, 2816, 1024], P('shard'), may hold values from -0.21875 to 0.21875
Outputs:
- output: bfloat16 [8, 1024, 1024], P('shard', 'ctx')
- loss: float32 [], replicated
- input_grad: float32 [8, 1024, 1024], P('shard', 'ctx')
- norm_attn_grad: float32 [1024], P(('ctx', 'shard'))
- w_query_grad: float32 [1024, 1024], P(('ctx', 'shard'))
- w_key_grad: float32 [1024, 1024], P(('ctx', 'shard'))
- w_value_grad: float32 [1024, 1024], P(('ctx', 'shard'))
- w_out_grad: float32 [1024, 1024], P(('ctx', 'shard'))
- rel_bias_grad: float32 [512], P(('ctx', 'shard'))
- norm_ffn_grad: float32 [1024], P(('ctx', 'shard'))
- w_router_grad: float32 [1024, 8], P(('ctx', 'shard'))
- w_gate_grad: float32 [8, 1024, 2816], P('shard', 'ctx')
- w_up_grad: float32 [8, 1024, 2816], P('shard', 'ctx')
- w_down_grad: float32 [8, 2816, 1024], P('shard', 'ctx')
The draws below stay inside these ranges and needn't reach their ends.
Inputs may be any that keep to these rules, and one draw needn't show every extreme that they name: `segments`: along each sequence the ids start at 0 and never fall. In each sequence one document begins among the first 128 positions and ends among the last 128. The first token of each sequence is valid. `routes`: each token names 2 different experts. Among the tokens of one device no expert is named more than 80 times, and in every draw some device names some expert exactly 80 times.
All inputs are finite; a program needn't handle non-finite values.
Results may differ from the reference program's by a relative error of at most 0.02.
Values may be sent and summed in bfloat16 or wider, within the bound.
A program may use at most 192 MiB of HBM per device.

```python
import math
import jax
import jax.numpy as jnp
import numpy as np
from jax import lax

D = 1024
HEADS = 16
HEAD = 64
FF = 2816
BUCKETS = 32
TOP = 2
TOK_DEV = 256
LEN = 1024
SEQS = 8
TOKENS = 8192
EXPERTS = 8
CAP = 80
N_CTX = 4


def draw_segments(key, part):
    key = jax.random.fold_in(key, 11)
    first_key, second_key, third_key, fourth_key = jax.random.split(key, 4)
    positions = jnp.arange(LEN, dtype=jnp.int32)[None, :]
    chosen = jax.random.randint(fourth_key, (), 0, SEQS)
    is_chosen = (jnp.arange(SEQS, dtype=jnp.int32) == chosen)[:, None]
    begin_at = jax.random.randint(first_key, (SEQS, 1), 1, max(2, TOK_DEV // 2))
    end_at = jax.random.randint(second_key, (SEQS, 1), LEN - TOK_DEV // 2 + 1, LEN - TOK_DEV // 4 + 1)
    begin_at = jnp.where(is_chosen, max(1, TOK_DEV // 2 - 1), begin_at)
    end_at = jnp.where(is_chosen, LEN - TOK_DEV // 2 + 1, end_at)
    breaks = (jax.random.randint(third_key, (SEQS, LEN), 0, 24) == 0).astype(jnp.int32)
    breaks = jnp.where(is_chosen, 1, breaks)
    inside = (positions > begin_at) & (positions < end_at)
    breaks = jnp.where(inside, 0, breaks)
    breaks = jnp.where((positions == begin_at) | (positions == end_at), 1, breaks)
    breaks = jnp.where(positions == 0, 0, breaks)
    return jnp.cumsum(breaks, axis=1).astype(jnp.int32)


def draw_valid(key, part):
    key = jax.random.fold_in(key, 12)
    positions = jnp.arange(LEN, dtype=jnp.int32)[None, :]
    levels = jax.random.randint(key, (SEQS, LEN), 0, 1000)
    threshold = 250 + 700 * positions // LEN
    marks = (levels < threshold) | (positions == 0)
    return marks.astype(jnp.int32)


def level_of(stream_key, shape, pieces, smallest, high):
    level = 1.0
    for axis_at, blocks in pieces:
        steps = jax.random.uniform(jax.random.fold_in(jax.random.fold_in(stream_key, 6), axis_at), (blocks,), jnp.float32, smallest / len(pieces), high / len(pieces))
        level = level * jnp.repeat(jnp.exp(steps), shape[axis_at] // blocks).reshape((-1,) + (1,) * (len(shape) - 1 - axis_at))
    return level


def assign_block(stream_key, own, number, rows, count, top, reach, lean):
    ranking = jax.random.permutation(stream_key, count)
    crowded, common = load_shares(count, rows * top, reach, lean, True), load_shares(count, rows * top, reach, lean, False)
    places = jnp.arange(count)

    def named(sizes, offset_by):
        used = int((sizes > 0).sum())
        fixed = max(1, used // 4)
        shifted = fixed + (places - fixed + offset_by * (used - fixed)) % max(1, count - fixed)
        return jnp.zeros((count,), jnp.int32).at[ranking[jnp.where(places < fixed, places, shifted)]].set(jnp.asarray(sizes, jnp.int32))

    sizes = jnp.where(number % 4 == 0, named(crowded, number // 4), named(common, number - number // 4 - 1))
    mixed = jax.random.permutation(jax.random.fold_in(own, 3), count)
    donor, receiver = mixed[0:count // 2 * 2:2], mixed[1:count // 2 * 2:2]
    margin = jnp.minimum(sizes[donor] - 1, reach - sizes[receiver]) // 2
    margin = jnp.where((donor == ranking[0]) | (receiver == ranking[0]) | (sizes[receiver] == 0), 0, jnp.maximum(margin, 0))
    shifted = jax.random.randint(jax.random.fold_in(own, 4), (count // 2,), 0, 1 << 20) % (margin + 1)
    sizes = sizes.at[donor].add(-shifted).at[receiver].add(shifted)
    items = jnp.searchsorted(jnp.cumsum(sizes), jnp.arange(rows * top), side="right").astype(jnp.int32)
    listing = items.reshape(top, rows).T
    listing = listing[jax.random.permutation(jax.random.fold_in(own, 1), rows)]
    offset_by = jax.random.randint(jax.random.fold_in(own, 2), (rows, 1), 0, top)
    return jnp.take_along_axis(listing, (jnp.arange(top)[None, :] + offset_by) % top, axis=1)


def load_shares(number_of, total, bound, skew, full):
    loads = [(1 << 20) // math.isqrt(rank ** skew) + 1 for rank in range(1, number_of + 1)]
    largest = bound if full else min(bound, max(-(-total // number_of), total * loads[0] // sum(loads)))
    least = 1 if total - largest >= number_of - 1 else 0
    counts, rest = [largest] + [least] * (number_of - 1), total - largest - least * (number_of - 1)
    while rest > 0:
        free = [i for i in range(1, number_of) if counts[i] < largest] or [i for i in range(1, number_of) if counts[i] < bound]
        pool, remaining = sum([loads[i] for i in free]), rest
        for i in free:
            more = min(bound - counts[i], max(1, remaining * loads[i] // pool), rest)
            counts[i] = counts[i] + more
            rest = rest - more
    return np.array(counts)


def normal_values(own_key, extent, width, limit, cuts=(), held_as=jnp.bfloat16):
    factor_of = level_of(own_key, extent, cuts, -0.22, 0.18) if cuts else 1.0
    drawn = jax.random.normal(own_key, extent, jnp.float32) * width * factor_of
    return jnp.minimum(jnp.maximum(drawn, -limit), limit).astype(held_as)


def setup_inputs(seed: int = 0) -> dict:
    key_of = jax.random.split(jax.random.key(seed), 17)
    tokens = normal_values(key_of[0], (SEQS, LEN, D), 1.0, 6.0, ((0, 8), (1, 4)))
    segments = draw_segments(jax.random.fold_in(key_of[16], 71), 0)
    valid = draw_valid(jax.random.fold_in(key_of[16], 71), 0)
    routes_keys = jax.random.split(jax.random.fold_in(key_of[3], 1), SEQS * LEN // TOK_DEV)
    routes_turns = jax.random.permutation(jax.random.fold_in(key_of[3], 3), SEQS * LEN // TOK_DEV)
    routes = jax.vmap(lambda own, number: assign_block(jax.random.fold_in(key_of[3], 2), own, number, TOK_DEV, EXPERTS, TOP, CAP, 2))(routes_keys, routes_turns).reshape((SEQS, LEN, TOP))
    teacher = normal_values(key_of[4], (SEQS, LEN, D), 1.0, 6.0, ((0, 8), (1, 4)))
    norm_attn = jnp.clip(1.0 + 0.1 * jax.random.normal(key_of[5], (D,), jnp.float32), 0.5, 1.5).astype(jnp.bfloat16)
    w_query = normal_values(key_of[6], (D, D), D ** -0.5, 0.1875, ((0, 32),))
    w_key = normal_values(key_of[7], (D, D), D ** -0.5, 0.1875, ((0, 32),))
    w_value = normal_values(key_of[8], (D, D), D ** -0.5, 0.1875, ((0, 32),))
    output_weight = normal_values(key_of[9], (D, D), (D // 64) ** -0.5, 1.5, ((0, 32),))
    rel_bias = normal_values(key_of[10], (BUCKETS * HEADS,), 1.0, 4.0, ((0, 32),))
    norm_ffn = jnp.clip(1.0 + 0.1 * jax.random.normal(key_of[11], (D,), jnp.float32), 0.5, 1.5).astype(jnp.bfloat16)
    w_router = normal_values(key_of[12], (D, EXPERTS), (2 * D) ** -0.5, 0.125, ((0, 32),))
    w_gate = normal_values(key_of[13], (EXPERTS, D, FF), D ** -0.5, 0.1875, ((0, 8),))
    w_up = normal_values(key_of[14], (EXPERTS, D, FF), D ** -0.5, 0.1875, ((0, 8),))
    w_down = normal_values(key_of[15], (EXPERTS, FF, D), (FF // 4) ** -0.5, 0.21875, ((0, 8),))
    return {"tokens": tokens, "segments": segments, "valid": valid, "routes": routes, "teacher": teacher, "norm_attn": norm_attn, "w_query": w_query, "w_key": w_key, "w_value": w_value, "output_weight": output_weight, "rel_bias": rel_bias, "norm_ffn": norm_ffn, "w_router": w_router, "w_gate": w_gate, "w_up": w_up, "w_down": w_down}


@jax.custom_vjp
def low(v):
    return lax.optimization_barrier(v.astype(jnp.bfloat16)).astype(jnp.float32)

@jax.custom_vjp
def low_back(v):
    return v

def low_keep(v):
    return (low(v), None)

def low_pass(kept, grad):
    return (grad,)

def back_keep(v):
    return (v, None)

def back_low(kept, grad):
    return (low(grad),)
low.defvjp(low_keep, low_pass)
low_back.defvjp(back_keep, back_low)
highest_precision = lax.Precision.HIGHEST
max_distance = 128
epsilon = 1e-06

def thresholds(buckets):
    exact_count = buckets // 2
    limits = list(range(1, exact_count))
    for bucket_level in range(exact_count, buckets):
        power = (bucket_level - exact_count) / exact_count
        limits.append(int(math.ceil(exact_count * (max_distance / exact_count) ** power)))
    return limits

def bucket_of(distance, buckets):
    bucket_total = jnp.zeros(distance.shape, jnp.int32)
    for threshold in thresholds(buckets):
        bucket_total = bucket_total + (distance >= threshold).astype(jnp.int32)
    return bucket_total

def rms_norm(values, gain_vector):
    return values * lax.rsqrt(lax.optimization_barrier(jnp.mean(values * values, axis=-1, keepdims=True)) + epsilon) * gain_vector

def attend_sequence(packed, bias_table):
    queries, key_rows, value_rows, segment_row, valid_row = packed
    seq_length = queries.shape[0]
    block_size = min(seq_length, 512)
    positions = jnp.arange(seq_length, dtype=jnp.int32)
    score_scale = 1.0 / math.sqrt(HEAD)

    def one_block(block_index):
        block_start = block_index * block_size
        query_part = lax.dynamic_slice_in_dim(queries, block_start, block_size, 0)
        query_seg = lax.dynamic_slice_in_dim(segment_row, block_start, block_size, 0)
        query_pos = block_start + jnp.arange(block_size, dtype=jnp.int32)
        raw_scores = low_back(jnp.einsum('qhd,khd->hqk', query_part, key_rows, precision=highest_precision) * score_scale)
        distance = query_pos[:, None] - positions[None, :]
        bias_block = jnp.transpose(bias_table[bucket_of(jnp.maximum(distance, 0), BUCKETS)], (2, 0, 1))
        allowed = (query_seg[:, None] == segment_row[None, :]) & (distance >= 0) & ((valid_row[None, :] > 0) | (distance == 0))
        scores = jnp.where(allowed[None], raw_scores + bias_block, -1e+30)
        weights = jax.nn.softmax(scores, axis=-1)
        return jnp.einsum('hqk,khd->qhd', low(weights), value_rows, precision=highest_precision)
    block_parts = lax.map(jax.checkpoint(one_block), jnp.arange(seq_length // block_size, dtype=jnp.int32))
    return block_parts.reshape(seq_length, queries.shape[1], queries.shape[2])

def destinations(routes):
    block_count = SEQS * N_CTX
    flat_routes = routes.reshape(block_count, TOK_DEV * TOP)
    route_hits = (flat_routes[:, :, None] == jnp.arange(EXPERTS, dtype=jnp.int32)[None, None, :]).astype(jnp.int32)
    before = jnp.cumsum(route_hits, axis=1) - route_hits
    slot_rank = lax.optimization_barrier(jnp.sum(before * route_hits, axis=2))
    block_ids = jnp.arange(block_count, dtype=jnp.int32)[:, None]
    placement = flat_routes * (block_count * CAP) + block_ids * CAP + slot_rank
    return placement.reshape(TOKENS, TOP).astype(jnp.int32)

def expert_apply(packed):
    expert_rows, gate_weight, up_weight, down_weight = packed
    gate_pre = low_back(jnp.dot(expert_rows, gate_weight, precision=highest_precision))
    up_pre = low_back(jnp.dot(expert_rows, up_weight, precision=highest_precision))
    inner = low(jax.nn.gelu(gate_pre) * up_pre)
    return low_back(low(jnp.dot(inner, down_weight, precision=highest_precision)))

def forward(tokens, norm_attn, w_query, w_key, w_value, output_weight, rel_bias, norm_ffn, w_router, w_gate, w_up, w_down, segments, valid, placement):
    first_operand = low(rms_norm(tokens, norm_attn))

    def project(weight_matrix):
        return low_back(low(jnp.einsum('hyz,zj->hyj', first_operand, weight_matrix, precision=highest_precision)))
    queries = project(w_query).reshape(SEQS, LEN, HEADS, HEAD)
    key_rows = project(w_key).reshape(SEQS, LEN, HEADS, HEAD)
    value_rows = project(w_value).reshape(SEQS, LEN, HEADS, HEAD)
    bias_table = rel_bias.reshape(BUCKETS, HEADS)
    attended = lax.map(lambda packed: attend_sequence(packed, bias_table), (queries, key_rows, value_rows, segments, valid))
    mixed_matmul = low_back(low(attended.reshape(SEQS, LEN, D)))
    attention_result = low_back(jnp.einsum('hyz,zj->hyj', mixed_matmul, output_weight, precision=highest_precision))
    residual = tokens + attention_result
    second = low(rms_norm(residual, norm_ffn))
    flat_in = second.reshape(TOKENS, D)
    logits = jnp.dot(flat_in, w_router, precision=highest_precision)
    picked = jnp.take_along_axis(logits, placement // (SEQS * N_CTX * CAP), axis=1)
    gate_probs = jax.nn.softmax(picked, axis=-1)
    slot_total = EXPERTS * SEQS * N_CTX * CAP
    source = jnp.full((slot_total,), -1, jnp.int32).at[placement.reshape(-1)].set(jnp.arange(TOKENS * TOP, dtype=jnp.int32))
    token_index = jnp.maximum(source, 0) // TOP
    gathered = low_back(jnp.where((source >= 0)[:, None], flat_in[token_index], 0.0))
    outputs = lax.map(jax.checkpoint(expert_apply), (gathered.reshape(EXPERTS, slot_total // EXPERTS, D), w_gate, w_up, w_down))
    assigned = outputs.reshape(slot_total, D)[placement]
    moe_out = lax.optimization_barrier(jnp.sum(gate_probs[:, :, None] * assigned, axis=1))
    return residual + moe_out.reshape(SEQS, LEN, D)

def reference(tokens, segments, valid, routes, teacher, norm_attn, w_query, w_key, w_value, output_weight, rel_bias, norm_ffn, w_router, w_gate, w_up, w_down):
    floats = [item.astype(jnp.float32) for item in (tokens, norm_attn, w_query, w_key, w_value, output_weight, rel_bias, norm_ffn, w_router, w_gate, w_up, w_down)]
    placement = destinations(routes)
    valid_mask = valid.astype(jnp.float32)[..., None]
    valid_count = jnp.sum(valid.astype(jnp.float32))
    target = teacher.astype(jnp.float32)

    def objective(*params):
        output_sum = forward(*params, segments, valid, placement)
        deviation = output_sum - target
        loss_value = jnp.sum(valid_mask * deviation * deviation) / (2.0 * D * valid_count)
        return (TOKENS * D * loss_value, (output_sum, loss_value))
    scaled, pullback, extras = jax.vjp(objective, *floats, has_aux=True)
    output_sum, loss_value = extras
    gradients = pullback(jnp.ones_like(scaled))
    return (output_sum.astype(jnp.bfloat16), loss_value, gradients[0], gradients[1], gradients[2], gradients[3], gradients[4], gradients[5], gradients[6], gradients[7], gradients[8], gradients[9], gradients[10], gradients[11])
```

```python
import math

import jax
import jax.numpy as jnp
from jax import lax
from jax.experimental import pallas as pl
from jax.experimental.pallas import tpu as pltpu
from jax.sharding import PartitionSpec as P

HEADS = 16
HEAD = 64
BUCKETS = 32
MESH = pl.DeviceIdType.MESH
ANY = pl.ANY
VMEM = pltpu.VMEM
SEM = pltpu.SemaphoreType

highest_precision = lax.Precision.HIGHEST
max_distance = 128
epsilon = 1e-06
negative = -1e30
EXTRA = 16


def thresholds(buckets):
    exact_count = buckets // 2
    limits = list(range(1, exact_count))
    for bucket_level in range(exact_count, buckets):
        power = (bucket_level - exact_count) / exact_count
        limits.append(int(math.ceil(exact_count * (max_distance / exact_count) ** power)))
    return limits


def bucket_of(distance, buckets):
    bucket_total = jnp.zeros(distance.shape, jnp.int32)
    for threshold in thresholds(buckets):
        bucket_total = bucket_total + (distance >= threshold).astype(jnp.int32)
    return bucket_total


def rms_norm(values, gain_vector):
    return (
        values
        * lax.rsqrt(jnp.mean(values * values, axis=-1, keepdims=True) + epsilon)
        * gain_vector
    )


def contract(left_side, right_side, left_axis, right_axis, precision_mode=None):
    return lax.dot_general(
        left_side,
        right_side,
        (((left_axis,), (right_axis,)), ((), ())),
        precision=precision_mode,
        preferred_element_type=jnp.float32,
    )


def dot32(left_side, right_side):
    return jnp.dot(left_side, right_side, preferred_element_type=jnp.float32)


def nt(left_side, right_side):
    return contract(left_side, right_side, 1, 1)


def tn(left_side, right_side):
    return contract(left_side, right_side, 0, 0)


class Place:
    def __init__(self, nc, ns):
        self.nc, self.ns, self.nj = nc, ns, ns // 2
        self.c = lax.axis_index("ctx")
        self.s = lax.axis_index("shard")
        self.core = self.s % 2
        self.j = self.s // 2

    def along(self, d):
        return (lax.rem(self.c + d + self.nc, self.nc), self.s)

    def across(self, k):
        return (self.c, self.s ^ (2 * k))

    def twin(self):
        return (self.c, self.s ^ 1)

    def greet(self):
        barrier = pltpu.get_barrier_semaphore()
        partners = (
            [self.along(d) for d in range(1, self.nc)]
            + [self.across(k) for k in range(1, self.nj)]
            + [self.twin()]
        )
        for partner in partners:
            pl.semaphore_signal(barrier, inc=1, device_id=partner, device_id_type=MESH)
        pl.semaphore_wait(barrier, len(partners))


def remote(source, target, send, recv, device):
    return pltpu.make_async_remote_copy(
        src_ref=source,
        dst_ref=target,
        send_sem=send,
        recv_sem=recv,
        device_id=device,
        device_id_type=MESH,
    )


def gather_all(weights, extra, rows, nc, ns):
    n_dev, nj = nc * ns, ns // 2
    parts, piece, width = weights.shape
    count = rows.shape[0]
    spread = piece % 16 == 0
    weight_shape = (parts, n_dev * piece, width) if spread else (n_dev, parts * piece, width)
    if not spread:
        weights = weights.reshape(parts * piece, width)

    def kernel(w_in, e_in, t_in, w_out, e_out, t_out, local, zs, zr, xs, xr, cs, cr, ts, tr):
        me = Place(nc, ns)

        def views(place, device):
            if spread:
                start = pl.multiple_of(device * piece, piece)
                return (w_out.at[:, pl.ds(start, piece), :], e_out.at[device])
            return (w_out.at[device], e_out.at[device])

        def index(d, k):
            return lax.rem(me.c - d + nc, nc) * ns + (me.s ^ (2 * k))

        own = (w_in, e_in)
        mine = me.c * ns + me.s
        locals_ = [
            pltpu.make_async_copy(source, target, local.at[i])
            for i, (source, target) in enumerate(
                zip(own + (t_in,), views(me, mine) + (t_out.at[nc - 1],))
            )
        ]
        for copy in locals_:
            copy.start()
        me.greet()
        sent = []

        def push(sources, targets, send, recv, device):
            for i in range(2):
                copy = remote(sources[i], targets[i], send.at[i], recv.at[i], device)
                copy.start()
                sent.append(copy)

        def arrive(targets, send, recv, device):
            for i in range(2):
                remote(targets[i], targets[i], send.at[i], recv.at[i], device).wait_recv()

        def token_copy(direction, hop, source=None):
            origin_slot = (nc - 1 - hop) if direction > 0 else (hop - 1)
            target_slot = (nc - 2 - hop) if direction > 0 else hop
            lane = 0 if direction > 0 else 1
            return remote(
                t_in if hop == 0 else t_out.at[origin_slot],
                t_out.at[target_slot],
                ts.at[lane, hop],
                tr.at[lane, hop],
                (lax.rem(me.c + direction + nc, nc), me.s),
            )

        def can_send(direction, hop):
            if direction > 0:
                return (me.c >= hop) & (me.c < nc - 1)
            return (me.c <= nc - 1 - hop) & (me.c > 0)

        def can_receive(direction, hop):
            if direction > 0:
                return me.c >= hop + 1
            return me.c <= nc - 2 - hop

        for d in range(1, nc):
            push(own, views(me, mine), zs.at[d], zr.at[d], me.along(d))
        for direction in (1, -1):

            @pl.when(can_send(direction, 0))
            def _():
                token_copy(direction, 0).start()

        for k in range(1, nj):
            push(own, views(me, mine), xs.at[0, k], xr.at[0, k], me.across(k))
        push(own, views(me, mine), cs.at[0, 0], cr.at[0, 0], me.twin())

        for copy in locals_:
            copy.wait()
        for d in range(1, nc):
            here = views(me, index(d, 0))
            arrive(here, zs.at[d], zr.at[d], me.along(-d))
            for k in range(1, nj):
                push(here, here, xs.at[d, k], xr.at[d, k], me.across(k))
            push(here, here, cs.at[d, 0], cr.at[d, 0], me.twin())
            if d < nc - 1:
                for direction in (1, -1):

                    @pl.when(can_receive(direction, d - 1))
                    def _():
                        token_copy(direction, d - 1).wait_recv()

                    @pl.when(can_send(direction, d))
                    def _():
                        token_copy(direction, d).start()

        for d in range(nc):
            for k in range(1, nj):
                here = views(me, index(d, k))
                arrive(here, xs.at[d, k], xr.at[d, k], me.across(k))
                push(here, here, cs.at[d, k], cr.at[d, k], me.twin())
        for d in range(nc):
            for k in range(nj):
                here = views(me, lax.rem(me.c - d + nc, nc) * ns + (me.s ^ 1 ^ (2 * k)))
                arrive(here, cs.at[d, k], cr.at[d, k], me.twin())
        for direction in (1, -1):

            @pl.when(can_receive(direction, nc - 2))
            def _():
                token_copy(direction, nc - 2).wait_recv()

        for copy in sent:
            copy.wait_send()
        for direction in (1, -1):
            for hop in range(nc - 1):

                @pl.when(can_send(direction, hop))
                def _():
                    token_copy(direction, hop).wait_send()

    full, extras, tokens = pl.pallas_call(
        kernel,
        name="gather_all",
        out_shape=(
            jax.ShapeDtypeStruct(weight_shape, weights.dtype),
            jax.ShapeDtypeStruct((n_dev,) + extra.shape, extra.dtype),
            jax.ShapeDtypeStruct((nc,) + rows.shape, rows.dtype),
        ),
        in_specs=[pl.BlockSpec(memory_space=ANY)] * 3,
        out_specs=[pl.BlockSpec(memory_space=ANY)] * 3,
        scratch_shapes=[
            SEM.DMA((3,)),
            SEM.DMA((nc, 2)),
            SEM.DMA((nc, 2)),
            SEM.DMA((nc, nj, 2)),
            SEM.DMA((nc, nj, 2)),
            SEM.DMA((nc, nj, 2)),
            SEM.DMA((nc, nj, 2)),
            SEM.DMA((2, nc)),
            SEM.DMA((2, nc)),
        ],
        compiler_params=pltpu.CompilerParams(collective_id=1, has_side_effects=True),
    )(weights, extra, rows)
    if not spread:
        full = full.reshape(n_dev, parts, piece, width).transpose(1, 0, 2, 3)
        full = full.reshape(parts, n_dev * piece, width)
    return full, extras, tokens.reshape(nc * count, width)


def reduce_all(grads, squares, away, own, nc, ns):
    nj = ns // 2
    piece, width = grads.shape[3:]
    count = own.shape[0]
    tile = squares.shape

    def kernel(g_in, q_in, a_in, o_in, g_out, q_out, o_out, total, cbuf, xbuf, zbuf, abuf,
               qz, qx, qc, qa, qb, cs, cr, xs, xr, zs, zr, as_, ar, q1s, q1r, q2s, q2r, q3s, q3r):
        me = Place(nc, ns)
        me.greet()

        def away_copy(r):
            return remote(
                a_in.at[nc - 1 - r], abuf.at[r - 1], as_.at[r], ar.at[r],
                (lax.rem(me.c - r + nc, nc), me.s),
            )

        def core_copy(d):
            row = lax.rem(me.c + d, nc)
            return remote(
                g_in.at[row, :, 1 - me.core], cbuf.at[d], cs.at[d], cr.at[d], me.twin()
            )

        def cross_copy(d, k):
            return remote(
                total.at[d, me.j ^ k], xbuf.at[d, k - 1], xs.at[d, k], xr.at[d, k], me.across(k)
            )

        def along_copy(d):
            return remote(total.at[d, me.j], zbuf.at[d - 1], zs.at[d], zr.at[d], me.along(d))

        def q_along(d):
            return remote(q_in, qz.at[d - 1], q1s.at[d], q1r.at[d], me.along(d))

        def q_across(k):
            return remote(qa, qx.at[k - 1], q2s.at[k], q2r.at[k], me.across(k))

        q_twin = remote(qb, qc, q3s.at[0], q3r.at[0], me.twin())
        order = list(range(1, nc)) + [0]
        for d in order:
            core_copy(d).start()
        for d in range(1, nc):
            q_along(d).start()
        for r in range(1, nc):

            @pl.when(me.c >= r)
            def _():
                away_copy(r).start()

        step = 16
        for d in order:
            core_copy(d).wait_recv()
            row = lax.rem(me.c + d, nc)

            def add_core(i, carry):
                at = pl.ds(pl.multiple_of(i * step, step), step)
                for k in range(nj):
                    total[d, k, at] = (
                        g_in[row, k, me.core, at].astype(jnp.float32)
                        + cbuf[d, k, at].astype(jnp.float32)
                    ).astype(total.dtype)
                return carry

            lax.fori_loop(0, piece // step, add_core, 0)
            for k in range(1, nj):
                cross_copy(d, k).start()
        for d in range(1, nc):
            q_along(d).wait_recv()
        value = q_in[...]
        for d in range(1, nc):
            value = value + qz[d - 1]
        qa[...] = value
        for k in range(1, nj):
            q_across(k).start()
        for d in order:
            for k in range(1, nj):
                cross_copy(d, k).wait_recv()

            def add_cross(i, carry):
                at = pl.ds(pl.multiple_of(i * step, step), step)
                value = total[d, me.j, at].astype(jnp.float32)
                for k in range(1, nj):
                    value = value + xbuf[d, k - 1, at].astype(jnp.float32)
                if d == 0:
                    g_out[at] = value
                else:
                    total[d, me.j, at] = value.astype(total.dtype)
                return carry

            lax.fori_loop(0, piece // step, add_cross, 0)
            if d:
                along_copy(d).start()
        for k in range(1, nj):
            q_across(k).wait_recv()
        value = qa[...]
        for k in range(1, nj):
            value = value + qx[k - 1]
        qb[...] = value
        q_twin.start()
        for d in range(1, nc):
            along_copy(d).wait_recv()

        def add_along(i, carry):
            at = pl.ds(pl.multiple_of(i * step, step), step)
            value = g_out[at]
            for d in range(1, nc):
                value = value + zbuf[d - 1, at].astype(jnp.float32)
            g_out[at] = value
            return carry

        lax.fori_loop(0, piece // step, add_along, 0)
        o_out[...] = o_in[...]
        for r in range(1, nc):

            @pl.when(me.c < nc - r)
            def _():
                away_copy(r).wait_recv()

                def add_away(i, carry):
                    at = pl.ds(pl.multiple_of(i * step, step), step)
                    o_out[at] = o_out[at] + abuf[r - 1, at].astype(jnp.float32)
                    return carry

                lax.fori_loop(0, count // step, add_away, 0)

        q_twin.wait()
        q_out[...] = qb[...] + qc[...]
        for d in order:
            core_copy(d).wait_send()
            for k in range(1, nj):
                cross_copy(d, k).wait_send()
            if d:
                along_copy(d).wait_send()
                q_along(d).wait_send()
        for k in range(1, nj):
            q_across(k).wait_send()
        for r in range(1, nc):

            @pl.when(me.c >= r)
            def _():
                away_copy(r).wait_send()

    low = grads.dtype
    return pl.pallas_call(
        kernel,
        name="reduce_all",
        out_shape=(
            jax.ShapeDtypeStruct((piece, width), jnp.float32),
            jax.ShapeDtypeStruct(tile, jnp.float32),
            jax.ShapeDtypeStruct(own.shape, jnp.float32),
        ),
        in_specs=[pl.BlockSpec(memory_space=VMEM)] * 4,
        out_specs=[pl.BlockSpec(memory_space=VMEM)] * 3,
        scratch_shapes=[
            VMEM((nc, nj, piece, width), low),
            VMEM((nc, nj, piece, width), low),
            VMEM((nc, nj - 1, piece, width), low),
            VMEM((nc - 1, piece, width), low),
            VMEM((nc - 1,) + own.shape, low),
            VMEM((nc - 1,) + tile, jnp.float32),
            VMEM((nj - 1,) + tile, jnp.float32),
            VMEM(tile, jnp.float32),
            VMEM(tile, jnp.float32),
            VMEM(tile, jnp.float32),
            SEM.DMA((nc,)),
            SEM.DMA((nc,)),
            SEM.DMA((nc, nj)),
            SEM.DMA((nc, nj)),
            SEM.DMA((nc,)),
            SEM.DMA((nc,)),
            SEM.DMA((nc,)),
            SEM.DMA((nc,)),
            SEM.DMA((nc,)),
            SEM.DMA((nc,)),
            SEM.DMA((nj,)),
            SEM.DMA((nj,)),
            SEM.DMA((1,)),
            SEM.DMA((1,)),
        ],
        compiler_params=pltpu.CompilerParams(
            collective_id=2, has_side_effects=True, vmem_limit_bytes=56 * 1024 * 1024
        ),
    )(grads, squares, away, own)


CHUNK = 16
QUAD = 256


def fill_mask(mask, query_seg, key_code, count, length):
    near = length - count
    seen = query_seg[...] == key_code[:, :near]
    mask[:, :near] = jnp.where(seen, 0.0, negative)
    row = lax.broadcasted_iota(jnp.int32, (count, count), 0)
    column = lax.broadcasted_iota(jnp.int32, (count, count), 1)
    seen = ((query_seg[...] == key_code[:, near:]) & (row >= column)) | (row == column)
    mask[:, near:] = jnp.where(seen, 0.0, negative)


def attend_forward(tokens, weights, gain, query_seg, key_code, slopes):
    length, width = tokens.shape
    count = query_seg.shape[0]
    band = slopes.shape[2]
    far = length - band
    heads_in = QUAD // HEAD

    def kernel(t_in, w_in, gain_in, qseg, kcode, toe, first, q_out, k_out, v_out, o_out, lse_out, x_out, sbuf, pbuf, mask, lsum):
        fill_mask(mask, qseg, kcode, count, length)

        def norm(i, carry):
            at = pl.ds(pl.multiple_of(i * 64, 64), 64)
            x = t_in[at].astype(jnp.float32)
            rate = lax.rsqrt(jnp.mean(x * x, axis=-1, keepdims=True) + epsilon)
            first[at] = (x * rate * gain_in[...]).astype(jnp.bfloat16)
            return carry

        lax.fori_loop(0, length // 64, norm, 0)
        lane = lax.broadcasted_iota(jnp.int32, (count, 2 * HEAD), 1)
        lse_out[...] = jnp.zeros_like(lse_out)

        def quad(n, carry):
            columns = pl.ds(pl.multiple_of(n * QUAD, QUAD), QUAD)
            own = pl.ds(length - count, count)
            q_out[:, columns] = dot32(first[own], w_in[0, :, columns]).astype(jnp.bfloat16)

            def project(i, inner):
                at = pl.ds(pl.multiple_of(i * count, count), count)
                block = first[at]
                k_out[at, columns] = dot32(block, w_in[1, :, columns]).astype(jnp.bfloat16)
                v_out[at, columns] = dot32(block, w_in[2, :, columns]).astype(jnp.bfloat16)
                return inner

            lax.fori_loop(0, length // count, project, 0)
            for pair in range(heads_in // 2):
                two = pl.ds(pl.multiple_of(n * QUAD + pair * 2 * HEAD, 2 * HEAD), 2 * HEAD)
                q_pair = q_out[:, two] * jnp.bfloat16(1.0 / math.sqrt(HEAD))
                k_pair = k_out[:, two]
                v_pair = v_out[:, two]
                parts = []
                for half in range(2):
                    head = n * heads_in + pair * 2 + half
                    inside = (lane >= HEAD) if half else (lane < HEAD)
                    q_one = jnp.where(inside, q_pair, jnp.bfloat16(0))
                    sbuf[...] = nt(q_one, k_pair)
                    slope = toe[head]

                    def soft(i, inner):
                        at = pl.ds(pl.multiple_of(i * CHUNK, CHUNK), CHUNK)
                        wide = sbuf[at, :far] + mask[at, :far]
                        tight = (
                            sbuf[at, far:] + mask[at, far:]
                            + pltpu.roll(slope, i * CHUNK, 1)
                        )
                        top = jnp.maximum(
                            jnp.max(wide, axis=1, keepdims=True), jnp.max(tight, axis=1, keepdims=True)
                        )
                        wide = jnp.exp(wide - top)
                        tight = jnp.exp(tight - top)
                        total = jnp.sum(wide, axis=1, keepdims=True) + jnp.sum(
                            tight, axis=1, keepdims=True
                        )
                        pbuf[at, :far] = wide.astype(jnp.bfloat16)
                        pbuf[at, far:] = tight.astype(jnp.bfloat16)
                        lsum[at] = jnp.broadcast_to(1.0 / total, (CHUNK, 2 * HEAD))
                        spot = lax.broadcasted_iota(jnp.int32, (CHUNK, 128), 1)
                        lse_out[at] = jnp.where(spot == head, top + jnp.log(total), lse_out[at])
                        return inner

                    lax.fori_loop(0, count // CHUNK, soft, 0, unroll=2)
                    parts.append(dot32(pbuf[...], v_pair) * lsum[...])
                o_out[:, two] = jnp.where(lane < HEAD, parts[0], parts[1]).astype(jnp.bfloat16)
            return carry

        lax.fori_loop(0, width // QUAD, quad, 0)

        def finish(n, carry):
            columns = pl.ds(pl.multiple_of(n * QUAD, QUAD), QUAD)
            x = t_in[pl.ds(length - count, count), columns].astype(jnp.float32)
            x_out[:, columns] = x + dot32(o_out[...], w_in[3, :, columns])
            return carry

        lax.fori_loop(0, width // QUAD, finish, 0)

    low = jnp.bfloat16
    return pl.pallas_call(
        kernel,
        name="attend_forward",
        out_shape=(
            jax.ShapeDtypeStruct((length, width), low),
            jax.ShapeDtypeStruct((count, width), low),
            jax.ShapeDtypeStruct((length, width), low),
            jax.ShapeDtypeStruct((length, width), low),
            jax.ShapeDtypeStruct((count, width), low),
            jax.ShapeDtypeStruct((count, 128), jnp.float32),
            jax.ShapeDtypeStruct((count, width), jnp.float32),
        ),
        in_specs=[pl.BlockSpec(memory_space=VMEM)] * 6,
        out_specs=[pl.BlockSpec(memory_space=VMEM)] * 7,
        scratch_shapes=[
            VMEM((count, length), jnp.float32),
            VMEM((count, length), low),
            VMEM((count, length), jnp.float32),
            VMEM((count, 2 * HEAD), jnp.float32),
        ],
        compiler_params=pltpu.CompilerParams(vmem_limit_bytes=56 * 1024 * 1024),
    )(tokens, weights, gain, query_seg, key_code, slopes)


def attend_backward(q_all, k_all, v_all, do_all, lse, query_seg, key_code, slopes):
    length, width = k_all.shape
    count = q_all.shape[0]
    band = slopes.shape[2]
    far = length - band
    heads = width // HEAD

    def kernel(q_in, k_in, v_in, do_in, lse_in, qseg, kcode, toe, dq_out, dk_out, dv_out, near_out, far_out, sbuf, dbuf, pbuf, gbuf, mask):
        fill_mask(mask, qseg, kcode, count, length)
        lane = lax.broadcasted_iota(jnp.int32, (count, 2 * HEAD), 1)

        def pair_step(n, carry):
            two = pl.ds(pl.multiple_of(n * 2 * HEAD, 2 * HEAD), 2 * HEAD)
            q_pair = q_in[:, two] * jnp.bfloat16(1.0 / math.sqrt(HEAD))
            do_pair = do_in[:, two]
            k_pair = k_in[:, two]
            v_pair = v_in[:, two]
            dq_parts, dk, dv = [], None, None
            for half in range(2):
                head = n * 2 + half
                inside = (lane >= HEAD) if half else (lane < HEAD)
                q_one = jnp.where(inside, q_pair, jnp.bfloat16(0))
                do_one = jnp.where(inside, do_pair, jnp.bfloat16(0))
                sbuf[...] = nt(q_one, k_pair)
                dbuf[...] = nt(do_one, v_pair)
                slope = toe[head]
                near_out[head] = jnp.zeros((CHUNK, band), jnp.float32)
                far_out[head] = jnp.zeros((CHUNK, 128), jnp.float32)

                def soft(i, inner):
                    at = pl.ds(pl.multiple_of(i * CHUNK, CHUNK), CHUNK)
                    spot = lax.broadcasted_iota(jnp.int32, (CHUNK, 128), 1)
                    level = jnp.sum(
                        jnp.where(spot == head, lse_in[at], 0.0), axis=1, keepdims=True
                    )
                    wide = jnp.exp(sbuf[at, :far] + mask[at, :far] - level)
                    tight = jnp.exp(
                        sbuf[at, far:] + mask[at, far:] + pltpu.roll(slope, i * CHUNK, 1) - level
                    )
                    pbuf[at, :far] = wide.astype(jnp.bfloat16)
                    pbuf[at, far:] = tight.astype(jnp.bfloat16)
                    d_wide = wide * dbuf[at, :far]
                    d_tight = tight * dbuf[at, far:]
                    delta = jnp.sum(d_wide, axis=1, keepdims=True) + jnp.sum(
                        d_tight, axis=1, keepdims=True
                    )
                    d_wide = d_wide - wide * delta
                    d_tight = d_tight - tight * delta
                    gbuf[at, :far] = d_wide.astype(jnp.bfloat16)
                    gbuf[at, far:] = d_tight.astype(jnp.bfloat16)
                    near_out[head] = near_out[head] + pltpu.roll(
                        d_tight, lax.rem(band - i * CHUNK, band), 1
                    )
                    summed = d_wide[:, :128]
                    for piece in range(1, far // 128):
                        summed = summed + d_wide[:, piece * 128 : (piece + 1) * 128]
                    far_out[head] = far_out[head] + summed
                    return inner

                lax.fori_loop(0, count // CHUNK, soft, 0, unroll=2)
                grads, probs = gbuf[...], pbuf[...]
                dq_parts.append(dot32(grads, k_pair))
                dk_half = tn(grads, q_one)
                dv_half = tn(probs, do_one)
                dk = dk_half if dk is None else dk + dk_half
                dv = dv_half if dv is None else dv + dv_half
            dq = jnp.where(lane < HEAD, dq_parts[0], dq_parts[1]) * (1.0 / math.sqrt(HEAD))
            dq_out[:, two] = dq.astype(jnp.bfloat16)
            dk_out[:, two] = dk.astype(jnp.bfloat16)
            dv_out[:, two] = dv.astype(jnp.bfloat16)
            return carry

        lax.fori_loop(0, width // (2 * HEAD), pair_step, 0)

    low = jnp.bfloat16
    return pl.pallas_call(
        kernel,
        name="attend_backward",
        out_shape=(
            jax.ShapeDtypeStruct((count, width), low),
            jax.ShapeDtypeStruct((length, width), low),
            jax.ShapeDtypeStruct((length, width), low),
            jax.ShapeDtypeStruct((heads, CHUNK, band), jnp.float32),
            jax.ShapeDtypeStruct((heads, CHUNK, 128), jnp.float32),
        ),
        in_specs=[pl.BlockSpec(memory_space=VMEM)] * 8,
        out_specs=[pl.BlockSpec(memory_space=VMEM)] * 5,
        scratch_shapes=[
            VMEM((count, length), jnp.float32),
            VMEM((count, length), jnp.float32),
            VMEM((count, length), low),
            VMEM((count, length), low),
            VMEM((count, length), jnp.float32),
        ],
        compiler_params=pltpu.CompilerParams(vmem_limit_bytes=56 * 1024 * 1024),
    )(q_all, k_all, v_all, do_all, lse, query_seg, key_code, slopes)


def per_device(
    tokens,
    segments,
    valid,
    routes,
    teacher,
    norm_attn,
    w_query,
    w_key,
    w_value,
    output_weight,
    rel_bias,
    norm_ffn,
    w_router,
    w_gate,
    w_up,
    w_down,
):
    nc = lax.axis_size("ctx")
    ns = lax.axis_size("shard")
    c, s = lax.axis_index("ctx"), lax.axis_index("shard")
    n_dev, nj = nc * ns, ns // 2
    row_count, width = tokens.shape[1:]
    top_count = routes.shape[2]
    experts = w_router.shape[1]
    capacity = (5 * row_count * top_count + 4 * experts - 1) // (4 * experts)
    length = row_count * nc
    low = jnp.bfloat16
    f32 = jnp.float32
    piece = w_query.shape[0]
    band = 2 * row_count

    smalls = (norm_attn, norm_ffn, rel_bias, w_router.reshape(-1))
    sizes = [x.shape[0] for x in smalls]
    head_row = jnp.concatenate(smalls + (jnp.zeros((width - sum(sizes),), low),))
    marks = jnp.concatenate(
        (
            segments[0].astype(low),
            valid[0].astype(low),
            jnp.zeros((width - 2 * row_count,), low),
        )
    )
    extra = jnp.concatenate(
        (head_row[None], marks[None], jnp.zeros((EXTRA - 2, width), low)), axis=0
    )
    weights, extras, tokens_all = gather_all(
        jnp.stack((w_query, w_key, w_value, output_weight)), extra, tokens[0], nc, ns
    )
    starts = [sum(sizes[:i]) for i in range(len(sizes))]
    gain_attn, gain_ffn, full_bias, full_router = (
        extras[:, 0, begin : begin + size].reshape(-1) for begin, size in zip(starts, sizes)
    )
    full_router = full_router.reshape(width, experts)
    table = full_bias.reshape(BUCKETS, HEADS).astype(f32)
    line_marks = lax.dynamic_slice_in_dim(extras.reshape(nc, ns, EXTRA, width), s, 1, 1)[:, 0, 1]
    line_marks = jnp.roll(line_marks, -(c + 1), axis=0)
    slot = jnp.arange(nc, dtype=jnp.int32)[:, None]
    past = slot >= nc - 1 - c
    line_seg = line_marks[:, :row_count].astype(jnp.int32)
    line_valid = line_marks[:, row_count : 2 * row_count] > 0
    key_code = jnp.where(line_valid & past, line_seg, -1).reshape(1, length)
    query_seg = segments[0][:, None]
    valid_count = jnp.sum(extras[:, 1, row_count : 2 * row_count].astype(f32))

    spot = (jnp.arange(band)[None, :] - jnp.arange(CHUNK)[:, None]) % band
    distance = jnp.where(spot <= row_count, row_count - spot, 3 * row_count - spot)
    level = bucket_of(distance, BUCKETS)
    level_hot = (level[:, :, None] == jnp.arange(BUCKETS)[None, None, :]).astype(f32)
    slopes = jnp.einsum(
        "ixb,bh->hix", level_hot, table - table[BUCKETS - 1 :], precision=highest_precision
    )

    gain_one = gain_attn.astype(f32)
    first_all, queries, keys, values, mixed_low, log_total, residual = attend_forward(
        tokens_all, weights, gain_one[None], query_seg, key_code, slopes
    )
    gain_two = gain_ffn.astype(f32)
    ffn_low = rms_norm(residual, gain_two).astype(low)
    ffn_in = ffn_low.astype(f32)
    router = full_router.astype(f32)
    logits = jnp.dot(ffn_in, router, precision=highest_precision)
    route_local = routes[0]
    expert_ids = jnp.arange(experts, dtype=jnp.int32)
    route_hot = route_local[:, :, None] == expert_ids[None, None, :]
    picked = jnp.sum(jnp.where(route_hot, logits[:, None, :], 0.0), axis=-1)
    gate_probs = jax.nn.softmax(picked, axis=-1)
    flat_routes = route_local.reshape(row_count * top_count)
    route_hits = (flat_routes[:, None] == expert_ids[None, :]).astype(jnp.int32)
    before = jnp.cumsum(route_hits, axis=0) - route_hits
    slot_rank = jnp.sum(before * route_hits, axis=1)
    target = (flat_routes * capacity + slot_rank).reshape(row_count, top_count)
    slot_ids = jnp.arange(experts * capacity, dtype=jnp.int32)
    pick_first = (slot_ids[:, None] == target[None, :, 0]).astype(low)
    pick_second = (slot_ids[:, None] == target[None, :, 1]).astype(low)

    def exchange(rows):
        return lax.all_to_all(
            rows.reshape(experts, capacity, width), "shard", split_axis=0, concat_axis=0, tiled=True
        ).reshape(experts * capacity, width)

    expert_rows = exchange(dot32(pick_first + pick_second, ffn_low).astype(low))
    gate_w, up_w, down_w = w_gate[0], w_up[0], w_down[0]
    gate_pre = dot32(expert_rows, gate_w)
    up_pre = dot32(expert_rows, up_w)

    def activation(gate_values, up_values):
        return jax.nn.gelu(gate_values) * up_values

    inner_value, activation_back = jax.vjp(activation, gate_pre, up_pre)
    inner = inner_value.astype(low)
    returned = exchange(dot32(inner, down_w).astype(low))
    picked_one, picked_two = tn(pick_first, returned), tn(pick_second, returned)
    output_sum = residual + gate_probs[:, :1] * picked_one + gate_probs[:, 1:] * picked_two
    valid_one = valid[0].astype(f32)
    deviation = output_sum - teacher[0].astype(f32)
    local_square = jnp.sum(valid_one[:, None] * deviation * deviation)
    everything = float(row_count * nc * ns)
    cotangent = everything / valid_count * deviation * valid_one[:, None]
    gate_grad = jnp.stack(
        (jnp.sum(cotangent * picked_one, axis=-1), jnp.sum(cotangent * picked_two, axis=-1)), axis=1
    )
    back_send = dot32(pick_first, (gate_probs[:, :1] * cotangent).astype(low)) + dot32(
        pick_second, (gate_probs[:, 1:] * cotangent).astype(low)
    )
    out_grad = exchange(back_send.astype(low))
    inner_grad = nt(out_grad, down_w)
    gate_pre_grad, up_pre_grad = activation_back(inner_grad)
    gate_low = gate_pre_grad.astype(low)
    up_low = up_pre_grad.astype(low)
    sent_back = exchange((nt(gate_low, gate_w) + nt(up_low, up_w)).astype(low))
    down_w_grad = tn(inner, out_grad).astype(low)
    gate_w_grad = tn(expert_rows, gate_low).astype(low)
    up_w_grad = tn(expert_rows, up_low).astype(low)
    gate_w_sum, up_w_sum, down_w_sum = (
        lax.psum_scatter(x[None], "ctx", scatter_dimension=1, tiled=True).astype(f32)
        for x in (gate_w_grad, up_w_grad, down_w_grad)
    )
    ffn_grad = tn(pick_first + pick_second, sent_back)
    pick_grad = gate_probs * (gate_grad - jnp.sum(gate_probs * gate_grad, axis=-1, keepdims=True))
    logits_grad = jnp.sum(jnp.where(route_hot, pick_grad[:, :, None], 0.0), axis=1)
    router_grad = contract(ffn_in, logits_grad, 0, 0, highest_precision)
    ffn_grad = ffn_grad + contract(logits_grad, router, 1, 1, highest_precision)
    unused, norm_two_back = jax.vjp(rms_norm, residual, gain_two)
    residual_from_norm, gain_two_grad = norm_two_back(ffn_grad)
    residual_grad = cotangent + residual_from_norm
    attn_grad_low = residual_grad.astype(low)
    out_w_grad = tn(mixed_low, attn_grad_low)
    mixed_grad = nt(attn_grad_low, weights[3]).astype(low)

    query_grad, key_grad, value_grad, near_sum, far_sum = attend_backward(
        queries, keys, values, mixed_grad, log_total, query_seg, key_code, slopes
    )
    bias_grad = jnp.einsum("hix,ixb->bh", near_sum, level_hot, precision=highest_precision)
    last_bucket = (jnp.arange(BUCKETS) == BUCKETS - 1).astype(f32)
    bias_grad = bias_grad + last_bucket[:, None] * jnp.sum(far_sum, axis=(1, 2))[None, :]
    first_own = first_all[length - row_count :]
    query_w_grad = tn(first_own, query_grad)
    key_w_grad = tn(first_all, key_grad)
    value_w_grad = tn(first_all, value_grad)
    hidden_grad = nt(key_grad, weights[1]) + nt(value_grad, weights[2])
    hidden_own = hidden_grad[length - row_count :] + nt(query_grad, weights[0])
    hidden_terms = jnp.concatenate((hidden_grad[: length - row_count], hidden_own), axis=0)
    inputs_all = tokens_all.astype(f32)
    rates_all = lax.rsqrt(jnp.mean(inputs_all * inputs_all, axis=-1, keepdims=True) + epsilon)
    gain_one_grad = jnp.sum(hidden_terms * inputs_all * rates_all, axis=0)

    small_grads = jnp.concatenate(
        [
            x.reshape(n_dev, -1).astype(low)
            for x in (gain_one_grad, gain_two_grad, bias_grad, router_grad)
        ],
        axis=1,
    )
    small_grads = jnp.pad(small_grads, ((0, 0), (0, width - small_grads.shape[1])))
    stacked = jnp.concatenate(
        [
            x.astype(low).reshape(n_dev, piece, width)
            for x in (query_w_grad, key_w_grad, value_w_grad, out_w_grad)
        ]
        + [jnp.pad(small_grads[:, None], ((0, 0), (0, EXTRA - 1), (0, 0)))],
        axis=1,
    ).reshape(nc, nj, 2, 4 * piece + EXTRA, width)
    squares = jnp.full((8, 128), local_square, f32)
    summed, square_sum, hidden_sum = reduce_all(
        stacked, squares, hidden_grad.astype(low).reshape(nc, row_count, width), hidden_own, nc, ns
    )
    loss_value = square_sum[0, 0] / (2.0 * width * valid_count)
    inputs = inputs_all[length - row_count :]
    rate = rates_all[length - row_count :]
    scaled = hidden_sum * gain_one
    input_grad = (
        residual_grad
        + rate * scaled
        - inputs * (rate * rate * rate) * jnp.mean(scaled * inputs, axis=-1, keepdims=True)
    )
    tail = summed[4 * piece]
    tails = [tail[begin : begin + size] for begin, size in zip(starts, sizes)]
    return (
        output_sum.astype(low)[None],
        loss_value,
        input_grad[None],
        tails[0],
        summed[:piece],
        summed[piece : 2 * piece],
        summed[2 * piece : 3 * piece],
        summed[3 * piece : 4 * piece],
        tails[2],
        tails[1],
        tails[3].reshape(w_router.shape),
        gate_w_sum,
        up_w_sum,
        down_w_sum,
    )


def solution(mesh):
    return jax.shard_map(
        per_device,
        mesh=mesh,
        in_specs=(
            P("shard", "ctx", None),
            P("shard", "ctx"),
            P("shard", "ctx"),
            P("shard", "ctx", None),
            P("shard", "ctx", None),
            P(("ctx", "shard")),
            P(("ctx", "shard"), None),
            P(("ctx", "shard"), None),
            P(("ctx", "shard"), None),
            P(("ctx", "shard"), None),
            P(("ctx", "shard")),
            P(("ctx", "shard")),
            P(("ctx", "shard"), None),
            P("shard", None, None),
            P("shard", None, None),
            P("shard", None, None),
        ),
        out_specs=(
            P("shard", "ctx", None),
            P(),
            P("shard", "ctx", None),
            P(("ctx", "shard")),
            P(("ctx", "shard"), None),
            P(("ctx", "shard"), None),
            P(("ctx", "shard"), None),
            P(("ctx", "shard"), None),
            P(("ctx", "shard")),
            P(("ctx", "shard")),
            P(("ctx", "shard"), None),
            P("shard", "ctx", None),
            P("shard", "ctx", None),
            P("shard", "ctx", None),
        ),
        check_vma=False,
    )
```

```python
import math

import jax
import jax.numpy as jnp
from jax import lax
from jax.experimental import pallas as pl
from jax.experimental.pallas import tpu as pltpu
from jax.sharding import PartitionSpec as P

HEADS = 16
HEAD = 64
BUCKETS = 32
MESH = pl.DeviceIdType.MESH
ANY = pl.ANY
VMEM = pltpu.VMEM
SEM = pltpu.SemaphoreType

highest_precision = lax.Precision.HIGHEST
max_distance = 128
epsilon = 1e-06
negative = -1e30
EXTRA = 16


def thresholds(buckets):
    exact_count = buckets // 2
    limits = list(range(1, exact_count))
    for bucket_level in range(exact_count, buckets):
        power = (bucket_level - exact_count) / exact_count
        limits.append(int(math.ceil(exact_count * (max_distance / exact_count) ** power)))
    return limits


def bucket_of(distance, buckets):
    bucket_total = jnp.zeros(distance.shape, jnp.int32)
    for threshold in thresholds(buckets):
        bucket_total = bucket_total + (distance >= threshold).astype(jnp.int32)
    return bucket_total


def rms_norm(values, gain_vector):
    return (
        values
        * lax.rsqrt(jnp.mean(values * values, axis=-1, keepdims=True) + epsilon)
        * gain_vector
    )


def contract(left_side, right_side, left_axis, right_axis, precision_mode=None):
    return lax.dot_general(
        left_side,
        right_side,
        (((left_axis,), (right_axis,)), ((), ())),
        precision=precision_mode,
        preferred_element_type=jnp.float32,
    )


def dot32(left_side, right_side):
    return jnp.dot(left_side, right_side, preferred_element_type=jnp.float32)


def nt(left_side, right_side):
    return contract(left_side, right_side, 1, 1)


def tn(left_side, right_side):
    return contract(left_side, right_side, 0, 0)


class Place:
    def __init__(self, nc, ns):
        self.nc, self.ns, self.nj = nc, ns, ns // 2
        self.c = lax.axis_index("ctx")
        self.s = lax.axis_index("shard")
        self.core = self.s % 2
        self.j = self.s // 2

    def along(self, d):
        return (lax.rem(self.c + d + self.nc, self.nc), self.s)

    def across(self, k):
        return (self.c, self.s ^ (2 * k))

    def twin(self):
        return (self.c, self.s ^ 1)

    def greet(self):
        barrier = pltpu.get_barrier_semaphore()
        partners = (
            [self.along(d) for d in range(1, self.nc)]
            + [self.across(k) for k in range(1, self.nj)]
            + [self.twin()]
        )
        for partner in partners:
            pl.semaphore_signal(barrier, inc=1, device_id=partner, device_id_type=MESH)
        pl.semaphore_wait(barrier, len(partners))


def remote(source, target, send, recv, device):
    return pltpu.make_async_remote_copy(
        src_ref=source,
        dst_ref=target,
        send_sem=send,
        recv_sem=recv,
        device_id=device,
        device_id_type=MESH,
    )


def gather_all(weights, extra, rows, nc, ns):
    n_dev, nj = nc * ns, ns // 2
    share = weights.shape[1:]
    full_shape = (share[0], nc, ns) + share[1:]

    def kernel(w_in, e_in, t_in, w_out, e_out, t_out, local, zs, zr, xs, xr, cs, cr, ts, tr):
        me = Place(nc, ns)

        def views(row, column):
            return (w_out.at[:, row, column], e_out.at[row, column])

        def piece(d, k):
            return views(lax.rem(me.c - d + nc, nc), me.s ^ (2 * k))

        mine = (w_in.at[me.c], e_in)
        locals_ = [
            pltpu.make_async_copy(source, target, local.at[i])
            for i, (source, target) in enumerate(
                zip(mine + (t_in,), views(me.c, me.s) + (t_out.at[me.c],))
            )
        ]
        for copy in locals_:
            copy.start()
        me.greet()
        sent = []

        def push(sources, targets, send, recv, device):
            for i in range(2):
                copy = remote(sources[i], targets[i], send.at[i], recv.at[i], device)
                copy.start()
                sent.append(copy)

        def arrive(targets, send, recv, device):
            for i in range(2):
                remote(targets[i], targets[i], send.at[i], recv.at[i], device).wait_recv()

        def token_copy(direction, hop):
            lane = 0 if direction > 0 else 1
            origin = lax.rem(me.c - direction * hop + nc, nc)
            return remote(
                t_in if hop == 0 else t_out.at[origin],
                t_out.at[origin],
                ts.at[lane, hop],
                tr.at[lane, hop],
                (lax.rem(me.c + direction + nc, nc), me.s),
            )

        def token_landing(direction, hop):
            lane = 0 if direction > 0 else 1
            origin = lax.rem(me.c - direction * (hop + 1) + nc, nc)
            landing = t_out.at[origin]
            return remote(landing, landing, ts.at[lane, hop], tr.at[lane, hop], me.along(1))

        def can_send(direction, hop):
            if direction > 0:
                return (me.c >= hop) & (me.c < nc - 1)
            return (me.c <= nc - 1 - hop) & (me.c > 0)

        def can_receive(direction, hop):
            if direction > 0:
                return me.c >= hop + 1
            return me.c <= nc - 2 - hop

        for d in range(1, nc):
            target = lax.rem(me.c + d, nc)
            push(
                (w_in.at[target], e_in), views(me.c, me.s), zs.at[d], zr.at[d], (target, me.s)
            )
        for direction in (1, -1):

            @pl.when(can_send(direction, 0))
            def _():
                token_copy(direction, 0).start()

        for k in range(1, nj):
            push(mine, views(me.c, me.s), xs.at[0, k], xr.at[0, k], me.across(k))
        push(mine, views(me.c, me.s), cs.at[0, 0], cr.at[0, 0], me.twin())

        for copy in locals_:
            copy.wait()
        for d in range(1, nc):
            here = piece(d, 0)
            arrive(here, zs.at[d], zr.at[d], me.along(-d))
            for k in range(1, nj):
                push(here, here, xs.at[d, k], xr.at[d, k], me.across(k))
            push(here, here, cs.at[d, 0], cr.at[d, 0], me.twin())
        for d in range(nc):
            for k in range(1, nj):
                here = piece(d, k)
                arrive(here, xs.at[d, k], xr.at[d, k], me.across(k))
                push(here, here, cs.at[d, k], cr.at[d, k], me.twin())
            if d < nc - 2:
                for direction in (1, -1):

                    @pl.when(can_receive(direction, d))
                    def _():
                        token_landing(direction, d).wait_recv()

                    @pl.when(can_send(direction, d + 1))
                    def _():
                        token_copy(direction, d + 1).start()

        for d in range(nc):
            for k in range(nj):
                here = views(lax.rem(me.c - d + nc, nc), me.s ^ 1 ^ (2 * k))
                arrive(here, cs.at[d, k], cr.at[d, k], me.twin())
        for direction in (1, -1):

            @pl.when(can_receive(direction, nc - 2))
            def _():
                token_landing(direction, nc - 2).wait_recv()

        for copy in sent:
            copy.wait_send()
        for direction in (1, -1):
            for hop in range(nc - 1):

                @pl.when(can_send(direction, hop))
                def _():
                    token_copy(direction, hop).wait_send()

    full, extras, tokens = pl.pallas_call(
        kernel,
        name="gather_all",
        out_shape=(
            jax.ShapeDtypeStruct(full_shape, weights.dtype),
            jax.ShapeDtypeStruct((nc, ns) + extra.shape, extra.dtype),
            jax.ShapeDtypeStruct((nc,) + rows.shape, rows.dtype),
        ),
        in_specs=[pl.BlockSpec(memory_space=ANY)] * 3,
        out_specs=[pl.BlockSpec(memory_space=ANY)] * 3,
        scratch_shapes=[
            SEM.DMA((3,)),
            SEM.DMA((nc, 2)),
            SEM.DMA((nc, 2)),
            SEM.DMA((nc, nj, 2)),
            SEM.DMA((nc, nj, 2)),
            SEM.DMA((nc, nj, 2)),
            SEM.DMA((nc, nj, 2)),
            SEM.DMA((2, nc)),
            SEM.DMA((2, nc)),
        ],
        compiler_params=pltpu.CompilerParams(collective_id=1, has_side_effects=True),
    )(weights, extra, rows)
    return (
        full.reshape(share[0], n_dev * share[1], share[2]),
        extras,
        tokens.reshape(nc * rows.shape[0], rows.shape[1]),
    )


def reduce_all(grads, small, squares, nc, ns, kept):
    nj = ns // 2
    parts, piece, width = grads.shape[0], grads.shape[4], grads.shape[5]
    low = grads.dtype
    tile = squares.shape

    def kernel(g_in, e_in, q_in, k_out, g_out, e_out, q_out,
               gt, et, gc, ec, gx, ex, gz, ez, qz, qx, qc, qa, qb,
               cs, cr, xs, xr, zs, zr, q1s, q1r, q2s, q2r, q3s, q3r):
        me = Place(nc, ns)
        me.greet()

        def both(pairs, send, recv, device):
            return [
                remote(source, target, send.at[i], recv.at[i], device)
                for i, (source, target) in enumerate(pairs)
            ]

        def core_copy(d):
            row = lax.rem(me.c + d, nc)
            other = 1 - me.core
            return both(
                ((g_in.at[:, row, :, other], gc.at[d]), (e_in.at[row, :, other], ec.at[d])),
                cs.at[d], cr.at[d], me.twin(),
            )

        def cross_copy(d, k):
            return both(
                ((gt.at[d, :, me.j ^ k], gx.at[d, k - 1]), (et.at[d, me.j ^ k], ex.at[d, k - 1])),
                xs.at[d, k], xr.at[d, k], me.across(k),
            )

        def along_copy(d):
            return both(
                ((gt.at[d, :, me.j], gz.at[d - 1]), (et.at[d, me.j], ez.at[d - 1])),
                zs.at[d], zr.at[d], me.along(d),
            )

        def start(copies):
            for copy in copies:
                copy.start()

        def landed(copies):
            for copy in copies:
                copy.wait_recv()

        def q_along(d):
            return remote(q_in, qz.at[d - 1], q1s.at[d], q1r.at[d], me.along(d))

        def q_across(k):
            return remote(qa, qx.at[k - 1], q2s.at[k], q2r.at[k], me.across(k))

        q_twin = remote(qb, qc, q3s.at[0], q3r.at[0], me.twin())
        order = list(range(1, nc)) + [0]
        for d in order:
            start(core_copy(d))
        for d in range(1, nc):
            q_along(d).start()

        for d in order:
            landed(core_copy(d))
            row = lax.rem(me.c + d, nc)

            def add_core(i, carry):
                for k in range(nj):
                    gt[d, i, k] = (
                        g_in[i, row, k, me.core].astype(jnp.float32)
                        + gc[d, i, k].astype(jnp.float32)
                    ).astype(low)
                return carry

            lax.fori_loop(0, parts, add_core, 0)
            for k in range(nj):
                et[d, k] = (
                    e_in[row, k, me.core].astype(jnp.float32) + ec[d, k].astype(jnp.float32)
                ).astype(low)
            for k in range(1, nj):
                start(cross_copy(d, k))
        for d in range(1, nc):
            q_along(d).wait_recv()
        value = q_in[...]
        for d in range(1, nc):
            value = value + qz[d - 1]
        qa[...] = value
        for k in range(1, nj):
            q_across(k).start()
        for d in order:
            for k in range(1, nj):
                landed(cross_copy(d, k))

            def add_cross(i, carry):
                value = gt[d, i, me.j].astype(jnp.float32)
                for k in range(1, nj):
                    value = value + gx[d, k - 1, i].astype(jnp.float32)
                if d == 0:
                    g_out[i] = value
                else:
                    gt[d, i, me.j] = value.astype(low)
                return carry

            lax.fori_loop(0, parts, add_cross, 0)
            value = et[d, me.j].astype(jnp.float32)
            for k in range(1, nj):
                value = value + ex[d, k - 1].astype(jnp.float32)
            if d:
                et[d, me.j] = value.astype(low)
                start(along_copy(d))
            else:
                e_out[...] = value
        for k in range(1, nj):
            q_across(k).wait_recv()
        value = qa[...]
        for k in range(1, nj):
            value = value + qx[k - 1]
        qb[...] = value
        q_twin.start()
        for i in range(kept):
            k_out[i, me.c] = g_out[i]
        for d in range(1, nc):
            landed(along_copy(d))
            row = lax.rem(me.c - d + nc, nc)
            for i in range(kept):
                k_out[i, row] = gz[d - 1, i].astype(jnp.float32)
            e_out[...] = e_out[...] + ez[d - 1].astype(jnp.float32)

        def add_along(i, carry):
            value = g_out[i]
            for d in range(1, nc):
                value = value + gz[d - 1, i].astype(jnp.float32)
            g_out[i] = value
            return carry

        lax.fori_loop(kept, parts, add_along, 0)
        q_twin.wait()
        q_out[...] = qb[...] + qc[...]
        for d in order:
            started = core_copy(d) + [copy for k in range(1, nj) for copy in cross_copy(d, k)]
            if d:
                started = started + along_copy(d) + [q_along(d)]
            for copy in started:
                copy.wait_send()
        for k in range(1, nj):
            q_across(k).wait_send()

    f32 = jnp.float32
    one, extra = (parts, piece, width), small.shape[3:]
    return pl.pallas_call(
        kernel,
        name="reduce_all",
        out_shape=(
            jax.ShapeDtypeStruct((kept, nc, piece, width), f32),
            jax.ShapeDtypeStruct(one, f32),
            jax.ShapeDtypeStruct(extra, f32),
            jax.ShapeDtypeStruct(tile, f32),
        ),
        in_specs=[pl.BlockSpec(memory_space=VMEM)] * 3,
        out_specs=[pl.BlockSpec(memory_space=VMEM)] * 4,
        scratch_shapes=[
            VMEM((nc, parts, nj, piece, width), low),
            VMEM((nc, nj) + extra, low),
            VMEM((nc, parts, nj, piece, width), low),
            VMEM((nc, nj) + extra, low),
            VMEM((nc, nj - 1) + one, low),
            VMEM((nc, nj - 1) + extra, low),
            VMEM((nc - 1,) + one, low),
            VMEM((nc - 1,) + extra, low),
            VMEM((nc - 1,) + tile, f32),
            VMEM((nj - 1,) + tile, f32),
            VMEM(tile, f32),
            VMEM(tile, f32),
            VMEM(tile, f32),
            SEM.DMA((nc, 2)),
            SEM.DMA((nc, 2)),
            SEM.DMA((nc, nj, 2)),
            SEM.DMA((nc, nj, 2)),
            SEM.DMA((nc, 2)),
            SEM.DMA((nc, 2)),
            SEM.DMA((nc,)),
            SEM.DMA((nc,)),
            SEM.DMA((nj,)),
            SEM.DMA((nj,)),
            SEM.DMA((1,)),
            SEM.DMA((1,)),
        ],
        compiler_params=pltpu.CompilerParams(
            collective_id=2, has_side_effects=True, vmem_limit_bytes=56 * 1024 * 1024
        ),
    )(grads, small, squares)


CHUNK = 16


def fill_mask(mask, query_code, key_code, block, count):
    near = block * count
    query = query_code[pl.ds(near, count)]
    if block:
        mask[:, :near] = jnp.where(query == key_code[:, :near], 0.0, negative)
    row = lax.broadcasted_iota(jnp.int32, (count, count), 0)
    column = lax.broadcasted_iota(jnp.int32, (count, count), 1)
    seen = ((query == key_code[:, near : near + count]) & (row >= column)) | (row == column)
    mask[:, near : near + count] = jnp.where(seen, 0.0, negative)


def fill_slopes(bank, slopes, head, count):
    for i in range(count // CHUNK):
        row = slopes[head]
        bank[head, i * CHUNK : (i + 1) * CHUNK] = pltpu.roll(row, i * CHUNK, 1) if i else row


def biased(scores, mask, slope, block, count):
    end = (block + 1) * count
    band = 2 * count
    if end < band:
        return scores + mask[:, :end] + slope[:, band - end :]
    if end == band:
        return scores + mask[:, :end] + slope[...]
    wide = scores[:, : end - band] + mask[:, : end - band]
    tight = scores[:, end - band :] + mask[:, end - band : end] + slope[...]
    return jnp.concatenate((wide, tight), axis=1)


def attend_forward(tokens, weights, gain, gain_next, query_code, key_code, slopes, nc, ns):
    length, width = tokens.shape
    count = length // nc
    part = width // nc
    heads, _, band = slopes.shape
    low, f32 = jnp.bfloat16, jnp.float32

    def kernel(t_in, w_in, gain_in, next_in, qcode, kcode, toe, first, q_out, k_out, v_out, o_out, lse_out, x_out, y_out,
               mask, bank, osend, ss, rs):
        me = Place(nc, ns)
        barrier = pltpu.get_barrier_semaphore()
        for d in range(1, nc):
            pl.semaphore_signal(barrier, inc=1, device_id=me.along(d), device_id_type=MESH)
        pl.semaphore_wait(barrier, nc - 1)

        def norm(i, carry):
            at = pl.ds(pl.multiple_of(i * 64, 64), 64)
            x = t_in[at].astype(f32)
            rate = lax.rsqrt(jnp.mean(x * x, axis=-1, keepdims=True) + epsilon)
            first[at] = (x * rate * gain_in[...]).astype(low)
            return carry

        lax.fori_loop(0, length // 64, norm, 0)

        def project(i, carry):
            at = pl.ds(pl.multiple_of(i * count, count), count)
            block = first[at]
            q_out[at] = dot32(block, w_in[0]).astype(low)
            k_out[at] = dot32(block, w_in[1]).astype(low)
            v_out[at] = dot32(block, w_in[2]).astype(low)
            return carry

        lax.fori_loop(0, nc, project, 0)
        for head in range(heads):
            fill_slopes(bank, toe, head, count)
        lane = lax.broadcasted_iota(jnp.int32, (count, 2 * HEAD), 1)
        spot = lax.broadcasted_iota(jnp.int32, (count, 128), 1)
        own_copy = [
            remote(osend.at[b], o_out.at[me.c], ss.at[b], rs.at[me.c], (b, me.s)) for b in range(nc)
        ]
        for b in reversed(range(nc)):
            end = (b + 1) * count
            rows = pl.ds(b * count, count)
            fill_mask(mask, qcode, kcode, b, count)
            level = jnp.zeros((count, 128), f32)
            for pair in range(heads // 2):
                two = slice(pair * 2 * HEAD, (pair + 1) * 2 * HEAD)
                q_pair = q_out[rows, two] * low(1.0 / math.sqrt(HEAD))
                k_pair = k_out[:end, two]
                v_pair = v_out[:end, two]
                halves = []
                for half in range(2):
                    head = pair * 2 + half
                    inside = (lane >= HEAD) if half else (lane < HEAD)
                    scores = nt(jnp.where(inside, q_pair, low(0)), k_pair)
                    scores = biased(scores, mask, bank.at[head], b, count)
                    top = jnp.max(scores, axis=1, keepdims=True)
                    scores = jnp.exp(scores - top)
                    total = jnp.sum(scores, axis=1, keepdims=True)
                    halves.append(dot32(scores.astype(low), v_pair) * (1.0 / total))
                    level = jnp.where(spot == head, top + jnp.log(total), level)
                osend[b, :, two] = jnp.where(lane < HEAD, halves[0], halves[1]).astype(low)
            lse_out[rows] = level

            @pl.when(me.c == b)
            def _():
                o_out[me.c] = osend[b]

            @pl.when(me.c != b)
            def _():
                own_copy[b].start()

        for d in range(1, nc):
            origin = lax.rem(me.c + d, nc)
            remote(
                osend.at[0], o_out.at[origin], ss.at[0], rs.at[origin], me.along(d)
            ).wait_recv()
        own = pl.ds(pl.multiple_of(me.c * count, count), count)
        squares = jnp.zeros((count, 1), f32)
        for n in range(nc):
            columns = slice(n * part, (n + 1) * part)
            x = t_in[own, columns].astype(f32)
            for origin in range(nc):
                x = x + dot32(o_out[origin], w_in[3 + n, origin * part : (origin + 1) * part])
            x_out[:, columns] = x
            squares = squares + jnp.sum(x * x, axis=1, keepdims=True)
        rate = lax.rsqrt(squares * (1.0 / width) + epsilon)
        for n in range(nc):
            columns = slice(n * part, (n + 1) * part)
            y_out[:, columns] = (x_out[:, columns] * rate * next_in[:, columns]).astype(low)
        for b in range(nc):

            @pl.when(me.c != b)
            def _():
                own_copy[b].wait_send()

    return pl.pallas_call(
        kernel,
        name="attend_forward",
        out_shape=(
            jax.ShapeDtypeStruct((length, width), low),
            jax.ShapeDtypeStruct((length, part), low),
            jax.ShapeDtypeStruct((length, part), low),
            jax.ShapeDtypeStruct((length, part), low),
            jax.ShapeDtypeStruct((nc, count, part), low),
            jax.ShapeDtypeStruct((length, 128), f32),
            jax.ShapeDtypeStruct((count, width), f32),
            jax.ShapeDtypeStruct((count, width), low),
        ),
        in_specs=[pl.BlockSpec(memory_space=VMEM)] * 7,
        out_specs=[pl.BlockSpec(memory_space=VMEM)] * 8,
        scratch_shapes=[
            VMEM((count, length), f32),
            VMEM((heads, count, band), f32),
            VMEM((nc, count, part), low),
            SEM.DMA((nc,)),
            SEM.DMA((nc,)),
        ],
        compiler_params=pltpu.CompilerParams(
            collective_id=3, has_side_effects=True, vmem_limit_bytes=56 * 1024 * 1024
        ),
    )(tokens, weights, gain, gain_next, query_code, key_code, slopes)


def attend_backward(
    dattn, dh, o_all, tokens, first, q_all, k_all, v_all, lse, weights, gain, query_code, key_code, slopes, nc, ns
):
    length, width = tokens.shape
    count = length // nc
    part = width // nc
    heads, _, band = slopes.shape
    low, f32 = jnp.bfloat16, jnp.float32
    scale = 1.0 / math.sqrt(HEAD)

    def kernel(a_in, dh_in, o_in, t_in, first_in, q_in, k_in, v_in, lse_in, w_in, gain_in, qcode, kcode, toe,
               x_out, w_out, gain_out, near_out, far_out,
               mask, bank, dsend, dall, dq, dk, dv, fsend, frecv, fown, ss, rs, fs, fr):
        me = Place(nc, ns)
        barrier = pltpu.get_barrier_semaphore()
        for d in range(1, nc):
            pl.semaphore_signal(barrier, inc=1, device_id=me.along(d), device_id_type=MESH)
        pl.semaphore_wait(barrier, nc - 1)

        def do_copy(d):
            return remote(dsend.at[d], dall.at[me.c], ss.at[d], rs.at[d], me.along(d))

        for d in list(range(1, nc)) + [0]:
            target = lax.rem(me.c + d, nc)
            at = pl.ds(pl.multiple_of(target * part, part), part)
            value = nt(a_in[:, :part], w_in[3, at])
            for n in range(1, nc):
                value = value + nt(a_in[:, n * part : (n + 1) * part], w_in[3 + n, at])
            if d:
                dsend[d] = value.astype(low)
                do_copy(d).start()
            else:
                dall[me.c] = value.astype(low)
        for n in range(nc):
            for origin in range(nc):
                w_out[3 + n, origin * part : (origin + 1) * part] = tn(
                    o_in[origin], a_in[:, n * part : (n + 1) * part]
                ).astype(low)
        for head in range(heads):
            fill_slopes(bank, toe, head, count)
        lane = lax.broadcasted_iota(jnp.int32, (count, 2 * HEAD), 1)
        spot = lax.broadcasted_iota(jnp.int32, (count, 128), 1)
        dk[...] = jnp.zeros_like(dk)
        dv[...] = jnp.zeros_like(dv)
        near_out[...] = jnp.zeros_like(near_out)
        far_out[...] = jnp.zeros_like(far_out)
        gain_out[...] = jnp.zeros_like(gain_out)
        for d in range(1, nc):
            origin = lax.rem(me.c - d + nc, nc)
            remote(dsend.at[d], dall.at[origin], ss.at[d], rs.at[d], me.along(d)).wait_recv()
        out_copy = [
            remote(fsend.at[b], frecv.at[me.c], fs.at[b], fr.at[me.c], (b, me.s)) for b in range(nc)
        ]
        for b in reversed(range(nc)):
            end = (b + 1) * count
            rows = pl.ds(b * count, count)
            fill_mask(mask, qcode, kcode, b, count)
            level = lse_in[rows]
            for pair in range(heads // 2):
                two = slice(pair * 2 * HEAD, (pair + 1) * 2 * HEAD)
                q_pair = q_in[rows, two] * low(scale)
                do_pair = dall[b, :, two]
                k_pair = k_in[:end, two]
                v_pair = v_in[:end, two]
                parts = []
                for half in range(2):
                    head = pair * 2 + half
                    inside = (lane >= HEAD) if half else (lane < HEAD)
                    q_one = jnp.where(inside, q_pair, low(0))
                    do_one = jnp.where(inside, do_pair, low(0))
                    own_level = jnp.sum(
                        jnp.where(spot == head, level, 0.0), axis=1, keepdims=True
                    )
                    probs = jnp.exp(
                        biased(nt(q_one, k_pair), mask, bank.at[head], b, count) - own_level
                    )
                    grads = probs * nt(do_one, v_pair)
                    grads = grads - probs * jnp.sum(grads, axis=1, keepdims=True)
                    low_grads = grads.astype(low)
                    parts.append(dot32(low_grads, k_pair))
                    dk[:end, two] += tn(low_grads, q_one)
                    dv[:end, two] += tn(probs.astype(low), do_one)
                    near = grads[:, max(end - band, 0) :]
                    if end < band:
                        near = jnp.concatenate((jnp.zeros((count, band - end), f32), near), axis=1)
                    height = count
                    while height > CHUNK:
                        height = height // 2
                        near = near[:height] + pltpu.roll(near[height:], band - height, 1)
                    near_out[head] += near
                    if end > band:
                        far = grads[:, : end - band]
                        total = far[:, :128]
                        for piece in range(1, (end - band) // 128):
                            total = total + far[:, piece * 128 : (piece + 1) * 128]
                        height = count
                        while height > 8:
                            height = height // 2
                            total = total[:height] + total[height:]
                        far_out[head] += total
                dq[rows, two] = (jnp.where(lane < HEAD, parts[0], parts[1]) * scale).astype(low)
            dq_low, dk_low, dv_low = dq[rows], dk[rows].astype(low), dv[rows].astype(low)
            for n in range(nc):
                columns = slice(n * part, (n + 1) * part)
                at = pl.ds(n * part, part)
                value = nt(dq_low, w_in[0, at]) + nt(dk_low, w_in[1, at]) + nt(dv_low, w_in[2, at])
                fown[:, columns] = value
            x = t_in[rows].astype(f32)
            rate = lax.rsqrt(jnp.mean(x * x, axis=-1, keepdims=True) + epsilon)
            gain_out[...] += jnp.sum(fown[...] * x * rate, axis=0, keepdims=True)
            fsend[b] = fown[...].astype(low)

            @pl.when(me.c == b)
            def _():
                x_out[...] = fown[...]

            @pl.when(me.c != b)
            def _():
                out_copy[b].start()

        for i, grads in enumerate((dq, dk, dv)):
            for n in range(nc):
                at = slice(n * part, (n + 1) * part)
                w_out[i, at] = tn(first_in[:, at], grads[...].astype(low)).astype(low)
        for d in range(1, nc):
            origin = lax.rem(me.c + d, nc)
            remote(
                fsend.at[0], frecv.at[origin], fs.at[0], fr.at[origin], me.along(d)
            ).wait_recv()
            x_out[...] += frecv[origin].astype(f32)
        own = pl.ds(pl.multiple_of(me.c * count, count), count)
        x = t_in[own].astype(f32)
        rate = lax.rsqrt(jnp.mean(x * x, axis=-1, keepdims=True) + epsilon)
        scaled = x_out[...] * gain_in[...]
        pull = jnp.mean(scaled * x, axis=-1, keepdims=True)
        x_out[...] = dh_in[...] + rate * scaled - x * (rate * rate * rate * pull)
        for d in range(1, nc):
            do_copy(d).wait_send()
        for b in range(nc):

            @pl.when(me.c != b)
            def _():
                out_copy[b].wait_send()

    return pl.pallas_call(
        kernel,
        name="attend_backward",
        out_shape=(
            jax.ShapeDtypeStruct((count, width), f32),
            jax.ShapeDtypeStruct((3 + nc, width, part), low),
            jax.ShapeDtypeStruct((1, width), f32),
            jax.ShapeDtypeStruct((heads, CHUNK, band), f32),
            jax.ShapeDtypeStruct((heads, 8, 128), f32),
        ),
        in_specs=[pl.BlockSpec(memory_space=VMEM)] * 14,
        out_specs=[pl.BlockSpec(memory_space=VMEM)] * 5,
        scratch_shapes=[
            VMEM((count, length), f32),
            VMEM((heads, count, band), f32),
            VMEM((nc, count, part), low),
            VMEM((nc, count, part), low),
            VMEM((length, part), low),
            VMEM((length, part), f32),
            VMEM((length, part), f32),
            VMEM((nc, count, width), low),
            VMEM((nc, count, width), low),
            VMEM((count, width), f32),
            SEM.DMA((nc,)),
            SEM.DMA((nc,)),
            SEM.DMA((nc,)),
            SEM.DMA((nc,)),
        ],
        compiler_params=pltpu.CompilerParams(
            collective_id=4, has_side_effects=True, vmem_limit_bytes=56 * 1024 * 1024
        ),
    )(dattn, dh, o_all, tokens, first, q_all, k_all, v_all, lse, weights, gain, query_code, key_code, slopes)


def activation(gate_values, up_values):
    return jax.nn.gelu(gate_values) * up_values


def per_device(
    tokens,
    segments,
    valid,
    routes,
    teacher,
    norm_attn,
    w_query,
    w_key,
    w_value,
    output_weight,
    rel_bias,
    norm_ffn,
    w_router,
    w_gate,
    w_up,
    w_down,
):
    nc = lax.axis_size("ctx")
    ns = lax.axis_size("shard")
    c, s = lax.axis_index("ctx"), lax.axis_index("shard")
    n_dev, nj = nc * ns, ns // 2
    row_count, width = tokens.shape[1:]
    top_count = routes.shape[2]
    experts = w_router.shape[1]
    capacity = (5 * row_count * top_count + 4 * experts - 1) // (4 * experts)
    length = row_count * nc
    low = jnp.bfloat16
    f32 = jnp.float32
    piece = w_query.shape[0]
    band = 2 * row_count

    part = width // nc
    smalls = (norm_attn, norm_ffn, rel_bias, w_router.reshape(-1), segments[0].astype(low), valid[0].astype(low))
    sizes = [x.shape[0] for x in smalls]
    starts = [sum(sizes[:i]) for i in range(len(sizes))]
    extra = jnp.concatenate(smalls + (jnp.zeros((EXTRA * part - sum(sizes),), low),))
    shares = [w.reshape(piece, nc, part).transpose(1, 0, 2) for w in (w_query, w_key, w_value, output_weight)]
    shares = jnp.concatenate(
        [x[:, None] for x in shares[:3]] + [jnp.broadcast_to(shares[3][None], (nc, nc, piece, part))], axis=1
    )
    weights, extras, tokens_all = gather_all(
        shares, extra.reshape(EXTRA, part), tokens[0], nc, ns
    )
    extras = extras.reshape(nc, ns, EXTRA * part)
    gain_attn, gain_ffn, full_bias, full_router = (
        extras[:, :, begin : begin + size].reshape(-1)
        for begin, size in zip(starts[:4], sizes[:4])
    )
    full_router = full_router.reshape(width, experts)
    table = full_bias.reshape(BUCKETS, HEADS).astype(f32)
    line = lax.dynamic_slice_in_dim(extras, s, 1, 1)[:, 0]
    line_seg = line[:, starts[4] : starts[4] + row_count].reshape(length).astype(jnp.int32)
    line_valid = line[:, starts[5] : starts[5] + row_count].reshape(length) > 0
    key_code = jnp.where(line_valid, line_seg, -1)[None]
    query_code = line_seg[:, None]
    valid_count = jnp.sum(extras[:, :, starts[5] : starts[5] + row_count].astype(f32))

    spot = (jnp.arange(band)[None, :] - jnp.arange(CHUNK)[:, None]) % band
    distance = jnp.where(spot <= row_count, row_count - spot, 3 * row_count - spot)
    level = bucket_of(distance, BUCKETS)
    level_hot = (level[:, :, None] == jnp.arange(BUCKETS)[None, None, :]).astype(f32)
    heads = HEADS // nc
    own_table = lax.dynamic_slice_in_dim(table, c * heads, heads, 1)
    slopes = jnp.einsum(
        "ixb,bh->hix", level_hot, own_table - own_table[BUCKETS - 1 :], precision=highest_precision
    )

    gain_one, gain_two = gain_attn.astype(f32), gain_ffn.astype(f32)
    first_all, queries, keys, values, mixed, log_total, residual, ffn_low = attend_forward(
        tokens_all, weights, gain_one[None], gain_two[None], query_code, key_code, slopes, nc, ns
    )
    ffn_in = ffn_low.astype(f32)
    router = full_router.astype(f32)
    logits = jnp.dot(ffn_in, router, precision=highest_precision)
    route_local = routes[0]
    expert_ids = jnp.arange(experts, dtype=jnp.int32)
    route_hot = route_local[:, :, None] == expert_ids[None, None, :]
    picked = jnp.sum(jnp.where(route_hot, logits[:, None, :], 0.0), axis=-1)
    gate_probs = jax.nn.softmax(picked, axis=-1)
    flat_routes = route_local.reshape(row_count * top_count)
    route_hits = (flat_routes[:, None] == expert_ids[None, :]).astype(jnp.int32)
    before = jnp.cumsum(route_hits, axis=0) - route_hits
    slot_rank = jnp.sum(before * route_hits, axis=1)
    target = (flat_routes * capacity + slot_rank).reshape(row_count, top_count)
    slot_ids = jnp.arange(experts * capacity, dtype=jnp.int32)
    pick_first = (slot_ids[:, None] == target[None, :, 0]).astype(low)
    pick_second = (slot_ids[:, None] == target[None, :, 1]).astype(low)

    def exchange(rows):
        return lax.all_to_all(
            rows.reshape(experts, capacity, width), "shard", split_axis=0, concat_axis=0, tiled=True
        ).reshape(experts * capacity, width)

    expert_rows = exchange(dot32(pick_first + pick_second, ffn_low).astype(low))
    gate_w, up_w, down_w = w_gate[0], w_up[0], w_down[0]
    gate_pre = dot32(expert_rows, gate_w)
    up_pre = dot32(expert_rows, up_w)

    inner_value, activation_back = jax.vjp(activation, gate_pre, up_pre)
    inner = inner_value.astype(low)
    returned = exchange(dot32(inner, down_w).astype(low))
    picked_one, picked_two = tn(pick_first, returned), tn(pick_second, returned)
    output_sum = residual + gate_probs[:, :1] * picked_one + gate_probs[:, 1:] * picked_two
    valid_one = valid[0].astype(f32)
    deviation = output_sum - teacher[0].astype(f32)
    local_square = jnp.sum(valid_one[:, None] * deviation * deviation)
    everything = float(row_count * nc * ns)
    cotangent = everything / valid_count * deviation * valid_one[:, None]
    gate_grad = jnp.stack(
        (jnp.sum(cotangent * picked_one, axis=-1), jnp.sum(cotangent * picked_two, axis=-1)), axis=1
    )
    back_send = dot32(pick_first, (gate_probs[:, :1] * cotangent).astype(low)) + dot32(
        pick_second, (gate_probs[:, 1:] * cotangent).astype(low)
    )
    out_grad = exchange(back_send.astype(low))
    inner_grad = nt(out_grad, down_w)
    gate_pre_grad, up_pre_grad = activation_back(inner_grad)
    gate_low = gate_pre_grad.astype(low)
    up_low = up_pre_grad.astype(low)
    sent_back = exchange((nt(gate_low, gate_w) + nt(up_low, up_w)).astype(low))
    down_w_grad = tn(inner, out_grad).astype(low)
    gate_w_grad = tn(expert_rows, gate_low).astype(low)
    up_w_grad = tn(expert_rows, up_low).astype(low)
    gate_w_sum, up_w_sum, down_w_sum = (
        lax.psum_scatter(x[None], "ctx", scatter_dimension=1, tiled=True).astype(f32)
        for x in (gate_w_grad, up_w_grad, down_w_grad)
    )
    ffn_grad = tn(pick_first + pick_second, sent_back)
    pick_grad = gate_probs * (gate_grad - jnp.sum(gate_probs * gate_grad, axis=-1, keepdims=True))
    logits_grad = jnp.sum(jnp.where(route_hot, pick_grad[:, :, None], 0.0), axis=1)
    router_grad = contract(ffn_in, logits_grad, 0, 0, highest_precision)
    ffn_grad = ffn_grad + contract(logits_grad, router, 1, 1, highest_precision)
    unused, norm_two_back = jax.vjp(rms_norm, residual, gain_two)
    residual_from_norm, gain_two_grad = norm_two_back(ffn_grad)
    residual_grad = cotangent + residual_from_norm
    attn_grad_low = residual_grad.astype(low)
    input_grad, w_grads, gain_one_grad, near_sum, far_sum = attend_backward(
        attn_grad_low, residual_grad, mixed, tokens_all, first_all, queries, keys, values, log_total, weights,
        gain_one[None], query_code, key_code, slopes, nc, ns,
    )
    own_bias = jnp.einsum("hix,ixb->bh", near_sum, level_hot, precision=highest_precision)
    last_bucket = (jnp.arange(BUCKETS) == BUCKETS - 1).astype(f32)
    own_bias = own_bias + last_bucket[:, None] * jnp.sum(far_sum, axis=(1, 2))[None, :]
    bias_grad = lax.dynamic_update_slice_in_dim(
        jnp.zeros((BUCKETS, HEADS), f32), own_bias, c * heads, 1
    )
    small_grads = jnp.concatenate(
        [
            x.reshape(n_dev, -1).astype(low)
            for x in (gain_one_grad, gain_two_grad, bias_grad, router_grad)
        ],
        axis=1,
    )
    small_grads = jnp.pad(small_grads, ((0, 0), (0, EXTRA * part - small_grads.shape[1])))
    kept_sum, w_sum, small_sum, square_sum = reduce_all(
        w_grads.reshape(3 + nc, nc, nj, 2, piece, part),
        small_grads.reshape(nc, nj, 2, EXTRA, part),
        jnp.full((8, 128), local_square, f32),
        nc,
        ns,
        3,
    )
    loss_value = square_sum[0, 0] / (2.0 * width * valid_count)
    kept_sum = kept_sum.transpose(0, 2, 1, 3).reshape(3, piece, width)
    out_sum = w_sum[3:].transpose(1, 0, 2).reshape(piece, width)
    small_sum = small_sum.reshape(-1)
    tails = [small_sum[begin : begin + size] for begin, size in zip(starts[:4], sizes[:4])]
    return (
        output_sum.astype(low)[None],
        loss_value,
        input_grad[None],
        tails[0],
        kept_sum[0],
        kept_sum[1],
        kept_sum[2],
        out_sum,
        tails[2],
        tails[1],
        tails[3].reshape(w_router.shape),
        gate_w_sum,
        up_w_sum,
        down_w_sum,
    )


def solution(mesh):
    return jax.shard_map(
        per_device,
        mesh=mesh,
        in_specs=(
            P("shard", "ctx", None),
            P("shard", "ctx"),
            P("shard", "ctx"),
            P("shard", "ctx", None),
            P("shard", "ctx", None),
            P(("ctx", "shard")),
            P(("ctx", "shard"), None),
            P(("ctx", "shard"), None),
            P(("ctx", "shard"), None),
            P(("ctx", "shard"), None),
            P(("ctx", "shard")),
            P(("ctx", "shard")),
            P(("ctx", "shard"), None),
            P("shard", None, None),
            P("shard", None, None),
            P("shard", None, None),
        ),
        out_specs=(
            P("shard", "ctx", None),
            P(),
            P("shard", "ctx", None),
            P(("ctx", "shard")),
            P(("ctx", "shard"), None),
            P(("ctx", "shard"), None),
            P(("ctx", "shard"), None),
            P(("ctx", "shard"), None),
            P(("ctx", "shard")),
            P(("ctx", "shard")),
            P(("ctx", "shard"), None),
            P("shard", "ctx", None),
            P("shard", "ctx", None),
            P("shard", "ctx", None),
        ),
        check_vma=False,
    )
```

```python
import math

import jax
import jax.numpy as jnp
from jax import lax
from jax.experimental import pallas as pl
from jax.experimental.pallas import tpu as pltpu
from jax.sharding import PartitionSpec as P

HEADS = 16
HEAD = 64
BUCKETS = 32
MESH = pl.DeviceIdType.MESH
ANY = pl.ANY
VMEM = pltpu.VMEM
SEM = pltpu.SemaphoreType

highest_precision = lax.Precision.HIGHEST
max_distance = 128
epsilon = 1e-06
negative = -1e30
EXTRA = 16


def thresholds(buckets):
    exact_count = buckets // 2
    limits = list(range(1, exact_count))
    for bucket_level in range(exact_count, buckets):
        power = (bucket_level - exact_count) / exact_count
        limits.append(int(math.ceil(exact_count * (max_distance / exact_count) ** power)))
    return limits


def bucket_of(distance, buckets):
    bucket_total = jnp.zeros(distance.shape, jnp.int32)
    for threshold in thresholds(buckets):
        bucket_total = bucket_total + (distance >= threshold).astype(jnp.int32)
    return bucket_total


def rms_norm(values, gain_vector):
    return (
        values
        * lax.rsqrt(jnp.mean(values * values, axis=-1, keepdims=True) + epsilon)
        * gain_vector
    )


def contract(left_side, right_side, left_axis, right_axis, precision_mode=None):
    return lax.dot_general(
        left_side,
        right_side,
        (((left_axis,), (right_axis,)), ((), ())),
        precision=precision_mode,
        preferred_element_type=jnp.float32,
    )


def dot32(left_side, right_side):
    return jnp.dot(left_side, right_side, preferred_element_type=jnp.float32)


def nt(left_side, right_side):
    return contract(left_side, right_side, 1, 1)


def tn(left_side, right_side):
    return contract(left_side, right_side, 0, 0)


class Place:
    def __init__(self, nc, ns):
        self.nc, self.ns, self.nj = nc, ns, ns // 2
        self.c = lax.axis_index("ctx")
        self.s = lax.axis_index("shard")
        self.core = self.s % 2
        self.j = self.s // 2

    def along(self, d):
        return (lax.rem(self.c + d + self.nc, self.nc), self.s)

    def across(self, k):
        return (self.c, self.s ^ (2 * k))

    def twin(self):
        return (self.c, self.s ^ 1)

    def greet(self):
        barrier = pltpu.get_barrier_semaphore()
        partners = (
            [self.along(d) for d in range(1, self.nc)]
            + [self.across(k) for k in range(1, self.nj)]
            + [self.twin()]
        )
        for partner in partners:
            pl.semaphore_signal(barrier, inc=1, device_id=partner, device_id_type=MESH)
        pl.semaphore_wait(barrier, len(partners))


def remote(source, target, send, recv, device):
    return pltpu.make_async_remote_copy(
        src_ref=source,
        dst_ref=target,
        send_sem=send,
        recv_sem=recv,
        device_id=device,
        device_id_type=MESH,
    )


def gather_all(weights, extra, rows, nc, ns):
    n_dev, nj = nc * ns, ns // 2
    share = weights.shape[1:]
    full_shape = (share[0], nc, ns) + share[1:]

    def kernel(w_in, e_in, t_in, w_out, e_out, t_out, local, zs, zr, xs, xr, cs, cr, ts, tr):
        me = Place(nc, ns)

        def views(row, column):
            return (w_out.at[:, row, column], e_out.at[row, column])

        def piece(d, k):
            return views(lax.rem(me.c - d + nc, nc), me.s ^ (2 * k))

        mine = (w_in.at[me.c], e_in)
        locals_ = [
            pltpu.make_async_copy(source, target, local.at[i])
            for i, (source, target) in enumerate(
                zip(mine + (t_in,), views(me.c, me.s) + (t_out.at[me.c],))
            )
        ]
        for copy in locals_:
            copy.start()
        me.greet()
        sent = []

        def push(sources, targets, send, recv, device):
            for i in range(2):
                copy = remote(sources[i], targets[i], send.at[i], recv.at[i], device)
                copy.start()
                sent.append(copy)

        def arrive(targets, send, recv, device):
            for i in range(2):
                remote(targets[i], targets[i], send.at[i], recv.at[i], device).wait_recv()

        def token_copy(direction, hop):
            lane = 0 if direction > 0 else 1
            origin = lax.rem(me.c - direction * hop + nc, nc)
            return remote(
                t_in if hop == 0 else t_out.at[origin],
                t_out.at[origin],
                ts.at[lane, hop],
                tr.at[lane, hop],
                (lax.rem(me.c + direction + nc, nc), me.s),
            )

        def token_landing(direction, hop):
            lane = 0 if direction > 0 else 1
            origin = lax.rem(me.c - direction * (hop + 1) + nc, nc)
            landing = t_out.at[origin]
            return remote(landing, landing, ts.at[lane, hop], tr.at[lane, hop], me.along(1))

        def can_send(direction, hop):
            if direction > 0:
                return (me.c >= hop) & (me.c < nc - 1)
            return (me.c <= nc - 1 - hop) & (me.c > 0)

        def can_receive(direction, hop):
            if direction > 0:
                return me.c >= hop + 1
            return me.c <= nc - 2 - hop

        for d in range(1, nc):
            target = lax.rem(me.c + d, nc)
            push(
                (w_in.at[target], e_in), views(me.c, me.s), zs.at[d], zr.at[d], (target, me.s)
            )
        for direction in (1, -1):

            @pl.when(can_send(direction, 0))
            def _():
                token_copy(direction, 0).start()

        for k in range(1, nj):
            push(mine, views(me.c, me.s), xs.at[0, k], xr.at[0, k], me.across(k))
        push(mine, views(me.c, me.s), cs.at[0, 0], cr.at[0, 0], me.twin())

        for copy in locals_:
            copy.wait()
        for d in range(1, nc):
            here = piece(d, 0)
            arrive(here, zs.at[d], zr.at[d], me.along(-d))
            for k in range(1, nj):
                push(here, here, xs.at[d, k], xr.at[d, k], me.across(k))
            push(here, here, cs.at[d, 0], cr.at[d, 0], me.twin())
        for d in range(nc):
            for k in range(1, nj):
                here = piece(d, k)
                arrive(here, xs.at[d, k], xr.at[d, k], me.across(k))
                push(here, here, cs.at[d, k], cr.at[d, k], me.twin())
            if d < nc - 2:
                for direction in (1, -1):

                    @pl.when(can_receive(direction, d))
                    def _():
                        token_landing(direction, d).wait_recv()

                    @pl.when(can_send(direction, d + 1))
                    def _():
                        token_copy(direction, d + 1).start()

        for d in range(nc):
            for k in range(nj):
                here = views(lax.rem(me.c - d + nc, nc), me.s ^ 1 ^ (2 * k))
                arrive(here, cs.at[d, k], cr.at[d, k], me.twin())
        for direction in (1, -1):

            @pl.when(can_receive(direction, nc - 2))
            def _():
                token_landing(direction, nc - 2).wait_recv()

        for copy in sent:
            copy.wait_send()
        for direction in (1, -1):
            for hop in range(nc - 1):

                @pl.when(can_send(direction, hop))
                def _():
                    token_copy(direction, hop).wait_send()

    full, extras, tokens = pl.pallas_call(
        kernel,
        name="gather_all",
        cost_estimate=pl.CostEstimate(flops=50 * 10**9, bytes_accessed=10**7, transcendentals=0),
        out_shape=(
            jax.ShapeDtypeStruct(full_shape, weights.dtype),
            jax.ShapeDtypeStruct((nc, ns) + extra.shape, extra.dtype),
            jax.ShapeDtypeStruct((nc,) + rows.shape, rows.dtype),
        ),
        in_specs=[pl.BlockSpec(memory_space=ANY)] * 3,
        out_specs=[pl.BlockSpec(memory_space=ANY)] * 3,
        scratch_shapes=[
            SEM.DMA((3,)),
            SEM.DMA((nc, 2)),
            SEM.DMA((nc, 2)),
            SEM.DMA((nc, nj, 2)),
            SEM.DMA((nc, nj, 2)),
            SEM.DMA((nc, nj, 2)),
            SEM.DMA((nc, nj, 2)),
            SEM.DMA((2, nc)),
            SEM.DMA((2, nc)),
        ],
        compiler_params=pltpu.CompilerParams(collective_id=1, has_side_effects=True),
    )(weights, extra, rows)
    return (
        full.reshape(share[0], n_dev * share[1], share[2]),
        extras,
        tokens.reshape(nc * rows.shape[0], rows.shape[1]),
    )


def reduce_all(grads, small, squares, slices, hidden, nc, ns, kept):
    nj = ns // 2
    parts, piece, width = grads.shape[0], grads.shape[4], grads.shape[5]
    low = grads.dtype
    tile = squares.shape
    begins, wide = slice_plan(hidden, nc)
    height = slices[0].shape[1]

    def kernel(g_in, e_in, q_in, sa_in, sb_in, k_out, g_out, e_out, q_out, sa_out, sb_out, srecv, ss, sr,
               gt, et, gc, ec, gx, ex, gz, ez, qz, qx, qc, qa, qb,
               cs, cr, xs, xr, zs, zr, q1s, q1r, q2s, q2r, q3s, q3r):
        me = Place(nc, ns)
        me.greet()

        def both(pairs, send, recv, device):
            return [
                remote(source, target, send.at[i], recv.at[i], device)
                for i, (source, target) in enumerate(pairs)
            ]

        def core_copy(d):
            row = lax.rem(me.c + d, nc)
            other = 1 - me.core
            return both(
                ((g_in.at[:, row, :, other], gc.at[d]), (e_in.at[row, :, other], ec.at[d])),
                cs.at[d], cr.at[d], me.twin(),
            )

        def cross_copy(d, k):
            return both(
                ((gt.at[d, :, me.j ^ k], gx.at[d, k - 1]), (et.at[d, me.j ^ k], ex.at[d, k - 1])),
                xs.at[d, k], xr.at[d, k], me.across(k),
            )

        def along_copy(d):
            return both(
                ((gt.at[d, :, me.j], gz.at[d - 1]), (et.at[d, me.j], ez.at[d - 1])),
                zs.at[d], zr.at[d], me.along(d),
            )

        def start(copies):
            for copy in copies:
                copy.start()

        def landed(copies):
            for copy in copies:
                copy.wait_recv()

        def q_along(d):
            return remote(q_in, qz.at[d - 1], q1s.at[d], q1r.at[d], me.along(d))

        def q_across(k):
            return remote(qa, qx.at[k - 1], q2s.at[k], q2r.at[k], me.across(k))

        def slice_copy(i, d):
            source = (sa_in, sb_in)[i].at[lax.rem(me.c + d, nc)]
            return remote(source, srecv.at[i, me.c], ss.at[i, d], sr.at[i, d], me.along(d))

        q_twin = remote(qb, qc, q3s.at[0], q3r.at[0], me.twin())
        order = list(range(1, nc)) + [0]
        for i in range(2):
            for d in range(1, nc):
                slice_copy(i, d).start()
        for d in order:
            start(core_copy(d))
        for d in range(1, nc):
            q_along(d).start()

        for d in order:
            landed(core_copy(d))
            row = lax.rem(me.c + d, nc)

            def add_core(i, carry):
                for k in range(nj):
                    gt[d, i, k] = (
                        g_in[i, row, k, me.core].astype(jnp.float32)
                        + gc[d, i, k].astype(jnp.float32)
                    ).astype(low)
                return carry

            lax.fori_loop(0, parts, add_core, 0)
            for k in range(nj):
                et[d, k] = (
                    e_in[row, k, me.core].astype(jnp.float32) + ec[d, k].astype(jnp.float32)
                ).astype(low)
            for k in range(1, nj):
                start(cross_copy(d, k))
        for d in range(1, nc):
            q_along(d).wait_recv()
        value = q_in[...]
        for d in range(1, nc):
            value = value + qz[d - 1]
        qa[...] = value
        for k in range(1, nj):
            q_across(k).start()
        for d in order:
            for k in range(1, nj):
                landed(cross_copy(d, k))

            def add_cross(i, carry):
                value = gt[d, i, me.j].astype(jnp.float32)
                for k in range(1, nj):
                    value = value + gx[d, k - 1, i].astype(jnp.float32)
                if d == 0:
                    g_out[i] = value
                else:
                    gt[d, i, me.j] = value.astype(low)
                return carry

            lax.fori_loop(0, parts, add_cross, 0)
            value = et[d, me.j].astype(jnp.float32)
            for k in range(1, nj):
                value = value + ex[d, k - 1].astype(jnp.float32)
            if d:
                et[d, me.j] = value.astype(low)
                start(along_copy(d))
            else:
                e_out[...] = value
        for k in range(1, nj):
            q_across(k).wait_recv()
        value = qa[...]
        for k in range(1, nj):
            value = value + qx[k - 1]
        qb[...] = value
        q_twin.start()
        for i in range(kept):
            k_out[i, :, pl.ds(pl.multiple_of(me.c * width, width), width)] = g_out[i]
        for d in range(1, nc):
            landed(along_copy(d))
            row = lax.rem(me.c - d + nc, nc)
            for i in range(kept):
                at = pl.ds(pl.multiple_of(row * width, width), width)
                k_out[i, :, at] = gz[d - 1, i].astype(jnp.float32)
            e_out[...] = e_out[...] + ez[d - 1].astype(jnp.float32)

        for i in range(kept, parts):
            value = g_out[i]
            for d in range(1, nc):
                value = value + gz[d - 1, i].astype(jnp.float32)
            k_out[kept, :, (i - kept) * width : (i - kept + 1) * width] = value
        q_twin.wait()
        q_out[...] = qb[...] + qc[...]
        srecv[0, me.c] = sa_in[me.c]
        srecv[1, me.c] = sb_in[me.c]
        for i, target in enumerate((sa_out, sb_out)):
            for d in range(1, nc):
                origin = lax.rem(me.c - d + nc, nc)
                landing = srecv.at[i, origin]
                remote(landing, landing, ss.at[i, d], sr.at[i, d], me.along(-d)).wait_recv()
            for origin in range(nc):
                at = slice(begins[origin], begins[origin] + wide)
                target[:, at] = srecv[i, origin].astype(jnp.float32)
        for d in order:
            started = core_copy(d) + [copy for k in range(1, nj) for copy in cross_copy(d, k)]
            if d:
                started = started + along_copy(d) + [q_along(d), slice_copy(0, d), slice_copy(1, d)]
            for copy in started:
                copy.wait_send()
        for k in range(1, nj):
            q_across(k).wait_send()

    f32 = jnp.float32
    one, extra = (parts, piece, width), small.shape[3:]
    return pl.pallas_call(
        kernel,
        name="reduce_all",
        cost_estimate=pl.CostEstimate(flops=45 * 10**9, bytes_accessed=10**7, transcendentals=0),
        out_shape=(
            jax.ShapeDtypeStruct((kept + 1, piece, nc * width), f32),
            jax.ShapeDtypeStruct(one, f32),
            jax.ShapeDtypeStruct(extra, f32),
            jax.ShapeDtypeStruct(tile, f32),
            jax.ShapeDtypeStruct((height, hidden), f32),
            jax.ShapeDtypeStruct((height, hidden), f32),
        ),
        in_specs=[pl.BlockSpec(memory_space=VMEM)] * 5,
        out_specs=[pl.BlockSpec(memory_space=VMEM)] * 6,
        scratch_shapes=[
            VMEM((2, nc, height, wide), low),
            SEM.DMA((2, nc)),
            SEM.DMA((2, nc)),
            VMEM((nc, parts, nj, piece, width), low),
            VMEM((nc, nj) + extra, low),
            VMEM((nc, parts, nj, piece, width), low),
            VMEM((nc, nj) + extra, low),
            VMEM((nc, nj - 1) + one, low),
            VMEM((nc, nj - 1) + extra, low),
            VMEM((nc - 1,) + one, low),
            VMEM((nc - 1,) + extra, low),
            VMEM((nc - 1,) + tile, f32),
            VMEM((nj - 1,) + tile, f32),
            VMEM(tile, f32),
            VMEM(tile, f32),
            VMEM(tile, f32),
            SEM.DMA((nc, 2)),
            SEM.DMA((nc, 2)),
            SEM.DMA((nc, nj, 2)),
            SEM.DMA((nc, nj, 2)),
            SEM.DMA((nc, 2)),
            SEM.DMA((nc, 2)),
            SEM.DMA((nc,)),
            SEM.DMA((nc,)),
            SEM.DMA((nj,)),
            SEM.DMA((nj,)),
            SEM.DMA((1,)),
            SEM.DMA((1,)),
        ],
        compiler_params=pltpu.CompilerParams(
            collective_id=2, has_side_effects=True, vmem_limit_bytes=56 * 1024 * 1024
        ),
    )(grads, small, squares, *slices)


CHUNK = 16


def fill_mask(mask, query_code, key_code, block, count):
    near = block * count
    query = query_code[pl.ds(near, count)]
    if block:
        mask[:, :near] = jnp.where(query == key_code[:, :near], 0.0, negative)
    row = lax.broadcasted_iota(jnp.int32, (count, count), 0)
    column = lax.broadcasted_iota(jnp.int32, (count, count), 1)
    seen = ((query == key_code[:, near : near + count]) & (row >= column)) | (row == column)
    mask[:, near : near + count] = jnp.where(seen, 0.0, negative)


def fill_slopes(bank, slopes, head, count):
    for i in range(count // CHUNK):
        row = slopes[head]
        bank[head, i * CHUNK : (i + 1) * CHUNK] = pltpu.roll(row, i * CHUNK, 1) if i else row


def biased(scores, mask, slope, block, count):
    end = (block + 1) * count
    band = 2 * count
    if end < band:
        return scores + mask[:, :end] + slope[:, band - end :]
    if end == band:
        return scores + mask[:, :end] + slope[...]
    wide = scores[:, : end - band] + mask[:, : end - band]
    tight = scores[:, end - band :] + mask[:, end - band : end] + slope[...]
    return jnp.concatenate((wide, tight), axis=1)


def attend_forward(tokens, weights, gain, gain_next, query_code, key_code, slopes, nc, ns):
    length, width = tokens.shape
    count = length // nc
    part = width // nc
    heads, _, band = slopes.shape
    low, f32 = jnp.bfloat16, jnp.float32

    def kernel(t_in, w_in, gain_in, next_in, qcode, kcode, toe, first, q_out, k_out, v_out, o_out, lse_out, x_out, y_out,
               mask, bank, osend, ss, rs):
        me = Place(nc, ns)
        barrier = pltpu.get_barrier_semaphore()
        for d in range(1, nc):
            pl.semaphore_signal(barrier, inc=1, device_id=me.along(d), device_id_type=MESH)
        pl.semaphore_wait(barrier, nc - 1)

        def norm(i, carry):
            at = pl.ds(pl.multiple_of(i * 64, 64), 64)
            x = t_in[at].astype(f32)
            rate = lax.rsqrt(jnp.mean(x * x, axis=-1, keepdims=True) + epsilon)
            first[at] = (x * rate * gain_in[...]).astype(low)
            return carry

        lax.fori_loop(0, length // 64, norm, 0)

        def project(i, carry):
            at = pl.ds(pl.multiple_of(i * count, count), count)
            block = first[at]
            q_out[at] = dot32(block, w_in[0]).astype(low)
            k_out[at] = dot32(block, w_in[1]).astype(low)
            v_out[at] = dot32(block, w_in[2]).astype(low)
            return carry

        lax.fori_loop(0, nc, project, 0)
        for head in range(heads):
            fill_slopes(bank, toe, head, count)
        lane = lax.broadcasted_iota(jnp.int32, (count, 2 * HEAD), 1)
        spot = lax.broadcasted_iota(jnp.int32, (count, 128), 1)
        own_copy = [
            remote(osend.at[b], o_out.at[me.c], ss.at[b], rs.at[me.c], (b, me.s)) for b in range(nc)
        ]
        for b in reversed(range(nc)):
            end = (b + 1) * count
            rows = pl.ds(b * count, count)
            fill_mask(mask, qcode, kcode, b, count)
            level = jnp.zeros((count, 128), f32)
            for pair in range(heads // 2):
                two = slice(pair * 2 * HEAD, (pair + 1) * 2 * HEAD)
                q_pair = q_out[rows, two] * low(1.0 / math.sqrt(HEAD))
                k_pair = k_out[:end, two]
                v_pair = v_out[:end, two]
                halves = []
                for half in range(2):
                    head = pair * 2 + half
                    inside = (lane >= HEAD) if half else (lane < HEAD)
                    scores = nt(jnp.where(inside, q_pair, low(0)), k_pair)
                    scores = biased(scores, mask, bank.at[head], b, count)
                    top = jnp.max(scores, axis=1, keepdims=True)
                    scores = jnp.exp(scores - top)
                    total = jnp.sum(scores, axis=1, keepdims=True)
                    halves.append(dot32(scores.astype(low), v_pair) * (1.0 / total))
                    level = jnp.where(spot == head, top + jnp.log(total), level)
                osend[b, :, two] = jnp.where(lane < HEAD, halves[0], halves[1]).astype(low)
            lse_out[rows] = level

            @pl.when(me.c == b)
            def _():
                o_out[me.c] = osend[b]

            @pl.when(me.c != b)
            def _():
                own_copy[b].start()

        for d in range(1, nc):
            origin = lax.rem(me.c + d, nc)
            remote(
                osend.at[0], o_out.at[origin], ss.at[0], rs.at[origin], me.along(d)
            ).wait_recv()
        own = pl.ds(pl.multiple_of(me.c * count, count), count)
        squares = jnp.zeros((count, 1), f32)
        for n in range(nc):
            columns = slice(n * part, (n + 1) * part)
            x = t_in[own, columns].astype(f32)
            for origin in range(nc):
                x = x + dot32(o_out[origin], w_in[3 + n, origin * part : (origin + 1) * part])
            x_out[:, columns] = x
            squares = squares + jnp.sum(x * x, axis=1, keepdims=True)
        rate = lax.rsqrt(squares * (1.0 / width) + epsilon)
        for n in range(nc):
            columns = slice(n * part, (n + 1) * part)
            y_out[:, columns] = (x_out[:, columns] * rate * next_in[:, columns]).astype(low)
        for b in range(nc):

            @pl.when(me.c != b)
            def _():
                own_copy[b].wait_send()

    return pl.pallas_call(
        kernel,
        name="attend_forward",
        cost_estimate=pl.CostEstimate(flops=25 * 10**9, bytes_accessed=10**7, transcendentals=0),
        out_shape=(
            jax.ShapeDtypeStruct((length, width), low),
            jax.ShapeDtypeStruct((length, part), low),
            jax.ShapeDtypeStruct((length, part), low),
            jax.ShapeDtypeStruct((length, part), low),
            jax.ShapeDtypeStruct((nc, count, part), low),
            jax.ShapeDtypeStruct((length, 128), f32),
            jax.ShapeDtypeStruct((count, width), f32),
            jax.ShapeDtypeStruct((count, width), low),
        ),
        in_specs=[pl.BlockSpec(memory_space=VMEM)] * 7,
        out_specs=[pl.BlockSpec(memory_space=VMEM)] * 8,
        scratch_shapes=[
            VMEM((count, length), f32),
            VMEM((heads, count, band), f32),
            VMEM((nc, count, part), low),
            SEM.DMA((nc,)),
            SEM.DMA((nc,)),
        ],
        compiler_params=pltpu.CompilerParams(
            collective_id=3, has_side_effects=True, vmem_limit_bytes=56 * 1024 * 1024
        ),
    )(tokens, weights, gain, gain_next, query_code, key_code, slopes)


def attend_backward(
    dattn, dh, o_all, tokens, first, q_all, k_all, v_all, lse, weights, gain, query_code, key_code, slopes,
    picks, weighted, normed, cotangents, nc, ns,
):
    length, width = tokens.shape
    count = length // nc
    part = width // nc
    heads, _, band = slopes.shape
    low, f32 = jnp.bfloat16, jnp.float32
    scale = 1.0 / math.sqrt(HEAD)
    more = normed.shape[0]
    exchange = picks.shape[1:3] + (width,)

    def kernel(a_in, dh_in, o_in, t_in, first_in, q_in, k_in, v_in, lse_in, w_in, gain_in, qcode, kcode, toe,
               p_in, pw_in, n_in, c_in,
               x_out, w_out, gain_out, near_out, far_out, n_out, c_out,
               mask, bank, dsend, dall, dq, dk, dv, fsend, frecv, fown, nsend, ss, rs, fs, fr, ns_, nr):
        me = Place(nc, ns)
        barrier = pltpu.get_barrier_semaphore()
        partners = [me.along(d) for d in range(1, nc)] + [(me.c, me.s ^ m) for m in range(1, ns)]
        for partner in partners:
            pl.semaphore_signal(barrier, inc=1, device_id=partner, device_id_type=MESH)
        pl.semaphore_wait(barrier, len(partners))

        def do_copy(d):
            return remote(dsend.at[d], dall.at[me.c], ss.at[d], rs.at[d], me.along(d))

        for d in list(range(1, nc)) + [0]:
            target = lax.rem(me.c + d, nc)
            at = pl.ds(pl.multiple_of(target * part, part), part)
            value = nt(a_in[:, :part], w_in[3, at])
            for n in range(1, nc):
                value = value + nt(a_in[:, n * part : (n + 1) * part], w_in[3 + n, at])
            if d:
                dsend[d] = value.astype(low)
                do_copy(d).start()
            else:
                dall[me.c] = value.astype(low)
        jobs = [(pw_in.at[d], c_in.at[me.c ^ (d + 1)], c_out.at[d]) for d in range(nc - 1)]
        jobs = jobs + [(p_in.at[d], n_in.at[d], n_out.at[d]) for d in range(more)]
        spread = Spread(me, jobs, nsend, ns_, nr)
        for i in range(len(jobs)):
            spread.start(i)
        for n in range(nc):
            for origin in range(nc):
                w_out[3 + n, origin * part : (origin + 1) * part] = tn(
                    o_in[origin], a_in[:, n * part : (n + 1) * part]
                ).astype(low)
        for head in range(heads):
            fill_slopes(bank, toe, head, count)
        lane = lax.broadcasted_iota(jnp.int32, (count, 2 * HEAD), 1)
        spot = lax.broadcasted_iota(jnp.int32, (count, 128), 1)
        dk[...] = jnp.zeros_like(dk)
        dv[...] = jnp.zeros_like(dv)
        near_out[...] = jnp.zeros_like(near_out)
        far_out[...] = jnp.zeros_like(far_out)
        gain_out[...] = jnp.zeros_like(gain_out)
        for d in range(1, nc):
            origin = lax.rem(me.c - d + nc, nc)
            remote(dsend.at[d], dall.at[origin], ss.at[d], rs.at[d], me.along(d)).wait_recv()
        out_copy = [
            remote(fsend.at[b], frecv.at[me.c], fs.at[b], fr.at[me.c], (b, me.s)) for b in range(nc)
        ]
        for b in reversed(range(nc)):
            end = (b + 1) * count
            rows = pl.ds(b * count, count)
            fill_mask(mask, qcode, kcode, b, count)
            level = lse_in[rows]
            for pair in range(heads // 2):
                two = slice(pair * 2 * HEAD, (pair + 1) * 2 * HEAD)
                q_pair = q_in[rows, two] * low(scale)
                do_pair = dall[b, :, two]
                k_pair = k_in[:end, two]
                v_pair = v_in[:end, two]
                parts = []
                for half in range(2):
                    head = pair * 2 + half
                    inside = (lane >= HEAD) if half else (lane < HEAD)
                    q_one = jnp.where(inside, q_pair, low(0))
                    do_one = jnp.where(inside, do_pair, low(0))
                    own_level = jnp.sum(
                        jnp.where(spot == head, level, 0.0), axis=1, keepdims=True
                    )
                    probs = jnp.exp(
                        biased(nt(q_one, k_pair), mask, bank.at[head], b, count) - own_level
                    )
                    grads = probs * nt(do_one, v_pair)
                    grads = grads - probs * jnp.sum(grads, axis=1, keepdims=True)
                    low_grads = grads.astype(low)
                    parts.append(dot32(low_grads, k_pair))
                    dk[:end, two] += tn(low_grads, q_one)
                    dv[:end, two] += tn(probs.astype(low), do_one)
                    near = grads[:, max(end - band, 0) :]
                    if end < band:
                        near = jnp.concatenate((jnp.zeros((count, band - end), f32), near), axis=1)
                    height = count
                    while height > CHUNK:
                        height = height // 2
                        near = near[:height] + pltpu.roll(near[height:], band - height, 1)
                    near_out[head] += near
                    if end > band:
                        far = grads[:, : end - band]
                        total = far[:, :128]
                        for piece in range(1, (end - band) // 128):
                            total = total + far[:, piece * 128 : (piece + 1) * 128]
                        height = count
                        while height > 8:
                            height = height // 2
                            total = total[:height] + total[height:]
                        far_out[head] += total
                dq[rows, two] = (jnp.where(lane < HEAD, parts[0], parts[1]) * scale).astype(low)
            dq_low, dk_low, dv_low = dq[rows], dk[rows].astype(low), dv[rows].astype(low)
            for n in range(nc):
                columns = slice(n * part, (n + 1) * part)
                at = pl.ds(n * part, part)
                value = nt(dq_low, w_in[0, at]) + nt(dk_low, w_in[1, at]) + nt(dv_low, w_in[2, at])
                fown[:, columns] = value
            x = t_in[rows].astype(f32)
            rate = lax.rsqrt(jnp.mean(x * x, axis=-1, keepdims=True) + epsilon)
            gain_out[...] += jnp.sum(fown[...] * x * rate, axis=0, keepdims=True)
            fsend[b] = fown[...].astype(low)

            @pl.when(me.c == b)
            def _():
                x_out[...] = fown[...]

            @pl.when(me.c != b)
            def _():
                out_copy[b].start()

        for i, grads in enumerate((dq, dk, dv)):
            for n in range(nc):
                at = slice(n * part, (n + 1) * part)
                w_out[i, at] = tn(first_in[:, at], grads[...].astype(low)).astype(low)
        for d in range(1, nc):
            origin = lax.rem(me.c + d, nc)
            remote(
                fsend.at[0], frecv.at[origin], fs.at[0], fr.at[origin], me.along(d)
            ).wait_recv()
            x_out[...] += frecv[origin].astype(f32)
        own = pl.ds(pl.multiple_of(me.c * count, count), count)
        x = t_in[own].astype(f32)
        rate = lax.rsqrt(jnp.mean(x * x, axis=-1, keepdims=True) + epsilon)
        scaled = x_out[...] * gain_in[...]
        pull = jnp.mean(scaled * x, axis=-1, keepdims=True)
        x_out[...] = dh_in[...] + rate * scaled - x * (rate * rate * rate * pull)
        spread.finish()
        for d in range(1, nc):
            do_copy(d).wait_send()
        for b in range(nc):

            @pl.when(me.c != b)
            def _():
                out_copy[b].wait_send()

    return pl.pallas_call(
        kernel,
        name="attend_backward",
        cost_estimate=pl.CostEstimate(flops=50 * 10**9, bytes_accessed=10**7, transcendentals=0),
        out_shape=(
            jax.ShapeDtypeStruct((count, width), f32),
            jax.ShapeDtypeStruct((3 + nc, width, part), low),
            jax.ShapeDtypeStruct((1, width), f32),
            jax.ShapeDtypeStruct((heads, CHUNK, band), f32),
            jax.ShapeDtypeStruct((heads, 8, 128), f32),
            jax.ShapeDtypeStruct((more,) + exchange, low),
            jax.ShapeDtypeStruct((nc - 1,) + exchange, low),
        ),
        in_specs=[pl.BlockSpec(memory_space=VMEM)] * 18,
        out_specs=[pl.BlockSpec(memory_space=VMEM)] * 5 + [pl.BlockSpec(memory_space=ANY)] * 2,
        scratch_shapes=[
            VMEM((count, length), f32),
            VMEM((heads, count, band), f32),
            VMEM((nc, count, part), low),
            VMEM((nc, count, part), low),
            VMEM((length, part), low),
            VMEM((length, part), f32),
            VMEM((length, part), f32),
            VMEM((nc, count, width), low),
            VMEM((nc, count, width), low),
            VMEM((count, width), f32),
            VMEM((4,) + exchange, low),
            SEM.DMA((nc,)),
            SEM.DMA((nc,)),
            SEM.DMA((nc,)),
            SEM.DMA((nc,)),
            SEM.DMA((nc - 1 + more, ns)),
            SEM.DMA((nc - 1 + more, ns)),
        ],
        compiler_params=pltpu.CompilerParams(
            collective_id=4, has_side_effects=True, vmem_limit_bytes=56 * 1024 * 1024
        ),
    )(dattn, dh, o_all, tokens, first, q_all, k_all, v_all, lse, weights, gain, query_code, key_code, slopes,
      picks, weighted, normed, cotangents)


def activation(gate_values, up_values):
    return jax.nn.gelu(gate_values) * up_values


def gelu_parts(x):
    c, a = math.sqrt(2.0 / math.pi), 0.044715
    square = x * x
    t = jnp.tanh(c * x * (1.0 + a * square))
    half = 0.5 * (1.0 + t)
    return x * half, half + (0.5 * c) * x * (1.0 - t * t) * (1.0 + (3.0 * a) * square)


class Chain:
    def __init__(self, me, pairs, send, recv):
        self.me, self.pairs, self.send, self.recv, self.nc = me, pairs, send, recv, me.nc

    def copies(self, direction, hop, landing):
        me, nc = self.me, self.nc
        lane = 0 if direction > 0 else 1
        origin = lax.rem(me.c - direction * (hop + 1 if landing else hop) + 2 * nc, nc)
        result = []
        for i, (own, every) in enumerate(self.pairs):
            target = every.at[origin]
            source = own if hop == 0 and not landing else target
            result.append(
                remote(
                    source, target, self.send.at[lane, hop, i], self.recv.at[lane, hop, i],
                    me.along(direction),
                )
            )
        return result

    def sends(self, direction, hop):
        c, nc = self.me.c, self.nc
        if direction > 0:
            return (c >= hop) & (c < nc - 1)
        return (c <= nc - 1 - hop) & (c > 0)

    def lands(self, direction, hop):
        c, nc = self.me.c, self.nc
        if direction > 0:
            return c >= hop + 1
        return c <= nc - 2 - hop

    def start(self, hop):
        for direction in (1, -1):
            if hop:

                @pl.when(self.lands(direction, hop - 1))
                def _():
                    for copy in self.copies(direction, hop - 1, True):
                        copy.wait_recv()

            if hop < self.nc - 1:

                @pl.when(self.sends(direction, hop))
                def _():
                    for copy in self.copies(direction, hop, False):
                        copy.start()

    def finish(self):
        for direction in (1, -1):
            for hop in range(self.nc - 1):

                @pl.when(self.sends(direction, hop))
                def _():
                    for copy in self.copies(direction, hop, False):
                        copy.wait_send()


def greet_experts(me):
    barrier = pltpu.get_barrier_semaphore()
    partners = [(me.c, me.s ^ m) for m in range(1, me.ns)] + [me.along(1), me.along(-1)]
    for partner in partners:
        pl.semaphore_signal(barrier, inc=1, device_id=partner, device_id_type=MESH)
    pl.semaphore_wait(barrier, len(partners))


TILE = 256


class Spread:
    def __init__(self, me, jobs, send, send_sem, recv_sem):
        self.me, self.jobs, self.send = me, jobs, send
        self.send_sem, self.recv_sem = send_sem, recv_sem
        self.order = list(range(2, me.ns)) + [1]
        self.turns = send.shape[0]

    def copy(self, i, m):
        return remote(
            self.send.at[i % self.turns, m], self.jobs[i][2].at[m],
            self.send_sem.at[i, m], self.recv_sem.at[i, m], (self.me.c, self.me.s ^ m),
        )

    def own(self, i):
        return pltpu.make_async_copy(
            self.send.at[i % self.turns, 0], self.jobs[i][2].at[0], self.send_sem.at[i, 0]
        )

    def left(self, i):
        for m in self.order:
            self.copy(i, m).wait_send()
        self.own(i).wait()

    def start(self, i):
        if i >= self.turns:
            self.left(i - self.turns)
        picks, tokens = self.jobs[i][:2]
        for m in self.order + [0]:
            self.send[i % self.turns, m] = dot32(picks[m], tokens[...]).astype(self.send.dtype)
            if m:
                self.copy(i, m).start()
            else:
                self.own(i).start()

    def finish(self):
        for i in range(len(self.jobs)):
            for m in self.order:
                self.copy(i, m).wait_recv()
            if i >= len(self.jobs) - self.turns:
                self.left(i)


def moe_forward(pick, pick_next, tokens, gates, gate_w, up_w, down_w, nc, ns):
    cap, count = pick.shape[1:]
    width, hidden = gate_w.shape
    low, f32 = jnp.bfloat16, jnp.float32
    half = ns // 2
    rows_in_half = half * cap

    def kernel(p_in, n_in, t_in, s_in, g_hbm, u_hbm, d_hbm, r_out, y_out, t_all, s_all, n_out,
               wg, wu, wd, send, yield_, nsend, inner, ws, ss, rs, ys, yr, ts, tr, ls, ns_, nr):
        me = Place(nc, ns)
        loads = [
            pltpu.make_async_copy(source, target, ws.at[i])
            for i, (source, target) in enumerate(((g_hbm, wg), (u_hbm, wu), (d_hbm, wd)))
        ]
        for load in loads:
            load.start()
        keep = [
            pltpu.make_async_copy(t_in, t_all.at[me.c], ls.at[0]),
            pltpu.make_async_copy(s_in, s_all.at[me.c], ls.at[1]),
        ]
        for copy in keep:
            copy.start()
        greet_experts(me)

        def there(m):
            return (me.c, me.s ^ m)

        def out_copy(m):
            return remote(send.at[m], r_out.at[m], ss.at[m], rs.at[m], there(m))

        def back_copy(m):
            return remote(yield_.at[m], y_out.at[m], ys.at[m], yr.at[m], there(m))

        order = list(range(2, ns)) + [1]
        for m in order:
            send[m] = dot32(p_in[m], t_in[...]).astype(low)
            out_copy(m).start()
        chain = Chain(me, ((t_in, t_all), (s_in, s_all)), ts, tr)
        chain.start(0)
        r_out[0] = dot32(p_in[0], t_in[...]).astype(low)
        for load in loads:
            load.wait()
        for part in range(2):
            for m in range(part * half, (part + 1) * half):
                if m:
                    out_copy(m).wait_recv()

            def up(n, carry):
                rows = r_out[part * half : (part + 1) * half].reshape(rows_in_half, width)
                at = pl.ds(pl.multiple_of(n * TILE, TILE), TILE)
                value = activation(dot32(rows, wg[:, at]), dot32(rows, wu[:, at]))
                inner[:, at] = value.astype(low)
                return carry

            lax.fori_loop(0, hidden // TILE, up, 0)

            def down(n, carry):
                at = pl.ds(pl.multiple_of(n * TILE, TILE), TILE)
                value = dot32(inner[...], wd[:, at]).astype(low).reshape(half, cap, TILE)
                yield_[part * half : (part + 1) * half, :, at] = value
                return carry

            lax.fori_loop(0, width // TILE, down, 0)
            for m in range(part * half, (part + 1) * half):
                if m:
                    back_copy(m).start()
            if part == 0:
                chain.start(1)
                spread = Spread(me, [(n_in, t_all.at[me.c ^ 1], n_out)], nsend, ns_, nr)
                spread.start(0)
        y_out[0] = yield_[0]
        for hop in range(2, nc):
            chain.start(hop)
        for m in order:
            back_copy(m).wait_recv()
        for copy in keep:
            copy.wait()
        for m in order:
            out_copy(m).wait_send()
            back_copy(m).wait_send()
        spread.finish()
        chain.finish()

    exchange = (ns, cap, width)
    return pl.pallas_call(
        kernel,
        name="moe_forward",
        cost_estimate=pl.CostEstimate(flops=45 * 10**9, bytes_accessed=10**7, transcendentals=0),
        out_shape=(
            jax.ShapeDtypeStruct(exchange, low),
            jax.ShapeDtypeStruct(exchange, low),
            jax.ShapeDtypeStruct((nc,) + tokens.shape, low),
            jax.ShapeDtypeStruct((nc,) + gates.shape, f32),
            jax.ShapeDtypeStruct(exchange, low),
        ),
        in_specs=[pl.BlockSpec(memory_space=VMEM)] * 4 + [pl.BlockSpec(memory_space=ANY)] * 3,
        out_specs=[pl.BlockSpec(memory_space=VMEM)] * 4 + [pl.BlockSpec(memory_space=ANY)],
        scratch_shapes=[
            VMEM((width, hidden), low),
            VMEM((width, hidden), low),
            VMEM((hidden, width), low),
            VMEM(exchange, low),
            VMEM(exchange, low),
            VMEM((1,) + exchange, low),
            VMEM((rows_in_half, hidden), low),
            SEM.DMA((3,)),
            SEM.DMA((ns,)),
            SEM.DMA((ns,)),
            SEM.DMA((ns,)),
            SEM.DMA((ns,)),
            SEM.DMA((2, nc, 2)),
            SEM.DMA((2, nc, 2)),
            SEM.DMA((2,)),
            SEM.DMA((1, ns)),
            SEM.DMA((1, ns)),
        ],
        compiler_params=pltpu.CompilerParams(
            collective_id=5, has_side_effects=True, vmem_limit_bytes=56 * 1024 * 1024
        ),
    )(pick, pick_next, tokens, gates, gate_w, up_w, down_w)


def moe_backward(grads, rows, cotangents, pick_next, tokens, gate_w, up_w, down_w, nc, ns):
    cap = rows.shape[1]
    width, hidden = gate_w.shape
    low, f32 = jnp.bfloat16, jnp.float32
    half = ns // 2
    rows_in_half = half * cap
    more = tokens.shape[0]

    def kernel(g_in, r_in, t_in, n_in, f_in, g_hbm, u_hbm, d_hbm, g_out, x_out, t_all, n_out,
               wg, wu, wd, yield_, nsend, slope_g, slope_u, dg, du, ws, ss, rs, ys, yr, ts, tr, ls, ns_, nr):
        me = Place(nc, ns)
        loads = [
            pltpu.make_async_copy(source, target, ws.at[i])
            for i, (source, target) in enumerate(((g_hbm, wg), (u_hbm, wu), (d_hbm, wd)))
        ]
        for load in loads:
            load.start()
        keep = pltpu.make_async_copy(t_in, t_all.at[me.c], ls.at[0])
        keep.start()
        greet_experts(me)

        def there(m):
            return (me.c, me.s ^ m)

        def out_copy(m):
            return remote(g_in.at[m], g_out.at[m], ss.at[m], rs.at[m], there(m))

        def back_copy(m):
            return remote(yield_.at[m], x_out.at[m], ys.at[m], yr.at[m], there(m))

        order = list(range(2, ns)) + [1]
        for m in order:
            out_copy(m).start()
        chain = Chain(me, ((t_in, t_all),), ts, tr)
        chain.start(0)
        g_out[0] = g_in[0]
        for load in loads:
            load.wait()

        def again(n, carry):
            every = r_in[...].reshape(ns * cap, width)
            at = pl.ds(pl.multiple_of(n * TILE, TILE), TILE)
            value, slope = gelu_parts(dot32(every, wg[:, at]))
            slope_g[:, at] = (slope * dot32(every, wu[:, at])).astype(slope_g.dtype)
            slope_u[:, at] = value.astype(slope_u.dtype)
            return carry

        lax.fori_loop(0, hidden // TILE, again, 0)
        chain.start(1)
        jobs = [(n_in.at[i], f_in.at[i], n_out.at[i]) for i in range(more)]
        spread = Spread(me, jobs, nsend, ns_, nr)
        for i in range(more):
            spread.start(i)
        for part in range(2):
            for m in range(part * half, (part + 1) * half):
                if m:
                    out_copy(m).wait_recv()
            here = slice(part * rows_in_half, (part + 1) * rows_in_half)

            def up(n, carry):
                taken = g_out[part * half : (part + 1) * half].reshape(rows_in_half, width)
                at = pl.ds(pl.multiple_of(n * TILE, TILE), TILE)
                value = nt(taken, wd[at])
                dg[:, at] = (value * slope_g[here, at].astype(f32)).astype(low)
                du[:, at] = (value * slope_u[here, at].astype(f32)).astype(low)
                return carry

            lax.fori_loop(0, hidden // TILE, up, 0)

            def down(n, carry):
                at = pl.ds(pl.multiple_of(n * TILE, TILE), TILE)
                value = nt(dg[...], wg[at]) + nt(du[...], wu[at])
                yield_[part * half : (part + 1) * half, :, at] = value.astype(low).reshape(
                    half, cap, TILE
                )
                return carry

            lax.fori_loop(0, width // TILE, down, 0)
            for m in range(part * half, (part + 1) * half):
                if m:
                    back_copy(m).start()
            if part == 0:
                chain.start(2)
        x_out[0] = yield_[0]
        for hop in range(3, nc):
            chain.start(hop)
        for m in order:
            back_copy(m).wait_recv()
        keep.wait()
        for m in order:
            out_copy(m).wait_send()
            back_copy(m).wait_send()
        spread.finish()
        chain.finish()

    exchange = (ns, cap, width)
    return pl.pallas_call(
        kernel,
        name="moe_backward",
        cost_estimate=pl.CostEstimate(flops=45 * 10**9, bytes_accessed=10**7, transcendentals=0),
        out_shape=(
            jax.ShapeDtypeStruct(exchange, low),
            jax.ShapeDtypeStruct(exchange, low),
            jax.ShapeDtypeStruct((nc,) + cotangents.shape, low),
            jax.ShapeDtypeStruct((more,) + exchange, low),
        ),
        in_specs=[pl.BlockSpec(memory_space=VMEM)] * 5 + [pl.BlockSpec(memory_space=ANY)] * 3,
        out_specs=[pl.BlockSpec(memory_space=VMEM)] * 2 + [pl.BlockSpec(memory_space=ANY)] * 2,
        scratch_shapes=[
            VMEM((width, hidden), low),
            VMEM((width, hidden), low),
            VMEM((hidden, width), low),
            VMEM(exchange, low),
            VMEM((1,) + exchange, low),
            VMEM((ns * cap, hidden), low),
            VMEM((ns * cap, hidden), low),
            VMEM((rows_in_half, hidden), low),
            VMEM((rows_in_half, hidden), low),
            SEM.DMA((3,)),
            SEM.DMA((ns,)),
            SEM.DMA((ns,)),
            SEM.DMA((ns,)),
            SEM.DMA((ns,)),
            SEM.DMA((2, nc, 1)),
            SEM.DMA((2, nc, 1)),
            SEM.DMA((1,)),
            SEM.DMA((more, ns)),
            SEM.DMA((more, ns)),
        ],
        compiler_params=pltpu.CompilerParams(
            collective_id=6, has_side_effects=True, vmem_limit_bytes=60 * 1024 * 1024
        ),
    )(grads, rows, cotangents, pick_next, tokens, gate_w, up_w, down_w)


def slice_plan(hidden, nc):
    exact, tiles = hidden // nc, hidden // 128
    wide = max(-(-((c + 1) * exact) // 128) - (c * exact) // 128 for c in range(nc))
    return [min((c * exact) // 128, tiles - wide) * 128 for c in range(nc)], wide * 128


def slice_grads(rows, grads, gate_w, up_w, down_w, nc):
    width, hidden = gate_w.shape
    exact = hidden // nc
    starts, wide = slice_plan(hidden, nc)
    low, f32 = jnp.bfloat16, jnp.float32
    row_at = [(i, n) for i, x in enumerate(rows) for n in range(x.shape[0])]
    grad_at = [(len(rows) + i, n) for i, x in enumerate(grads) for n in range(x.shape[0])]
    count, block = len(rows) + len(grads), rows[0].shape[1]
    cuts = [(i, min(i + TILE, wide)) for i in range(0, wide, TILE)]

    def kernel(*refs):
        g_hbm, u_hbm, d_hbm, wg_out, wu_out, wd_out, xs, ys, wg, wu, wd, inner, dg, du, ag, au, ad, ws, rs = refs[count:]
        c = lax.axis_index("ctx")
        exact_tile = (c * exact) // 128
        begin = pl.multiple_of(jnp.minimum(exact_tile, (hidden - wide) // 128) * 128, 128)

        def fetch(i):
            (a, n), (b, k) = row_at[i], grad_at[i]
            return [
                pltpu.make_async_copy(refs[a].at[n], xs.at[i % 2], rs.at[i % 2, 0]),
                pltpu.make_async_copy(refs[b].at[k], ys.at[i % 2], rs.at[i % 2, 1]),
            ]

        loads = fetch(0) + [
            pltpu.make_async_copy(g_hbm.at[:, pl.ds(begin, wide)], wg, ws.at[0]),
            pltpu.make_async_copy(u_hbm.at[:, pl.ds(begin, wide)], wu, ws.at[1]),
            pltpu.make_async_copy(d_hbm.at[pl.ds(begin, wide)], wd, ws.at[2]),
        ]
        for load in loads:
            load.start()
        for load in loads:
            load.wait()
        for i in range(len(row_at)):
            if i:
                for load in fetch(i):
                    load.wait()
            if i + 1 < len(row_at):
                for load in fetch(i + 1):
                    load.start()
            x, dy = xs.at[i % 2], ys.at[i % 2]
            for left, right in cuts:
                value, slope = gelu_parts(dot32(x[...], wg[:, left:right]))
                linear = dot32(x[...], wu[:, left:right])
                down = nt(dy[...], wd[left:right])
                inner[:, left:right] = (value * linear).astype(low)
                dg[:, left:right] = (down * linear * slope).astype(low)
                du[:, left:right] = (down * value).astype(low)
            for total, one, other in ((ag, x, dg), (au, x, du), (ad, inner, dy)):
                if i:
                    total[...] += tn(one[...], other[...])
                else:
                    total[...] = tn(one[...], other[...])
        wg_out[...] = ag[...].astype(low)
        wu_out[...] = au[...].astype(low)
        wd_out[...] = ad[pl.ds(pl.multiple_of(c * exact - begin, 16), exact)]

    return pl.pallas_call(
        kernel,
        name="slice_grads",
        cost_estimate=pl.CostEstimate(flops=38 * 10**9, bytes_accessed=10**7, transcendentals=0),
        out_shape=(
            jax.ShapeDtypeStruct((width, wide), low),
            jax.ShapeDtypeStruct((width, wide), low),
            jax.ShapeDtypeStruct((exact, width), f32),
        ),
        in_specs=[pl.BlockSpec(memory_space=ANY)] * (count + 3),
        out_specs=[pl.BlockSpec(memory_space=VMEM)] * 3,
        scratch_shapes=[
            VMEM((2, block, width), low),
            VMEM((2, block, width), low),
            VMEM((width, wide), low),
            VMEM((width, wide), low),
            VMEM((wide, width), low),
            VMEM((block, wide), low),
            VMEM((block, wide), low),
            VMEM((block, wide), low),
            VMEM((width, wide), f32),
            VMEM((width, wide), f32),
            VMEM((wide, width), f32),
            SEM.DMA((3,)),
            SEM.DMA((2, 2)),
        ],
        compiler_params=pltpu.CompilerParams(vmem_limit_bytes=60 * 1024 * 1024),
    )(*rows, *grads, gate_w, up_w, down_w)


def per_device(
    tokens,
    segments,
    valid,
    routes,
    teacher,
    norm_attn,
    w_query,
    w_key,
    w_value,
    output_weight,
    rel_bias,
    norm_ffn,
    w_router,
    w_gate,
    w_up,
    w_down,
):
    nc = lax.axis_size("ctx")
    ns = lax.axis_size("shard")
    c, s = lax.axis_index("ctx"), lax.axis_index("shard")
    n_dev, nj = nc * ns, ns // 2
    row_count, width = tokens.shape[1:]
    top_count = routes.shape[2]
    experts = w_router.shape[1]
    capacity = (5 * row_count * top_count + 4 * experts - 1) // (4 * experts)
    length = row_count * nc
    low = jnp.bfloat16
    f32 = jnp.float32
    piece = w_query.shape[0]
    band = 2 * row_count

    route_local = routes[0]
    expert_ids = jnp.arange(experts, dtype=jnp.int32)
    route_hot = route_local[:, :, None] == expert_ids[None, None, :]
    flat_routes = route_local.reshape(row_count * top_count)
    route_hits = (flat_routes[:, None] == expert_ids[None, :]).astype(jnp.int32)
    before = jnp.cumsum(route_hits, axis=0) - route_hits
    slot_rank = jnp.sum(before * route_hits, axis=1).reshape(row_count, top_count)

    part = width // nc
    smalls = (
        norm_attn, norm_ffn, rel_bias, w_router.reshape(-1), segments[0].astype(low), valid[0].astype(low),
        route_local.astype(low).T.reshape(-1), slot_rank.astype(low).T.reshape(-1),
    )
    sizes = [x.shape[0] for x in smalls]
    starts = [sum(sizes[:i]) for i in range(len(sizes))]
    extra = jnp.concatenate(smalls + (jnp.zeros((EXTRA * part - sum(sizes),), low),))
    shares = [w.reshape(piece, nc, part).transpose(1, 0, 2) for w in (w_query, w_key, w_value, output_weight)]
    shares = jnp.concatenate(
        [x[:, None] for x in shares[:3]] + [jnp.broadcast_to(shares[3][None], (nc, nc, piece, part))], axis=1
    )
    weights, extras, tokens_all = gather_all(
        shares, extra.reshape(EXTRA, part), tokens[0], nc, ns
    )
    extras = extras.reshape(nc, ns, EXTRA * part)
    gain_attn, gain_ffn, full_bias, full_router = (
        extras[:, :, begin : begin + size].reshape(-1)
        for begin, size in zip(starts[:4], sizes[:4])
    )
    full_router = full_router.reshape(width, experts)
    table = full_bias.reshape(BUCKETS, HEADS).astype(f32)
    line = lax.dynamic_slice_in_dim(extras, s, 1, 1)[:, 0]
    line_seg = line[:, starts[4] : starts[4] + row_count].reshape(length).astype(jnp.int32)
    line_valid = line[:, starts[5] : starts[5] + row_count].reshape(length) > 0
    key_code = jnp.where(line_valid, line_seg, -1)[None]
    query_code = line_seg[:, None]
    valid_count = jnp.sum(extras[:, :, starts[5] : starts[5] + row_count].astype(f32))

    spot = (jnp.arange(band)[None, :] - jnp.arange(CHUNK)[:, None]) % band
    distance = jnp.where(spot <= row_count, row_count - spot, 3 * row_count - spot)
    level = bucket_of(distance, BUCKETS)
    level_hot = (level[:, :, None] == jnp.arange(BUCKETS)[None, None, :]).astype(f32)
    heads = HEADS // nc
    own_table = lax.dynamic_slice_in_dim(table, c * heads, heads, 1)
    slopes = jnp.einsum(
        "ixb,bh->hix", level_hot, own_table - own_table[BUCKETS - 1 :], precision=highest_precision
    )

    gain_one, gain_two = gain_attn.astype(f32), gain_ffn.astype(f32)
    first_all, queries, keys, values, mixed, log_total, residual, ffn_low = attend_forward(
        tokens_all, weights, gain_one[None], gain_two[None], query_code, key_code, slopes, nc, ns
    )
    ffn_in = ffn_low.astype(f32)
    router = full_router.astype(f32)
    logits = jnp.dot(ffn_in, router, precision=highest_precision)
    picked = jnp.sum(jnp.where(route_hot, logits[:, None, :], 0.0), axis=-1)
    gate_probs = jax.nn.softmax(picked, axis=-1)

    slots = -(-capacity // 16) * 16
    target = (route_local ^ s) * slots + slot_rank
    slot_ids = jnp.arange(experts * slots, dtype=jnp.int32)
    pick_first = (slot_ids[:, None] == target[None, :, 0]).astype(low)
    pick_second = (slot_ids[:, None] == target[None, :, 1]).astype(low)
    pick_both = pick_first + pick_second
    gate_w, up_w, down_w = w_gate[0], w_up[0], w_down[0]
    gate_rows = jnp.concatenate((gate_probs.T, jnp.zeros((8 - top_count, row_count), f32)), axis=0)
    other_line = line[c ^ jnp.arange(1, nc)]
    other_routes, other_slots = (
        other_line[:, starts[i] : starts[i] + top_count * row_count]
        .astype(jnp.int32)
        .reshape(nc - 1, top_count, row_count)
        for i in (6, 7)
    )
    other_target = (other_routes ^ s) * slots + other_slots
    other_first, other_second = (
        slot_ids[None, :, None] == other_target[:, m, None, :] for m in range(2)
    )
    other_picks = (other_first | other_second).astype(low).reshape(nc - 1, experts, slots, row_count)
    expert_rows, returned, ffn_all, gates_all, rows_next = moe_forward(
        pick_both.reshape(experts, slots, row_count), other_picks[0], ffn_low, gate_rows,
        gate_w, up_w, down_w, nc, ns,
    )
    returned = returned.reshape(experts * slots, width)
    picked_one, picked_two = tn(pick_first, returned), tn(pick_second, returned)
    output_sum = residual + gate_probs[:, :1] * picked_one + gate_probs[:, 1:] * picked_two
    valid_one = valid[0].astype(f32)
    deviation = output_sum - teacher[0].astype(f32)
    local_square = jnp.sum(valid_one[:, None] * deviation * deviation)
    everything = float(row_count * nc * ns)
    cotangent = everything / valid_count * deviation * valid_one[:, None]
    gate_grad = jnp.stack(
        (jnp.sum(cotangent * picked_one, axis=-1), jnp.sum(cotangent * picked_two, axis=-1)), axis=1
    )
    back_send = dot32(pick_first, (gate_probs[:, :1] * cotangent).astype(low)) + dot32(
        pick_second, (gate_probs[:, 1:] * cotangent).astype(low)
    )
    other_gates = gates_all[c ^ jnp.arange(1, nc)].astype(low)
    other_weighted = (
        jnp.where(other_first, other_gates[:, 0, None, :], low(0))
        + jnp.where(other_second, other_gates[:, 1, None, :], low(0))
    ).reshape(other_picks.shape)
    out_grad, sent_back, cotangent_all, rows_later = moe_backward(
        back_send.astype(low).reshape(experts, slots, width), expert_rows, cotangent.astype(low),
        other_picks[1 : nc // 2], ffn_all[c ^ jnp.arange(2, nc // 2 + 1)], gate_w, up_w, down_w, nc, ns,
    )
    ffn_grad = tn(pick_both, sent_back.reshape(experts * slots, width))
    pick_grad = gate_probs * (gate_grad - jnp.sum(gate_probs * gate_grad, axis=-1, keepdims=True))
    logits_grad = jnp.sum(jnp.where(route_hot, pick_grad[:, :, None], 0.0), axis=1)
    router_grad = contract(ffn_in, logits_grad, 0, 0, highest_precision)
    ffn_grad = ffn_grad + contract(logits_grad, router, 1, 1, highest_precision)
    unused, norm_two_back = jax.vjp(rms_norm, residual, gain_two)
    residual_from_norm, gain_two_grad = norm_two_back(ffn_grad)
    residual_grad = cotangent + residual_from_norm
    attn_grad_low = residual_grad.astype(low)
    input_grad, w_grads, gain_one_grad, near_sum, far_sum, rows_last, other_grads = attend_backward(
        attn_grad_low, residual_grad, mixed, tokens_all, first_all, queries, keys, values, log_total, weights,
        gain_one[None], query_code, key_code, slopes,
        other_picks[nc // 2 :], other_weighted, ffn_all[c ^ jnp.arange(nc // 2 + 1, nc)], cotangent_all, nc, ns,
    )
    gate_slice, up_slice, down_slice = slice_grads(
        [
            x.reshape(-1, experts * slots, width)
            for x in (expert_rows, rows_next, rows_later, rows_last)
        ],
        [x.reshape(-1, experts * slots, width) for x in (out_grad, other_grads)],
        gate_w, up_w, down_w, nc,
    )
    own_bias = jnp.einsum("hix,ixb->bh", near_sum, level_hot, precision=highest_precision)
    last_bucket = (jnp.arange(BUCKETS) == BUCKETS - 1).astype(f32)
    own_bias = own_bias + last_bucket[:, None] * jnp.sum(far_sum, axis=(1, 2))[None, :]
    bias_grad = lax.dynamic_update_slice_in_dim(
        jnp.zeros((BUCKETS, HEADS), f32), own_bias, c * heads, 1
    )
    small_grads = jnp.concatenate(
        [
            x.reshape(n_dev, -1).astype(low)
            for x in (gain_one_grad, gain_two_grad, bias_grad, router_grad)
        ],
        axis=1,
    )
    small_grads = jnp.pad(small_grads, ((0, 0), (0, EXTRA * part - small_grads.shape[1])))
    attn_sums, unused, small_sum, square_sum, gate_w_sum, up_w_sum = reduce_all(
        w_grads.reshape(3 + nc, nc, nj, 2, piece, part),
        small_grads.reshape(nc, nj, 2, EXTRA, part),
        jnp.full((8, 128), local_square, f32),
        [x.reshape(nc, width // nc, -1) for x in (gate_slice, up_slice)],
        gate_w.shape[1],
        nc,
        ns,
        3,
    )
    loss_value = square_sum[0, 0] / (2.0 * width * valid_count)
    small_sum = small_sum.reshape(-1)
    tails = [small_sum[begin : begin + size] for begin, size in zip(starts[:4], sizes[:4])]
    return (
        output_sum.astype(low)[None],
        loss_value,
        input_grad[None],
        tails[0],
        attn_sums[0],
        attn_sums[1],
        attn_sums[2],
        attn_sums[3],
        tails[2],
        tails[1],
        tails[3].reshape(w_router.shape),
        gate_w_sum[None],
        up_w_sum[None],
        down_slice[None],
    )


def solution(mesh):
    return jax.shard_map(
        per_device,
        mesh=mesh,
        in_specs=(
            P("shard", "ctx", None),
            P("shard", "ctx"),
            P("shard", "ctx"),
            P("shard", "ctx", None),
            P("shard", "ctx", None),
            P(("ctx", "shard")),
            P(("ctx", "shard"), None),
            P(("ctx", "shard"), None),
            P(("ctx", "shard"), None),
            P(("ctx", "shard"), None),
            P(("ctx", "shard")),
            P(("ctx", "shard")),
            P(("ctx", "shard"), None),
            P("shard", None, None),
            P("shard", None, None),
            P("shard", None, None),
        ),
        out_specs=(
            P("shard", "ctx", None),
            P(),
            P("shard", "ctx", None),
            P(("ctx", "shard")),
            P(("ctx", "shard"), None),
            P(("ctx", "shard"), None),
            P(("ctx", "shard"), None),
            P(("ctx", "shard"), None),
            P(("ctx", "shard")),
            P(("ctx", "shard")),
            P(("ctx", "shard"), None),
            P("shard", "ctx", None),
            P("shard", "ctx", None),
            P("shard", "ctx", None),
        ),
        check_vma=False,
    )
```

```python
import math

import jax
import jax.numpy as jnp
from jax import lax
from jax.experimental import pallas as pl
from jax.experimental.pallas import tpu as pltpu
from jax.sharding import PartitionSpec as P

HEADS = 16
HEAD = 64
BUCKETS = 32
MESH = pl.DeviceIdType.MESH
ANY = pl.ANY
VMEM = pltpu.VMEM
SEM = pltpu.SemaphoreType

highest_precision = lax.Precision.HIGHEST
max_distance = 128
epsilon = 1e-06
negative = -1e30
EXTRA = 16


def thresholds(buckets):
    exact_count = buckets // 2
    limits = list(range(1, exact_count))
    for bucket_level in range(exact_count, buckets):
        power = (bucket_level - exact_count) / exact_count
        limits.append(int(math.ceil(exact_count * (max_distance / exact_count) ** power)))
    return limits


def bucket_of(distance, buckets):
    bucket_total = jnp.zeros(distance.shape, jnp.int32)
    for threshold in thresholds(buckets):
        bucket_total = bucket_total + (distance >= threshold).astype(jnp.int32)
    return bucket_total


def rms_norm(values, gain_vector):
    return (
        values
        * lax.rsqrt(jnp.mean(values * values, axis=-1, keepdims=True) + epsilon)
        * gain_vector
    )


def contract(left_side, right_side, left_axis, right_axis, precision_mode=None):
    return lax.dot_general(
        left_side,
        right_side,
        (((left_axis,), (right_axis,)), ((), ())),
        precision=precision_mode,
        preferred_element_type=jnp.float32,
    )


def dot32(left_side, right_side):
    return jnp.dot(left_side, right_side, preferred_element_type=jnp.float32)


def nt(left_side, right_side):
    return contract(left_side, right_side, 1, 1)


def tn(left_side, right_side):
    return contract(left_side, right_side, 0, 0)


class Place:
    def __init__(self, nc, ns):
        self.nc, self.ns, self.nj = nc, ns, ns // 2
        self.c = lax.axis_index("ctx")
        self.s = lax.axis_index("shard")
        self.core = self.s % 2
        self.j = self.s // 2

    def along(self, d):
        return (lax.rem(self.c + d + self.nc, self.nc), self.s)

    def across(self, k):
        return (self.c, self.s ^ (2 * k))

    def twin(self):
        return (self.c, self.s ^ 1)

    def greet(self):
        barrier = pltpu.get_barrier_semaphore()
        partners = (
            [self.along(d) for d in range(1, self.nc)]
            + [self.across(k) for k in range(1, self.nj)]
            + [self.twin()]
        )
        for partner in partners:
            pl.semaphore_signal(barrier, inc=1, device_id=partner, device_id_type=MESH)
        pl.semaphore_wait(barrier, len(partners))


def remote(source, target, send, recv, device):
    return pltpu.make_async_remote_copy(
        src_ref=source,
        dst_ref=target,
        send_sem=send,
        recv_sem=recv,
        device_id=device,
        device_id_type=MESH,
    )


def gather_all(weights, extra, rows, nc, ns):
    n_dev, nj = nc * ns, ns // 2
    share = weights.shape[1:]
    full_shape = (share[0], nc, ns) + share[1:]

    def kernel(w_in, e_in, t_in, w_out, e_out, t_out, local, zs, zr, xs, xr, cs, cr, ts, tr):
        me = Place(nc, ns)

        def views(row, column):
            return (w_out.at[:, row, column], e_out.at[row, column])

        def piece(d, k):
            return views(lax.rem(me.c - d + nc, nc), me.s ^ (2 * k))

        mine = (w_in.at[me.c], e_in)
        locals_ = [
            pltpu.make_async_copy(source, target, local.at[i])
            for i, (source, target) in enumerate(
                zip(mine + (t_in,), views(me.c, me.s) + (t_out.at[me.c],))
            )
        ]
        for copy in locals_:
            copy.start()
        me.greet()
        sent = []

        def push(sources, targets, send, recv, device):
            for i in range(2):
                copy = remote(sources[i], targets[i], send.at[i], recv.at[i], device)
                copy.start()
                sent.append(copy)

        def arrive(targets, send, recv, device):
            for i in range(2):
                remote(targets[i], targets[i], send.at[i], recv.at[i], device).wait_recv()

        def token_copy(direction, hop):
            lane = 0 if direction > 0 else 1
            origin = lax.rem(me.c - direction * hop + nc, nc)
            return remote(
                t_in if hop == 0 else t_out.at[origin],
                t_out.at[origin],
                ts.at[lane, hop],
                tr.at[lane, hop],
                (lax.rem(me.c + direction + nc, nc), me.s),
            )

        def token_landing(direction, hop):
            lane = 0 if direction > 0 else 1
            origin = lax.rem(me.c - direction * (hop + 1) + nc, nc)
            landing = t_out.at[origin]
            return remote(landing, landing, ts.at[lane, hop], tr.at[lane, hop], me.along(1))

        def can_send(direction, hop):
            if direction > 0:
                return (me.c >= hop) & (me.c < nc - 1)
            return (me.c <= nc - 1 - hop) & (me.c > 0)

        def can_receive(direction, hop):
            if direction > 0:
                return me.c >= hop + 1
            return me.c <= nc - 2 - hop

        for d in range(1, nc):
            target = lax.rem(me.c + d, nc)
            push(
                (w_in.at[target], e_in), views(me.c, me.s), zs.at[d], zr.at[d], (target, me.s)
            )
        for direction in (1, -1):

            @pl.when(can_send(direction, 0))
            def _():
                token_copy(direction, 0).start()

        for k in range(1, nj):
            push(mine, views(me.c, me.s), xs.at[0, k], xr.at[0, k], me.across(k))
        push(mine, views(me.c, me.s), cs.at[0, 0], cr.at[0, 0], me.twin())

        for copy in locals_:
            copy.wait()
        for d in range(1, nc):
            here = piece(d, 0)
            arrive(here, zs.at[d], zr.at[d], me.along(-d))
            for k in range(1, nj):
                push(here, here, xs.at[d, k], xr.at[d, k], me.across(k))
            push(here, here, cs.at[d, 0], cr.at[d, 0], me.twin())
        for d in range(nc):
            for k in range(1, nj):
                here = piece(d, k)
                arrive(here, xs.at[d, k], xr.at[d, k], me.across(k))
                push(here, here, cs.at[d, k], cr.at[d, k], me.twin())
            if d < nc - 2:
                for direction in (1, -1):

                    @pl.when(can_receive(direction, d))
                    def _():
                        token_landing(direction, d).wait_recv()

                    @pl.when(can_send(direction, d + 1))
                    def _():
                        token_copy(direction, d + 1).start()

        for d in range(nc):
            for k in range(nj):
                here = views(lax.rem(me.c - d + nc, nc), me.s ^ 1 ^ (2 * k))
                arrive(here, cs.at[d, k], cr.at[d, k], me.twin())
        for direction in (1, -1):

            @pl.when(can_receive(direction, nc - 2))
            def _():
                token_landing(direction, nc - 2).wait_recv()

        for copy in sent:
            copy.wait_send()
        for direction in (1, -1):
            for hop in range(nc - 1):

                @pl.when(can_send(direction, hop))
                def _():
                    token_copy(direction, hop).wait_send()

    full, extras, tokens = pl.pallas_call(
        kernel,
        name="gather_all",
        cost_estimate=pl.CostEstimate(flops=50 * 10**9, bytes_accessed=10**7, transcendentals=0),
        out_shape=(
            jax.ShapeDtypeStruct(full_shape, weights.dtype),
            jax.ShapeDtypeStruct((nc, ns) + extra.shape, extra.dtype),
            jax.ShapeDtypeStruct((nc,) + rows.shape, rows.dtype),
        ),
        in_specs=[pl.BlockSpec(memory_space=ANY)] * 3,
        out_specs=[pl.BlockSpec(memory_space=ANY)] * 3,
        scratch_shapes=[
            SEM.DMA((3,)),
            SEM.DMA((nc, 2)),
            SEM.DMA((nc, 2)),
            SEM.DMA((nc, nj, 2)),
            SEM.DMA((nc, nj, 2)),
            SEM.DMA((nc, nj, 2)),
            SEM.DMA((nc, nj, 2)),
            SEM.DMA((2, nc)),
            SEM.DMA((2, nc)),
        ],
        compiler_params=pltpu.CompilerParams(collective_id=1, has_side_effects=True),
    )(weights, extra, rows)
    return (
        full.reshape(share[0], n_dev * share[1], share[2]),
        extras,
        tokens.reshape(nc * rows.shape[0], rows.shape[1]),
    )


CHUNK = 16


def fill_mask(mask, query_code, key_code, block, count):
    near = block * count
    query = query_code[pl.ds(near, count)]
    if block:
        mask[:, :near] = jnp.where(query == key_code[:, :near], 0.0, negative)
    row = lax.broadcasted_iota(jnp.int32, (count, count), 0)
    column = lax.broadcasted_iota(jnp.int32, (count, count), 1)
    seen = ((query == key_code[:, near : near + count]) & (row >= column)) | (row == column)
    mask[:, near : near + count] = jnp.where(seen, 0.0, negative)


def fill_slopes(bank, slopes, head, count):
    for i in range(count // CHUNK):
        row = slopes[head]
        bank[head, i * CHUNK : (i + 1) * CHUNK] = pltpu.roll(row, i * CHUNK, 1) if i else row


def biased(scores, mask, slope, block, count):
    end = (block + 1) * count
    band = 2 * count
    if end < band:
        return scores + mask[:, :end] + slope[:, band - end :]
    if end == band:
        return scores + mask[:, :end] + slope[...]
    wide = scores[:, : end - band] + mask[:, : end - band]
    tight = scores[:, end - band :] + mask[:, end - band : end] + slope[...]
    return jnp.concatenate((wide, tight), axis=1)


def attend_forward(tokens, weights, gain, gain_next, query_code, key_code, slopes, nc, ns):
    length, width = tokens.shape
    count = length // nc
    part = width // nc
    heads, _, band = slopes.shape
    low, f32 = jnp.bfloat16, jnp.float32

    def kernel(t_in, w_in, gain_in, next_in, qcode, kcode, toe, first, q_out, k_out, v_out, o_out, lse_out, x_out, y_out,
               mask, bank, osend, ss, rs):
        me = Place(nc, ns)
        barrier = pltpu.get_barrier_semaphore()
        for d in range(1, nc):
            pl.semaphore_signal(barrier, inc=1, device_id=me.along(d), device_id_type=MESH)
        pl.semaphore_wait(barrier, nc - 1)

        def norm(i, carry):
            at = pl.ds(pl.multiple_of(i * 64, 64), 64)
            x = t_in[at].astype(f32)
            rate = lax.rsqrt(jnp.mean(x * x, axis=-1, keepdims=True) + epsilon)
            first[at] = (x * rate * gain_in[...]).astype(low)
            return carry

        lax.fori_loop(0, length // 64, norm, 0)

        def project(i, carry):
            at = pl.ds(pl.multiple_of(i * count, count), count)
            block = first[at]
            q_out[at] = dot32(block, w_in[0]).astype(low)
            k_out[at] = dot32(block, w_in[1]).astype(low)
            v_out[at] = dot32(block, w_in[2]).astype(low)
            return carry

        lax.fori_loop(0, nc, project, 0)
        for head in range(heads):
            fill_slopes(bank, toe, head, count)
        lane = lax.broadcasted_iota(jnp.int32, (count, 2 * HEAD), 1)
        spot = lax.broadcasted_iota(jnp.int32, (count, 128), 1)
        own_copy = [
            remote(osend.at[b], o_out.at[me.c], ss.at[b], rs.at[me.c], (b, me.s)) for b in range(nc)
        ]
        for b in reversed(range(nc)):
            end = (b + 1) * count
            rows = pl.ds(b * count, count)
            fill_mask(mask, qcode, kcode, b, count)
            level = jnp.zeros((count, 128), f32)
            for pair in range(heads // 2):
                two = slice(pair * 2 * HEAD, (pair + 1) * 2 * HEAD)
                q_pair = q_out[rows, two] * low(1.0 / math.sqrt(HEAD))
                k_pair = k_out[:end, two]
                v_pair = v_out[:end, two]
                halves = []
                for half in range(2):
                    head = pair * 2 + half
                    inside = (lane >= HEAD) if half else (lane < HEAD)
                    scores = nt(jnp.where(inside, q_pair, low(0)), k_pair)
                    scores = biased(scores, mask, bank.at[head], b, count)
                    top = jnp.max(scores, axis=1, keepdims=True)
                    scores = jnp.exp(scores - top)
                    total = jnp.sum(scores, axis=1, keepdims=True)
                    halves.append(dot32(scores.astype(low), v_pair) * (1.0 / total))
                    level = jnp.where(spot == head, top + jnp.log(total), level)
                osend[b, :, two] = jnp.where(lane < HEAD, halves[0], halves[1]).astype(low)
            lse_out[rows] = level

            @pl.when(me.c == b)
            def _():
                o_out[me.c] = osend[b]

            @pl.when(me.c != b)
            def _():
                own_copy[b].start()

        for d in range(1, nc):
            origin = lax.rem(me.c + d, nc)
            remote(
                osend.at[0], o_out.at[origin], ss.at[0], rs.at[origin], me.along(d)
            ).wait_recv()
        own = pl.ds(pl.multiple_of(me.c * count, count), count)
        squares = jnp.zeros((count, 1), f32)
        for n in range(nc):
            columns = slice(n * part, (n + 1) * part)
            x = t_in[own, columns].astype(f32)
            for origin in range(nc):
                x = x + dot32(o_out[origin], w_in[3 + n, origin * part : (origin + 1) * part])
            x_out[:, columns] = x
            squares = squares + jnp.sum(x * x, axis=1, keepdims=True)
        rate = lax.rsqrt(squares * (1.0 / width) + epsilon)
        for n in range(nc):
            columns = slice(n * part, (n + 1) * part)
            y_out[:, columns] = (x_out[:, columns] * rate * next_in[:, columns]).astype(low)
        for b in range(nc):

            @pl.when(me.c != b)
            def _():
                own_copy[b].wait_send()

    return pl.pallas_call(
        kernel,
        name="attend_forward",
        cost_estimate=pl.CostEstimate(flops=25 * 10**9, bytes_accessed=10**7, transcendentals=0),
        out_shape=(
            jax.ShapeDtypeStruct((length, width), low),
            jax.ShapeDtypeStruct((length, part), low),
            jax.ShapeDtypeStruct((length, part), low),
            jax.ShapeDtypeStruct((length, part), low),
            jax.ShapeDtypeStruct((nc, count, part), low),
            jax.ShapeDtypeStruct((length, 128), f32),
            jax.ShapeDtypeStruct((count, width), f32),
            jax.ShapeDtypeStruct((count, width), low),
        ),
        in_specs=[pl.BlockSpec(memory_space=VMEM)] * 7,
        out_specs=[pl.BlockSpec(memory_space=VMEM)] * 8,
        scratch_shapes=[
            VMEM((count, length), f32),
            VMEM((heads, count, band), f32),
            VMEM((nc, count, part), low),
            SEM.DMA((nc,)),
            SEM.DMA((nc,)),
        ],
        compiler_params=pltpu.CompilerParams(
            collective_id=3, has_side_effects=True, vmem_limit_bytes=56 * 1024 * 1024
        ),
    )(tokens, weights, gain, gain_next, query_code, key_code, slopes)


def attend_backward(
    dattn, dh, o_all, tokens, first, q_all, k_all, v_all, lse, weights, gain, query_code, key_code, slopes,
    picks, weighted, normed, cotangents, nc, ns,
):
    length, width = tokens.shape
    count = length // nc
    part = width // nc
    heads, _, band = slopes.shape
    low, f32 = jnp.bfloat16, jnp.float32
    scale = 1.0 / math.sqrt(HEAD)
    more = picks.shape[0]
    exchange = picks.shape[1:3] + (width,)

    def kernel(a_in, dh_in, o_in, t_in, first_in, q_in, k_in, v_in, lse_in, w_in, gain_in, qcode, kcode, toe,
               p_in, pw_in, n_in, c_in,
               x_out, w_out, gain_out, near_out, far_out, n_out, c_out,
               mask, bank, dsend, dall, dq, dk, dv, fsend, frecv, fown, nsend, ss, rs, fs, fr, ns_, nr):
        me = Place(nc, ns)
        barrier = pltpu.get_barrier_semaphore()
        partners = [me.along(d) for d in range(1, nc)] + [(me.c, me.s ^ m) for m in range(1, ns)]
        for partner in partners:
            pl.semaphore_signal(barrier, inc=1, device_id=partner, device_id_type=MESH)
        pl.semaphore_wait(barrier, len(partners))

        def do_copy(d):
            return remote(dsend.at[d], dall.at[me.c], ss.at[d], rs.at[d], me.along(d))

        for d in list(range(1, nc)) + [0]:
            target = lax.rem(me.c + d, nc)
            at = pl.ds(pl.multiple_of(target * part, part), part)
            value = nt(a_in[:, :part], w_in[3, at])
            for n in range(1, nc):
                value = value + nt(a_in[:, n * part : (n + 1) * part], w_in[3 + n, at])
            if d:
                dsend[d] = value.astype(low)
                do_copy(d).start()
            else:
                dall[me.c] = value.astype(low)
        jobs = [(pw_in.at[d], c_in.at[me.c ^ (d + 1)], c_out.at[d]) for d in range(nc - 1)]
        jobs = jobs + [(p_in.at[d], n_in.at[me.c ^ (nc - more + d)], n_out.at[d]) for d in range(more)]
        spread = Spread(me, jobs, nsend, ns_, nr)
        for i in range(len(jobs)):
            spread.start(i)
        for n in range(nc):
            for origin in range(nc):
                w_out[3 + n, origin * part : (origin + 1) * part] = tn(
                    o_in[origin], a_in[:, n * part : (n + 1) * part]
                ).astype(low)
        for head in range(heads):
            fill_slopes(bank, toe, head, count)
        lane = lax.broadcasted_iota(jnp.int32, (count, 2 * HEAD), 1)
        spot = lax.broadcasted_iota(jnp.int32, (count, 128), 1)
        dk[...] = jnp.zeros_like(dk)
        dv[...] = jnp.zeros_like(dv)
        near_out[...] = jnp.zeros_like(near_out)
        far_out[...] = jnp.zeros_like(far_out)
        gain_out[...] = jnp.zeros_like(gain_out)
        for d in range(1, nc):
            origin = lax.rem(me.c - d + nc, nc)
            remote(dsend.at[d], dall.at[origin], ss.at[d], rs.at[d], me.along(d)).wait_recv()
        out_copy = [
            remote(fsend.at[b], frecv.at[me.c], fs.at[b], fr.at[me.c], (b, me.s)) for b in range(nc)
        ]
        for b in reversed(range(nc)):
            end = (b + 1) * count
            rows = pl.ds(b * count, count)
            fill_mask(mask, qcode, kcode, b, count)
            level = lse_in[rows]
            for pair in range(heads // 2):
                two = slice(pair * 2 * HEAD, (pair + 1) * 2 * HEAD)
                q_pair = q_in[rows, two] * low(scale)
                do_pair = dall[b, :, two]
                k_pair = k_in[:end, two]
                v_pair = v_in[:end, two]
                parts = []
                for half in range(2):
                    head = pair * 2 + half
                    inside = (lane >= HEAD) if half else (lane < HEAD)
                    q_one = jnp.where(inside, q_pair, low(0))
                    do_one = jnp.where(inside, do_pair, low(0))
                    own_level = jnp.sum(
                        jnp.where(spot == head, level, 0.0), axis=1, keepdims=True
                    )
                    probs = jnp.exp(
                        biased(nt(q_one, k_pair), mask, bank.at[head], b, count) - own_level
                    )
                    grads = probs * nt(do_one, v_pair)
                    grads = grads - probs * jnp.sum(grads, axis=1, keepdims=True)
                    low_grads = grads.astype(low)
                    parts.append(dot32(low_grads, k_pair))
                    dk[:end, two] += tn(low_grads, q_one)
                    dv[:end, two] += tn(probs.astype(low), do_one)
                    near = grads[:, max(end - band, 0) :]
                    if end < band:
                        near = jnp.concatenate((jnp.zeros((count, band - end), f32), near), axis=1)
                    height = count
                    while height > CHUNK:
                        height = height // 2
                        near = near[:height] + pltpu.roll(near[height:], band - height, 1)
                    near_out[head] += near
                    if end > band:
                        far = grads[:, : end - band]
                        total = far[:, :128]
                        for piece in range(1, (end - band) // 128):
                            total = total + far[:, piece * 128 : (piece + 1) * 128]
                        height = count
                        while height > 8:
                            height = height // 2
                            total = total[:height] + total[height:]
                        far_out[head] += total
                dq[rows, two] = (jnp.where(lane < HEAD, parts[0], parts[1]) * scale).astype(low)
            dq_low, dk_low, dv_low = dq[rows], dk[rows].astype(low), dv[rows].astype(low)
            for n in range(nc):
                columns = slice(n * part, (n + 1) * part)
                at = pl.ds(n * part, part)
                value = nt(dq_low, w_in[0, at]) + nt(dk_low, w_in[1, at]) + nt(dv_low, w_in[2, at])
                fown[:, columns] = value
            x = t_in[rows].astype(f32)
            rate = lax.rsqrt(jnp.mean(x * x, axis=-1, keepdims=True) + epsilon)
            gain_out[...] += jnp.sum(fown[...] * x * rate, axis=0, keepdims=True)
            fsend[b] = fown[...].astype(low)

            @pl.when(me.c == b)
            def _():
                x_out[...] = fown[...]

            @pl.when(me.c != b)
            def _():
                out_copy[b].start()

        for i, grads in enumerate((dq, dk, dv)):
            for n in range(nc):
                at = slice(n * part, (n + 1) * part)
                w_out[i, at] = tn(first_in[:, at], grads[...].astype(low)).astype(low)
        for d in range(1, nc):
            origin = lax.rem(me.c + d, nc)
            remote(
                fsend.at[0], frecv.at[origin], fs.at[0], fr.at[origin], me.along(d)
            ).wait_recv()
            x_out[...] += frecv[origin].astype(f32)
        own = pl.ds(pl.multiple_of(me.c * count, count), count)
        x = t_in[own].astype(f32)
        rate = lax.rsqrt(jnp.mean(x * x, axis=-1, keepdims=True) + epsilon)
        scaled = x_out[...] * gain_in[...]
        pull = jnp.mean(scaled * x, axis=-1, keepdims=True)
        x_out[...] = dh_in[...] + rate * scaled - x * (rate * rate * rate * pull)
        spread.finish()
        for d in range(1, nc):
            do_copy(d).wait_send()
        for b in range(nc):

            @pl.when(me.c != b)
            def _():
                out_copy[b].wait_send()

    return pl.pallas_call(
        kernel,
        name="attend_backward",
        cost_estimate=pl.CostEstimate(flops=50 * 10**9, bytes_accessed=10**7, transcendentals=0),
        out_shape=(
            jax.ShapeDtypeStruct((count, width), f32),
            jax.ShapeDtypeStruct((3 + nc, width, part), low),
            jax.ShapeDtypeStruct((1, width), f32),
            jax.ShapeDtypeStruct((heads, CHUNK, band), f32),
            jax.ShapeDtypeStruct((heads, 8, 128), f32),
            jax.ShapeDtypeStruct((more,) + exchange, low),
            jax.ShapeDtypeStruct((nc - 1,) + exchange, low),
        ),
        in_specs=[pl.BlockSpec(memory_space=VMEM)] * 18,
        out_specs=[pl.BlockSpec(memory_space=VMEM)] * 5 + [pl.BlockSpec(memory_space=ANY)] * 2,
        scratch_shapes=[
            VMEM((count, length), f32),
            VMEM((heads, count, band), f32),
            VMEM((nc, count, part), low),
            VMEM((nc, count, part), low),
            VMEM((length, part), low),
            VMEM((length, part), f32),
            VMEM((length, part), f32),
            VMEM((nc, count, width), low),
            VMEM((nc, count, width), low),
            VMEM((count, width), f32),
            VMEM((4,) + exchange, low),
            SEM.DMA((nc,)),
            SEM.DMA((nc,)),
            SEM.DMA((nc,)),
            SEM.DMA((nc,)),
            SEM.DMA((nc - 1 + more, ns)),
            SEM.DMA((nc - 1 + more, ns)),
        ],
        compiler_params=pltpu.CompilerParams(
            collective_id=4, has_side_effects=True, vmem_limit_bytes=61 * 1024 * 1024
        ),
    )(dattn, dh, o_all, tokens, first, q_all, k_all, v_all, lse, weights, gain, query_code, key_code, slopes,
      picks, weighted, normed, cotangents)


def activation(gate_values, up_values):
    return jax.nn.gelu(gate_values) * up_values


def gelu_parts(x):
    c, a = math.sqrt(2.0 / math.pi), 0.044715
    square = x * x
    t = jnp.tanh(c * x * (1.0 + a * square))
    half = 0.5 * (1.0 + t)
    return x * half, half + (0.5 * c) * x * (1.0 - t * t) * (1.0 + (3.0 * a) * square)


class Chain:
    def __init__(self, me, pairs, send, recv):
        self.me, self.pairs, self.send, self.recv, self.nc = me, pairs, send, recv, me.nc

    def copies(self, direction, hop, landing):
        me, nc = self.me, self.nc
        lane = 0 if direction > 0 else 1
        origin = lax.rem(me.c - direction * (hop + 1 if landing else hop) + 2 * nc, nc)
        result = []
        for i, (own, every) in enumerate(self.pairs):
            target = every.at[origin]
            source = own if hop == 0 and not landing else target
            result.append(
                remote(
                    source, target, self.send.at[lane, hop, i], self.recv.at[lane, hop, i],
                    me.along(direction),
                )
            )
        return result

    def sends(self, direction, hop):
        c, nc = self.me.c, self.nc
        if direction > 0:
            return (c >= hop) & (c < nc - 1)
        return (c <= nc - 1 - hop) & (c > 0)

    def lands(self, direction, hop):
        c, nc = self.me.c, self.nc
        if direction > 0:
            return c >= hop + 1
        return c <= nc - 2 - hop

    def start(self, hop):
        if hop >= self.nc:
            return
        for direction in (1, -1):
            if hop:

                @pl.when(self.lands(direction, hop - 1))
                def _():
                    for copy in self.copies(direction, hop - 1, True):
                        copy.wait_recv()

            if hop < self.nc - 1:

                @pl.when(self.sends(direction, hop))
                def _():
                    for copy in self.copies(direction, hop, False):
                        copy.start()

    def finish(self):
        for direction in (1, -1):
            for hop in range(self.nc - 1):

                @pl.when(self.sends(direction, hop))
                def _():
                    for copy in self.copies(direction, hop, False):
                        copy.wait_send()


def greet_experts(me):
    barrier = pltpu.get_barrier_semaphore()
    partners = [(me.c, me.s ^ m) for m in range(1, me.ns)] + [me.along(1), me.along(-1)]
    for partner in partners:
        pl.semaphore_signal(barrier, inc=1, device_id=partner, device_id_type=MESH)
    pl.semaphore_wait(barrier, len(partners))


TILE = 256


class Spread:
    def __init__(self, me, jobs, send, send_sem, recv_sem):
        self.me, self.jobs, self.send = me, jobs, send
        self.send_sem, self.recv_sem = send_sem, recv_sem
        self.order = list(range(2, me.ns)) + [1]
        self.turns = send.shape[0]

    def copy(self, i, m):
        return remote(
            self.send.at[i % self.turns, m], self.jobs[i][2].at[m],
            self.send_sem.at[i, m], self.recv_sem.at[i, m], (self.me.c, self.me.s ^ m),
        )

    def own(self, i):
        return pltpu.make_async_copy(
            self.send.at[i % self.turns, 0], self.jobs[i][2].at[0], self.send_sem.at[i, 0]
        )

    def left(self, i):
        for m in self.order:
            self.copy(i, m).wait_send()
        self.own(i).wait()

    def start(self, i):
        if i >= self.turns:
            self.left(i - self.turns)
        picks, tokens = self.jobs[i][:2]
        for m in self.order + [0]:
            self.send[i % self.turns, m] = dot32(picks[m], tokens[...]).astype(self.send.dtype)
            if m:
                self.copy(i, m).start()
            else:
                self.own(i).start()

    def finish(self):
        for i in range(len(self.jobs)):
            for m in self.order:
                self.copy(i, m).wait_recv()
            if i >= len(self.jobs) - self.turns:
                self.left(i)


def row_groups(ns):
    return [(2, 6), (6, ns), (0, 2)]


def moe_forward(pick, pick_next, tokens, gates, gate_w, up_w, down_w, nc, ns):
    cap, count = pick.shape[1:]
    width, hidden = gate_w.shape
    low, f32 = jnp.bfloat16, jnp.float32
    groups = row_groups(ns)
    most = max(end - start for start, end in groups) * cap

    def kernel(p_in, n_in, t_in, s_in, g_hbm, u_hbm, d_hbm, r_out, y_out, t_all, s_all, n_out,
               wg, wu, wd, send, yield_, nsend, inner, ws, ss, rs, ys, yr, ts, tr, ls, ns_, nr):
        me = Place(nc, ns)
        loads = [
            pltpu.make_async_copy(source, target, ws.at[i])
            for i, (source, target) in enumerate(((g_hbm, wg), (u_hbm, wu), (d_hbm, wd)))
        ]
        for load in loads:
            load.start()
        keep = [
            pltpu.make_async_copy(t_in, t_all.at[me.c], ls.at[0]),
            pltpu.make_async_copy(s_in, s_all.at[me.c], ls.at[1]),
        ]
        for copy in keep:
            copy.start()
        greet_experts(me)

        def there(m):
            return (me.c, me.s ^ m)

        def out_copy(m):
            return remote(send.at[m], r_out.at[m], ss.at[m], rs.at[m], there(m))

        def back_copy(m):
            return remote(yield_.at[m], y_out.at[m], ys.at[m], yr.at[m], there(m))

        for m in list(range(2, 6)) + [1]:
            send[m] = dot32(p_in[m], t_in[...]).astype(low)
            out_copy(m).start()
        chain = Chain(me, ((t_in, t_all), (s_in, s_all)), ts, tr)
        chain.start(0)
        r_out[0] = dot32(p_in[0], t_in[...]).astype(low)
        for m in range(6, ns):
            send[m] = dot32(p_in[m], t_in[...]).astype(low)
        for load in loads:
            load.wait()
        for turn, (begin, end) in enumerate(groups):
            size = (end - begin) * cap
            for m in range(begin, end):
                if m:
                    out_copy(m).wait_recv()
            if turn == 0:
                for m in range(6, ns):
                    out_copy(m).start()

            def up(n, carry):
                rows = r_out[begin:end].reshape(size, width)
                at = pl.ds(pl.multiple_of(n * TILE, TILE), TILE)
                value = activation(dot32(rows, wg[:, at]), dot32(rows, wu[:, at]))
                inner[:size, at] = value.astype(low)
                return carry

            lax.fori_loop(0, hidden // TILE, up, 0)
            chain.start(turn + 1)
            if turn == 0:
                spread = Spread(me, [(n_in, t_all.at[me.c ^ 1], n_out)], nsend, ns_, nr)
                spread.start(0)

            def down(n, carry):
                at = pl.ds(pl.multiple_of(n * TILE, TILE), TILE)
                value = dot32(inner[:size], wd[:, at]).astype(low)
                yield_[begin:end, :, at] = value.reshape(end - begin, cap, TILE)
                return carry

            lax.fori_loop(0, width // TILE, down, 0)
            for m in range(begin, end):
                if m:
                    back_copy(m).start()
        y_out[0] = yield_[0]
        for hop in range(len(groups) + 1, nc):
            chain.start(hop)
        for m in range(1, ns):
            back_copy(m).wait_recv()
        for copy in keep:
            copy.wait()
        for m in range(1, ns):
            out_copy(m).wait_send()
            back_copy(m).wait_send()
        spread.finish()
        chain.finish()

    exchange = (ns, cap, width)
    return pl.pallas_call(
        kernel,
        name="moe_forward",
        cost_estimate=pl.CostEstimate(flops=45 * 10**9, bytes_accessed=10**7, transcendentals=0),
        out_shape=(
            jax.ShapeDtypeStruct(exchange, low),
            jax.ShapeDtypeStruct(exchange, low),
            jax.ShapeDtypeStruct((nc,) + tokens.shape, low),
            jax.ShapeDtypeStruct((nc,) + gates.shape, f32),
            jax.ShapeDtypeStruct(exchange, low),
        ),
        in_specs=[pl.BlockSpec(memory_space=VMEM)] * 4 + [pl.BlockSpec(memory_space=ANY)] * 3,
        out_specs=[pl.BlockSpec(memory_space=VMEM)] * 4 + [pl.BlockSpec(memory_space=ANY)],
        scratch_shapes=[
            VMEM((width, hidden), low),
            VMEM((width, hidden), low),
            VMEM((hidden, width), low),
            VMEM(exchange, low),
            VMEM(exchange, low),
            VMEM((1,) + exchange, low),
            VMEM((most, hidden), low),
            SEM.DMA((3,)),
            SEM.DMA((ns,)),
            SEM.DMA((ns,)),
            SEM.DMA((ns,)),
            SEM.DMA((ns,)),
            SEM.DMA((2, nc, 2)),
            SEM.DMA((2, nc, 2)),
            SEM.DMA((2,)),
            SEM.DMA((1, ns)),
            SEM.DMA((1, ns)),
        ],
        compiler_params=pltpu.CompilerParams(
            collective_id=5, has_side_effects=True, vmem_limit_bytes=56 * 1024 * 1024
        ),
    )(pick, pick_next, tokens, gates, gate_w, up_w, down_w)


def moe_backward(grads, rows, cotangents, pick_next, tokens, gate_w, up_w, down_w, nc, ns):
    cap = rows.shape[1]
    width, hidden = gate_w.shape
    low, f32 = jnp.bfloat16, jnp.float32
    groups = [(2, 6), (0, 2), (6, ns)]
    most = max(end - start for start, end in groups) * cap
    more = pick_next.shape[0]

    def kernel(g_in, r_in, t_in, n_in, f_in, g_hbm, u_hbm, d_hbm, g_out, x_out, t_all, n_out,
               wg, wu, wd, yield_, nsend, slope_g, slope_u, dg, du, ws, ss, rs, ys, yr, ts, tr, ls, ns_, nr):
        me = Place(nc, ns)
        loads = [
            pltpu.make_async_copy(source, target, ws.at[i])
            for i, (source, target) in enumerate(((g_hbm, wg), (u_hbm, wu), (d_hbm, wd)))
        ]
        for load in loads:
            load.start()
        keep = pltpu.make_async_copy(t_in, t_all.at[me.c], ls.at[0])
        keep.start()
        greet_experts(me)

        def there(m):
            return (me.c, me.s ^ m)

        def out_copy(m):
            return remote(g_in.at[m], g_out.at[m], ss.at[m], rs.at[m], there(m))

        def back_copy(m):
            return remote(yield_.at[m], x_out.at[m], ys.at[m], yr.at[m], there(m))

        for m in list(range(2, 6)) + [1]:
            out_copy(m).start()
        chain = Chain(me, ((t_in, t_all),), ts, tr)
        chain.start(0)
        g_out[0] = g_in[0]
        for load in loads:
            load.wait()

        def again(n, carry):
            every = r_in[...].reshape(ns * cap, width)
            at = pl.ds(pl.multiple_of(n * TILE, TILE), TILE)
            value, slope = gelu_parts(dot32(every, wg[:, at]))
            slope_g[:, at] = (slope * dot32(every, wu[:, at])).astype(slope_g.dtype)
            slope_u[:, at] = value.astype(slope_u.dtype)
            return carry

        lax.fori_loop(0, hidden // TILE, again, 0)
        jobs = [(n_in.at[i], f_in.at[me.c ^ (i + 2)], n_out.at[i]) for i in range(more)]
        spread = Spread(me, jobs, nsend, ns_, nr)
        chain.start(1)
        for turn, (begin, end) in enumerate(groups):
            size = (end - begin) * cap
            for m in range(begin, end):
                if m:
                    out_copy(m).wait_recv()
            if turn == 0:
                for m in range(6, ns):
                    out_copy(m).start()
                for i in range(more):
                    spread.start(i)
            here = slice(begin * cap, end * cap)

            def up(n, carry):
                taken = g_out[begin:end].reshape(size, width)
                at = pl.ds(pl.multiple_of(n * TILE, TILE), TILE)
                value = nt(taken, wd[at])
                dg[:size, at] = (value * slope_g[here, at].astype(f32)).astype(low)
                du[:size, at] = (value * slope_u[here, at].astype(f32)).astype(low)
                return carry

            lax.fori_loop(0, hidden // TILE, up, 0)

            def down(n, carry):
                at = pl.ds(pl.multiple_of(n * TILE, TILE), TILE)
                value = nt(dg[:size], wg[at]) + nt(du[:size], wu[at])
                yield_[begin:end, :, at] = value.astype(low).reshape(end - begin, cap, TILE)
                return carry

            lax.fori_loop(0, width // TILE, down, 0)
            for m in range(begin, end):
                if m:
                    back_copy(m).start()
            chain.start(turn + 2)
        x_out[0] = yield_[0]
        for hop in range(len(groups) + 2, nc):
            chain.start(hop)
        for m in range(1, ns):
            back_copy(m).wait_recv()
        keep.wait()
        for m in range(1, ns):
            out_copy(m).wait_send()
            back_copy(m).wait_send()
        spread.finish()
        chain.finish()

    exchange = (ns, cap, width)
    return pl.pallas_call(
        kernel,
        name="moe_backward",
        cost_estimate=pl.CostEstimate(flops=45 * 10**9, bytes_accessed=10**7, transcendentals=0),
        out_shape=(
            jax.ShapeDtypeStruct(exchange, low),
            jax.ShapeDtypeStruct(exchange, low),
            jax.ShapeDtypeStruct((nc,) + cotangents.shape, low),
            jax.ShapeDtypeStruct((more,) + exchange, low),
        ),
        in_specs=[pl.BlockSpec(memory_space=VMEM)] * 5 + [pl.BlockSpec(memory_space=ANY)] * 3,
        out_specs=[pl.BlockSpec(memory_space=VMEM)] * 2 + [pl.BlockSpec(memory_space=ANY)] * 2,
        scratch_shapes=[
            VMEM((width, hidden), low),
            VMEM((width, hidden), low),
            VMEM((hidden, width), low),
            VMEM(exchange, low),
            VMEM((1,) + exchange, low),
            VMEM((ns * cap, hidden), low),
            VMEM((ns * cap, hidden), low),
            VMEM((most, hidden), low),
            VMEM((most, hidden), low),
            SEM.DMA((3,)),
            SEM.DMA((ns,)),
            SEM.DMA((ns,)),
            SEM.DMA((ns,)),
            SEM.DMA((ns,)),
            SEM.DMA((2, nc, 1)),
            SEM.DMA((2, nc, 1)),
            SEM.DMA((1,)),
            SEM.DMA((more, ns)),
            SEM.DMA((more, ns)),
        ],
        compiler_params=pltpu.CompilerParams(
            collective_id=6, has_side_effects=True, vmem_limit_bytes=60 * 1024 * 1024
        ),
    )(grads, rows, cotangents, pick_next, tokens, gate_w, up_w, down_w)


def slice_plan(hidden, nc):
    exact, tiles = hidden // nc, hidden // 128
    wide = max(-(-((c + 1) * exact) // 128) - (c * exact) // 128 for c in range(nc))
    return [min((c * exact) // 128, tiles - wide) * 128 for c in range(nc)], wide * 128


def finish_all(grads, small, squares, rows, row_grads, gate_w, up_w, down_w, nc, ns, kept):
    nj = ns // 2
    parts, piece, width = grads.shape[0], grads.shape[4], grads.shape[5]
    low, f32 = jnp.bfloat16, jnp.float32
    tile = squares.shape
    features, hidden = gate_w.shape
    band, half, exact = features // nc, hidden // 2, hidden // nc
    wide = slice_plan(half, nc // 2)[1]
    row_at = [(i, n) for i, x in enumerate(rows) for n in range(x.shape[0])]
    grad_at = [(len(rows) + i, n) for i, x in enumerate(row_grads) for n in range(x.shape[0])]
    count, block = len(rows) + len(row_grads), rows[0].shape[1]
    blocks = len(row_at)
    rest = half - wide if nc == 4 else 128
    widths = [wide] + [rest] * ((half - wide) // rest)

    def kernel(g_in, e_in, q_in, *refs):
        (g_hbm, u_hbm, d_hbm, k0_out, k1_out, k2_out, k3_out, e_out, q_out, wg_out, wu_out, wd_out,
         gt, et, gc, ec, gx, ex, gz, ez, g_sum, qz, qx, qc, qa, qb,
         cs, cr, xs, xr, zs, zr, q1s, q1r, q2s, q2r, q3s, q3r,
         xb, yb, wg, wu, wd, inner, dg, du, ag, au, ad, pair_send, down_send, ws, rs, ps, pr, ds, dr) = refs[count:]
        me = Place(nc, ns)
        k_out = (k0_out, k1_out, k2_out, k3_out)
        high, lower = me.c // 2, me.c % 2
        begin = pl.multiple_of(lower * half, 128)
        place = lower * (nc // 2) + high
        source = (me.c % (nc // 2)) * 2 + me.c // (nc // 2)
        offset = high * exact
        cut = pl.multiple_of(jnp.minimum(offset // 128, (half - wide) // 128) * 128, 128)
        begins = [cut] + [lax.rem(cut + wide + n * rest, half) for n in range((half - wide) // rest)]

        def fetch(i):
            (a, n), (b, k) = row_at[i % blocks], grad_at[i % blocks]
            return [
                pltpu.make_async_copy(refs[a].at[n], xb.at[i % 2], rs.at[i % 2, 0]),
                pltpu.make_async_copy(refs[b].at[k], yb.at[i % 2], rs.at[i % 2, 1]),
            ]

        loads = fetch(0) + [
            pltpu.make_async_copy(g_hbm.at[:, pl.ds(begin, half)], wg, ws.at[0]),
            pltpu.make_async_copy(u_hbm.at[:, pl.ds(begin, half)], wu, ws.at[1]),
            pltpu.make_async_copy(d_hbm.at[pl.ds(begin, half)], wd, ws.at[2]),
        ]
        for load in loads:
            load.start()
        me.greet()

        def both(pairs, send, recv, device):
            return [
                remote(one, target, send.at[i], recv.at[i], device)
                for i, (one, target) in enumerate(pairs)
            ]

        def core_copy(d):
            row = lax.rem(me.c + d, nc)
            other = 1 - me.core
            return both(
                ((g_in.at[:, row, :, other], gc.at[d]), (e_in.at[row, :, other], ec.at[d])),
                cs.at[d], cr.at[d], me.twin(),
            )

        def cross_copy(d, k):
            return both(
                ((gt.at[d, :, me.j ^ k], gx.at[d, k - 1]), (et.at[d, me.j ^ k], ex.at[d, k - 1])),
                xs.at[d, k], xr.at[d, k], me.across(k),
            )

        def along_copy(d):
            return both(
                ((gt.at[d, :, me.j], gz.at[d - 1]), (et.at[d, me.j], ez.at[d - 1])),
                zs.at[d], zr.at[d], me.along(d),
            )

        def start(copies):
            for copy in copies:
                copy.start()

        def landed(copies):
            for copy in copies:
                copy.wait_recv()

        def q_along(d):
            return remote(q_in, qz.at[d - 1], q1s.at[d], q1r.at[d], me.along(d))

        def q_across(k):
            return remote(qa, qx.at[k - 1], q2s.at[k], q2r.at[k], me.across(k))

        q_twin = remote(qb, qc, q3s.at[0], q3r.at[0], me.twin())
        order = list(range(1, nc)) + [0]

        def core_stage():
            for d in order:
                landed(core_copy(d))
                row = lax.rem(me.c + d, nc)

                def add_core(i, carry):
                    for k in range(nj):
                        gt[d, i, k] = (
                            g_in[i, row, k, me.core].astype(f32) + gc[d, i, k].astype(f32)
                        ).astype(low)
                    return carry

                lax.fori_loop(0, parts, add_core, 0)
                for k in range(nj):
                    et[d, k] = (
                        e_in[row, k, me.core].astype(f32) + ec[d, k].astype(f32)
                    ).astype(low)
                for k in range(1, nj):
                    start(cross_copy(d, k))
            for d in range(1, nc):
                q_along(d).wait_recv()
            value = q_in[...]
            for d in range(1, nc):
                value = value + qz[d - 1]
            qa[...] = value
            for k in range(1, nj):
                q_across(k).start()

        def cross_stage():
            for d in order:
                for k in range(1, nj):
                    landed(cross_copy(d, k))

                def add_cross(i, carry):
                    value = gt[d, i, me.j].astype(f32)
                    for k in range(1, nj):
                        value = value + gx[d, k - 1, i].astype(f32)
                    if d == 0:
                        g_sum[i] = value
                    else:
                        gt[d, i, me.j] = value.astype(low)
                    return carry

                lax.fori_loop(0, parts, add_cross, 0)
                value = et[d, me.j].astype(f32)
                for k in range(1, nj):
                    value = value + ex[d, k - 1].astype(f32)
                if d:
                    et[d, me.j] = value.astype(low)
                    start(along_copy(d))
                else:
                    e_out[...] = value
            for k in range(1, nj):
                q_across(k).wait_recv()
            value = qa[...]
            for k in range(1, nj):
                value = value + qx[k - 1]
            qb[...] = value
            q_twin.start()

        def along_stage():
            for i in range(kept):
                k_out[i][:, pl.ds(pl.multiple_of(me.c * width, width), width)] = g_sum[i]
            for d in range(1, nc):
                landed(along_copy(d))
                row = lax.rem(me.c - d + nc, nc)
                for i in range(kept):
                    at = pl.ds(pl.multiple_of(row * width, width), width)
                    k_out[i][:, at] = gz[d - 1, i].astype(f32)
                e_out[...] = e_out[...] + ez[d - 1].astype(f32)
            for i in range(kept, parts):
                value = g_sum[i]
                for d in range(1, nc):
                    value = value + gz[d - 1, i].astype(f32)
                k_out[kept][:, (i - kept) * width : (i - kept + 1) * width] = value
            q_twin.wait()
            q_out[...] = qb[...] + qc[...]

        def pair_copy(i, p):
            at = pl.multiple_of(begins[p], 128)
            return remote(
                pair_send.at[i, :, pl.ds(at, widths[p])],
                (wg_out, wu_out)[i].at[:, pl.ds(pl.multiple_of(begin + at, 128), widths[p])],
                ps.at[i, p], pr.at[i, p], (me.c + 1 - 2 * lower, me.s),
            )

        def pair_landing(i, p):
            at = pl.multiple_of(half - begin + begins[p], 128)
            landing = (wg_out, wu_out)[i].at[:, pl.ds(at, widths[p])]
            return remote(landing, landing, ps.at[i, p], pr.at[i, p], me.along(1))

        down_copy = remote(down_send, wd_out, ds.at[0], dr.at[0], (place, me.s))

        def give(i, p, total):
            at = pl.multiple_of(begins[p], 128)
            other = total[pl.ds(pl.multiple_of((1 - lower) * band, band), band), : widths[p]]
            pair_send[i, :, pl.ds(at, widths[p])] = other.astype(low)
            pair_copy(i, p).start()
            own = total[pl.ds(pl.multiple_of(lower * band, band), band), : widths[p]]
            at = pl.multiple_of(begin + at, 128)
            (wg_out, wu_out)[i][:, pl.ds(at, widths[p])] = own.astype(low)

        for d in order:
            start(core_copy(d))
        for d in range(1, nc):
            q_along(d).start()
        for load in loads:
            load.wait()
        stages = [core_stage, cross_stage, along_stage]
        last = blocks - 1
        for p, size in enumerate(widths):
            cuts = [(n, min(n + TILE, size)) for n in range(0, size, TILE)]
            for i in range(blocks):
                turn = p * blocks + i
                if turn:
                    for load in fetch(turn):
                        load.wait()
                if turn + 1 < blocks * len(widths):
                    for load in fetch(turn + 1):
                        load.start()
                x, dy = xb.at[turn % 2], yb.at[turn % 2]
                for left, right in cuts:
                    at = pl.ds(pl.multiple_of(begins[p] + left, 128), right - left)
                    value, slope = gelu_parts(dot32(x[...], wg[:, at]))
                    linear = dot32(x[...], wu[:, at])
                    down = nt(dy[...], wd[at])
                    inner[:, left:right] = (value * linear).astype(low)
                    dg[:, left:right] = (down * linear * slope).astype(low)
                    du[:, left:right] = (down * value).astype(low)
                mine = x[:, pl.ds(pl.multiple_of(high * 2 * band, 2 * band), 2 * band)]
                for n, (total, grad) in enumerate(((ag, dg), (au, du))):
                    if i:
                        total[:, :size] += tn(mine, grad[:, :size])
                    else:
                        total[:, :size] = tn(mine, grad[:, :size])
                    if i == last:
                        give(n, p, total)
                if p == 0:
                    if i:
                        ad[...] += tn(inner[...], dy[...])
                    else:
                        ad[...] = tn(inner[...], dy[...])
                    if i == last:
                        at = pl.ds(pl.multiple_of(offset - cut, 16), exact)
                        down_send[...] = ad[at].astype(low)

                        @pl.when(place != me.c)
                        def _():
                            down_copy.start()

                        @pl.when(place == me.c)
                        def _():
                            wd_out[...] = down_send[...]

                if stages and turn + 1 < blocks * len(widths):
                    stages.pop(0)()
        for stage in stages:
            stage()
        for i in range(2):
            for p in range(len(widths)):
                pair_landing(i, p).wait_recv()

        @pl.when(source != me.c)
        def _():
            down_copy.wait_recv()

        @pl.when(place != me.c)
        def _():
            down_copy.wait_send()

        for d in order:
            started = core_copy(d) + [copy for k in range(1, nj) for copy in cross_copy(d, k)]
            if d:
                started = started + along_copy(d) + [q_along(d)]
            for copy in started:
                copy.wait_send()
        for k in range(1, nj):
            q_across(k).wait_send()
        for i in range(2):
            for p in range(len(widths)):
                pair_copy(i, p).wait_send()

    one, extra = (parts, piece, width), small.shape[3:]
    return pl.pallas_call(
        kernel,
        name="finish_all",
        cost_estimate=pl.CostEstimate(flops=80 * 10**9, bytes_accessed=10**7, transcendentals=0),
        out_shape=(
            *[jax.ShapeDtypeStruct((piece, nc * width), f32)] * 4,
            jax.ShapeDtypeStruct(extra, f32),
            jax.ShapeDtypeStruct(tile, f32),
            jax.ShapeDtypeStruct((band, hidden), low),
            jax.ShapeDtypeStruct((band, hidden), low),
            jax.ShapeDtypeStruct((exact, features), low),
        ),
        in_specs=[pl.BlockSpec(memory_space=VMEM)] * 3 + [pl.BlockSpec(memory_space=ANY)] * (count + 3),
        out_specs=[pl.BlockSpec(memory_space=VMEM)] * 9,
        scratch_shapes=[
            VMEM((nc, parts, nj, piece, width), low),
            VMEM((nc, nj) + extra, low),
            VMEM((nc, parts, nj, piece, width), low),
            VMEM((nc, nj) + extra, low),
            VMEM((nc, nj - 1) + one, low),
            VMEM((nc, nj - 1) + extra, low),
            VMEM((nc - 1,) + one, low),
            VMEM((nc - 1,) + extra, low),
            VMEM(one, f32),
            VMEM((nc - 1,) + tile, f32),
            VMEM((nj - 1,) + tile, f32),
            VMEM(tile, f32),
            VMEM(tile, f32),
            VMEM(tile, f32),
            SEM.DMA((nc, 2)),
            SEM.DMA((nc, 2)),
            SEM.DMA((nc, nj, 2)),
            SEM.DMA((nc, nj, 2)),
            SEM.DMA((nc, 2)),
            SEM.DMA((nc, 2)),
            SEM.DMA((nc,)),
            SEM.DMA((nc,)),
            SEM.DMA((nj,)),
            SEM.DMA((nj,)),
            SEM.DMA((1,)),
            SEM.DMA((1,)),
            VMEM((2, block, features), low),
            VMEM((2, block, features), low),
            VMEM((features, half), low),
            VMEM((features, half), low),
            VMEM((half, features), low),
            VMEM((block, wide), low),
            VMEM((block, wide), low),
            VMEM((block, wide), low),
            VMEM((2 * band, wide), f32),
            VMEM((2 * band, wide), f32),
            VMEM((wide, features), f32),
            VMEM((2, band, half), low),
            VMEM((exact, features), low),
            SEM.DMA((3,)),
            SEM.DMA((2, 2)),
            SEM.DMA((2, len(widths))),
            SEM.DMA((2, len(widths))),
            SEM.DMA((1,)),
            SEM.DMA((1,)),
        ],
        compiler_params=pltpu.CompilerParams(
            collective_id=2, has_side_effects=True, vmem_limit_bytes=60 * 1024 * 1024
        ),
    )(grads, small, squares, *rows, *row_grads, gate_w, up_w, down_w)


def per_device(
    tokens,
    segments,
    valid,
    routes,
    teacher,
    norm_attn,
    w_query,
    w_key,
    w_value,
    output_weight,
    rel_bias,
    norm_ffn,
    w_router,
    w_gate,
    w_up,
    w_down,
):
    nc = lax.axis_size("ctx")
    ns = lax.axis_size("shard")
    c, s = lax.axis_index("ctx"), lax.axis_index("shard")
    n_dev, nj = nc * ns, ns // 2
    row_count, width = tokens.shape[1:]
    top_count = routes.shape[2]
    experts = w_router.shape[1]
    capacity = (5 * row_count * top_count + 4 * experts - 1) // (4 * experts)
    length = row_count * nc
    low = jnp.bfloat16
    f32 = jnp.float32
    piece = w_query.shape[0]
    band = 2 * row_count

    route_local = routes[0]
    expert_ids = jnp.arange(experts, dtype=jnp.int32)
    route_hot = route_local[:, :, None] == expert_ids[None, None, :]
    flat_routes = route_local.reshape(row_count * top_count)
    route_hits = (flat_routes[:, None] == expert_ids[None, :]).astype(jnp.int32)
    before = jnp.cumsum(route_hits, axis=0) - route_hits
    slot_rank = jnp.sum(before * route_hits, axis=1).reshape(row_count, top_count)

    part = width // nc
    smalls = (
        norm_attn, norm_ffn, rel_bias, w_router.reshape(-1), segments[0].astype(low), valid[0].astype(low),
        route_local.astype(low).T.reshape(-1), slot_rank.astype(low).T.reshape(-1),
    )
    sizes = [x.shape[0] for x in smalls]
    starts = [sum(sizes[:i]) for i in range(len(sizes))]
    extra = jnp.concatenate(smalls + (jnp.zeros((EXTRA * part - sum(sizes),), low),))
    shares = [w.reshape(piece, nc, part).transpose(1, 0, 2) for w in (w_query, w_key, w_value, output_weight)]
    shares = jnp.concatenate(
        [x[:, None] for x in shares[:3]] + [jnp.broadcast_to(shares[3][None], (nc, nc, piece, part))], axis=1
    )
    weights, extras, tokens_all = gather_all(
        shares, extra.reshape(EXTRA, part), tokens[0], nc, ns
    )
    extras = extras.reshape(nc, ns, EXTRA * part)
    gain_attn, gain_ffn, full_bias, full_router = (
        extras[:, :, begin : begin + size].reshape(-1)
        for begin, size in zip(starts[:4], sizes[:4])
    )
    full_router = full_router.reshape(width, experts)
    table = full_bias.reshape(BUCKETS, HEADS).astype(f32)
    line = lax.dynamic_slice_in_dim(extras, s, 1, 1)[:, 0]
    line_seg = line[:, starts[4] : starts[4] + row_count].reshape(length).astype(jnp.int32)
    line_valid = line[:, starts[5] : starts[5] + row_count].reshape(length) > 0
    key_code = jnp.where(line_valid, line_seg, -1)[None]
    query_code = line_seg[:, None]
    valid_count = jnp.sum(extras[:, :, starts[5] : starts[5] + row_count].astype(f32))

    spot = (jnp.arange(band)[None, :] - jnp.arange(CHUNK)[:, None]) % band
    distance = jnp.where(spot <= row_count, row_count - spot, 3 * row_count - spot)
    level = bucket_of(distance, BUCKETS)
    level_hot = (level[:, :, None] == jnp.arange(BUCKETS)[None, None, :]).astype(f32)
    heads = HEADS // nc
    own_table = lax.dynamic_slice_in_dim(table, c * heads, heads, 1)
    slopes = jnp.einsum(
        "ixb,bh->hix", level_hot, own_table - own_table[BUCKETS - 1 :], precision=highest_precision
    )

    gain_one, gain_two = gain_attn.astype(f32), gain_ffn.astype(f32)
    first_all, queries, keys, values, mixed, log_total, residual, ffn_low = attend_forward(
        tokens_all, weights, gain_one[None], gain_two[None], query_code, key_code, slopes, nc, ns
    )
    ffn_in = ffn_low.astype(f32)
    router = full_router.astype(f32)
    logits = jnp.dot(ffn_in, router, precision=highest_precision)
    picked = jnp.sum(jnp.where(route_hot, logits[:, None, :], 0.0), axis=-1)
    gate_probs = jax.nn.softmax(picked, axis=-1)

    slots = -(-capacity // 16) * 16
    target = (route_local ^ s) * slots + slot_rank
    slot_ids = jnp.arange(experts * slots, dtype=jnp.int32)
    pick_first = (slot_ids[:, None] == target[None, :, 0]).astype(low)
    pick_second = (slot_ids[:, None] == target[None, :, 1]).astype(low)
    pick_both = pick_first + pick_second
    gate_w, up_w, down_w = w_gate[0], w_up[0], w_down[0]
    gate_rows = jnp.concatenate((gate_probs.T, jnp.zeros((8 - top_count, row_count), f32)), axis=0)
    other_line = line[c ^ jnp.arange(1, nc)]
    other_routes, other_slots = (
        other_line[:, starts[i] : starts[i] + top_count * row_count]
        .astype(jnp.int32)
        .reshape(nc - 1, top_count, row_count)
        for i in (6, 7)
    )
    other_target = (other_routes ^ s) * slots + other_slots
    other_first, other_second = (
        slot_ids[None, :, None] == other_target[:, m, None, :] for m in range(2)
    )
    other_picks = (other_first | other_second).astype(low).reshape(nc - 1, experts, slots, row_count)
    expert_rows, returned, ffn_all, gates_all, rows_next = moe_forward(
        pick_both.reshape(experts, slots, row_count), other_picks[0], ffn_low, gate_rows,
        gate_w, up_w, down_w, nc, ns,
    )
    returned = returned.reshape(experts * slots, width)
    picked_one, picked_two = tn(pick_first, returned), tn(pick_second, returned)
    output_sum = residual + gate_probs[:, :1] * picked_one + gate_probs[:, 1:] * picked_two
    valid_one = valid[0].astype(f32)
    deviation = output_sum - teacher[0].astype(f32)
    local_square = jnp.sum(valid_one[:, None] * deviation * deviation)
    everything = float(row_count * nc * ns)
    cotangent = everything / valid_count * deviation * valid_one[:, None]
    gate_grad = jnp.stack(
        (jnp.sum(cotangent * picked_one, axis=-1), jnp.sum(cotangent * picked_two, axis=-1)), axis=1
    )
    back_send = dot32(pick_first, (gate_probs[:, :1] * cotangent).astype(low)) + dot32(
        pick_second, (gate_probs[:, 1:] * cotangent).astype(low)
    )
    other_gates = gates_all[c ^ jnp.arange(1, nc)].astype(low)
    other_weighted = (
        jnp.where(other_first, other_gates[:, 0, None, :], low(0))
        + jnp.where(other_second, other_gates[:, 1, None, :], low(0))
    ).reshape(other_picks.shape)
    out_grad, sent_back, cotangent_all, rows_later = moe_backward(
        back_send.astype(low).reshape(experts, slots, width), expert_rows, cotangent.astype(low),
        other_picks[1 : nc // 2], ffn_all, gate_w, up_w, down_w, nc, ns,
    )
    ffn_grad = tn(pick_both, sent_back.reshape(experts * slots, width))
    pick_grad = gate_probs * (gate_grad - jnp.sum(gate_probs * gate_grad, axis=-1, keepdims=True))
    logits_grad = jnp.sum(jnp.where(route_hot, pick_grad[:, :, None], 0.0), axis=1)
    router_grad = contract(ffn_in, logits_grad, 0, 0, highest_precision)
    ffn_grad = ffn_grad + contract(logits_grad, router, 1, 1, highest_precision)
    unused, norm_two_back = jax.vjp(rms_norm, residual, gain_two)
    residual_from_norm, gain_two_grad = norm_two_back(ffn_grad)
    residual_grad = cotangent + residual_from_norm
    attn_grad_low = residual_grad.astype(low)
    input_grad, w_grads, gain_one_grad, near_sum, far_sum, rows_last, other_grads = attend_backward(
        attn_grad_low, residual_grad, mixed, tokens_all, first_all, queries, keys, values, log_total, weights,
        gain_one[None], query_code, key_code, slopes,
        other_picks[nc // 2 :], other_weighted, ffn_all, cotangent_all, nc, ns,
    )
    own_bias = jnp.einsum("hix,ixb->bh", near_sum, level_hot, precision=highest_precision)
    last_bucket = (jnp.arange(BUCKETS) == BUCKETS - 1).astype(f32)
    own_bias = own_bias + last_bucket[:, None] * jnp.sum(far_sum, axis=(1, 2))[None, :]
    bias_grad = lax.dynamic_update_slice_in_dim(
        jnp.zeros((BUCKETS, HEADS), f32), own_bias, c * heads, 1
    )
    small_grads = jnp.concatenate(
        [
            x.reshape(n_dev, -1).astype(low)
            for x in (gain_one_grad, gain_two_grad, bias_grad, router_grad)
        ],
        axis=1,
    )
    small_grads = jnp.pad(small_grads, ((0, 0), (0, EXTRA * part - small_grads.shape[1])))
    *attn_sums, small_sum, square_sum, gate_w_sum, up_w_sum, down_w_sum = finish_all(
        w_grads.reshape(3 + nc, nc, nj, 2, piece, part),
        small_grads.reshape(nc, nj, 2, EXTRA, part),
        jnp.full((8, 128), local_square, f32),
        [
            x.reshape(-1, experts * slots, width)
            for x in (expert_rows, rows_next, rows_later, rows_last)
        ],
        [x.reshape(-1, experts * slots, width) for x in (out_grad, other_grads)],
        gate_w,
        up_w,
        down_w,
        nc,
        ns,
        3,
    )
    loss_value = square_sum[0, 0] / (2.0 * width * valid_count)
    small_sum = small_sum.reshape(-1)
    tails = [small_sum[begin : begin + size] for begin, size in zip(starts[:4], sizes[:4])]
    return (
        output_sum.astype(low)[None],
        loss_value,
        input_grad[None],
        tails[0],
        attn_sums[0],
        attn_sums[1],
        attn_sums[2],
        attn_sums[3],
        tails[2],
        tails[1],
        tails[3].reshape(w_router.shape),
        gate_w_sum[None].astype(f32),
        up_w_sum[None].astype(f32),
        down_w_sum[None].astype(f32),
    )


def solution(mesh):
    return jax.shard_map(
        per_device,
        mesh=mesh,
        in_specs=(
            P("shard", "ctx", None),
            P("shard", "ctx"),
            P("shard", "ctx"),
            P("shard", "ctx", None),
            P("shard", "ctx", None),
            P(("ctx", "shard")),
            P(("ctx", "shard"), None),
            P(("ctx", "shard"), None),
            P(("ctx", "shard"), None),
            P(("ctx", "shard"), None),
            P(("ctx", "shard")),
            P(("ctx", "shard")),
            P(("ctx", "shard"), None),
            P("shard", None, None),
            P("shard", None, None),
            P("shard", None, None),
        ),
        out_specs=(
            P("shard", "ctx", None),
            P(),
            P("shard", "ctx", None),
            P(("ctx", "shard")),
            P(("ctx", "shard"), None),
            P(("ctx", "shard"), None),
            P(("ctx", "shard"), None),
            P(("ctx", "shard"), None),
            P(("ctx", "shard")),
            P(("ctx", "shard")),
            P(("ctx", "shard"), None),
            P("shard", "ctx", None),
            P("shard", "ctx", None),
            P("shard", "ctx", None),
        ),
        check_vma=False,
    )
```

```python
import math

import jax
import jax.numpy as jnp
from jax import lax
from jax.experimental import pallas as pl
from jax.experimental.pallas import tpu as pltpu
from jax.sharding import PartitionSpec as P

HEADS = 16
HEAD = 64
BUCKETS = 32
MESH = pl.DeviceIdType.MESH
ANY = pl.ANY
VMEM = pltpu.VMEM
SEM = pltpu.SemaphoreType

highest_precision = lax.Precision.HIGHEST
max_distance = 128
epsilon = 1e-06
negative = -1e30
EXTRA = 16


def thresholds(buckets):
    exact_count = buckets // 2
    limits = list(range(1, exact_count))
    for bucket_level in range(exact_count, buckets):
        power = (bucket_level - exact_count) / exact_count
        limits.append(int(math.ceil(exact_count * (max_distance / exact_count) ** power)))
    return limits


def bucket_of(distance, buckets):
    bucket_total = jnp.zeros(distance.shape, jnp.int32)
    for threshold in thresholds(buckets):
        bucket_total = bucket_total + (distance >= threshold).astype(jnp.int32)
    return bucket_total


def rms_norm(values, gain_vector):
    return (
        values
        * lax.rsqrt(jnp.mean(values * values, axis=-1, keepdims=True) + epsilon)
        * gain_vector
    )


def contract(left_side, right_side, left_axis, right_axis, precision_mode=None):
    return lax.dot_general(
        left_side,
        right_side,
        (((left_axis,), (right_axis,)), ((), ())),
        precision=precision_mode,
        preferred_element_type=jnp.float32,
    )


def dot32(left_side, right_side):
    return jnp.dot(left_side, right_side, preferred_element_type=jnp.float32)


def nt(left_side, right_side):
    return contract(left_side, right_side, 1, 1)


def tn(left_side, right_side):
    return contract(left_side, right_side, 0, 0)


class Place:
    def __init__(self, nc, ns):
        self.nc, self.ns, self.nj = nc, ns, ns // 2
        self.c = lax.axis_index("ctx")
        self.s = lax.axis_index("shard")
        self.core = self.s % 2
        self.j = self.s // 2

    def along(self, d):
        return (lax.rem(self.c + d + self.nc, self.nc), self.s)

    def across(self, k):
        return (self.c, self.s ^ (2 * k))

    def twin(self):
        return (self.c, self.s ^ 1)

    def greet(self):
        barrier = pltpu.get_barrier_semaphore()
        partners = (
            [self.along(d) for d in range(1, self.nc)]
            + [self.across(k) for k in range(1, self.nj)]
            + [self.twin()]
        )
        for partner in partners:
            pl.semaphore_signal(barrier, inc=1, device_id=partner, device_id_type=MESH)
        pl.semaphore_wait(barrier, len(partners))


def remote(source, target, send, recv, device):
    return pltpu.make_async_remote_copy(
        src_ref=source,
        dst_ref=target,
        send_sem=send,
        recv_sem=recv,
        device_id=device,
        device_id_type=MESH,
    )


def gather_all(weights, extra, rows, nc, ns):
    n_dev, nj = nc * ns, ns // 2
    share = weights.shape[1:]
    full_shape = (share[0], nc, ns) + share[1:]

    def kernel(w_in, e_in, t_in, w_out, e_out, t_out, local, zs, zr, xs, xr, cs, cr, ts, tr):
        me = Place(nc, ns)

        def views(row, column):
            return (w_out.at[:, row, column], e_out.at[row, column])

        def piece(d, k):
            return views(lax.rem(me.c - d + nc, nc), me.s ^ (2 * k))

        mine = (w_in.at[me.c], e_in)
        locals_ = [
            pltpu.make_async_copy(source, target, local.at[i])
            for i, (source, target) in enumerate(
                zip(mine + (t_in,), views(me.c, me.s) + (t_out.at[me.c],))
            )
        ]
        for copy in locals_:
            copy.start()
        me.greet()
        sent = []

        def push(sources, targets, send, recv, device):
            for i in range(2):
                copy = remote(sources[i], targets[i], send.at[i], recv.at[i], device)
                copy.start()
                sent.append(copy)

        def arrive(targets, send, recv, device):
            for i in range(2):
                remote(targets[i], targets[i], send.at[i], recv.at[i], device).wait_recv()

        def token_copy(direction, hop):
            lane = 0 if direction > 0 else 1
            origin = lax.rem(me.c - direction * hop + nc, nc)
            return remote(
                t_in if hop == 0 else t_out.at[origin],
                t_out.at[origin],
                ts.at[lane, hop],
                tr.at[lane, hop],
                (lax.rem(me.c + direction + nc, nc), me.s),
            )

        def token_landing(direction, hop):
            lane = 0 if direction > 0 else 1
            origin = lax.rem(me.c - direction * (hop + 1) + nc, nc)
            landing = t_out.at[origin]
            return remote(landing, landing, ts.at[lane, hop], tr.at[lane, hop], me.along(1))

        def can_send(direction, hop):
            if direction > 0:
                return (me.c >= hop) & (me.c < nc - 1)
            return (me.c <= nc - 1 - hop) & (me.c > 0)

        def can_receive(direction, hop):
            if direction > 0:
                return me.c >= hop + 1
            return me.c <= nc - 2 - hop

        for d in range(1, nc):
            target = lax.rem(me.c + d, nc)
            push(
                (w_in.at[target], e_in), views(me.c, me.s), zs.at[d], zr.at[d], (target, me.s)
            )
        for direction in (1, -1):

            @pl.when(can_send(direction, 0))
            def _():
                token_copy(direction, 0).start()

        for k in range(1, nj):
            push(mine, views(me.c, me.s), xs.at[0, k], xr.at[0, k], me.across(k))
        push(mine, views(me.c, me.s), cs.at[0, 0], cr.at[0, 0], me.twin())

        for copy in locals_:
            copy.wait()
        for d in range(1, nc):
            here = piece(d, 0)
            arrive(here, zs.at[d], zr.at[d], me.along(-d))
            for k in range(1, nj):
                push(here, here, xs.at[d, k], xr.at[d, k], me.across(k))
            push(here, here, cs.at[d, 0], cr.at[d, 0], me.twin())
        for d in range(nc):
            for k in range(1, nj):
                here = piece(d, k)
                arrive(here, xs.at[d, k], xr.at[d, k], me.across(k))
                push(here, here, cs.at[d, k], cr.at[d, k], me.twin())
            if d < nc - 2:
                for direction in (1, -1):

                    @pl.when(can_receive(direction, d))
                    def _():
                        token_landing(direction, d).wait_recv()

                    @pl.when(can_send(direction, d + 1))
                    def _():
                        token_copy(direction, d + 1).start()

        for d in range(nc):
            for k in range(nj):
                here = views(lax.rem(me.c - d + nc, nc), me.s ^ 1 ^ (2 * k))
                arrive(here, cs.at[d, k], cr.at[d, k], me.twin())
        for direction in (1, -1):

            @pl.when(can_receive(direction, nc - 2))
            def _():
                token_landing(direction, nc - 2).wait_recv()

        for copy in sent:
            copy.wait_send()
        for direction in (1, -1):
            for hop in range(nc - 1):

                @pl.when(can_send(direction, hop))
                def _():
                    token_copy(direction, hop).wait_send()

    full, extras, tokens = pl.pallas_call(
        kernel,
        name="gather_all",
        cost_estimate=pl.CostEstimate(flops=50 * 10**9, bytes_accessed=10**7, transcendentals=0),
        out_shape=(
            jax.ShapeDtypeStruct(full_shape, weights.dtype),
            jax.ShapeDtypeStruct((nc, ns) + extra.shape, extra.dtype),
            jax.ShapeDtypeStruct((nc,) + rows.shape, rows.dtype),
        ),
        in_specs=[pl.BlockSpec(memory_space=ANY)] * 3,
        out_specs=[pl.BlockSpec(memory_space=ANY)] * 3,
        scratch_shapes=[
            SEM.DMA((3,)),
            SEM.DMA((nc, 2)),
            SEM.DMA((nc, 2)),
            SEM.DMA((nc, nj, 2)),
            SEM.DMA((nc, nj, 2)),
            SEM.DMA((nc, nj, 2)),
            SEM.DMA((nc, nj, 2)),
            SEM.DMA((2, nc)),
            SEM.DMA((2, nc)),
        ],
        compiler_params=pltpu.CompilerParams(collective_id=1, has_side_effects=True),
    )(weights, extra, rows)
    return (
        full.reshape(share[0], n_dev * share[1], share[2]),
        extras,
        tokens.reshape(nc * rows.shape[0], rows.shape[1]),
    )


CHUNK = 16


def fill_mask(mask, query_code, key_code, block, count):
    near = block * count
    query = query_code[pl.ds(near, count)]
    if block:
        mask[:, :near] = jnp.where(query == key_code[:, :near], 0.0, negative)
    row = lax.broadcasted_iota(jnp.int32, (count, count), 0)
    column = lax.broadcasted_iota(jnp.int32, (count, count), 1)
    seen = ((query == key_code[:, near : near + count]) & (row >= column)) | (row == column)
    mask[:, near : near + count] = jnp.where(seen, 0.0, negative)


def fill_slopes(bank, slopes, head, count):
    for i in range(count // CHUNK):
        row = slopes[head]
        bank[head, i * CHUNK : (i + 1) * CHUNK] = pltpu.roll(row, i * CHUNK, 1) if i else row


def biased(scores, mask, slope, block, count):
    end = (block + 1) * count
    band = 2 * count
    if end < band:
        return scores + mask[:, :end] + slope[:, band - end :]
    if end == band:
        return scores + mask[:, :end] + slope[...]
    wide = scores[:, : end - band] + mask[:, : end - band]
    tight = scores[:, end - band :] + mask[:, end - band : end] + slope[...]
    return jnp.concatenate((wide, tight), axis=1)


def attend_forward(tokens, weights, gain, gain_next, query_code, key_code, slopes, nc, ns):
    length, width = tokens.shape
    count = length // nc
    part = width // nc
    heads, _, band = slopes.shape
    low, f32 = jnp.bfloat16, jnp.float32

    def kernel(t_in, w_in, gain_in, next_in, qcode, kcode, toe, first, q_out, k_out, v_out, o_out, lse_out, x_out, y_out,
               mask, bank, osend, ss, rs):
        me = Place(nc, ns)
        barrier = pltpu.get_barrier_semaphore()
        for d in range(1, nc):
            pl.semaphore_signal(barrier, inc=1, device_id=me.along(d), device_id_type=MESH)
        pl.semaphore_wait(barrier, nc - 1)

        def norm(i, carry):
            at = pl.ds(pl.multiple_of(i * 64, 64), 64)
            x = t_in[at].astype(f32)
            rate = lax.rsqrt(jnp.mean(x * x, axis=-1, keepdims=True) + epsilon)
            first[at] = (x * rate * gain_in[...]).astype(low)
            return carry

        lax.fori_loop(0, length // 64, norm, 0)

        def project(i, carry):
            at = pl.ds(pl.multiple_of(i * count, count), count)
            block = first[at]
            q_out[at] = dot32(block, w_in[0]).astype(low)
            k_out[at] = dot32(block, w_in[1]).astype(low)
            v_out[at] = dot32(block, w_in[2]).astype(low)
            return carry

        lax.fori_loop(0, nc, project, 0)
        for head in range(heads):
            fill_slopes(bank, toe, head, count)
        lane = lax.broadcasted_iota(jnp.int32, (count, 2 * HEAD), 1)
        spot = lax.broadcasted_iota(jnp.int32, (count, 128), 1)
        own_copy = [
            remote(osend.at[b], o_out.at[me.c], ss.at[b], rs.at[me.c], (b, me.s)) for b in range(nc)
        ]
        for b in reversed(range(nc)):
            end = (b + 1) * count
            rows = pl.ds(b * count, count)
            fill_mask(mask, qcode, kcode, b, count)
            level = jnp.zeros((count, 128), f32)
            for pair in range(heads // 2):
                two = slice(pair * 2 * HEAD, (pair + 1) * 2 * HEAD)
                q_pair = q_out[rows, two] * low(1.0 / math.sqrt(HEAD))
                k_pair = k_out[:end, two]
                v_pair = v_out[:end, two]
                halves = []
                for half in range(2):
                    head = pair * 2 + half
                    inside = (lane >= HEAD) if half else (lane < HEAD)
                    scores = nt(jnp.where(inside, q_pair, low(0)), k_pair)
                    scores = biased(scores, mask, bank.at[head], b, count)
                    top = jnp.max(scores, axis=1, keepdims=True)
                    scores = jnp.exp(scores - top)
                    total = jnp.sum(scores, axis=1, keepdims=True)
                    halves.append(dot32(scores.astype(low), v_pair) * (1.0 / total))
                    level = jnp.where(spot == head, top + jnp.log(total), level)
                osend[b, :, two] = jnp.where(lane < HEAD, halves[0], halves[1]).astype(low)
            lse_out[rows] = level

            @pl.when(me.c == b)
            def _():
                o_out[me.c] = osend[b]

            @pl.when(me.c != b)
            def _():
                own_copy[b].start()

        for d in range(1, nc):
            origin = lax.rem(me.c + d, nc)
            remote(
                osend.at[0], o_out.at[origin], ss.at[0], rs.at[origin], me.along(d)
            ).wait_recv()
        own = pl.ds(pl.multiple_of(me.c * count, count), count)
        squares = jnp.zeros((count, 1), f32)
        for n in range(nc):
            columns = slice(n * part, (n + 1) * part)
            x = t_in[own, columns].astype(f32)
            for origin in range(nc):
                x = x + dot32(o_out[origin], w_in[3 + n, origin * part : (origin + 1) * part])
            x_out[:, columns] = x
            squares = squares + jnp.sum(x * x, axis=1, keepdims=True)
        rate = lax.rsqrt(squares * (1.0 / width) + epsilon)
        for n in range(nc):
            columns = slice(n * part, (n + 1) * part)
            y_out[:, columns] = (x_out[:, columns] * rate * next_in[:, columns]).astype(low)
        for b in range(nc):

            @pl.when(me.c != b)
            def _():
                own_copy[b].wait_send()

    return pl.pallas_call(
        kernel,
        name="attend_forward",
        cost_estimate=pl.CostEstimate(flops=25 * 10**9, bytes_accessed=10**7, transcendentals=0),
        out_shape=(
            jax.ShapeDtypeStruct((length, width), low),
            jax.ShapeDtypeStruct((length, part), low),
            jax.ShapeDtypeStruct((length, part), low),
            jax.ShapeDtypeStruct((length, part), low),
            jax.ShapeDtypeStruct((nc, count, part), low),
            jax.ShapeDtypeStruct((length, 128), f32),
            jax.ShapeDtypeStruct((count, width), f32),
            jax.ShapeDtypeStruct((count, width), low),
        ),
        in_specs=[pl.BlockSpec(memory_space=VMEM)] * 7,
        out_specs=[pl.BlockSpec(memory_space=VMEM)] * 8,
        scratch_shapes=[
            VMEM((count, length), f32),
            VMEM((heads, count, band), f32),
            VMEM((nc, count, part), low),
            SEM.DMA((nc,)),
            SEM.DMA((nc,)),
        ],
        compiler_params=pltpu.CompilerParams(
            collective_id=3, has_side_effects=True, vmem_limit_bytes=56 * 1024 * 1024
        ),
    )(tokens, weights, gain, gain_next, query_code, key_code, slopes)


def attend_backward(
    dattn, o_all, tokens, first, q_all, k_all, v_all, lse, weights, query_code, key_code, slopes,
    weighted, cotangents, nc, ns,
):
    length, width = tokens.shape
    count = length // nc
    part = width // nc
    heads, _, band = slopes.shape
    low, f32 = jnp.bfloat16, jnp.float32
    scale = 1.0 / math.sqrt(HEAD)
    exchange = weighted.shape[1:3] + (width,)

    def kernel(a_in, o_in, t_in, first_in, q_in, k_in, v_in, lse_in, w_in, qcode, kcode, toe, pw_in, c_in,
               x_out, fsend, w_out, gain_out, near_out, far_out, c_out,
               mask, bank, dsend, dall, dq, dk, dv, fown, nsend, ss, rs, ns_, nr):
        me = Place(nc, ns)
        barrier = pltpu.get_barrier_semaphore()
        partners = [me.along(d) for d in range(1, nc)] + [(me.c, me.s ^ m) for m in range(1, ns)]
        for partner in partners:
            pl.semaphore_signal(barrier, inc=1, device_id=partner, device_id_type=MESH)
        pl.semaphore_wait(barrier, len(partners))

        def do_copy(d):
            return remote(dsend.at[d], dall.at[me.c], ss.at[d], rs.at[d], me.along(d))

        for d in list(range(1, nc)) + [0]:
            target = lax.rem(me.c + d, nc)
            at = pl.ds(pl.multiple_of(target * part, part), part)
            value = nt(a_in[:, :part], w_in[3, at])
            for n in range(1, nc):
                value = value + nt(a_in[:, n * part : (n + 1) * part], w_in[3 + n, at])
            if d:
                dsend[d] = value.astype(low)
                do_copy(d).start()
            else:
                dall[me.c] = value.astype(low)
        jobs = [(pw_in.at[d], c_in.at[me.c ^ (d + 1)], c_out.at[d]) for d in range(nc - 1)]
        spread = Spread(me, jobs, nsend, ns_, nr)
        for i in range(len(jobs)):
            spread.start(i)
        for n in range(nc):
            for origin in range(nc):
                w_out[3 + n, origin * part : (origin + 1) * part] = tn(
                    o_in[origin], a_in[:, n * part : (n + 1) * part]
                ).astype(low)
        for head in range(heads):
            fill_slopes(bank, toe, head, count)
        lane = lax.broadcasted_iota(jnp.int32, (count, 2 * HEAD), 1)
        spot = lax.broadcasted_iota(jnp.int32, (count, 128), 1)
        dk[...] = jnp.zeros_like(dk)
        dv[...] = jnp.zeros_like(dv)
        near_out[...] = jnp.zeros_like(near_out)
        far_out[...] = jnp.zeros_like(far_out)
        gain_out[...] = jnp.zeros_like(gain_out)
        for d in range(1, nc):
            origin = lax.rem(me.c - d + nc, nc)
            remote(dsend.at[d], dall.at[origin], ss.at[d], rs.at[d], me.along(d)).wait_recv()
        for b in reversed(range(nc)):
            end = (b + 1) * count
            rows = pl.ds(b * count, count)
            fill_mask(mask, qcode, kcode, b, count)
            level = lse_in[rows]
            for pair in range(heads // 2):
                two = slice(pair * 2 * HEAD, (pair + 1) * 2 * HEAD)
                q_pair = q_in[rows, two] * low(scale)
                do_pair = dall[b, :, two]
                k_pair = k_in[:end, two]
                v_pair = v_in[:end, two]
                parts = []
                for half in range(2):
                    head = pair * 2 + half
                    inside = (lane >= HEAD) if half else (lane < HEAD)
                    q_one = jnp.where(inside, q_pair, low(0))
                    do_one = jnp.where(inside, do_pair, low(0))
                    own_level = jnp.sum(
                        jnp.where(spot == head, level, 0.0), axis=1, keepdims=True
                    )
                    probs = jnp.exp(
                        biased(nt(q_one, k_pair), mask, bank.at[head], b, count) - own_level
                    )
                    grads = probs * nt(do_one, v_pair)
                    grads = grads - probs * jnp.sum(grads, axis=1, keepdims=True)
                    low_grads = grads.astype(low)
                    parts.append(dot32(low_grads, k_pair))
                    dk[:end, two] += tn(low_grads, q_one)
                    dv[:end, two] += tn(probs.astype(low), do_one)
                    near = grads[:, max(end - band, 0) :]
                    if end < band:
                        near = jnp.concatenate((jnp.zeros((count, band - end), f32), near), axis=1)
                    height = count
                    while height > CHUNK:
                        height = height // 2
                        near = near[:height] + pltpu.roll(near[height:], band - height, 1)
                    near_out[head] += near
                    if end > band:
                        far = grads[:, : end - band]
                        total = far[:, :128]
                        for piece in range(1, (end - band) // 128):
                            total = total + far[:, piece * 128 : (piece + 1) * 128]
                        height = count
                        while height > 8:
                            height = height // 2
                            total = total[:height] + total[height:]
                        far_out[head] += total
                dq[rows, two] = (jnp.where(lane < HEAD, parts[0], parts[1]) * scale).astype(low)
            dq_low, dk_low, dv_low = dq[rows], dk[rows].astype(low), dv[rows].astype(low)
            for n in range(nc):
                columns = slice(n * part, (n + 1) * part)
                at = pl.ds(n * part, part)
                value = nt(dq_low, w_in[0, at]) + nt(dk_low, w_in[1, at]) + nt(dv_low, w_in[2, at])
                fown[:, columns] = value
            x = t_in[rows].astype(f32)
            rate = lax.rsqrt(jnp.mean(x * x, axis=-1, keepdims=True) + epsilon)
            gain_out[...] += jnp.sum(fown[...] * x * rate, axis=0, keepdims=True)
            fsend[b] = fown[...].astype(low)

            @pl.when(me.c == b)
            def _():
                x_out[...] = fown[...]

        for i, grads in enumerate((dq, dk, dv)):
            for n in range(nc):
                at = slice(n * part, (n + 1) * part)
                w_out[i, at] = tn(first_in[:, at], grads[...].astype(low)).astype(low)
        spread.finish()
        for d in range(1, nc):
            do_copy(d).wait_send()

    return pl.pallas_call(
        kernel,
        name="attend_backward",
        cost_estimate=pl.CostEstimate(flops=50 * 10**9, bytes_accessed=10**7, transcendentals=0),
        out_shape=(
            jax.ShapeDtypeStruct((count, width), f32),
            jax.ShapeDtypeStruct((nc, count, width), low),
            jax.ShapeDtypeStruct((3 + nc, width, part), low),
            jax.ShapeDtypeStruct((1, width), f32),
            jax.ShapeDtypeStruct((heads, CHUNK, band), f32),
            jax.ShapeDtypeStruct((heads, 8, 128), f32),
            jax.ShapeDtypeStruct((nc - 1,) + exchange, low),
        ),
        in_specs=[pl.BlockSpec(memory_space=VMEM)] * 14,
        out_specs=[pl.BlockSpec(memory_space=VMEM)] * 6 + [pl.BlockSpec(memory_space=ANY)],
        scratch_shapes=[
            VMEM((count, length), f32),
            VMEM((heads, count, band), f32),
            VMEM((nc, count, part), low),
            VMEM((nc, count, part), low),
            VMEM((length, part), low),
            VMEM((length, part), f32),
            VMEM((length, part), f32),
            VMEM((count, width), f32),
            VMEM((4,) + exchange, low),
            SEM.DMA((nc,)),
            SEM.DMA((nc,)),
            SEM.DMA((nc - 1, ns)),
            SEM.DMA((nc - 1, ns)),
        ],
        compiler_params=pltpu.CompilerParams(
            collective_id=4, has_side_effects=True, vmem_limit_bytes=61 * 1024 * 1024
        ),
    )(dattn, o_all, tokens, first, q_all, k_all, v_all, lse, weights, query_code, key_code, slopes,
      weighted, cotangents)


def activation(gate_values, up_values):
    return jax.nn.gelu(gate_values) * up_values


def gelu_parts(x):
    c, a = math.sqrt(2.0 / math.pi), 0.044715
    square = x * x
    t = jnp.tanh(c * x * (1.0 + a * square))
    half = 0.5 * (1.0 + t)
    return x * half, half + (0.5 * c) * x * (1.0 - t * t) * (1.0 + (3.0 * a) * square)


class Chain:
    def __init__(self, me, pairs, send, recv):
        self.me, self.pairs, self.send, self.recv, self.nc = me, pairs, send, recv, me.nc

    def copies(self, direction, hop, landing):
        me, nc = self.me, self.nc
        lane = 0 if direction > 0 else 1
        origin = lax.rem(me.c - direction * (hop + 1 if landing else hop) + 2 * nc, nc)
        result = []
        for i, (own, every) in enumerate(self.pairs):
            target = every.at[origin]
            source = own if hop == 0 and not landing else target
            result.append(
                remote(
                    source, target, self.send.at[lane, hop, i], self.recv.at[lane, hop, i],
                    me.along(direction),
                )
            )
        return result

    def sends(self, direction, hop):
        c, nc = self.me.c, self.nc
        if direction > 0:
            return (c >= hop) & (c < nc - 1)
        return (c <= nc - 1 - hop) & (c > 0)

    def lands(self, direction, hop):
        c, nc = self.me.c, self.nc
        if direction > 0:
            return c >= hop + 1
        return c <= nc - 2 - hop

    def start(self, hop):
        if hop >= self.nc:
            return
        for direction in (1, -1):
            if hop:

                @pl.when(self.lands(direction, hop - 1))
                def _():
                    for copy in self.copies(direction, hop - 1, True):
                        copy.wait_recv()

            if hop < self.nc - 1:

                @pl.when(self.sends(direction, hop))
                def _():
                    for copy in self.copies(direction, hop, False):
                        copy.start()

    def finish(self):
        for direction in (1, -1):
            for hop in range(self.nc - 1):

                @pl.when(self.sends(direction, hop))
                def _():
                    for copy in self.copies(direction, hop, False):
                        copy.wait_send()


def greet_experts(me):
    barrier = pltpu.get_barrier_semaphore()
    partners = [(me.c, me.s ^ m) for m in range(1, me.ns)] + [me.along(1), me.along(-1)]
    for partner in partners:
        pl.semaphore_signal(barrier, inc=1, device_id=partner, device_id_type=MESH)
    pl.semaphore_wait(barrier, len(partners))


TILE = 256


class Spread:
    def __init__(self, me, jobs, send, send_sem, recv_sem):
        self.me, self.jobs, self.send = me, jobs, send
        self.send_sem, self.recv_sem = send_sem, recv_sem
        self.order = list(range(2, me.ns)) + [1]
        self.turns = send.shape[0]

    def copy(self, i, m):
        return remote(
            self.send.at[i % self.turns, m], self.jobs[i][2].at[m],
            self.send_sem.at[i, m], self.recv_sem.at[i, m], (self.me.c, self.me.s ^ m),
        )

    def own(self, i):
        return pltpu.make_async_copy(
            self.send.at[i % self.turns, 0], self.jobs[i][2].at[0], self.send_sem.at[i, 0]
        )

    def left(self, i):
        for m in self.order:
            self.copy(i, m).wait_send()
        self.own(i).wait()

    def start(self, i):
        if i >= self.turns:
            self.left(i - self.turns)
        picks, tokens = self.jobs[i][:2]
        for m in self.order + [0]:
            self.send[i % self.turns, m] = dot32(picks[m], tokens[...]).astype(self.send.dtype)
            if m:
                self.copy(i, m).start()
            else:
                self.own(i).start()

    def landed(self, i):
        for m in self.order:
            self.copy(i, m).wait_recv()
        if i >= len(self.jobs) - self.turns:
            self.left(i)

    def finish(self):
        for i in range(len(self.jobs)):
            self.landed(i)


def row_groups(ns):
    return [(2, 6), (6, ns), (0, 2)]


def moe_forward(pick, pick_next, tokens, gates, gate_w, up_w, down_w, nc, ns):
    cap, count = pick.shape[1:]
    width, hidden = gate_w.shape
    low, f32 = jnp.bfloat16, jnp.float32
    groups = row_groups(ns)
    most = max(end - start for start, end in groups) * cap

    def kernel(p_in, n_in, t_in, s_in, g_hbm, u_hbm, d_hbm, r_out, y_out, t_all, s_all, n_out, kg_out, ku_out,
               wg, wu, wd, send, yield_, nsend, inner, keep_g, keep_u, ks, ws, ss, rs, ys, yr, ts, tr, ls, ns_, nr):
        me = Place(nc, ns)
        loads = [
            pltpu.make_async_copy(source, target, ws.at[i])
            for i, (source, target) in enumerate(((g_hbm, wg), (u_hbm, wu), (d_hbm, wd)))
        ]
        for load in loads:
            load.start()
        keep = [
            pltpu.make_async_copy(t_in, t_all.at[me.c], ls.at[0]),
            pltpu.make_async_copy(s_in, s_all.at[me.c], ls.at[1]),
        ]
        for copy in keep:
            copy.start()
        greet_experts(me)

        def there(m):
            return (me.c, me.s ^ m)

        def out_copy(m):
            return remote(send.at[m], r_out.at[m], ss.at[m], rs.at[m], there(m))

        def back_copy(m):
            return remote(yield_.at[m], y_out.at[m], ys.at[m], yr.at[m], there(m))

        for m in list(range(2, 6)) + [1]:
            send[m] = dot32(p_in[m], t_in[...]).astype(low)
            out_copy(m).start()
        chain = Chain(me, ((t_in, t_all), (s_in, s_all)), ts, tr)
        chain.start(0)
        r_out[0] = dot32(p_in[0], t_in[...]).astype(low)
        for m in range(6, ns):
            send[m] = dot32(p_in[m], t_in[...]).astype(low)
        for load in loads:
            load.wait()
        for turn, (begin, end) in enumerate(groups):
            size = (end - begin) * cap
            here = pl.ds(begin * cap, size)
            for m in range(begin, end):
                if m:
                    out_copy(m).wait_recv()
            if turn == 0:
                for m in range(6, ns):
                    out_copy(m).start()

            def up(n, carry):
                rows = r_out[begin:end].reshape(size, width)
                at = pl.ds(pl.multiple_of(n * TILE, TILE), TILE)
                value, slope = gelu_parts(dot32(rows, wg[:, at]))
                linear = dot32(rows, wu[:, at])
                inner[:size, at] = (value * linear).astype(low)
                keep_g[here, at] = (slope * linear).astype(low)
                keep_u[here, at] = value.astype(low)
                return carry

            lax.fori_loop(0, hidden // TILE, up, 0)
            for i, (kept, target) in enumerate(((keep_g, kg_out), (keep_u, ku_out))):
                copy = pltpu.make_async_copy(kept.at[here], target.at[here], ks.at[turn, i])
                copy.start()
                keep.append(copy)
            chain.start(turn + 1)
            if turn == 0:
                spread = Spread(me, [(n_in, t_all.at[me.c ^ 1], n_out)], nsend, ns_, nr)
                spread.start(0)

            def down(n, carry):
                at = pl.ds(pl.multiple_of(n * TILE, TILE), TILE)
                value = dot32(inner[:size], wd[:, at]).astype(low)
                yield_[begin:end, :, at] = value.reshape(end - begin, cap, TILE)
                return carry

            lax.fori_loop(0, width // TILE, down, 0)
            for m in range(begin, end):
                if m:
                    back_copy(m).start()
        y_out[0] = yield_[0]
        for hop in range(len(groups) + 1, nc):
            chain.start(hop)
        for m in range(1, ns):
            back_copy(m).wait_recv()
        for copy in keep:
            copy.wait()
        for m in range(1, ns):
            out_copy(m).wait_send()
            back_copy(m).wait_send()
        spread.finish()
        chain.finish()

    exchange = (ns, cap, width)
    return pl.pallas_call(
        kernel,
        name="moe_forward",
        cost_estimate=pl.CostEstimate(flops=45 * 10**9, bytes_accessed=10**7, transcendentals=0),
        out_shape=(
            jax.ShapeDtypeStruct(exchange, low),
            jax.ShapeDtypeStruct(exchange, low),
            jax.ShapeDtypeStruct((nc,) + tokens.shape, low),
            jax.ShapeDtypeStruct((nc,) + gates.shape, f32),
            jax.ShapeDtypeStruct(exchange, low),
            jax.ShapeDtypeStruct((ns * cap, hidden), low),
            jax.ShapeDtypeStruct((ns * cap, hidden), low),
        ),
        in_specs=[pl.BlockSpec(memory_space=VMEM)] * 4 + [pl.BlockSpec(memory_space=ANY)] * 3,
        out_specs=[pl.BlockSpec(memory_space=VMEM)] * 4 + [pl.BlockSpec(memory_space=ANY)] * 3,
        scratch_shapes=[
            VMEM((width, hidden), low),
            VMEM((width, hidden), low),
            VMEM((hidden, width), low),
            VMEM(exchange, low),
            VMEM(exchange, low),
            VMEM((1,) + exchange, low),
            VMEM((most, hidden), low),
            VMEM((ns * cap, hidden), low),
            VMEM((ns * cap, hidden), low),
            SEM.DMA((3, 2)),
            SEM.DMA((3,)),
            SEM.DMA((ns,)),
            SEM.DMA((ns,)),
            SEM.DMA((ns,)),
            SEM.DMA((ns,)),
            SEM.DMA((2, nc, 2)),
            SEM.DMA((2, nc, 2)),
            SEM.DMA((2,)),
            SEM.DMA((1, ns)),
            SEM.DMA((1, ns)),
        ],
        compiler_params=pltpu.CompilerParams(
            collective_id=5, has_side_effects=True, vmem_limit_bytes=56 * 1024 * 1024
        ),
    )(pick, pick_next, tokens, gates, gate_w, up_w, down_w)


def moe_backward(grads, kept_g, kept_u, cotangents, pick_next, tokens, gate_w, up_w, down_w, nc, ns):
    cap = grads.shape[1]
    width, hidden = gate_w.shape
    low, f32 = jnp.bfloat16, jnp.float32
    groups = row_groups(ns)
    most = max(end - start for start, end in groups) * cap
    more = pick_next.shape[0]

    def kernel(g_in, t_in, n_in, f_in, g_hbm, u_hbm, d_hbm, kg_hbm, ku_hbm, g_out, x_out, t_all, n_out,
               wg, wu, wd, yield_, nsend, slope_g, slope_u, dg, du, ws, ss, rs, ys, yr, ts, tr, ls, ns_, nr):
        me = Place(nc, ns)
        loads = [
            pltpu.make_async_copy(source, target, ws.at[i])
            for i, (source, target) in enumerate(
                ((d_hbm, wd), (kg_hbm, slope_g), (ku_hbm, slope_u), (g_hbm, wg), (u_hbm, wu))
            )
        ]
        for load in loads:
            load.start()
        keep = pltpu.make_async_copy(t_in, t_all.at[me.c], ls.at[0])
        keep.start()
        greet_experts(me)

        def there(m):
            return (me.c, me.s ^ m)

        def out_copy(m):
            return remote(g_in.at[m], g_out.at[m], ss.at[m], rs.at[m], there(m))

        def back_copy(m):
            return remote(yield_.at[m], x_out.at[m], ys.at[m], yr.at[m], there(m))

        for m in list(range(2, 6)) + [1]:
            out_copy(m).start()
        chain = Chain(me, ((t_in, t_all),), ts, tr)
        chain.start(0)
        g_out[0] = g_in[0]
        for load in loads:
            load.wait()

        jobs = [(n_in.at[i], f_in.at[me.c ^ (i + 2)], n_out.at[i]) for i in range(more)]
        spread = Spread(me, jobs, nsend, ns_, nr)
        for turn, (begin, end) in enumerate(groups):
            size = (end - begin) * cap
            for m in range(begin, end):
                if m:
                    out_copy(m).wait_recv()
            if turn == 0:
                for m in range(6, ns):
                    out_copy(m).start()
            here = slice(begin * cap, end * cap)

            def up(n, carry):
                taken = g_out[begin:end].reshape(size, width)
                at = pl.ds(pl.multiple_of(n * TILE, TILE), TILE)
                value = nt(taken, wd[at])
                dg[:size, at] = (value * slope_g[here, at].astype(f32)).astype(low)
                du[:size, at] = (value * slope_u[here, at].astype(f32)).astype(low)
                return carry

            lax.fori_loop(0, hidden // TILE, up, 0)
            chain.start(turn + 1)
            if turn == 0:
                for i in range(more):
                    spread.start(i)

            def down(n, carry):
                at = pl.ds(pl.multiple_of(n * TILE, TILE), TILE)
                value = nt(dg[:size], wg[at]) + nt(du[:size], wu[at])
                yield_[begin:end, :, at] = value.astype(low).reshape(end - begin, cap, TILE)
                return carry

            lax.fori_loop(0, width // TILE, down, 0)
            for m in range(begin, end):
                if m:
                    back_copy(m).start()
        x_out[0] = yield_[0]
        for hop in range(len(groups) + 1, nc):
            chain.start(hop)
        for m in range(1, ns):
            back_copy(m).wait_recv()
        keep.wait()
        for m in range(1, ns):
            out_copy(m).wait_send()
            back_copy(m).wait_send()
        spread.finish()
        chain.finish()

    exchange = (ns, cap, width)
    return pl.pallas_call(
        kernel,
        name="moe_backward",
        cost_estimate=pl.CostEstimate(flops=45 * 10**9, bytes_accessed=10**7, transcendentals=0),
        out_shape=(
            jax.ShapeDtypeStruct(exchange, low),
            jax.ShapeDtypeStruct(exchange, low),
            jax.ShapeDtypeStruct((nc,) + cotangents.shape, low),
            jax.ShapeDtypeStruct((more,) + exchange, low),
        ),
        in_specs=[pl.BlockSpec(memory_space=VMEM)] * 4 + [pl.BlockSpec(memory_space=ANY)] * 5,
        out_specs=[pl.BlockSpec(memory_space=VMEM)] * 2 + [pl.BlockSpec(memory_space=ANY)] * 2,
        scratch_shapes=[
            VMEM((width, hidden), low),
            VMEM((width, hidden), low),
            VMEM((hidden, width), low),
            VMEM(exchange, low),
            VMEM((1,) + exchange, low),
            VMEM((ns * cap, hidden), low),
            VMEM((ns * cap, hidden), low),
            VMEM((most, hidden), low),
            VMEM((most, hidden), low),
            SEM.DMA((5,)),
            SEM.DMA((ns,)),
            SEM.DMA((ns,)),
            SEM.DMA((ns,)),
            SEM.DMA((ns,)),
            SEM.DMA((2, nc, 1)),
            SEM.DMA((2, nc, 1)),
            SEM.DMA((1,)),
            SEM.DMA((more, ns)),
            SEM.DMA((more, ns)),
        ],
        compiler_params=pltpu.CompilerParams(
            collective_id=6, has_side_effects=True, vmem_limit_bytes=60 * 1024 * 1024
        ),
    )(grads, cotangents, pick_next, tokens, gate_w, up_w, down_w, kept_g, kept_u)


def slice_plan(hidden, nc):
    exact, tiles = hidden // nc, hidden // 128
    wide = max(-(-((c + 1) * exact) // 128) - (c * exact) // 128 for c in range(nc))
    return [min((c * exact) // 128, tiles - wide) * 128 for c in range(nc)], wide * 128


def finish_all(
    grads, small, squares, terms, own_terms, dh, inputs, gain, picks, normed, rows, row_grads, gate_w, up_w, down_w, nc, ns, kept
):
    nj = ns // 2
    parts, piece, width = grads.shape[0], grads.shape[4], grads.shape[5]
    low, f32 = jnp.bfloat16, jnp.float32
    tile = squares.shape
    features, hidden = gate_w.shape
    band, half, exact = features // nc, hidden // 2, hidden // nc
    wide = slice_plan(half, nc // 2)[1]
    more = picks.shape[0]
    exchange = picks.shape[1:3] + (features,)
    row_at = [(i, n) for i, x in enumerate(rows) for n in range(x.shape[0])]
    row_at = row_at + [(None, n) for n in range(more)]
    grad_at = [(len(rows) + i, n) for i, x in enumerate(row_grads) for n in range(x.shape[0])]
    count, block = len(rows) + len(row_grads), rows[0].shape[1]
    blocks = len(row_at)
    positions = own_terms.shape[0]
    rest = half - wide if nc == 4 else 128
    widths = [wide] + [rest] * ((half - wide) // rest)

    def kernel(g_in, e_in, q_in, f_in, fo_in, dh_in, t_in, gain_in, p_in, n_in, *refs):
        (g_hbm, u_hbm, d_hbm, k0_out, k1_out, k2_out, k3_out, e_out, q_out, wg_out, wu_out, wd_out, x_out, n_out,
         gt, et, gc, ec, gx, ex, gz, ez, g_sum, qz, qx, qc, qa, qb,
         cs, cr, xs, xr, zs, zr, q1s, q1r, q2s, q2r, q3s, q3r,
         xb, yb, wg, wu, wd, inner, dg, du, ag, au, ad, pair_send, down_send, ws, rs, ps, pr, ds, dr,
         fland, fs, fr, nsend, ns_, nr) = refs[count:]
        me = Place(nc, ns)
        k_out = (k0_out, k1_out, k2_out, k3_out)
        high, lower = me.c // 2, me.c % 2
        begin = pl.multiple_of(lower * half, 128)
        place = lower * (nc // 2) + high
        source = (me.c % (nc // 2)) * 2 + me.c // (nc // 2)
        offset = high * exact
        cut = pl.multiple_of(jnp.minimum(offset // 128, (half - wide) // 128) * 128, 128)
        begins = [cut] + [lax.rem(cut + wide + n * rest, half) for n in range((half - wide) // rest)]

        def fetch(i):
            (a, n), (b, k) = row_at[i % blocks], grad_at[i % blocks]
            if a is None:
                return [
                    pltpu.make_async_copy(
                        n_out.at[n, m], xb.at[i % 2, pl.ds(m * cap, cap)], rs.at[i % 2, 2 + m]
                    )
                    for m in range(ns)
                ] + [pltpu.make_async_copy(refs[b].at[k], yb.at[i % 2], rs.at[i % 2, 1])]
            return [
                pltpu.make_async_copy(refs[a].at[n], xb.at[i % 2], rs.at[i % 2, 0]),
                pltpu.make_async_copy(refs[b].at[k], yb.at[i % 2], rs.at[i % 2, 1]),
            ]

        loads = fetch(0) + [
            pltpu.make_async_copy(g_hbm.at[:, pl.ds(begin, half)], wg, ws.at[0]),
            pltpu.make_async_copy(u_hbm.at[:, pl.ds(begin, half)], wu, ws.at[1]),
            pltpu.make_async_copy(d_hbm.at[pl.ds(begin, half)], wd, ws.at[2]),
        ]
        for load in loads:
            load.start()
        barrier = pltpu.get_barrier_semaphore()
        partners = [me.along(d) for d in range(1, nc)] + [(me.c, me.s ^ m) for m in range(1, ns)]
        for partner in partners:
            pl.semaphore_signal(barrier, inc=1, device_id=partner, device_id_type=MESH)
        pl.semaphore_wait(barrier, len(partners))

        def pass_terms(step):
            for side, direction in enumerate((-1, 1)):
                here = me.c if direction < 0 else nc - 1 - me.c
                ahead = step - (nc - 1 - here)
                number = ahead if direction < 0 else nc - 1 - ahead
                sends = (ahead >= 0) & (ahead < here)

                @pl.when(sends & (here < nc - 1))
                def _():
                    term_copy(side, direction, number, True).wait_recv()
                    for i in range(0, positions, 64):
                        at = pl.ds(i, 64)
                        fland[number, at] = (
                            fland[number, at].astype(f32) + f_in[number, at].astype(f32)
                        ).astype(low)

                @pl.when(sends & (here == nc - 1))
                def _():
                    fland[number] = f_in[number]

                @pl.when(sends)
                def _():
                    term_copy(side, direction, number, False).start()

        def term_copy(side, direction, number, landing):
            target = me.c if landing else lax.rem(me.c + direction + nc, nc)
            place = jnp.where(number == target, nc, number) if direction > 0 else number
            source = place if landing else number
            return remote(
                fland.at[source], fland.at[place], fs.at[side, number], fr.at[side, number],
                (lax.rem(me.c + direction + nc, nc), me.s),
            )

        def end_terms():
            x_out[...] = fo_in[...]
            for side, direction in enumerate((-1, 1)):
                here = me.c if direction < 0 else nc - 1 - me.c

                @pl.when(here < nc - 1)
                def _():
                    term_copy(side, direction, me.c, True).wait_recv()
                    x_out[...] += fland[nc if direction > 0 else me.c].astype(f32)

            x = t_in[...].astype(f32)
            rate = lax.rsqrt(jnp.mean(x * x, axis=-1, keepdims=True) + epsilon)
            scaled = x_out[...] * gain_in[...]
            pull = jnp.mean(scaled * x, axis=-1, keepdims=True)
            x_out[...] = dh_in[...] + rate * scaled - x * (rate * rate * rate * pull)

        def sent_terms():
            for side, direction in enumerate((-1, 1)):
                here = me.c if direction < 0 else nc - 1 - me.c
                for ahead in range(nc - 1):

                    @pl.when(ahead < here)
                    def _():
                        number = ahead if direction < 0 else nc - 1 - ahead
                        term_copy(side, direction, number, False).wait_send()

        cap = exchange[1]
        jobs = [(p_in.at[i], n_in.at[me.c ^ (nc - more + i)], n_out.at[i]) for i in range(more)]
        spread = Spread(me, jobs, nsend, ns_, nr)
        pass_terms(0)
        for i in range(more):
            spread.start(i)

        def both(pairs, send, recv, device):
            return [
                remote(one, target, send.at[i], recv.at[i], device)
                for i, (one, target) in enumerate(pairs)
            ]

        def core_copy(d):
            row = lax.rem(me.c + d, nc)
            other = 1 - me.core
            return both(
                ((g_in.at[:, row, :, other], gc.at[d]), (e_in.at[row, :, other], ec.at[d])),
                cs.at[d], cr.at[d], me.twin(),
            )

        def cross_copy(d, k):
            return both(
                ((gt.at[d, :, me.j ^ k], gx.at[d, k - 1]), (et.at[d, me.j ^ k], ex.at[d, k - 1])),
                xs.at[d, k], xr.at[d, k], me.across(k),
            )

        def along_copy(d):
            return both(
                ((gt.at[d, :, me.j], gz.at[d - 1]), (et.at[d, me.j], ez.at[d - 1])),
                zs.at[d], zr.at[d], me.along(d),
            )

        def start(copies):
            for copy in copies:
                copy.start()

        def landed(copies):
            for copy in copies:
                copy.wait_recv()

        def q_along(d):
            return remote(q_in, qz.at[d - 1], q1s.at[d], q1r.at[d], me.along(d))

        def q_across(k):
            return remote(qa, qx.at[k - 1], q2s.at[k], q2r.at[k], me.across(k))

        q_twin = remote(qb, qc, q3s.at[0], q3r.at[0], me.twin())
        order = list(range(1, nc)) + [0]

        def core_stage():
            for d in order:
                landed(core_copy(d))
                row = lax.rem(me.c + d, nc)

                def add_core(i, carry):
                    for k in range(nj):
                        gt[d, i, k] = (
                            g_in[i, row, k, me.core].astype(f32) + gc[d, i, k].astype(f32)
                        ).astype(low)
                    return carry

                lax.fori_loop(0, parts, add_core, 0)
                for k in range(nj):
                    et[d, k] = (
                        e_in[row, k, me.core].astype(f32) + ec[d, k].astype(f32)
                    ).astype(low)
                for k in range(1, nj):
                    start(cross_copy(d, k))
            for d in range(1, nc):
                q_along(d).wait_recv()
            value = q_in[...]
            for d in range(1, nc):
                value = value + qz[d - 1]
            qa[...] = value
            for k in range(1, nj):
                q_across(k).start()

        def cross_stage():
            for d in order:
                for k in range(1, nj):
                    landed(cross_copy(d, k))

                def add_cross(i, carry):
                    value = gt[d, i, me.j].astype(f32)
                    for k in range(1, nj):
                        value = value + gx[d, k - 1, i].astype(f32)
                    if d == 0:
                        g_sum[i] = value
                    else:
                        gt[d, i, me.j] = value.astype(low)
                    return carry

                lax.fori_loop(0, parts, add_cross, 0)
                value = et[d, me.j].astype(f32)
                for k in range(1, nj):
                    value = value + ex[d, k - 1].astype(f32)
                if d:
                    et[d, me.j] = value.astype(low)
                    start(along_copy(d))
                else:
                    e_out[...] = value
            for k in range(1, nj):
                q_across(k).wait_recv()
            value = qa[...]
            for k in range(1, nj):
                value = value + qx[k - 1]
            qb[...] = value
            q_twin.start()

        def along_stage():
            for i in range(kept):
                k_out[i][:, pl.ds(pl.multiple_of(me.c * width, width), width)] = g_sum[i]
            for d in range(1, nc):
                landed(along_copy(d))
                row = lax.rem(me.c - d + nc, nc)
                for i in range(kept):
                    at = pl.ds(pl.multiple_of(row * width, width), width)
                    k_out[i][:, at] = gz[d - 1, i].astype(f32)
                e_out[...] = e_out[...] + ez[d - 1].astype(f32)
            for i in range(kept, parts):
                value = g_sum[i]
                for d in range(1, nc):
                    value = value + gz[d - 1, i].astype(f32)
                k_out[kept][:, (i - kept) * width : (i - kept + 1) * width] = value
            q_twin.wait()
            q_out[...] = qb[...] + qc[...]

        def pair_copy(i, p):
            at = pl.multiple_of(begins[p], 128)
            return remote(
                pair_send.at[i, :, pl.ds(at, widths[p])],
                (wg_out, wu_out)[i].at[:, pl.ds(pl.multiple_of(begin + at, 128), widths[p])],
                ps.at[i, p], pr.at[i, p], (me.c + 1 - 2 * lower, me.s),
            )

        def pair_landing(i, p):
            at = pl.multiple_of(half - begin + begins[p], 128)
            landing = (wg_out, wu_out)[i].at[:, pl.ds(at, widths[p])]
            return remote(landing, landing, ps.at[i, p], pr.at[i, p], me.along(1))

        down_copy = remote(down_send, wd_out, ds.at[0], dr.at[0], (place, me.s))

        def give(i, p, total):
            at = pl.multiple_of(begins[p], 128)
            other = total[pl.ds(pl.multiple_of((1 - lower) * band, band), band), : widths[p]]
            pair_send[i, :, pl.ds(at, widths[p])] = other.astype(low)
            pair_copy(i, p).start()
            own = total[pl.ds(pl.multiple_of(lower * band, band), band), : widths[p]]
            at = pl.multiple_of(begin + at, 128)
            (wg_out, wu_out)[i][:, pl.ds(at, widths[p])] = own.astype(low)

        for d in order:
            start(core_copy(d))
        for d in range(1, nc):
            q_along(d).start()
        for load in loads:
            load.wait()
        steps = [[core_stage], [], [cross_stage], [], [], [], [along_stage]]
        places = [2 * n + 1 for n in range(nc - 2)]
        stages = [
            (steps[n] if n < len(steps) else [])
            + [lambda step=step + 1: pass_terms(step) for step, place_ in enumerate(places) if place_ == n]
            for n in range(max(len(steps), len(places) and places[-1] + 1))
        ]
        last = blocks - 1
        for p, size in enumerate(widths):
            cuts = [(n, min(n + TILE, size)) for n in range(0, size, TILE)]
            for i in range(blocks):
                turn = p * blocks + i
                if turn:
                    for load in fetch(turn):
                        load.wait()
                x, dy = xb.at[turn % 2], yb.at[turn % 2]
                for left, right in cuts:
                    at = pl.ds(pl.multiple_of(begins[p] + left, 128), right - left)
                    value, slope = gelu_parts(dot32(x[...], wg[:, at]))
                    linear = dot32(x[...], wu[:, at])
                    down = nt(dy[...], wd[at])
                    inner[:, left:right] = (value * linear).astype(low)
                    dg[:, left:right] = (down * linear * slope).astype(low)
                    du[:, left:right] = (down * value).astype(low)
                if turn + 1 < blocks * len(widths):
                    if turn + 1 < blocks and row_at[turn + 1][0] is None:
                        spread.landed(row_at[turn + 1][1])
                    for load in fetch(turn + 1):
                        load.start()
                mine = x[:, pl.ds(pl.multiple_of(high * 2 * band, 2 * band), 2 * band)]
                for n, (total, grad) in enumerate(((ag, dg), (au, du))):
                    if i:
                        total[:, :size] += tn(mine, grad[:, :size])
                    else:
                        total[:, :size] = tn(mine, grad[:, :size])
                    if i == last:
                        give(n, p, total)
                if p == 0:
                    if i:
                        ad[...] += tn(inner[...], dy[...])
                    else:
                        ad[...] = tn(inner[...], dy[...])
                    if i == last:
                        at = pl.ds(pl.multiple_of(offset - cut, 16), exact)
                        down_send[...] = ad[at].astype(low)

                        @pl.when(place != me.c)
                        def _():
                            down_copy.start()

                        @pl.when(place == me.c)
                        def _():
                            wd_out[...] = down_send[...]

                if stages and turn + 1 < blocks * len(widths):
                    for stage in stages.pop(0):
                        stage()
        for group in stages:
            for stage in group:
                stage()
        end_terms()
        for i in range(2):
            for p in range(len(widths)):
                pair_landing(i, p).wait_recv()

        @pl.when(source != me.c)
        def _():
            down_copy.wait_recv()

        @pl.when(place != me.c)
        def _():
            down_copy.wait_send()

        for d in order:
            started = core_copy(d) + [copy for k in range(1, nj) for copy in cross_copy(d, k)]
            if d:
                started = started + along_copy(d) + [q_along(d)]
            for copy in started:
                copy.wait_send()
        for k in range(1, nj):
            q_across(k).wait_send()
        for i in range(2):
            for p in range(len(widths)):
                pair_copy(i, p).wait_send()
        sent_terms()

    one, extra = (parts, piece, width), small.shape[3:]
    return pl.pallas_call(
        kernel,
        name="finish_all",
        cost_estimate=pl.CostEstimate(flops=80 * 10**9, bytes_accessed=10**7, transcendentals=0),
        out_shape=(
            *[jax.ShapeDtypeStruct((piece, nc * width), f32)] * 4,
            jax.ShapeDtypeStruct(extra, f32),
            jax.ShapeDtypeStruct(tile, f32),
            jax.ShapeDtypeStruct((band, hidden), low),
            jax.ShapeDtypeStruct((band, hidden), low),
            jax.ShapeDtypeStruct((exact, features), low),
            jax.ShapeDtypeStruct(own_terms.shape, f32),
            jax.ShapeDtypeStruct((more,) + exchange, low),
        ),
        in_specs=[pl.BlockSpec(memory_space=VMEM)] * 10 + [pl.BlockSpec(memory_space=ANY)] * (count + 3),
        out_specs=[pl.BlockSpec(memory_space=VMEM)] * 10 + [pl.BlockSpec(memory_space=ANY)],
        scratch_shapes=[
            VMEM((nc, parts, nj, piece, width), low),
            VMEM((nc, nj) + extra, low),
            VMEM((nc, parts, nj, piece, width), low),
            VMEM((nc, nj) + extra, low),
            VMEM((nc, nj - 1) + one, low),
            VMEM((nc, nj - 1) + extra, low),
            VMEM((nc - 1,) + one, low),
            VMEM((nc - 1,) + extra, low),
            VMEM(one, f32),
            VMEM((nc - 1,) + tile, f32),
            VMEM((nj - 1,) + tile, f32),
            VMEM(tile, f32),
            VMEM(tile, f32),
            VMEM(tile, f32),
            SEM.DMA((nc, 2)),
            SEM.DMA((nc, 2)),
            SEM.DMA((nc, nj, 2)),
            SEM.DMA((nc, nj, 2)),
            SEM.DMA((nc, 2)),
            SEM.DMA((nc, 2)),
            SEM.DMA((nc,)),
            SEM.DMA((nc,)),
            SEM.DMA((nj,)),
            SEM.DMA((nj,)),
            SEM.DMA((1,)),
            SEM.DMA((1,)),
            VMEM((2, block, features), low),
            VMEM((2, block, features), low),
            VMEM((features, half), low),
            VMEM((features, half), low),
            VMEM((half, features), low),
            VMEM((block, wide), low),
            VMEM((block, wide), low),
            VMEM((block, wide), low),
            VMEM((2 * band, wide), f32),
            VMEM((2 * band, wide), f32),
            VMEM((wide, features), f32),
            VMEM((2, band, half), low),
            VMEM((exact, features), low),
            SEM.DMA((3,)),
            SEM.DMA((2, 2 + ns)),
            SEM.DMA((2, len(widths))),
            SEM.DMA((2, len(widths))),
            SEM.DMA((1,)),
            SEM.DMA((1,)),
            VMEM((nc + 1,) + own_terms.shape, low),
            SEM.DMA((2, nc)),
            SEM.DMA((2, nc)),
            VMEM((1,) + exchange, low),
            SEM.DMA((more, ns)),
            SEM.DMA((more, ns)),
        ],
        compiler_params=pltpu.CompilerParams(
            collective_id=2, has_side_effects=True, vmem_limit_bytes=60 * 1024 * 1024
        ),
    )(grads, small, squares, terms, own_terms, dh, inputs, gain, picks, normed, *rows, *row_grads, gate_w, up_w, down_w)


def per_device(
    tokens,
    segments,
    valid,
    routes,
    teacher,
    norm_attn,
    w_query,
    w_key,
    w_value,
    output_weight,
    rel_bias,
    norm_ffn,
    w_router,
    w_gate,
    w_up,
    w_down,
):
    nc = lax.axis_size("ctx")
    ns = lax.axis_size("shard")
    c, s = lax.axis_index("ctx"), lax.axis_index("shard")
    n_dev, nj = nc * ns, ns // 2
    row_count, width = tokens.shape[1:]
    top_count = routes.shape[2]
    experts = w_router.shape[1]
    capacity = (5 * row_count * top_count + 4 * experts - 1) // (4 * experts)
    length = row_count * nc
    low = jnp.bfloat16
    f32 = jnp.float32
    piece = w_query.shape[0]
    band = 2 * row_count

    route_local = routes[0]
    expert_ids = jnp.arange(experts, dtype=jnp.int32)
    route_hot = route_local[:, :, None] == expert_ids[None, None, :]
    flat_routes = route_local.reshape(row_count * top_count)
    route_hits = (flat_routes[:, None] == expert_ids[None, :]).astype(jnp.int32)
    before = jnp.cumsum(route_hits, axis=0) - route_hits
    slot_rank = jnp.sum(before * route_hits, axis=1).reshape(row_count, top_count)

    part = width // nc
    smalls = (
        norm_attn, norm_ffn, rel_bias, w_router.reshape(-1), segments[0].astype(low), valid[0].astype(low),
        route_local.astype(low).T.reshape(-1), slot_rank.astype(low).T.reshape(-1),
    )
    sizes = [x.shape[0] for x in smalls]
    starts = [sum(sizes[:i]) for i in range(len(sizes))]
    extra = jnp.concatenate(smalls + (jnp.zeros((EXTRA * part - sum(sizes),), low),))
    shares = [w.reshape(piece, nc, part).transpose(1, 0, 2) for w in (w_query, w_key, w_value, output_weight)]
    shares = jnp.concatenate(
        [x[:, None] for x in shares[:3]] + [jnp.broadcast_to(shares[3][None], (nc, nc, piece, part))], axis=1
    )
    weights, extras, tokens_all = gather_all(
        shares, extra.reshape(EXTRA, part), tokens[0], nc, ns
    )
    extras = extras.reshape(nc, ns, EXTRA * part)
    gain_attn, gain_ffn, full_bias, full_router = (
        extras[:, :, begin : begin + size].reshape(-1)
        for begin, size in zip(starts[:4], sizes[:4])
    )
    full_router = full_router.reshape(width, experts)
    table = full_bias.reshape(BUCKETS, HEADS).astype(f32)
    line = lax.dynamic_slice_in_dim(extras, s, 1, 1)[:, 0]
    line_seg = line[:, starts[4] : starts[4] + row_count].reshape(length).astype(jnp.int32)
    line_valid = line[:, starts[5] : starts[5] + row_count].reshape(length) > 0
    key_code = jnp.where(line_valid, line_seg, -1)[None]
    query_code = line_seg[:, None]
    valid_count = jnp.sum(extras[:, :, starts[5] : starts[5] + row_count].astype(f32))

    spot = (jnp.arange(band)[None, :] - jnp.arange(CHUNK)[:, None]) % band
    distance = jnp.where(spot <= row_count, row_count - spot, 3 * row_count - spot)
    level = bucket_of(distance, BUCKETS)
    level_hot = (level[:, :, None] == jnp.arange(BUCKETS)[None, None, :]).astype(f32)
    heads = HEADS // nc
    own_table = lax.dynamic_slice_in_dim(table, c * heads, heads, 1)
    slopes = jnp.einsum(
        "ixb,bh->hix", level_hot, own_table - own_table[BUCKETS - 1 :], precision=highest_precision
    )

    gain_one, gain_two = gain_attn.astype(f32), gain_ffn.astype(f32)
    first_all, queries, keys, values, mixed, log_total, residual, ffn_low = attend_forward(
        tokens_all, weights, gain_one[None], gain_two[None], query_code, key_code, slopes, nc, ns
    )
    ffn_in = ffn_low.astype(f32)
    router = full_router.astype(f32)
    logits = jnp.dot(ffn_in, router, precision=highest_precision)
    picked = jnp.sum(jnp.where(route_hot, logits[:, None, :], 0.0), axis=-1)
    gate_probs = jax.nn.softmax(picked, axis=-1)

    slots = -(-capacity // 16) * 16
    target = (route_local ^ s) * slots + slot_rank
    slot_ids = jnp.arange(experts * slots, dtype=jnp.int32)
    pick_first = (slot_ids[:, None] == target[None, :, 0]).astype(low)
    pick_second = (slot_ids[:, None] == target[None, :, 1]).astype(low)
    pick_both = pick_first + pick_second
    gate_w, up_w, down_w = w_gate[0], w_up[0], w_down[0]
    gate_rows = jnp.concatenate((gate_probs.T, jnp.zeros((8 - top_count, row_count), f32)), axis=0)
    other_line = line[c ^ jnp.arange(1, nc)]
    other_routes, other_slots = (
        other_line[:, starts[i] : starts[i] + top_count * row_count]
        .astype(jnp.int32)
        .reshape(nc - 1, top_count, row_count)
        for i in (6, 7)
    )
    other_target = (other_routes ^ s) * slots + other_slots
    other_first, other_second = (
        slot_ids[None, :, None] == other_target[:, m, None, :] for m in range(2)
    )
    other_picks = (other_first | other_second).astype(low).reshape(nc - 1, experts, slots, row_count)
    expert_rows, returned, ffn_all, gates_all, rows_next, kept_g, kept_u = moe_forward(
        pick_both.reshape(experts, slots, row_count), other_picks[0], ffn_low, gate_rows,
        gate_w, up_w, down_w, nc, ns,
    )
    returned = returned.reshape(experts * slots, width)
    picked_one, picked_two = tn(pick_first, returned), tn(pick_second, returned)
    output_sum = residual + gate_probs[:, :1] * picked_one + gate_probs[:, 1:] * picked_two
    valid_one = valid[0].astype(f32)
    deviation = output_sum - teacher[0].astype(f32)
    local_square = jnp.sum(valid_one[:, None] * deviation * deviation)
    everything = float(row_count * nc * ns)
    cotangent = everything / valid_count * deviation * valid_one[:, None]
    gate_grad = jnp.stack(
        (jnp.sum(cotangent * picked_one, axis=-1), jnp.sum(cotangent * picked_two, axis=-1)), axis=1
    )
    back_send = dot32(pick_first, (gate_probs[:, :1] * cotangent).astype(low)) + dot32(
        pick_second, (gate_probs[:, 1:] * cotangent).astype(low)
    )
    other_gates = gates_all[c ^ jnp.arange(1, nc)].astype(low)
    other_weighted = (
        jnp.where(other_first, other_gates[:, 0, None, :], low(0))
        + jnp.where(other_second, other_gates[:, 1, None, :], low(0))
    ).reshape(other_picks.shape)
    out_grad, sent_back, cotangent_all, rows_later = moe_backward(
        back_send.astype(low).reshape(experts, slots, width), kept_g, kept_u, cotangent.astype(low),
        other_picks[1 : nc // 2], ffn_all, gate_w, up_w, down_w, nc, ns,
    )
    ffn_grad = tn(pick_both, sent_back.reshape(experts * slots, width))
    pick_grad = gate_probs * (gate_grad - jnp.sum(gate_probs * gate_grad, axis=-1, keepdims=True))
    logits_grad = jnp.sum(jnp.where(route_hot, pick_grad[:, :, None], 0.0), axis=1)
    router_grad = contract(ffn_in, logits_grad, 0, 0, highest_precision)
    ffn_grad = ffn_grad + contract(logits_grad, router, 1, 1, highest_precision)
    unused, norm_two_back = jax.vjp(rms_norm, residual, gain_two)
    residual_from_norm, gain_two_grad = norm_two_back(ffn_grad)
    residual_grad = cotangent + residual_from_norm
    attn_grad_low = residual_grad.astype(low)
    hidden_own, hidden_terms, w_grads, gain_one_grad, near_sum, far_sum, other_grads = attend_backward(
        attn_grad_low, mixed, tokens_all, first_all, queries, keys, values, log_total, weights,
        query_code, key_code, slopes, other_weighted, cotangent_all, nc, ns,
    )
    own_bias = jnp.einsum("hix,ixb->bh", near_sum, level_hot, precision=highest_precision)
    last_bucket = (jnp.arange(BUCKETS) == BUCKETS - 1).astype(f32)
    own_bias = own_bias + last_bucket[:, None] * jnp.sum(far_sum, axis=(1, 2))[None, :]
    bias_grad = lax.dynamic_update_slice_in_dim(
        jnp.zeros((BUCKETS, HEADS), f32), own_bias, c * heads, 1
    )
    small_grads = jnp.concatenate(
        [
            x.reshape(n_dev, -1).astype(low)
            for x in (gain_one_grad, gain_two_grad, bias_grad, router_grad)
        ],
        axis=1,
    )
    small_grads = jnp.pad(small_grads, ((0, 0), (0, EXTRA * part - small_grads.shape[1])))
    *attn_sums, small_sum, square_sum, gate_w_sum, up_w_sum, down_w_sum, input_grad, unused = finish_all(
        w_grads.reshape(3 + nc, nc, nj, 2, piece, part),
        small_grads.reshape(nc, nj, 2, EXTRA, part),
        jnp.full((8, 128), local_square, f32),
        hidden_terms,
        hidden_own,
        residual_grad,
        tokens[0],
        gain_one[None],
        other_picks[nc // 2 :],
        ffn_all,
        [x.reshape(-1, experts * slots, width) for x in (expert_rows, rows_next, rows_later)],
        [x.reshape(-1, experts * slots, width) for x in (out_grad, other_grads)],
        gate_w,
        up_w,
        down_w,
        nc,
        ns,
        3,
    )
    loss_value = square_sum[0, 0] / (2.0 * width * valid_count)
    small_sum = small_sum.reshape(-1)
    tails = [small_sum[begin : begin + size] for begin, size in zip(starts[:4], sizes[:4])]
    return (
        output_sum.astype(low)[None],
        loss_value,
        input_grad[None],
        tails[0],
        attn_sums[0],
        attn_sums[1],
        attn_sums[2],
        attn_sums[3],
        tails[2],
        tails[1],
        tails[3].reshape(w_router.shape),
        gate_w_sum[None].astype(f32),
        up_w_sum[None].astype(f32),
        down_w_sum[None].astype(f32),
    )


def solution(mesh):
    return jax.shard_map(
        per_device,
        mesh=mesh,
        in_specs=(
            P("shard", "ctx", None),
            P("shard", "ctx"),
            P("shard", "ctx"),
            P("shard", "ctx", None),
            P("shard", "ctx", None),
            P(("ctx", "shard")),
            P(("ctx", "shard"), None),
            P(("ctx", "shard"), None),
            P(("ctx", "shard"), None),
            P(("ctx", "shard"), None),
            P(("ctx", "shard")),
            P(("ctx", "shard")),
            P(("ctx", "shard"), None),
            P("shard", None, None),
            P("shard", None, None),
            P("shard", None, None),
        ),
        out_specs=(
            P("shard", "ctx", None),
            P(),
            P("shard", "ctx", None),
            P(("ctx", "shard")),
            P(("ctx", "shard"), None),
            P(("ctx", "shard"), None),
            P(("ctx", "shard"), None),
            P(("ctx", "shard"), None),
            P(("ctx", "shard")),
            P(("ctx", "shard")),
            P(("ctx", "shard"), None),
            P("shard", "ctx", None),
            P("shard", "ctx", None),
            P("shard", "ctx", None),
        ),
        check_vma=False,
    )
```

```python
import math

import jax
import jax.numpy as jnp
from jax import lax
from jax.experimental import pallas as pl
from jax.experimental.pallas import tpu as pltpu
from jax.sharding import PartitionSpec as P

HEADS = 16
HEAD = 64
BUCKETS = 32
MESH = pl.DeviceIdType.MESH
ANY = pl.ANY
VMEM = pltpu.VMEM
SEM = pltpu.SemaphoreType

highest_precision = lax.Precision.HIGHEST
max_distance = 128
epsilon = 1e-06
negative = -1e30
EXTRA = 16


def thresholds(buckets):
    exact_count = buckets // 2
    limits = list(range(1, exact_count))
    for bucket_level in range(exact_count, buckets):
        power = (bucket_level - exact_count) / exact_count
        limits.append(int(math.ceil(exact_count * (max_distance / exact_count) ** power)))
    return limits


def bucket_of(distance, buckets):
    bucket_total = jnp.zeros(distance.shape, jnp.int32)
    for threshold in thresholds(buckets):
        bucket_total = bucket_total + (distance >= threshold).astype(jnp.int32)
    return bucket_total


def rms_norm(values, gain_vector):
    return (
        values
        * lax.rsqrt(jnp.mean(values * values, axis=-1, keepdims=True) + epsilon)
        * gain_vector
    )


def contract(left_side, right_side, left_axis, right_axis, precision_mode=None):
    return lax.dot_general(
        left_side,
        right_side,
        (((left_axis,), (right_axis,)), ((), ())),
        precision=precision_mode,
        preferred_element_type=jnp.float32,
    )


def dot32(left_side, right_side):
    return jnp.dot(left_side, right_side, preferred_element_type=jnp.float32)


def nt(left_side, right_side):
    return contract(left_side, right_side, 1, 1)


def tn(left_side, right_side):
    return contract(left_side, right_side, 0, 0)


class Place:
    def __init__(self, nc, ns):
        self.nc, self.ns, self.nj = nc, ns, ns // 2
        self.c = lax.axis_index("ctx")
        self.s = lax.axis_index("shard")
        self.core = self.s % 2
        self.j = self.s // 2

    def along(self, d):
        return (lax.rem(self.c + d + self.nc, self.nc), self.s)

    def across(self, k):
        return (self.c, self.s ^ (2 * k))

    def twin(self):
        return (self.c, self.s ^ 1)

    def greet(self):
        barrier = pltpu.get_barrier_semaphore()
        partners = (
            [self.along(d) for d in range(1, self.nc)]
            + [self.across(k) for k in range(1, self.nj)]
            + [self.twin()]
        )
        for partner in partners:
            pl.semaphore_signal(barrier, inc=1, device_id=partner, device_id_type=MESH)
        pl.semaphore_wait(barrier, len(partners))


def remote(source, target, send, recv, device):
    return pltpu.make_async_remote_copy(
        src_ref=source,
        dst_ref=target,
        send_sem=send,
        recv_sem=recv,
        device_id=device,
        device_id_type=MESH,
    )


def gather_all(weights, extra, rows, nc, ns):
    n_dev, nj = nc * ns, ns // 2
    share = weights.shape[1:]
    full_shape = (share[0], nc, ns) + share[1:]

    def kernel(w_in, e_in, t_in, w_out, e_out, t_out, local, zs, zr, xs, xr, cs, cr, ts, tr):
        me = Place(nc, ns)

        def views(row, column):
            return (w_out.at[:, row, column], e_out.at[row, column])

        def piece(d, k):
            return views(lax.rem(me.c - d + nc, nc), me.s ^ (2 * k))

        mine = (w_in.at[me.c], e_in)
        locals_ = [
            pltpu.make_async_copy(source, target, local.at[i])
            for i, (source, target) in enumerate(
                zip(mine + (t_in,), views(me.c, me.s) + (t_out.at[me.c],))
            )
        ]
        for copy in locals_:
            copy.start()
        me.greet()
        sent = []

        def push(sources, targets, send, recv, device):
            for i in range(2):
                copy = remote(sources[i], targets[i], send.at[i], recv.at[i], device)
                copy.start()
                sent.append(copy)

        def arrive(targets, send, recv, device):
            for i in range(2):
                remote(targets[i], targets[i], send.at[i], recv.at[i], device).wait_recv()

        def token_copy(direction, hop):
            lane = 0 if direction > 0 else 1
            origin = lax.rem(me.c - direction * hop + nc, nc)
            return remote(
                t_in if hop == 0 else t_out.at[origin],
                t_out.at[origin],
                ts.at[lane, hop],
                tr.at[lane, hop],
                (lax.rem(me.c + direction + nc, nc), me.s),
            )

        def token_landing(direction, hop):
            lane = 0 if direction > 0 else 1
            origin = lax.rem(me.c - direction * (hop + 1) + nc, nc)
            landing = t_out.at[origin]
            return remote(landing, landing, ts.at[lane, hop], tr.at[lane, hop], me.along(1))

        def can_send(direction, hop):
            if direction > 0:
                return (me.c >= hop) & (me.c < nc - 1)
            return (me.c <= nc - 1 - hop) & (me.c > 0)

        def can_receive(direction, hop):
            if direction > 0:
                return me.c >= hop + 1
            return me.c <= nc - 2 - hop

        for d in range(1, nc):
            target = lax.rem(me.c + d, nc)
            push(
                (w_in.at[target], e_in), views(me.c, me.s), zs.at[d], zr.at[d], (target, me.s)
            )
        for direction in (1, -1):

            @pl.when(can_send(direction, 0))
            def _():
                token_copy(direction, 0).start()

        for k in range(1, nj):
            push(mine, views(me.c, me.s), xs.at[0, k], xr.at[0, k], me.across(k))
        push(mine, views(me.c, me.s), cs.at[0, 0], cr.at[0, 0], me.twin())

        for copy in locals_:
            copy.wait()
        for d in range(1, nc):
            here = piece(d, 0)
            arrive(here, zs.at[d], zr.at[d], me.along(-d))
            for k in range(1, nj):
                push(here, here, xs.at[d, k], xr.at[d, k], me.across(k))
            push(here, here, cs.at[d, 0], cr.at[d, 0], me.twin())
        for d in range(nc):
            for k in range(1, nj):
                here = piece(d, k)
                arrive(here, xs.at[d, k], xr.at[d, k], me.across(k))
                push(here, here, cs.at[d, k], cr.at[d, k], me.twin())
            if d < nc - 2:
                for direction in (1, -1):

                    @pl.when(can_receive(direction, d))
                    def _():
                        token_landing(direction, d).wait_recv()

                    @pl.when(can_send(direction, d + 1))
                    def _():
                        token_copy(direction, d + 1).start()

        for d in range(nc):
            for k in range(nj):
                here = views(lax.rem(me.c - d + nc, nc), me.s ^ 1 ^ (2 * k))
                arrive(here, cs.at[d, k], cr.at[d, k], me.twin())
        for direction in (1, -1):

            @pl.when(can_receive(direction, nc - 2))
            def _():
                token_landing(direction, nc - 2).wait_recv()

        for copy in sent:
            copy.wait_send()
        for direction in (1, -1):
            for hop in range(nc - 1):

                @pl.when(can_send(direction, hop))
                def _():
                    token_copy(direction, hop).wait_send()

    full, extras, tokens = pl.pallas_call(
        kernel,
        name="gather_all",
        cost_estimate=pl.CostEstimate(flops=50 * 10**9, bytes_accessed=10**7, transcendentals=0),
        out_shape=(
            jax.ShapeDtypeStruct(full_shape, weights.dtype),
            jax.ShapeDtypeStruct((nc, ns) + extra.shape, extra.dtype),
            jax.ShapeDtypeStruct((nc,) + rows.shape, rows.dtype),
        ),
        in_specs=[pl.BlockSpec(memory_space=ANY)] * 3,
        out_specs=[pl.BlockSpec(memory_space=ANY)] * 3,
        scratch_shapes=[
            SEM.DMA((3,)),
            SEM.DMA((nc, 2)),
            SEM.DMA((nc, 2)),
            SEM.DMA((nc, nj, 2)),
            SEM.DMA((nc, nj, 2)),
            SEM.DMA((nc, nj, 2)),
            SEM.DMA((nc, nj, 2)),
            SEM.DMA((2, nc)),
            SEM.DMA((2, nc)),
        ],
        compiler_params=pltpu.CompilerParams(collective_id=1, has_side_effects=True),
    )(weights, extra, rows)
    return (
        full.reshape(share[0], n_dev * share[1], share[2]),
        extras,
        tokens.reshape(nc * rows.shape[0], rows.shape[1]),
    )


CHUNK = 16


def fill_mask(mask, query_code, key_code, block, count):
    near = block * count
    query = query_code[pl.ds(near, count)]
    if block:
        mask[:, :near] = jnp.where(query == key_code[:, :near], 0.0, negative)
    row = lax.broadcasted_iota(jnp.int32, (count, count), 0)
    column = lax.broadcasted_iota(jnp.int32, (count, count), 1)
    seen = ((query == key_code[:, near : near + count]) & (row >= column)) | (row == column)
    mask[:, near : near + count] = jnp.where(seen, 0.0, negative)


def fill_slopes(bank, slopes, head, count):
    for i in range(count // CHUNK):
        row = slopes[head]
        bank[head, i * CHUNK : (i + 1) * CHUNK] = pltpu.roll(row, i * CHUNK, 1) if i else row


def biased(scores, mask, slope, block, count):
    end = (block + 1) * count
    band = 2 * count
    if end < band:
        return scores + mask[:, :end] + slope[:, band - end :]
    if end == band:
        return scores + mask[:, :end] + slope[...]
    wide = scores[:, : end - band] + mask[:, : end - band]
    tight = scores[:, end - band :] + mask[:, end - band : end] + slope[...]
    return jnp.concatenate((wide, tight), axis=1)


def attend_forward(tokens, weights, gain, gain_next, query_code, key_code, slopes, nc, ns):
    length, width = tokens.shape
    count = length // nc
    part = width // nc
    heads, _, band = slopes.shape
    low, f32 = jnp.bfloat16, jnp.float32

    def kernel(t_in, w_in, gain_in, next_in, qcode, kcode, toe, first, q_out, k_out, v_out, o_out, lse_out, x_out, y_out,
               mask, bank, osend, ss, rs):
        me = Place(nc, ns)
        barrier = pltpu.get_barrier_semaphore()
        for d in range(1, nc):
            pl.semaphore_signal(barrier, inc=1, device_id=me.along(d), device_id_type=MESH)
        pl.semaphore_wait(barrier, nc - 1)

        def norm(i, carry):
            at = pl.ds(pl.multiple_of(i * 64, 64), 64)
            x = t_in[at].astype(f32)
            rate = lax.rsqrt(jnp.mean(x * x, axis=-1, keepdims=True) + epsilon)
            first[at] = (x * rate * gain_in[...]).astype(low)
            return carry

        lax.fori_loop(0, length // 64, norm, 0)

        def project(i, carry):
            at = pl.ds(pl.multiple_of(i * count, count), count)
            block = first[at]
            q_out[at] = dot32(block, w_in[0]).astype(low)
            k_out[at] = dot32(block, w_in[1]).astype(low)
            v_out[at] = dot32(block, w_in[2]).astype(low)
            return carry

        lax.fori_loop(0, nc, project, 0)
        for head in range(heads):
            fill_slopes(bank, toe, head, count)
        lane = lax.broadcasted_iota(jnp.int32, (count, 2 * HEAD), 1)
        spot = lax.broadcasted_iota(jnp.int32, (count, 128), 1)
        own_copy = [
            remote(osend.at[b], o_out.at[me.c], ss.at[b], rs.at[me.c], (b, me.s)) for b in range(nc)
        ]
        for b in reversed(range(nc)):
            end = (b + 1) * count
            rows = pl.ds(b * count, count)
            fill_mask(mask, qcode, kcode, b, count)
            level = jnp.zeros((count, 128), f32)
            for pair in range(heads // 2):
                two = slice(pair * 2 * HEAD, (pair + 1) * 2 * HEAD)
                q_pair = q_out[rows, two] * low(1.0 / math.sqrt(HEAD))
                k_pair = k_out[:end, two]
                v_pair = v_out[:end, two]
                halves = []
                for half in range(2):
                    head = pair * 2 + half
                    inside = (lane >= HEAD) if half else (lane < HEAD)
                    scores = nt(jnp.where(inside, q_pair, low(0)), k_pair)
                    scores = biased(scores, mask, bank.at[head], b, count)
                    top = jnp.max(scores, axis=1, keepdims=True)
                    scores = jnp.exp(scores - top)
                    total = jnp.sum(scores, axis=1, keepdims=True)
                    halves.append(dot32(scores.astype(low), v_pair) * (1.0 / total))
                    level = jnp.where(spot == head, top + jnp.log(total), level)
                osend[b, :, two] = jnp.where(lane < HEAD, halves[0], halves[1]).astype(low)
            lse_out[rows] = level

            @pl.when(me.c == b)
            def _():
                o_out[me.c] = osend[b]

            @pl.when(me.c != b)
            def _():
                own_copy[b].start()

        for d in range(1, nc):
            origin = lax.rem(me.c + d, nc)
            remote(
                osend.at[0], o_out.at[origin], ss.at[0], rs.at[origin], me.along(d)
            ).wait_recv()
        own = pl.ds(pl.multiple_of(me.c * count, count), count)
        squares = jnp.zeros((count, 1), f32)
        for n in range(nc):
            columns = slice(n * part, (n + 1) * part)
            x = t_in[own, columns].astype(f32)
            for origin in range(nc):
                x = x + dot32(o_out[origin], w_in[3 + n, origin * part : (origin + 1) * part])
            x_out[:, columns] = x
            squares = squares + jnp.sum(x * x, axis=1, keepdims=True)
        rate = lax.rsqrt(squares * (1.0 / width) + epsilon)
        for n in range(nc):
            columns = slice(n * part, (n + 1) * part)
            y_out[:, columns] = (x_out[:, columns] * rate * next_in[:, columns]).astype(low)
        for b in range(nc):

            @pl.when(me.c != b)
            def _():
                own_copy[b].wait_send()

    return pl.pallas_call(
        kernel,
        name="attend_forward",
        cost_estimate=pl.CostEstimate(flops=25 * 10**9, bytes_accessed=10**7, transcendentals=0),
        out_shape=(
            jax.ShapeDtypeStruct((length, width), low),
            jax.ShapeDtypeStruct((length, part), low),
            jax.ShapeDtypeStruct((length, part), low),
            jax.ShapeDtypeStruct((length, part), low),
            jax.ShapeDtypeStruct((nc, count, part), low),
            jax.ShapeDtypeStruct((length, 128), f32),
            jax.ShapeDtypeStruct((count, width), f32),
            jax.ShapeDtypeStruct((count, width), low),
        ),
        in_specs=[pl.BlockSpec(memory_space=VMEM)] * 7,
        out_specs=[pl.BlockSpec(memory_space=VMEM)] * 8,
        scratch_shapes=[
            VMEM((count, length), f32),
            VMEM((heads, count, band), f32),
            VMEM((nc, count, part), low),
            SEM.DMA((nc,)),
            SEM.DMA((nc,)),
        ],
        compiler_params=pltpu.CompilerParams(
            collective_id=3, has_side_effects=True, vmem_limit_bytes=56 * 1024 * 1024
        ),
    )(tokens, weights, gain, gain_next, query_code, key_code, slopes)


def attend_backward(
    dattn, o_all, tokens, first, q_all, k_all, v_all, lse, weights, query_code, key_code, slopes,
    weighted, cotangents, nc, ns,
):
    length, width = tokens.shape
    count = length // nc
    part = width // nc
    heads, _, band = slopes.shape
    low, f32 = jnp.bfloat16, jnp.float32
    scale = 1.0 / math.sqrt(HEAD)
    exchange = weighted.shape[1:3] + (width,)

    def kernel(a_in, o_in, t_in, first_in, q_in, k_in, v_in, lse_in, w_in, qcode, kcode, toe, pw_in, c_in,
               x_out, fsend, w_out, gain_out, near_out, far_out, c_out,
               mask, bank, dsend, dall, dq, dk, dv, fown, nsend, ss, rs, ns_, nr):
        me = Place(nc, ns)
        barrier = pltpu.get_barrier_semaphore()
        partners = [me.along(d) for d in range(1, nc)] + [(me.c, me.s ^ m) for m in range(1, ns)]
        for partner in partners:
            pl.semaphore_signal(barrier, inc=1, device_id=partner, device_id_type=MESH)
        pl.semaphore_wait(barrier, len(partners))

        def do_copy(d):
            return remote(dsend.at[d], dall.at[me.c], ss.at[d], rs.at[d], me.along(d))

        for d in list(range(1, nc)) + [0]:
            target = lax.rem(me.c + d, nc)
            at = pl.ds(pl.multiple_of(target * part, part), part)
            value = nt(a_in[:, :part], w_in[3, at])
            for n in range(1, nc):
                value = value + nt(a_in[:, n * part : (n + 1) * part], w_in[3 + n, at])
            if d:
                dsend[d] = value.astype(low)
                do_copy(d).start()
            else:
                dall[me.c] = value.astype(low)
        jobs = [(pw_in.at[d], c_in.at[me.c ^ (d + 1)], c_out.at[d]) for d in range(nc - 1)]
        spread = Spread(me, jobs, nsend, ns_, nr)
        for i in range(len(jobs)):
            spread.start(i)
        for n in range(nc):
            for origin in range(nc):
                w_out[3 + n, origin * part : (origin + 1) * part] = tn(
                    o_in[origin], a_in[:, n * part : (n + 1) * part]
                ).astype(low)
        for head in range(heads):
            fill_slopes(bank, toe, head, count)
        lane = lax.broadcasted_iota(jnp.int32, (count, 2 * HEAD), 1)
        spot = lax.broadcasted_iota(jnp.int32, (count, 128), 1)
        dk[...] = jnp.zeros_like(dk)
        dv[...] = jnp.zeros_like(dv)
        near_out[...] = jnp.zeros_like(near_out)
        far_out[...] = jnp.zeros_like(far_out)
        gain_out[...] = jnp.zeros_like(gain_out)
        for d in range(1, nc):
            origin = lax.rem(me.c - d + nc, nc)
            remote(dsend.at[d], dall.at[origin], ss.at[d], rs.at[d], me.along(d)).wait_recv()
        for b in reversed(range(nc)):
            end = (b + 1) * count
            rows = pl.ds(b * count, count)
            fill_mask(mask, qcode, kcode, b, count)
            level = lse_in[rows]
            for pair in range(heads // 2):
                two = slice(pair * 2 * HEAD, (pair + 1) * 2 * HEAD)
                q_pair = q_in[rows, two] * low(scale)
                do_pair = dall[b, :, two]
                k_pair = k_in[:end, two]
                v_pair = v_in[:end, two]
                parts = []
                for half in range(2):
                    head = pair * 2 + half
                    inside = (lane >= HEAD) if half else (lane < HEAD)
                    q_one = jnp.where(inside, q_pair, low(0))
                    do_one = jnp.where(inside, do_pair, low(0))
                    own_level = jnp.sum(
                        jnp.where(spot == head, level, 0.0), axis=1, keepdims=True
                    )
                    probs = jnp.exp(
                        biased(nt(q_one, k_pair), mask, bank.at[head], b, count) - own_level
                    )
                    grads = probs * nt(do_one, v_pair)
                    grads = grads - probs * jnp.sum(grads, axis=1, keepdims=True)
                    low_grads = grads.astype(low)
                    parts.append(dot32(low_grads, k_pair))
                    dk[:end, two] += tn(low_grads, q_one)
                    dv[:end, two] += tn(probs.astype(low), do_one)
                    near = grads[:, max(end - band, 0) :]
                    if end < band:
                        near = jnp.concatenate((jnp.zeros((count, band - end), f32), near), axis=1)
                    height = count
                    while height > CHUNK:
                        height = height // 2
                        near = near[:height] + pltpu.roll(near[height:], band - height, 1)
                    near_out[head] += near
                    if end > band:
                        far = grads[:, : end - band]
                        total = far[:, :128]
                        for piece in range(1, (end - band) // 128):
                            total = total + far[:, piece * 128 : (piece + 1) * 128]
                        height = count
                        while height > 8:
                            height = height // 2
                            total = total[:height] + total[height:]
                        far_out[head] += total
                dq[rows, two] = (jnp.where(lane < HEAD, parts[0], parts[1]) * scale).astype(low)
            dq_low, dk_low, dv_low = dq[rows], dk[rows].astype(low), dv[rows].astype(low)
            for n in range(nc):
                columns = slice(n * part, (n + 1) * part)
                at = pl.ds(n * part, part)
                value = nt(dq_low, w_in[0, at]) + nt(dk_low, w_in[1, at]) + nt(dv_low, w_in[2, at])
                fown[:, columns] = value
            x = t_in[rows].astype(f32)
            rate = lax.rsqrt(jnp.mean(x * x, axis=-1, keepdims=True) + epsilon)
            gain_out[...] += jnp.sum(fown[...] * x * rate, axis=0, keepdims=True)
            fsend[b] = fown[...].astype(low)

            @pl.when(me.c == b)
            def _():
                x_out[...] = fown[...]

        for i, grads in enumerate((dq, dk, dv)):
            for n in range(nc):
                at = slice(n * part, (n + 1) * part)
                w_out[i, at] = tn(first_in[:, at], grads[...].astype(low)).astype(low)
        spread.finish()
        for d in range(1, nc):
            do_copy(d).wait_send()

    return pl.pallas_call(
        kernel,
        name="attend_backward",
        cost_estimate=pl.CostEstimate(flops=50 * 10**9, bytes_accessed=10**7, transcendentals=0),
        out_shape=(
            jax.ShapeDtypeStruct((count, width), f32),
            jax.ShapeDtypeStruct((nc, count, width), low),
            jax.ShapeDtypeStruct((3 + nc, width, part), low),
            jax.ShapeDtypeStruct((1, width), f32),
            jax.ShapeDtypeStruct((heads, CHUNK, band), f32),
            jax.ShapeDtypeStruct((heads, 8, 128), f32),
            jax.ShapeDtypeStruct((nc - 1,) + exchange, low),
        ),
        in_specs=[pl.BlockSpec(memory_space=VMEM)] * 14,
        out_specs=[pl.BlockSpec(memory_space=VMEM)] * 6 + [pl.BlockSpec(memory_space=ANY)],
        scratch_shapes=[
            VMEM((count, length), f32),
            VMEM((heads, count, band), f32),
            VMEM((nc, count, part), low),
            VMEM((nc, count, part), low),
            VMEM((length, part), low),
            VMEM((length, part), f32),
            VMEM((length, part), f32),
            VMEM((count, width), f32),
            VMEM((4,) + exchange, low),
            SEM.DMA((nc,)),
            SEM.DMA((nc,)),
            SEM.DMA((nc - 1, ns)),
            SEM.DMA((nc - 1, ns)),
        ],
        compiler_params=pltpu.CompilerParams(
            collective_id=4, has_side_effects=True, vmem_limit_bytes=61 * 1024 * 1024
        ),
    )(dattn, o_all, tokens, first, q_all, k_all, v_all, lse, weights, query_code, key_code, slopes,
      weighted, cotangents)


def activation(gate_values, up_values):
    return jax.nn.gelu(gate_values) * up_values


def gelu_parts(x):
    c, a = math.sqrt(2.0 / math.pi), 0.044715
    square = x * x
    t = jnp.tanh(c * x * (1.0 + a * square))
    half = 0.5 * (1.0 + t)
    return x * half, half + (0.5 * c) * x * (1.0 - t * t) * (1.0 + (3.0 * a) * square)


class Chain:
    def __init__(self, me, pairs, send, recv):
        self.me, self.pairs, self.send, self.recv, self.nc = me, pairs, send, recv, me.nc

    def copies(self, direction, hop, landing):
        me, nc = self.me, self.nc
        lane = 0 if direction > 0 else 1
        origin = lax.rem(me.c - direction * (hop + 1 if landing else hop) + 2 * nc, nc)
        result = []
        for i, (own, every) in enumerate(self.pairs):
            target = every.at[origin]
            source = own if hop == 0 and not landing else target
            result.append(
                remote(
                    source, target, self.send.at[lane, hop, i], self.recv.at[lane, hop, i],
                    me.along(direction),
                )
            )
        return result

    def sends(self, direction, hop):
        c, nc = self.me.c, self.nc
        if direction > 0:
            return (c >= hop) & (c < nc - 1)
        return (c <= nc - 1 - hop) & (c > 0)

    def lands(self, direction, hop):
        c, nc = self.me.c, self.nc
        if direction > 0:
            return c >= hop + 1
        return c <= nc - 2 - hop

    def start(self, hop):
        if hop >= self.nc:
            return
        for direction in (1, -1):
            if hop:

                @pl.when(self.lands(direction, hop - 1))
                def _():
                    for copy in self.copies(direction, hop - 1, True):
                        copy.wait_recv()

            if hop < self.nc - 1:

                @pl.when(self.sends(direction, hop))
                def _():
                    for copy in self.copies(direction, hop, False):
                        copy.start()

    def finish(self):
        for direction in (1, -1):
            for hop in range(self.nc - 1):

                @pl.when(self.sends(direction, hop))
                def _():
                    for copy in self.copies(direction, hop, False):
                        copy.wait_send()


def greet_experts(me):
    barrier = pltpu.get_barrier_semaphore()
    partners = [(me.c, me.s ^ m) for m in range(1, me.ns)] + [me.along(1), me.along(-1)]
    for partner in partners:
        pl.semaphore_signal(barrier, inc=1, device_id=partner, device_id_type=MESH)
    pl.semaphore_wait(barrier, len(partners))


TILE = 256


class Spread:
    def __init__(self, me, jobs, send, send_sem, recv_sem):
        self.me, self.jobs, self.send = me, jobs, send
        self.send_sem, self.recv_sem = send_sem, recv_sem
        self.order = list(range(2, me.ns)) + [1]
        self.turns = send.shape[0]

    def copy(self, i, m):
        return remote(
            self.send.at[i % self.turns, m], self.jobs[i][2].at[m],
            self.send_sem.at[i, m], self.recv_sem.at[i, m], (self.me.c, self.me.s ^ m),
        )

    def own(self, i):
        return pltpu.make_async_copy(
            self.send.at[i % self.turns, 0], self.jobs[i][2].at[0], self.send_sem.at[i, 0]
        )

    def left(self, i):
        for m in self.order:
            self.copy(i, m).wait_send()
        self.own(i).wait()

    def start(self, i):
        if i >= self.turns:
            self.left(i - self.turns)
        picks, tokens = self.jobs[i][:2]
        for m in self.order + [0]:
            self.send[i % self.turns, m] = dot32(picks[m], tokens[...]).astype(self.send.dtype)
            if m:
                self.copy(i, m).start()
            else:
                self.own(i).start()

    def landed(self, i):
        for m in self.order:
            self.copy(i, m).wait_recv()
        if i >= len(self.jobs) - self.turns:
            self.left(i)

    def finish(self):
        for i in range(len(self.jobs)):
            self.landed(i)


def row_groups(ns):
    return [(2, 6), (6, ns), (0, 2)]


def moe_forward(pick, pick_next, tokens, gates, gate_w, up_w, down_w, nc, ns):
    cap, count = pick.shape[1:]
    width, hidden = gate_w.shape
    low, f32 = jnp.bfloat16, jnp.float32
    groups = row_groups(ns)
    most = max(end - start for start, end in groups) * cap

    def kernel(p_in, n_in, t_in, s_in, g_hbm, u_hbm, d_hbm, r_out, y_out, t_all, s_all, n_out, kg_out, ku_out,
               wg, wu, wd, send, yield_, nsend, inner, keep_g, keep_u, ks, ws, ss, rs, ys, yr, ts, tr, ls, ns_, nr):
        me = Place(nc, ns)
        loads = [
            pltpu.make_async_copy(source, target, ws.at[i])
            for i, (source, target) in enumerate(((g_hbm, wg), (u_hbm, wu), (d_hbm, wd)))
        ]
        for load in loads:
            load.start()
        keep = [
            pltpu.make_async_copy(t_in, t_all.at[me.c], ls.at[0]),
            pltpu.make_async_copy(s_in, s_all.at[me.c], ls.at[1]),
        ]
        for copy in keep:
            copy.start()
        greet_experts(me)

        def there(m):
            return (me.c, me.s ^ m)

        def out_copy(m):
            return remote(send.at[m], r_out.at[m], ss.at[m], rs.at[m], there(m))

        def back_copy(m):
            return remote(yield_.at[m], y_out.at[m], ys.at[m], yr.at[m], there(m))

        for m in list(range(2, 6)) + [1]:
            send[m] = dot32(p_in[m], t_in[...]).astype(low)
            out_copy(m).start()
        chain = Chain(me, ((t_in, t_all), (s_in, s_all)), ts, tr)
        chain.start(0)
        r_out[0] = dot32(p_in[0], t_in[...]).astype(low)
        for m in range(6, ns):
            send[m] = dot32(p_in[m], t_in[...]).astype(low)
        for load in loads:
            load.wait()
        for turn, (begin, end) in enumerate(groups):
            size = (end - begin) * cap
            here = pl.ds(begin * cap, size)
            for m in range(begin, end):
                if m:
                    out_copy(m).wait_recv()
            if turn == 0:
                for m in range(6, ns):
                    out_copy(m).start()

            def up(n, carry):
                rows = r_out[begin:end].reshape(size, width)
                at = pl.ds(pl.multiple_of(n * TILE, TILE), TILE)
                value, slope = gelu_parts(dot32(rows, wg[:, at]))
                linear = dot32(rows, wu[:, at])
                inner[:size, at] = (value * linear).astype(low)
                keep_g[here, at] = (slope * linear).astype(low)
                keep_u[here, at] = value.astype(low)
                return carry

            lax.fori_loop(0, hidden // TILE, up, 0)
            for i, (kept, target) in enumerate(((keep_g, kg_out), (keep_u, ku_out))):
                copy = pltpu.make_async_copy(kept.at[here], target.at[here], ks.at[turn, i])
                copy.start()
                keep.append(copy)
            chain.start(turn + 1)
            if turn == 0:
                spread = Spread(me, [(n_in, t_all.at[me.c ^ 1], n_out)], nsend, ns_, nr)
                spread.start(0)

            def down(n, carry):
                at = pl.ds(pl.multiple_of(n * TILE, TILE), TILE)
                value = dot32(inner[:size], wd[:, at]).astype(low)
                yield_[begin:end, :, at] = value.reshape(end - begin, cap, TILE)
                return carry

            lax.fori_loop(0, width // TILE, down, 0)
            for m in range(begin, end):
                if m:
                    back_copy(m).start()
        y_out[0] = yield_[0]
        for hop in range(len(groups) + 1, nc):
            chain.start(hop)
        for m in range(1, ns):
            back_copy(m).wait_recv()
        for copy in keep:
            copy.wait()
        for m in range(1, ns):
            out_copy(m).wait_send()
            back_copy(m).wait_send()
        spread.finish()
        chain.finish()

    exchange = (ns, cap, width)
    return pl.pallas_call(
        kernel,
        name="moe_forward",
        cost_estimate=pl.CostEstimate(flops=45 * 10**9, bytes_accessed=10**7, transcendentals=0),
        out_shape=(
            jax.ShapeDtypeStruct(exchange, low),
            jax.ShapeDtypeStruct(exchange, low),
            jax.ShapeDtypeStruct((nc,) + tokens.shape, low),
            jax.ShapeDtypeStruct((nc,) + gates.shape, f32),
            jax.ShapeDtypeStruct(exchange, low),
            jax.ShapeDtypeStruct((ns * cap, hidden), low),
            jax.ShapeDtypeStruct((ns * cap, hidden), low),
        ),
        in_specs=[pl.BlockSpec(memory_space=VMEM)] * 4 + [pl.BlockSpec(memory_space=ANY)] * 3,
        out_specs=[pl.BlockSpec(memory_space=VMEM)] * 4 + [pl.BlockSpec(memory_space=ANY)] * 3,
        scratch_shapes=[
            VMEM((width, hidden), low),
            VMEM((width, hidden), low),
            VMEM((hidden, width), low),
            VMEM(exchange, low),
            VMEM(exchange, low),
            VMEM((1,) + exchange, low),
            VMEM((most, hidden), low),
            VMEM((ns * cap, hidden), low),
            VMEM((ns * cap, hidden), low),
            SEM.DMA((3, 2)),
            SEM.DMA((3,)),
            SEM.DMA((ns,)),
            SEM.DMA((ns,)),
            SEM.DMA((ns,)),
            SEM.DMA((ns,)),
            SEM.DMA((2, nc, 2)),
            SEM.DMA((2, nc, 2)),
            SEM.DMA((2,)),
            SEM.DMA((1, ns)),
            SEM.DMA((1, ns)),
        ],
        compiler_params=pltpu.CompilerParams(
            collective_id=5, has_side_effects=True, vmem_limit_bytes=56 * 1024 * 1024
        ),
    )(pick, pick_next, tokens, gates, gate_w, up_w, down_w)


def combine(returned, pick_first, pick_second, gates, residual, teacher, valid, ratio):
    rows, width = returned.shape
    count = residual.shape[0]
    low, f32 = jnp.bfloat16, jnp.float32

    def kernel(r_in, p1, p2, s_in, x_in, t_in, v_in, k_in, y_out, g_out, gl_out, b_out, d_out, q_out):
        first, second = s_in[:, 0:1], s_in[:, 1:2]
        pulls = [jnp.zeros((count, 1), f32)] * 2
        squares = jnp.zeros((8, 128), f32)
        for n in range(0, width, TILE):
            at = slice(n, n + TILE)
            one, two = tn(p1[...], r_in[:, at]), tn(p2[...], r_in[:, at])
            value = x_in[:, at] + first * one + second * two
            y_out[:, at] = value.astype(low)
            off = value - t_in[:, at].astype(f32)
            kept = v_in[...] * off
            square = jnp.sum((kept * off).reshape(count // 8, 8, TILE), axis=0)
            for left in range(0, TILE, 128):
                squares = squares + square[:, left : left + 128]
            pull = k_in[...] * kept
            g_out[:, at] = pull
            gl_out[:, at] = pull.astype(low)
            pulls = [
                total + jnp.sum(pull * part, axis=1, keepdims=True)
                for total, part in zip(pulls, (one, two))
            ]
            back = dot32(p1[...], (first * pull).astype(low)) + dot32(p2[...], (second * pull).astype(low))
            b_out[:, at] = back.astype(low)
        d_out[:, 0:1] = pulls[0]
        d_out[:, 1:2] = pulls[1]
        q_out[...] = squares

    return pl.pallas_call(
        kernel,
        name="combine",
        out_shape=(
            jax.ShapeDtypeStruct((count, width), low),
            jax.ShapeDtypeStruct((count, width), f32),
            jax.ShapeDtypeStruct((count, width), low),
            jax.ShapeDtypeStruct((rows, width), low),
            jax.ShapeDtypeStruct((count, 2), f32),
            jax.ShapeDtypeStruct((8, 128), f32),
        ),
        in_specs=[pl.BlockSpec(memory_space=VMEM)] * 8,
        out_specs=[pl.BlockSpec(memory_space=VMEM)] * 6,
        compiler_params=pltpu.CompilerParams(vmem_limit_bytes=48 * 1024 * 1024),
    )(returned, pick_first, pick_second, gates, residual, teacher, valid, ratio)


def moe_backward(grads, kept_g, kept_u, cotangents, pick_next, tokens, gate_w, up_w, down_w, nc, ns):
    cap = grads.shape[1]
    width, hidden = gate_w.shape
    low, f32 = jnp.bfloat16, jnp.float32
    groups = row_groups(ns)
    most = max(end - start for start, end in groups) * cap
    more = pick_next.shape[0]

    def kernel(g_in, t_in, n_in, f_in, g_hbm, u_hbm, d_hbm, kg_hbm, ku_hbm, g_out, x_out, t_all, n_out,
               wg, wu, wd, yield_, nsend, slope_g, slope_u, dg, du, ws, ss, rs, ys, yr, ts, tr, ls, ns_, nr):
        me = Place(nc, ns)
        loads = [
            pltpu.make_async_copy(source, target, ws.at[i])
            for i, (source, target) in enumerate(
                ((d_hbm, wd), (kg_hbm, slope_g), (ku_hbm, slope_u), (g_hbm, wg), (u_hbm, wu))
            )
        ]
        for load in loads:
            load.start()
        keep = pltpu.make_async_copy(t_in, t_all.at[me.c], ls.at[0])
        keep.start()
        greet_experts(me)

        def there(m):
            return (me.c, me.s ^ m)

        def out_copy(m):
            return remote(g_in.at[m], g_out.at[m], ss.at[m], rs.at[m], there(m))

        def back_copy(m):
            return remote(yield_.at[m], x_out.at[m], ys.at[m], yr.at[m], there(m))

        for m in list(range(2, 6)) + [1]:
            out_copy(m).start()
        chain = Chain(me, ((t_in, t_all),), ts, tr)
        chain.start(0)
        g_out[0] = g_in[0]
        for load in loads:
            load.wait()

        jobs = [(n_in.at[i], f_in.at[me.c ^ (i + 2)], n_out.at[i]) for i in range(more)]
        spread = Spread(me, jobs, nsend, ns_, nr)
        for turn, (begin, end) in enumerate(groups):
            size = (end - begin) * cap
            for m in range(begin, end):
                if m:
                    out_copy(m).wait_recv()
            if turn == 0:
                for m in range(6, ns):
                    out_copy(m).start()
            here = slice(begin * cap, end * cap)

            def up(n, carry):
                taken = g_out[begin:end].reshape(size, width)
                at = pl.ds(pl.multiple_of(n * TILE, TILE), TILE)
                value = nt(taken, wd[at])
                dg[:size, at] = (value * slope_g[here, at].astype(f32)).astype(low)
                du[:size, at] = (value * slope_u[here, at].astype(f32)).astype(low)
                return carry

            lax.fori_loop(0, hidden // TILE, up, 0)
            chain.start(turn + 1)
            if turn == 0:
                for i in range(more):
                    spread.start(i)

            def down(n, carry):
                at = pl.ds(pl.multiple_of(n * TILE, TILE), TILE)
                value = nt(dg[:size], wg[at]) + nt(du[:size], wu[at])
                yield_[begin:end, :, at] = value.astype(low).reshape(end - begin, cap, TILE)
                return carry

            lax.fori_loop(0, width // TILE, down, 0)
            for m in range(begin, end):
                if m:
                    back_copy(m).start()
        x_out[0] = yield_[0]
        for hop in range(len(groups) + 1, nc):
            chain.start(hop)
        for m in range(1, ns):
            back_copy(m).wait_recv()
        keep.wait()
        for m in range(1, ns):
            out_copy(m).wait_send()
            back_copy(m).wait_send()
        spread.finish()
        chain.finish()

    exchange = (ns, cap, width)
    return pl.pallas_call(
        kernel,
        name="moe_backward",
        cost_estimate=pl.CostEstimate(flops=45 * 10**9, bytes_accessed=10**7, transcendentals=0),
        out_shape=(
            jax.ShapeDtypeStruct(exchange, low),
            jax.ShapeDtypeStruct(exchange, low),
            jax.ShapeDtypeStruct((nc,) + cotangents.shape, low),
            jax.ShapeDtypeStruct((more,) + exchange, low),
        ),
        in_specs=[pl.BlockSpec(memory_space=VMEM)] * 4 + [pl.BlockSpec(memory_space=ANY)] * 5,
        out_specs=[pl.BlockSpec(memory_space=VMEM)] * 2 + [pl.BlockSpec(memory_space=ANY)] * 2,
        scratch_shapes=[
            VMEM((width, hidden), low),
            VMEM((width, hidden), low),
            VMEM((hidden, width), low),
            VMEM(exchange, low),
            VMEM((1,) + exchange, low),
            VMEM((ns * cap, hidden), low),
            VMEM((ns * cap, hidden), low),
            VMEM((most, hidden), low),
            VMEM((most, hidden), low),
            SEM.DMA((5,)),
            SEM.DMA((ns,)),
            SEM.DMA((ns,)),
            SEM.DMA((ns,)),
            SEM.DMA((ns,)),
            SEM.DMA((2, nc, 1)),
            SEM.DMA((2, nc, 1)),
            SEM.DMA((1,)),
            SEM.DMA((more, ns)),
            SEM.DMA((more, ns)),
        ],
        compiler_params=pltpu.CompilerParams(
            collective_id=6, has_side_effects=True, vmem_limit_bytes=60 * 1024 * 1024
        ),
    )(grads, cotangents, pick_next, tokens, gate_w, up_w, down_w, kept_g, kept_u)


def slice_plan(hidden, nc):
    exact, tiles = hidden // nc, hidden // 128
    wide = max(-(-((c + 1) * exact) // 128) - (c * exact) // 128 for c in range(nc))
    return [min((c * exact) // 128, tiles - wide) * 128 for c in range(nc)], wide * 128


def finish_all(
    grads, small, squares, terms, own_terms, dh, inputs, gain, picks, normed, rows, row_grads, gate_w, up_w, down_w, nc, ns, kept
):
    nj = ns // 2
    parts, piece, width = grads.shape[0], grads.shape[4], grads.shape[5]
    low, f32 = jnp.bfloat16, jnp.float32
    tile = squares.shape
    features, hidden = gate_w.shape
    band, half, exact = features // nc, hidden // 2, hidden // nc
    wide = slice_plan(half, nc // 2)[1]
    more = picks.shape[0]
    exchange = picks.shape[1:3] + (features,)
    row_at = [(i, n) for i, x in enumerate(rows) for n in range(x.shape[0])]
    row_at = row_at + [(None, n) for n in range(more)]
    grad_at = [(len(rows) + i, n) for i, x in enumerate(row_grads) for n in range(x.shape[0])]
    count, block = len(rows) + len(row_grads), rows[0].shape[1]
    blocks = len(row_at)
    positions = own_terms.shape[0]
    rest = half - wide
    widths = [wide] + ([rest - 128, 128] if nc == 4 else [128] * (rest // 128))

    def kernel(g_in, e_in, q_in, f_in, fo_in, dh_in, t_in, gain_in, p_in, n_in, *refs):
        (g_hbm, u_hbm, d_hbm, k0_out, k1_out, k2_out, k3_out, e_out, q_out, wg_out, wu_out, wd_out, x_out, n_out,
         gt, et, gc, ec, gx, ex, gz, ez, g_sum, qz, qx, qc, qa, qb,
         cs, cr, xs, xr, zs, zr, q1s, q1r, q2s, q2r, q3s, q3r,
         xb, yb, wg, wu, wd, inner, dg, du, ag, au, ad, pair_send, down_send, ws, rs, ps, pr, ds, dr,
         fland, fs, fr, nsend, ns_, nr) = refs[count:]
        me = Place(nc, ns)
        k_out = (k0_out, k1_out, k2_out, k3_out)
        high, lower = me.c // 2, me.c % 2
        begin = pl.multiple_of(lower * half, 128)
        place = lower * (nc // 2) + high
        source = (me.c % (nc // 2)) * 2 + me.c // (nc // 2)
        offset = high * exact
        cut = pl.multiple_of(jnp.minimum(offset // 128, (half - wide) // 128) * 128, 128)
        begins = [cut] + [lax.rem(cut + sum(widths[:n]), half) for n in range(1, len(widths))]

        def fetch(i):
            (a, n), (b, k) = row_at[i % blocks], grad_at[i % blocks]
            if a is None:
                return [
                    pltpu.make_async_copy(
                        n_out.at[n, m], xb.at[i % 2, pl.ds(m * cap, cap)], rs.at[i % 2, 2 + m]
                    )
                    for m in range(ns)
                ] + [pltpu.make_async_copy(refs[b].at[k], yb.at[i % 2], rs.at[i % 2, 1])]
            return [
                pltpu.make_async_copy(refs[a].at[n], xb.at[i % 2], rs.at[i % 2, 0]),
                pltpu.make_async_copy(refs[b].at[k], yb.at[i % 2], rs.at[i % 2, 1]),
            ]

        loads = fetch(0) + [
            pltpu.make_async_copy(g_hbm.at[:, pl.ds(begin, half)], wg, ws.at[0]),
            pltpu.make_async_copy(u_hbm.at[:, pl.ds(begin, half)], wu, ws.at[1]),
            pltpu.make_async_copy(d_hbm.at[pl.ds(begin, half)], wd, ws.at[2]),
        ]
        for load in loads:
            load.start()
        barrier = pltpu.get_barrier_semaphore()
        partners = [me.along(d) for d in range(1, nc)] + [(me.c, me.s ^ m) for m in range(1, ns)]
        for partner in partners:
            pl.semaphore_signal(barrier, inc=1, device_id=partner, device_id_type=MESH)
        pl.semaphore_wait(barrier, len(partners))

        def pass_terms(step):
            for side, direction in enumerate((-1, 1)):
                here = me.c if direction < 0 else nc - 1 - me.c
                ahead = step - (nc - 1 - here)
                number = ahead if direction < 0 else nc - 1 - ahead
                sends = (ahead >= 0) & (ahead < here)

                @pl.when(sends & (here < nc - 1))
                def _():
                    term_copy(side, direction, number, True).wait_recv()
                    for i in range(0, positions, 64):
                        at = pl.ds(i, 64)
                        fland[number, at] = (
                            fland[number, at].astype(f32) + f_in[number, at].astype(f32)
                        ).astype(low)

                @pl.when(sends & (here == nc - 1))
                def _():
                    fland[number] = f_in[number]

                @pl.when(sends)
                def _():
                    term_copy(side, direction, number, False).start()

        def term_copy(side, direction, number, landing):
            target = me.c if landing else lax.rem(me.c + direction + nc, nc)
            place = jnp.where(number == target, nc, number) if direction > 0 else number
            source = place if landing else number
            return remote(
                fland.at[source], fland.at[place], fs.at[side, number], fr.at[side, number],
                (lax.rem(me.c + direction + nc, nc), me.s),
            )

        def end_terms():
            x_out[...] = fo_in[...]
            for side, direction in enumerate((-1, 1)):
                here = me.c if direction < 0 else nc - 1 - me.c

                @pl.when(here < nc - 1)
                def _():
                    term_copy(side, direction, me.c, True).wait_recv()
                    x_out[...] += fland[nc if direction > 0 else me.c].astype(f32)

            x = t_in[...].astype(f32)
            rate = lax.rsqrt(jnp.mean(x * x, axis=-1, keepdims=True) + epsilon)
            scaled = x_out[...] * gain_in[...]
            pull = jnp.mean(scaled * x, axis=-1, keepdims=True)
            x_out[...] = dh_in[...] + rate * scaled - x * (rate * rate * rate * pull)

        def sent_terms():
            for side, direction in enumerate((-1, 1)):
                here = me.c if direction < 0 else nc - 1 - me.c
                for ahead in range(nc - 1):

                    @pl.when(ahead < here)
                    def _():
                        number = ahead if direction < 0 else nc - 1 - ahead
                        term_copy(side, direction, number, False).wait_send()

        cap = exchange[1]
        jobs = [(p_in.at[i], n_in.at[me.c ^ (nc - more + i)], n_out.at[i]) for i in range(more)]
        spread = Spread(me, jobs, nsend, ns_, nr)
        pass_terms(0)
        for i in range(more):
            spread.start(i)

        def both(pairs, send, recv, device):
            return [
                remote(one, target, send.at[i], recv.at[i], device)
                for i, (one, target) in enumerate(pairs)
            ]

        def core_copy(d):
            row = lax.rem(me.c + d, nc)
            other = 1 - me.core
            return both(
                ((g_in.at[:, row, :, other], gc.at[d]), (e_in.at[row, :, other], ec.at[d])),
                cs.at[d], cr.at[d], me.twin(),
            )

        def cross_copy(d, k):
            return both(
                ((gt.at[d, :, me.j ^ k], gx.at[d, k - 1]), (et.at[d, me.j ^ k], ex.at[d, k - 1])),
                xs.at[d, k], xr.at[d, k], me.across(k),
            )

        def along_copy(d):
            return both(
                ((gt.at[d, :, me.j], gz.at[d - 1]), (et.at[d, me.j], ez.at[d - 1])),
                zs.at[d], zr.at[d], me.along(d),
            )

        def start(copies):
            for copy in copies:
                copy.start()

        def landed(copies):
            for copy in copies:
                copy.wait_recv()

        def q_along(d):
            return remote(q_in, qz.at[d - 1], q1s.at[d], q1r.at[d], me.along(d))

        def q_across(k):
            return remote(qa, qx.at[k - 1], q2s.at[k], q2r.at[k], me.across(k))

        q_twin = remote(qb, qc, q3s.at[0], q3r.at[0], me.twin())
        order = list(range(1, nc)) + [0]

        def core_stage():
            for d in order:
                landed(core_copy(d))
                row = lax.rem(me.c + d, nc)

                def add_core(i, carry):
                    for k in range(nj):
                        gt[d, i, k] = (
                            g_in[i, row, k, me.core].astype(f32) + gc[d, i, k].astype(f32)
                        ).astype(low)
                    return carry

                lax.fori_loop(0, parts, add_core, 0)
                for k in range(nj):
                    et[d, k] = (
                        e_in[row, k, me.core].astype(f32) + ec[d, k].astype(f32)
                    ).astype(low)
                for k in range(1, nj):
                    start(cross_copy(d, k))
            for d in range(1, nc):
                q_along(d).wait_recv()
            value = q_in[...]
            for d in range(1, nc):
                value = value + qz[d - 1]
            qa[...] = value
            for k in range(1, nj):
                q_across(k).start()

        def cross_stage():
            for d in order:
                for k in range(1, nj):
                    landed(cross_copy(d, k))

                def add_cross(i, carry):
                    value = gt[d, i, me.j].astype(f32)
                    for k in range(1, nj):
                        value = value + gx[d, k - 1, i].astype(f32)
                    if d == 0:
                        g_sum[i] = value
                    else:
                        gt[d, i, me.j] = value.astype(low)
                    return carry

                lax.fori_loop(0, parts, add_cross, 0)
                value = et[d, me.j].astype(f32)
                for k in range(1, nj):
                    value = value + ex[d, k - 1].astype(f32)
                if d:
                    et[d, me.j] = value.astype(low)
                    start(along_copy(d))
                else:
                    e_out[...] = value
            for k in range(1, nj):
                q_across(k).wait_recv()
            value = qa[...]
            for k in range(1, nj):
                value = value + qx[k - 1]
            qb[...] = value
            q_twin.start()

        def along_stage():
            for i in range(kept):
                k_out[i][:, pl.ds(pl.multiple_of(me.c * width, width), width)] = g_sum[i]
            for d in range(1, nc):
                landed(along_copy(d))
                row = lax.rem(me.c - d + nc, nc)
                for i in range(kept):
                    at = pl.ds(pl.multiple_of(row * width, width), width)
                    k_out[i][:, at] = gz[d - 1, i].astype(f32)
                e_out[...] = e_out[...] + ez[d - 1].astype(f32)
            for i in range(kept, parts):
                value = g_sum[i]
                for d in range(1, nc):
                    value = value + gz[d - 1, i].astype(f32)
                k_out[kept][:, (i - kept) * width : (i - kept + 1) * width] = value
            q_twin.wait()
            q_out[...] = qb[...] + qc[...]

        def pair_copy(i, p):
            at = pl.multiple_of(begins[p], 128)
            return remote(
                pair_send.at[i, :, pl.ds(at, widths[p])],
                (wg_out, wu_out)[i].at[:, pl.ds(pl.multiple_of(begin + at, 128), widths[p])],
                ps.at[i, p], pr.at[i, p], (me.c + 1 - 2 * lower, me.s),
            )

        def pair_landing(i, p):
            at = pl.multiple_of(half - begin + begins[p], 128)
            landing = (wg_out, wu_out)[i].at[:, pl.ds(at, widths[p])]
            return remote(landing, landing, ps.at[i, p], pr.at[i, p], me.along(1))

        down_copy = remote(down_send, wd_out, ds.at[0], dr.at[0], (place, me.s))

        def give(i, p, total):
            at = pl.multiple_of(begins[p], 128)
            other = total[pl.ds(pl.multiple_of((1 - lower) * band, band), band), : widths[p]]
            pair_send[i, :, pl.ds(at, widths[p])] = other.astype(low)
            pair_copy(i, p).start()
            own = total[pl.ds(pl.multiple_of(lower * band, band), band), : widths[p]]
            at = pl.multiple_of(begin + at, 128)
            (wg_out, wu_out)[i][:, pl.ds(at, widths[p])] = own.astype(low)

        for d in order:
            start(core_copy(d))
        for d in range(1, nc):
            q_along(d).start()
        for load in loads:
            load.wait()
        steps = [[core_stage], [], [cross_stage], [], [], [], [along_stage]]
        places = [2 * n + 1 for n in range(nc - 2)]
        stages = [
            (steps[n] if n < len(steps) else [])
            + [lambda step=step + 1: pass_terms(step) for step, place_ in enumerate(places) if place_ == n]
            for n in range(max(len(steps), len(places) and places[-1] + 1))
        ]
        last = blocks - 1
        for p, size in enumerate(widths):
            cuts = [(n, min(n + TILE, size)) for n in range(0, size, TILE)]
            for i in range(blocks):
                turn = p * blocks + i
                if turn:
                    for load in fetch(turn):
                        load.wait()
                x, dy = xb.at[turn % 2], yb.at[turn % 2]
                for left, right in cuts:
                    at = pl.ds(pl.multiple_of(begins[p] + left, 128), right - left)
                    value, slope = gelu_parts(dot32(x[...], wg[:, at]))
                    linear = dot32(x[...], wu[:, at])
                    down = nt(dy[...], wd[at])
                    inner[:, left:right] = (value * linear).astype(low)
                    dg[:, left:right] = (down * linear * slope).astype(low)
                    du[:, left:right] = (down * value).astype(low)
                if turn + 1 < blocks * len(widths):
                    if turn + 1 < blocks and row_at[turn + 1][0] is None:
                        spread.landed(row_at[turn + 1][1])
                    for load in fetch(turn + 1):
                        load.start()
                mine = x[:, pl.ds(pl.multiple_of(high * 2 * band, 2 * band), 2 * band)]
                for n, (total, grad) in enumerate(((ag, dg), (au, du))):
                    if i:
                        total[:, :size] += tn(mine, grad[:, :size])
                    else:
                        total[:, :size] = tn(mine, grad[:, :size])
                    if i == last:
                        give(n, p, total)
                if p == 0:
                    if i:
                        ad[...] += tn(inner[...], dy[...])
                    else:
                        ad[...] = tn(inner[...], dy[...])
                    if i == last:
                        at = pl.ds(pl.multiple_of(offset - cut, 16), exact)
                        down_send[...] = ad[at].astype(low)

                        @pl.when(place != me.c)
                        def _():
                            down_copy.start()

                        @pl.when(place == me.c)
                        def _():
                            wd_out[...] = down_send[...]

                if stages and turn + 1 < blocks * len(widths):
                    for stage in stages.pop(0):
                        stage()
        for group in stages:
            for stage in group:
                stage()
        end_terms()
        for i in range(2):
            for p in range(len(widths)):
                pair_landing(i, p).wait_recv()

        @pl.when(source != me.c)
        def _():
            down_copy.wait_recv()

        @pl.when(place != me.c)
        def _():
            down_copy.wait_send()

        for d in order:
            started = core_copy(d) + [copy for k in range(1, nj) for copy in cross_copy(d, k)]
            if d:
                started = started + along_copy(d) + [q_along(d)]
            for copy in started:
                copy.wait_send()
        for k in range(1, nj):
            q_across(k).wait_send()
        for i in range(2):
            for p in range(len(widths)):
                pair_copy(i, p).wait_send()
        sent_terms()

    one, extra = (parts, piece, width), small.shape[3:]
    return pl.pallas_call(
        kernel,
        name="finish_all",
        cost_estimate=pl.CostEstimate(flops=80 * 10**9, bytes_accessed=10**7, transcendentals=0),
        out_shape=(
            *[jax.ShapeDtypeStruct((piece, nc * width), f32)] * 4,
            jax.ShapeDtypeStruct(extra, f32),
            jax.ShapeDtypeStruct(tile, f32),
            jax.ShapeDtypeStruct((band, hidden), low),
            jax.ShapeDtypeStruct((band, hidden), low),
            jax.ShapeDtypeStruct((exact, features), low),
            jax.ShapeDtypeStruct(own_terms.shape, f32),
            jax.ShapeDtypeStruct((more,) + exchange, low),
        ),
        in_specs=[pl.BlockSpec(memory_space=VMEM)] * 10 + [pl.BlockSpec(memory_space=ANY)] * (count + 3),
        out_specs=[pl.BlockSpec(memory_space=VMEM)] * 10 + [pl.BlockSpec(memory_space=ANY)],
        scratch_shapes=[
            VMEM((nc, parts, nj, piece, width), low),
            VMEM((nc, nj) + extra, low),
            VMEM((nc, parts, nj, piece, width), low),
            VMEM((nc, nj) + extra, low),
            VMEM((nc, nj - 1) + one, low),
            VMEM((nc, nj - 1) + extra, low),
            VMEM((nc - 1,) + one, low),
            VMEM((nc - 1,) + extra, low),
            VMEM(one, f32),
            VMEM((nc - 1,) + tile, f32),
            VMEM((nj - 1,) + tile, f32),
            VMEM(tile, f32),
            VMEM(tile, f32),
            VMEM(tile, f32),
            SEM.DMA((nc, 2)),
            SEM.DMA((nc, 2)),
            SEM.DMA((nc, nj, 2)),
            SEM.DMA((nc, nj, 2)),
            SEM.DMA((nc, 2)),
            SEM.DMA((nc, 2)),
            SEM.DMA((nc,)),
            SEM.DMA((nc,)),
            SEM.DMA((nj,)),
            SEM.DMA((nj,)),
            SEM.DMA((1,)),
            SEM.DMA((1,)),
            VMEM((2, block, features), low),
            VMEM((2, block, features), low),
            VMEM((features, half), low),
            VMEM((features, half), low),
            VMEM((half, features), low),
            VMEM((block, wide), low),
            VMEM((block, wide), low),
            VMEM((block, wide), low),
            VMEM((2 * band, wide), f32),
            VMEM((2 * band, wide), f32),
            VMEM((wide, features), f32),
            VMEM((2, band, half), low),
            VMEM((exact, features), low),
            SEM.DMA((3,)),
            SEM.DMA((2, 2 + ns)),
            SEM.DMA((2, len(widths))),
            SEM.DMA((2, len(widths))),
            SEM.DMA((1,)),
            SEM.DMA((1,)),
            VMEM((nc + 1,) + own_terms.shape, low),
            SEM.DMA((2, nc)),
            SEM.DMA((2, nc)),
            VMEM((1,) + exchange, low),
            SEM.DMA((more, ns)),
            SEM.DMA((more, ns)),
        ],
        compiler_params=pltpu.CompilerParams(
            collective_id=2, has_side_effects=True, vmem_limit_bytes=60 * 1024 * 1024
        ),
    )(grads, small, squares, terms, own_terms, dh, inputs, gain, picks, normed, *rows, *row_grads, gate_w, up_w, down_w)


def per_device(
    tokens,
    segments,
    valid,
    routes,
    teacher,
    norm_attn,
    w_query,
    w_key,
    w_value,
    output_weight,
    rel_bias,
    norm_ffn,
    w_router,
    w_gate,
    w_up,
    w_down,
):
    nc = lax.axis_size("ctx")
    ns = lax.axis_size("shard")
    c, s = lax.axis_index("ctx"), lax.axis_index("shard")
    n_dev, nj = nc * ns, ns // 2
    row_count, width = tokens.shape[1:]
    top_count = routes.shape[2]
    experts = w_router.shape[1]
    capacity = (5 * row_count * top_count + 4 * experts - 1) // (4 * experts)
    length = row_count * nc
    low = jnp.bfloat16
    f32 = jnp.float32
    piece = w_query.shape[0]
    band = 2 * row_count

    route_local = routes[0]
    expert_ids = jnp.arange(experts, dtype=jnp.int32)
    route_hot = route_local[:, :, None] == expert_ids[None, None, :]
    flat_routes = route_local.reshape(row_count * top_count)
    route_hits = (flat_routes[:, None] == expert_ids[None, :]).astype(jnp.int32)
    before = jnp.cumsum(route_hits, axis=0) - route_hits
    slot_rank = jnp.sum(before * route_hits, axis=1).reshape(row_count, top_count)

    part = width // nc
    smalls = (
        norm_attn, norm_ffn, rel_bias, w_router.reshape(-1), segments[0].astype(low), valid[0].astype(low),
        route_local.astype(low).T.reshape(-1), slot_rank.astype(low).T.reshape(-1),
    )
    sizes = [x.shape[0] for x in smalls]
    starts = [sum(sizes[:i]) for i in range(len(sizes))]
    extra = jnp.concatenate(smalls + (jnp.zeros((EXTRA * part - sum(sizes),), low),))
    shares = [w.reshape(piece, nc, part).transpose(1, 0, 2) for w in (w_query, w_key, w_value, output_weight)]
    shares = jnp.concatenate(
        [x[:, None] for x in shares[:3]] + [jnp.broadcast_to(shares[3][None], (nc, nc, piece, part))], axis=1
    )
    weights, extras, tokens_all = gather_all(
        shares, extra.reshape(EXTRA, part), tokens[0], nc, ns
    )
    extras = extras.reshape(nc, ns, EXTRA * part)
    gain_attn, gain_ffn, full_bias, full_router = (
        extras[:, :, begin : begin + size].reshape(-1)
        for begin, size in zip(starts[:4], sizes[:4])
    )
    full_router = full_router.reshape(width, experts)
    table = full_bias.reshape(BUCKETS, HEADS).astype(f32)
    line = lax.dynamic_slice_in_dim(extras, s, 1, 1)[:, 0]
    line_seg = line[:, starts[4] : starts[4] + row_count].reshape(length).astype(jnp.int32)
    line_valid = line[:, starts[5] : starts[5] + row_count].reshape(length) > 0
    key_code = jnp.where(line_valid, line_seg, -1)[None]
    query_code = line_seg[:, None]
    valid_count = jnp.sum(extras[:, :, starts[5] : starts[5] + row_count].astype(f32))

    spot = (jnp.arange(band)[None, :] - jnp.arange(CHUNK)[:, None]) % band
    distance = jnp.where(spot <= row_count, row_count - spot, 3 * row_count - spot)
    level = bucket_of(distance, BUCKETS)
    level_hot = (level[:, :, None] == jnp.arange(BUCKETS)[None, None, :]).astype(f32)
    heads = HEADS // nc
    own_table = lax.dynamic_slice_in_dim(table, c * heads, heads, 1)
    slopes = jnp.einsum(
        "ixb,bh->hix", level_hot, own_table - own_table[BUCKETS - 1 :], precision=highest_precision
    )

    gain_one, gain_two = gain_attn.astype(f32), gain_ffn.astype(f32)
    first_all, queries, keys, values, mixed, log_total, residual, ffn_low = attend_forward(
        tokens_all, weights, gain_one[None], gain_two[None], query_code, key_code, slopes, nc, ns
    )
    ffn_in = ffn_low.astype(f32)
    router = full_router.astype(f32)
    logits = jnp.dot(ffn_in, router, precision=highest_precision)
    picked = jnp.sum(jnp.where(route_hot, logits[:, None, :], 0.0), axis=-1)
    gate_probs = jax.nn.softmax(picked, axis=-1)

    slots = -(-capacity // 16) * 16
    target = (route_local ^ s) * slots + slot_rank
    slot_ids = jnp.arange(experts * slots, dtype=jnp.int32)
    pick_first = (slot_ids[:, None] == target[None, :, 0]).astype(low)
    pick_second = (slot_ids[:, None] == target[None, :, 1]).astype(low)
    pick_both = pick_first + pick_second
    gate_w, up_w, down_w = w_gate[0], w_up[0], w_down[0]
    gate_rows = jnp.concatenate((gate_probs.T, jnp.zeros((8 - top_count, row_count), f32)), axis=0)
    other_line = line[c ^ jnp.arange(1, nc)]
    other_routes, other_slots = (
        other_line[:, starts[i] : starts[i] + top_count * row_count]
        .astype(jnp.int32)
        .reshape(nc - 1, top_count, row_count)
        for i in (6, 7)
    )
    other_target = (other_routes ^ s) * slots + other_slots
    other_first, other_second = (
        slot_ids[None, :, None] == other_target[:, m, None, :] for m in range(2)
    )
    other_picks = (other_first | other_second).astype(low).reshape(nc - 1, experts, slots, row_count)
    expert_rows, returned, ffn_all, gates_all, rows_next, kept_g, kept_u = moe_forward(
        pick_both.reshape(experts, slots, row_count), other_picks[0], ffn_low, gate_rows,
        gate_w, up_w, down_w, nc, ns,
    )
    everything = float(row_count * nc * ns)
    output, cotangent, cotangent_low, back_send, gate_grad, squares = combine(
        returned.reshape(experts * slots, width), pick_first, pick_second, gate_probs, residual, teacher[0],
        valid[0].astype(f32)[:, None], (everything / valid_count).reshape(1, 1),
    )
    other_gates = gates_all[c ^ jnp.arange(1, nc)].astype(low)
    other_weighted = (
        jnp.where(other_first, other_gates[:, 0, None, :], low(0))
        + jnp.where(other_second, other_gates[:, 1, None, :], low(0))
    ).reshape(other_picks.shape)
    out_grad, sent_back, cotangent_all, rows_later = moe_backward(
        back_send.reshape(experts, slots, width), kept_g, kept_u, cotangent_low,
        other_picks[1 : nc // 2], ffn_all, gate_w, up_w, down_w, nc, ns,
    )
    ffn_grad = tn(pick_both, sent_back.reshape(experts * slots, width))
    pick_grad = gate_probs * (gate_grad - jnp.sum(gate_probs * gate_grad, axis=-1, keepdims=True))
    logits_grad = jnp.sum(jnp.where(route_hot, pick_grad[:, :, None], 0.0), axis=1)
    router_grad = contract(ffn_in, logits_grad, 0, 0, highest_precision)
    ffn_grad = ffn_grad + contract(logits_grad, router, 1, 1, highest_precision)
    unused, norm_two_back = jax.vjp(rms_norm, residual, gain_two)
    residual_from_norm, gain_two_grad = norm_two_back(ffn_grad)
    residual_grad = cotangent + residual_from_norm
    attn_grad_low = residual_grad.astype(low)
    hidden_own, hidden_terms, w_grads, gain_one_grad, near_sum, far_sum, other_grads = attend_backward(
        attn_grad_low, mixed, tokens_all, first_all, queries, keys, values, log_total, weights,
        query_code, key_code, slopes, other_weighted, cotangent_all, nc, ns,
    )
    own_bias = jnp.einsum("hix,ixb->bh", near_sum, level_hot, precision=highest_precision)
    last_bucket = (jnp.arange(BUCKETS) == BUCKETS - 1).astype(f32)
    own_bias = own_bias + last_bucket[:, None] * jnp.sum(far_sum, axis=(1, 2))[None, :]
    bias_grad = lax.dynamic_update_slice_in_dim(
        jnp.zeros((BUCKETS, HEADS), f32), own_bias, c * heads, 1
    )
    small_grads = jnp.concatenate(
        [
            x.reshape(n_dev, -1).astype(low)
            for x in (gain_one_grad, gain_two_grad, bias_grad, router_grad)
        ],
        axis=1,
    )
    small_grads = jnp.pad(small_grads, ((0, 0), (0, EXTRA * part - small_grads.shape[1])))
    *attn_sums, small_sum, square_sum, gate_w_sum, up_w_sum, down_w_sum, input_grad, unused = finish_all(
        w_grads.reshape(3 + nc, nc, nj, 2, piece, part),
        small_grads.reshape(nc, nj, 2, EXTRA, part),
        squares,
        hidden_terms,
        hidden_own,
        residual_grad,
        tokens[0],
        gain_one[None],
        other_picks[nc // 2 :],
        ffn_all,
        [x.reshape(-1, experts * slots, width) for x in (expert_rows, rows_next, rows_later)],
        [x.reshape(-1, experts * slots, width) for x in (out_grad, other_grads)],
        gate_w,
        up_w,
        down_w,
        nc,
        ns,
        3,
    )
    loss_value = jnp.sum(square_sum) / (2.0 * width * valid_count)
    small_sum = small_sum.reshape(-1)
    tails = [small_sum[begin : begin + size] for begin, size in zip(starts[:4], sizes[:4])]
    return (
        output[None],
        loss_value,
        input_grad[None],
        tails[0],
        attn_sums[0],
        attn_sums[1],
        attn_sums[2],
        attn_sums[3],
        tails[2],
        tails[1],
        tails[3].reshape(w_router.shape),
        gate_w_sum[None].astype(f32),
        up_w_sum[None].astype(f32),
        down_w_sum[None].astype(f32),
    )


def solution(mesh):
    return jax.shard_map(
        per_device,
        mesh=mesh,
        in_specs=(
            P("shard", "ctx", None),
            P("shard", "ctx"),
            P("shard", "ctx"),
            P("shard", "ctx", None),
            P("shard", "ctx", None),
            P(("ctx", "shard")),
            P(("ctx", "shard"), None),
            P(("ctx", "shard"), None),
            P(("ctx", "shard"), None),
            P(("ctx", "shard"), None),
            P(("ctx", "shard")),
            P(("ctx", "shard")),
            P(("ctx", "shard"), None),
            P("shard", None, None),
            P("shard", None, None),
            P("shard", None, None),
        ),
        out_specs=(
            P("shard", "ctx", None),
            P(),
            P("shard", "ctx", None),
            P(("ctx", "shard")),
            P(("ctx", "shard"), None),
            P(("ctx", "shard"), None),
            P(("ctx", "shard"), None),
            P(("ctx", "shard"), None),
            P(("ctx", "shard")),
            P(("ctx", "shard")),
            P(("ctx", "shard"), None),
            P("shard", "ctx", None),
            P("shard", "ctx", None),
            P("shard", "ctx", None),
        ),
        check_vma=False,
    )
```

```python
import math

import jax
import jax.numpy as jnp
from jax import lax
from jax.experimental import pallas as pl
from jax.experimental.pallas import tpu as pltpu
from jax.sharding import PartitionSpec as P

HEADS = 16
HEAD = 64
BUCKETS = 32
MESH = pl.DeviceIdType.MESH
ANY = pl.ANY
VMEM = pltpu.VMEM
SEM = pltpu.SemaphoreType

highest_precision = lax.Precision.HIGHEST
max_distance = 128
epsilon = 1e-06
negative = -1e30
EXTRA = 16


def thresholds(buckets):
    exact_count = buckets // 2
    limits = list(range(1, exact_count))
    for bucket_level in range(exact_count, buckets):
        power = (bucket_level - exact_count) / exact_count
        limits.append(int(math.ceil(exact_count * (max_distance / exact_count) ** power)))
    return limits


def bucket_of(distance, buckets):
    bucket_total = jnp.zeros(distance.shape, jnp.int32)
    for threshold in thresholds(buckets):
        bucket_total = bucket_total + (distance >= threshold).astype(jnp.int32)
    return bucket_total


def rms_norm(values, gain_vector):
    return (
        values
        * lax.rsqrt(jnp.mean(values * values, axis=-1, keepdims=True) + epsilon)
        * gain_vector
    )


def contract(left_side, right_side, left_axis, right_axis, precision_mode=None):
    return lax.dot_general(
        left_side,
        right_side,
        (((left_axis,), (right_axis,)), ((), ())),
        precision=precision_mode,
        preferred_element_type=jnp.float32,
    )


def dot32(left_side, right_side):
    return jnp.dot(left_side, right_side, preferred_element_type=jnp.float32)


def nt(left_side, right_side):
    return contract(left_side, right_side, 1, 1)


def tn(left_side, right_side):
    return contract(left_side, right_side, 0, 0)


class Place:
    def __init__(self, nc, ns):
        self.nc, self.ns, self.nj = nc, ns, ns // 2
        self.c = lax.axis_index("ctx")
        self.s = lax.axis_index("shard")
        self.core = self.s % 2
        self.j = self.s // 2

    def along(self, d):
        return (lax.rem(self.c + d + self.nc, self.nc), self.s)

    def across(self, k):
        return (self.c, self.s ^ (2 * k))

    def twin(self):
        return (self.c, self.s ^ 1)

    def greet(self):
        barrier = pltpu.get_barrier_semaphore()
        partners = (
            [self.along(d) for d in range(1, self.nc)]
            + [self.across(k) for k in range(1, self.nj)]
            + [self.twin()]
        )
        for partner in partners:
            pl.semaphore_signal(barrier, inc=1, device_id=partner, device_id_type=MESH)
        pl.semaphore_wait(barrier, len(partners))


def remote(source, target, send, recv, device):
    return pltpu.make_async_remote_copy(
        src_ref=source,
        dst_ref=target,
        send_sem=send,
        recv_sem=recv,
        device_id=device,
        device_id_type=MESH,
    )


def gather_all(weights, extra, rows, nc, ns):
    n_dev, nj = nc * ns, ns // 2
    share = weights.shape[1:]
    full_shape = (share[0], nc, ns) + share[1:]

    def kernel(w_in, e_in, t_in, w_out, e_out, t_out, local, zs, zr, xs, xr, cs, cr, ts, tr):
        me = Place(nc, ns)

        def views(row, column):
            return (w_out.at[:, row, column], e_out.at[row, column])

        def piece(d, k):
            return views(lax.rem(me.c - d + nc, nc), me.s ^ (2 * k))

        mine = (w_in.at[me.c], e_in)
        locals_ = [
            pltpu.make_async_copy(source, target, local.at[i])
            for i, (source, target) in enumerate(
                zip(mine + (t_in,), views(me.c, me.s) + (t_out.at[me.c],))
            )
        ]
        for copy in locals_:
            copy.start()
        me.greet()
        sent = []

        def push(sources, targets, send, recv, device):
            for i in range(2):
                copy = remote(sources[i], targets[i], send.at[i], recv.at[i], device)
                copy.start()
                sent.append(copy)

        def arrive(targets, send, recv, device):
            for i in range(2):
                remote(targets[i], targets[i], send.at[i], recv.at[i], device).wait_recv()

        def token_copy(direction, hop):
            lane = 0 if direction > 0 else 1
            origin = lax.rem(me.c - direction * hop + nc, nc)
            return remote(
                t_in if hop == 0 else t_out.at[origin],
                t_out.at[origin],
                ts.at[lane, hop],
                tr.at[lane, hop],
                (lax.rem(me.c + direction + nc, nc), me.s),
            )

        def token_landing(direction, hop):
            lane = 0 if direction > 0 else 1
            origin = lax.rem(me.c - direction * (hop + 1) + nc, nc)
            landing = t_out.at[origin]
            return remote(landing, landing, ts.at[lane, hop], tr.at[lane, hop], me.along(1))

        def can_send(direction, hop):
            if direction > 0:
                return (me.c >= hop) & (me.c < nc - 1)
            return (me.c <= nc - 1 - hop) & (me.c > 0)

        def can_receive(direction, hop):
            if direction > 0:
                return me.c >= hop + 1
            return me.c <= nc - 2 - hop

        for d in range(1, nc):
            target = lax.rem(me.c + d, nc)
            push(
                (w_in.at[target], e_in), views(me.c, me.s), zs.at[d], zr.at[d], (target, me.s)
            )
        for direction in (1, -1):

            @pl.when(can_send(direction, 0))
            def _():
                token_copy(direction, 0).start()

        for k in range(1, nj):
            push(mine, views(me.c, me.s), xs.at[0, k], xr.at[0, k], me.across(k))
        push(mine, views(me.c, me.s), cs.at[0, 0], cr.at[0, 0], me.twin())

        for copy in locals_:
            copy.wait()
        for d in range(1, nc):
            here = piece(d, 0)
            arrive(here, zs.at[d], zr.at[d], me.along(-d))
            for k in range(1, nj):
                push(here, here, xs.at[d, k], xr.at[d, k], me.across(k))
            push(here, here, cs.at[d, 0], cr.at[d, 0], me.twin())
        for d in range(nc):
            for k in range(1, nj):
                here = piece(d, k)
                arrive(here, xs.at[d, k], xr.at[d, k], me.across(k))
                push(here, here, cs.at[d, k], cr.at[d, k], me.twin())
            if d < nc - 2:
                for direction in (1, -1):

                    @pl.when(can_receive(direction, d))
                    def _():
                        token_landing(direction, d).wait_recv()

                    @pl.when(can_send(direction, d + 1))
                    def _():
                        token_copy(direction, d + 1).start()

        for d in range(nc):
            for k in range(nj):
                here = views(lax.rem(me.c - d + nc, nc), me.s ^ 1 ^ (2 * k))
                arrive(here, cs.at[d, k], cr.at[d, k], me.twin())
        for direction in (1, -1):

            @pl.when(can_receive(direction, nc - 2))
            def _():
                token_landing(direction, nc - 2).wait_recv()

        for copy in sent:
            copy.wait_send()
        for direction in (1, -1):
            for hop in range(nc - 1):

                @pl.when(can_send(direction, hop))
                def _():
                    token_copy(direction, hop).wait_send()

    full, extras, tokens = pl.pallas_call(
        kernel,
        name="gather_all",
        cost_estimate=pl.CostEstimate(flops=50 * 10**9, bytes_accessed=10**7, transcendentals=0),
        out_shape=(
            jax.ShapeDtypeStruct(full_shape, weights.dtype),
            jax.ShapeDtypeStruct((nc, ns) + extra.shape, extra.dtype),
            jax.ShapeDtypeStruct((nc,) + rows.shape, rows.dtype),
        ),
        in_specs=[pl.BlockSpec(memory_space=ANY)] * 3,
        out_specs=[pl.BlockSpec(memory_space=ANY)] * 3,
        scratch_shapes=[
            SEM.DMA((3,)),
            SEM.DMA((nc, 2)),
            SEM.DMA((nc, 2)),
            SEM.DMA((nc, nj, 2)),
            SEM.DMA((nc, nj, 2)),
            SEM.DMA((nc, nj, 2)),
            SEM.DMA((nc, nj, 2)),
            SEM.DMA((2, nc)),
            SEM.DMA((2, nc)),
        ],
        compiler_params=pltpu.CompilerParams(collective_id=1, has_side_effects=True),
    )(weights, extra, rows)
    return (
        full.reshape(share[0], n_dev * share[1], share[2]),
        extras,
        tokens.reshape(nc * rows.shape[0], rows.shape[1]),
    )


CHUNK = 16


def fill_mask(mask, query_code, key_code, block, count):
    near = block * count
    query = query_code[pl.ds(near, count)]
    if block:
        mask[:, :near] = jnp.where(query == key_code[:, :near], 0.0, negative)
    row = lax.broadcasted_iota(jnp.int32, (count, count), 0)
    column = lax.broadcasted_iota(jnp.int32, (count, count), 1)
    seen = ((query == key_code[:, near : near + count]) & (row >= column)) | (row == column)
    mask[:, near : near + count] = jnp.where(seen, 0.0, negative)


def fill_slopes(bank, slopes, head, count):
    for i in range(count // CHUNK):
        row = slopes[head]
        bank[head, i * CHUNK : (i + 1) * CHUNK] = pltpu.roll(row, i * CHUNK, 1) if i else row


def biased(scores, mask, slope, block, count):
    end = (block + 1) * count
    band = 2 * count
    if end < band:
        return scores + mask[:, :end] + slope[:, band - end :]
    if end == band:
        return scores + mask[:, :end] + slope[...]
    wide = scores[:, : end - band] + mask[:, : end - band]
    tight = scores[:, end - band :] + mask[:, end - band : end] + slope[...]
    return jnp.concatenate((wide, tight), axis=1)


def attend_forward(tokens, weights, gain, gain_next, query_code, key_code, slopes, nc, ns):
    length, width = tokens.shape
    count = length // nc
    part = width // nc
    heads, _, band = slopes.shape
    low, f32 = jnp.bfloat16, jnp.float32

    def kernel(t_in, w_in, gain_in, next_in, qcode, kcode, toe, first, q_out, k_out, v_out, o_out, lse_out, x_out, y_out,
               mask, bank, osend, ss, rs):
        me = Place(nc, ns)
        barrier = pltpu.get_barrier_semaphore()
        for d in range(1, nc):
            pl.semaphore_signal(barrier, inc=1, device_id=me.along(d), device_id_type=MESH)
        pl.semaphore_wait(barrier, nc - 1)

        def norm(i, carry):
            at = pl.ds(pl.multiple_of(i * 64, 64), 64)
            x = t_in[at].astype(f32)
            rate = lax.rsqrt(jnp.mean(x * x, axis=-1, keepdims=True) + epsilon)
            first[at] = (x * rate * gain_in[...]).astype(low)
            return carry

        lax.fori_loop(0, length // 64, norm, 0)

        def project(i, carry):
            at = pl.ds(pl.multiple_of(i * count, count), count)
            block = first[at]
            q_out[at] = dot32(block, w_in[0]).astype(low)
            k_out[at] = dot32(block, w_in[1]).astype(low)
            v_out[at] = dot32(block, w_in[2]).astype(low)
            return carry

        lax.fori_loop(0, nc, project, 0)
        for head in range(heads):
            fill_slopes(bank, toe, head, count)
        lane = lax.broadcasted_iota(jnp.int32, (count, 2 * HEAD), 1)
        spot = lax.broadcasted_iota(jnp.int32, (count, 128), 1)
        own_copy = [
            remote(osend.at[b], o_out.at[me.c], ss.at[b], rs.at[me.c], (b, me.s)) for b in range(nc)
        ]
        for b in reversed(range(nc)):
            end = (b + 1) * count
            rows = pl.ds(b * count, count)
            fill_mask(mask, qcode, kcode, b, count)
            level = jnp.zeros((count, 128), f32)
            for pair in range(heads // 2):
                two = slice(pair * 2 * HEAD, (pair + 1) * 2 * HEAD)
                q_pair = q_out[rows, two] * low(1.0 / math.sqrt(HEAD))
                k_pair = k_out[:end, two]
                v_pair = v_out[:end, two]
                halves = []
                for half in range(2):
                    head = pair * 2 + half
                    inside = (lane >= HEAD) if half else (lane < HEAD)
                    scores = nt(jnp.where(inside, q_pair, low(0)), k_pair)
                    scores = biased(scores, mask, bank.at[head], b, count)
                    top = jnp.max(scores, axis=1, keepdims=True)
                    scores = jnp.exp(scores - top)
                    total = jnp.sum(scores, axis=1, keepdims=True)
                    halves.append(dot32(scores.astype(low), v_pair) * (1.0 / total))
                    level = jnp.where(spot == head, top + jnp.log(total), level)
                osend[b, :, two] = jnp.where(lane < HEAD, halves[0], halves[1]).astype(low)
            lse_out[rows] = level

            @pl.when(me.c == b)
            def _():
                o_out[me.c] = osend[b]

            @pl.when(me.c != b)
            def _():
                own_copy[b].start()

        for d in range(1, nc):
            origin = lax.rem(me.c + d, nc)
            remote(
                osend.at[0], o_out.at[origin], ss.at[0], rs.at[origin], me.along(d)
            ).wait_recv()
        own = pl.ds(pl.multiple_of(me.c * count, count), count)
        squares = jnp.zeros((count, 1), f32)
        for n in range(nc):
            columns = slice(n * part, (n + 1) * part)
            x = t_in[own, columns].astype(f32)
            for origin in range(nc):
                x = x + dot32(o_out[origin], w_in[3 + n, origin * part : (origin + 1) * part])
            x_out[:, columns] = x
            squares = squares + jnp.sum(x * x, axis=1, keepdims=True)
        rate = lax.rsqrt(squares * (1.0 / width) + epsilon)
        for n in range(nc):
            columns = slice(n * part, (n + 1) * part)
            y_out[:, columns] = (x_out[:, columns] * rate * next_in[:, columns]).astype(low)
        for b in range(nc):

            @pl.when(me.c != b)
            def _():
                own_copy[b].wait_send()

    return pl.pallas_call(
        kernel,
        name="attend_forward",
        cost_estimate=pl.CostEstimate(flops=25 * 10**9, bytes_accessed=10**7, transcendentals=0),
        out_shape=(
            jax.ShapeDtypeStruct((length, width), low),
            jax.ShapeDtypeStruct((length, part), low),
            jax.ShapeDtypeStruct((length, part), low),
            jax.ShapeDtypeStruct((length, part), low),
            jax.ShapeDtypeStruct((nc, count, part), low),
            jax.ShapeDtypeStruct((length, 128), f32),
            jax.ShapeDtypeStruct((count, width), f32),
            jax.ShapeDtypeStruct((count, width), low),
        ),
        in_specs=[pl.BlockSpec(memory_space=VMEM)] * 7,
        out_specs=[pl.BlockSpec(memory_space=VMEM)] * 8,
        scratch_shapes=[
            VMEM((count, length), f32),
            VMEM((heads, count, band), f32),
            VMEM((nc, count, part), low),
            SEM.DMA((nc,)),
            SEM.DMA((nc,)),
        ],
        compiler_params=pltpu.CompilerParams(
            collective_id=3, has_side_effects=True, vmem_limit_bytes=56 * 1024 * 1024
        ),
    )(tokens, weights, gain, gain_next, query_code, key_code, slopes)


def attend_backward(
    dattn, o_all, tokens, first, q_all, k_all, v_all, lse, weights, query_code, key_code, slopes,
    weighted, cotangents, nc, ns,
):
    length, width = tokens.shape
    count = length // nc
    part = width // nc
    heads, _, band = slopes.shape
    low, f32 = jnp.bfloat16, jnp.float32
    scale = 1.0 / math.sqrt(HEAD)
    exchange = weighted.shape[1:3] + (width,)

    def kernel(a_in, o_in, t_in, first_in, q_in, k_in, v_in, lse_in, w_in, qcode, kcode, toe, pw_in, c_in,
               x_out, fsend, w_out, gain_out, near_out, far_out, c_out,
               mask, bank, dsend, dall, dq, dk, dv, fown, nsend, ss, rs, ns_, nr):
        me = Place(nc, ns)
        barrier = pltpu.get_barrier_semaphore()
        partners = [me.along(d) for d in range(1, nc)] + [(me.c, me.s ^ m) for m in range(1, ns)]
        for partner in partners:
            pl.semaphore_signal(barrier, inc=1, device_id=partner, device_id_type=MESH)
        pl.semaphore_wait(barrier, len(partners))

        def do_copy(d):
            return remote(dsend.at[d], dall.at[me.c], ss.at[d], rs.at[d], me.along(d))

        for d in list(range(1, nc)) + [0]:
            target = lax.rem(me.c + d, nc)
            at = pl.ds(pl.multiple_of(target * part, part), part)
            value = nt(a_in[:, :part], w_in[3, at])
            for n in range(1, nc):
                value = value + nt(a_in[:, n * part : (n + 1) * part], w_in[3 + n, at])
            if d:
                dsend[d] = value.astype(low)
                do_copy(d).start()
            else:
                dall[me.c] = value.astype(low)
        jobs = [(pw_in.at[d], c_in.at[me.c ^ (d + 1)], c_out.at[d]) for d in range(nc - 1)]
        spread = Spread(me, jobs, nsend, ns_, nr)
        for i in range(len(jobs)):
            spread.start(i)
        for n in range(nc):
            for origin in range(nc):
                w_out[3 + n, origin * part : (origin + 1) * part] = tn(
                    o_in[origin], a_in[:, n * part : (n + 1) * part]
                ).astype(low)
        for head in range(heads):
            fill_slopes(bank, toe, head, count)
        lane = lax.broadcasted_iota(jnp.int32, (count, 2 * HEAD), 1)
        spot = lax.broadcasted_iota(jnp.int32, (count, 128), 1)
        dk[...] = jnp.zeros_like(dk)
        dv[...] = jnp.zeros_like(dv)
        near_out[...] = jnp.zeros_like(near_out)
        far_out[...] = jnp.zeros_like(far_out)
        gain_out[...] = jnp.zeros_like(gain_out)
        for d in range(1, nc):
            origin = lax.rem(me.c - d + nc, nc)
            remote(dsend.at[d], dall.at[origin], ss.at[d], rs.at[d], me.along(d)).wait_recv()
        for b in reversed(range(nc)):
            end = (b + 1) * count
            rows = pl.ds(b * count, count)
            fill_mask(mask, qcode, kcode, b, count)
            level = lse_in[rows]
            for pair in range(heads // 2):
                two = slice(pair * 2 * HEAD, (pair + 1) * 2 * HEAD)
                q_pair = q_in[rows, two] * low(scale)
                do_pair = dall[b, :, two]
                k_pair = k_in[:end, two]
                v_pair = v_in[:end, two]
                parts = []
                for half in range(2):
                    head = pair * 2 + half
                    inside = (lane >= HEAD) if half else (lane < HEAD)
                    q_one = jnp.where(inside, q_pair, low(0))
                    do_one = jnp.where(inside, do_pair, low(0))
                    own_level = jnp.sum(
                        jnp.where(spot == head, level, 0.0), axis=1, keepdims=True
                    )
                    probs = jnp.exp(
                        biased(nt(q_one, k_pair), mask, bank.at[head], b, count) - own_level
                    )
                    grads = probs * nt(do_one, v_pair)
                    grads = grads - probs * jnp.sum(grads, axis=1, keepdims=True)
                    low_grads = grads.astype(low)
                    parts.append(dot32(low_grads, k_pair))
                    dk[:end, two] += tn(low_grads, q_one)
                    dv[:end, two] += tn(probs.astype(low), do_one)
                    near = grads[:, max(end - band, 0) :]
                    if end < band:
                        near = jnp.concatenate((jnp.zeros((count, band - end), f32), near), axis=1)
                    height = count
                    while height > CHUNK:
                        height = height // 2
                        near = near[:height] + pltpu.roll(near[height:], band - height, 1)
                    near_out[head] += near
                    if end > band:
                        far = grads[:, : end - band]
                        total = far[:, :128]
                        for piece in range(1, (end - band) // 128):
                            total = total + far[:, piece * 128 : (piece + 1) * 128]
                        height = count
                        while height > 8:
                            height = height // 2
                            total = total[:height] + total[height:]
                        far_out[head] += total
                dq[rows, two] = (jnp.where(lane < HEAD, parts[0], parts[1]) * scale).astype(low)
            dq_low, dk_low, dv_low = dq[rows], dk[rows].astype(low), dv[rows].astype(low)
            for n in range(nc):
                columns = slice(n * part, (n + 1) * part)
                at = pl.ds(n * part, part)
                value = nt(dq_low, w_in[0, at]) + nt(dk_low, w_in[1, at]) + nt(dv_low, w_in[2, at])
                fown[:, columns] = value
            x = t_in[rows].astype(f32)
            rate = lax.rsqrt(jnp.mean(x * x, axis=-1, keepdims=True) + epsilon)
            gain_out[...] += jnp.sum(fown[...] * x * rate, axis=0, keepdims=True)
            fsend[b] = fown[...].astype(low)

            @pl.when(me.c == b)
            def _():
                x_out[...] = fown[...]

        for i, grads in enumerate((dq, dk, dv)):
            for n in range(nc):
                at = slice(n * part, (n + 1) * part)
                w_out[i, at] = tn(first_in[:, at], grads[...].astype(low)).astype(low)
        spread.finish()
        for d in range(1, nc):
            do_copy(d).wait_send()

    return pl.pallas_call(
        kernel,
        name="attend_backward",
        cost_estimate=pl.CostEstimate(flops=50 * 10**9, bytes_accessed=10**7, transcendentals=0),
        out_shape=(
            jax.ShapeDtypeStruct((count, width), f32),
            jax.ShapeDtypeStruct((nc, count, width), low),
            jax.ShapeDtypeStruct((3 + nc, width, part), low),
            jax.ShapeDtypeStruct((1, width), f32),
            jax.ShapeDtypeStruct((heads, CHUNK, band), f32),
            jax.ShapeDtypeStruct((heads, 8, 128), f32),
            jax.ShapeDtypeStruct((nc - 1,) + exchange, low),
        ),
        in_specs=[pl.BlockSpec(memory_space=VMEM)] * 14,
        out_specs=[pl.BlockSpec(memory_space=VMEM)] * 6 + [pl.BlockSpec(memory_space=ANY)],
        scratch_shapes=[
            VMEM((count, length), f32),
            VMEM((heads, count, band), f32),
            VMEM((nc, count, part), low),
            VMEM((nc, count, part), low),
            VMEM((length, part), low),
            VMEM((length, part), f32),
            VMEM((length, part), f32),
            VMEM((count, width), f32),
            VMEM((4,) + exchange, low),
            SEM.DMA((nc,)),
            SEM.DMA((nc,)),
            SEM.DMA((nc - 1, ns)),
            SEM.DMA((nc - 1, ns)),
        ],
        compiler_params=pltpu.CompilerParams(
            collective_id=4, has_side_effects=True, vmem_limit_bytes=61 * 1024 * 1024
        ),
    )(dattn, o_all, tokens, first, q_all, k_all, v_all, lse, weights, query_code, key_code, slopes,
      weighted, cotangents)


def activation(gate_values, up_values):
    return jax.nn.gelu(gate_values) * up_values


def gelu_parts(x):
    c, a = math.sqrt(2.0 / math.pi), 0.044715
    square = x * x
    t = jnp.tanh(c * x * (1.0 + a * square))
    half = 0.5 * (1.0 + t)
    return x * half, half + (0.5 * c) * x * (1.0 - t * t) * (1.0 + (3.0 * a) * square)


class Chain:
    def __init__(self, me, pairs, send, recv):
        self.me, self.pairs, self.send, self.recv, self.nc = me, pairs, send, recv, me.nc

    def copies(self, direction, hop, landing):
        me, nc = self.me, self.nc
        lane = 0 if direction > 0 else 1
        origin = lax.rem(me.c - direction * (hop + 1 if landing else hop) + 2 * nc, nc)
        result = []
        for i, (own, every) in enumerate(self.pairs):
            target = every.at[origin]
            source = own if hop == 0 and not landing else target
            result.append(
                remote(
                    source, target, self.send.at[lane, hop, i], self.recv.at[lane, hop, i],
                    me.along(direction),
                )
            )
        return result

    def sends(self, direction, hop):
        c, nc = self.me.c, self.nc
        if direction > 0:
            return (c >= hop) & (c < nc - 1)
        return (c <= nc - 1 - hop) & (c > 0)

    def lands(self, direction, hop):
        c, nc = self.me.c, self.nc
        if direction > 0:
            return c >= hop + 1
        return c <= nc - 2 - hop

    def start(self, hop):
        if hop >= self.nc:
            return
        for direction in (1, -1):
            if hop:

                @pl.when(self.lands(direction, hop - 1))
                def _():
                    for copy in self.copies(direction, hop - 1, True):
                        copy.wait_recv()

            if hop < self.nc - 1:

                @pl.when(self.sends(direction, hop))
                def _():
                    for copy in self.copies(direction, hop, False):
                        copy.start()

    def finish(self):
        for direction in (1, -1):
            for hop in range(self.nc - 1):

                @pl.when(self.sends(direction, hop))
                def _():
                    for copy in self.copies(direction, hop, False):
                        copy.wait_send()


def greet_experts(me):
    barrier = pltpu.get_barrier_semaphore()
    partners = [(me.c, me.s ^ m) for m in range(1, me.ns)] + [me.along(1), me.along(-1)]
    for partner in partners:
        pl.semaphore_signal(barrier, inc=1, device_id=partner, device_id_type=MESH)
    pl.semaphore_wait(barrier, len(partners))


TILE = 256


class Spread:
    def __init__(self, me, jobs, send, send_sem, recv_sem):
        self.me, self.jobs, self.send = me, jobs, send
        self.send_sem, self.recv_sem = send_sem, recv_sem
        self.order = list(range(2, me.ns)) + [1]
        self.turns = send.shape[0]

    def copy(self, i, m):
        return remote(
            self.send.at[i % self.turns, m], self.jobs[i][2].at[m],
            self.send_sem.at[i, m], self.recv_sem.at[i, m], (self.me.c, self.me.s ^ m),
        )

    def own(self, i):
        return pltpu.make_async_copy(
            self.send.at[i % self.turns, 0], self.jobs[i][2].at[0], self.send_sem.at[i, 0]
        )

    def left(self, i):
        for m in self.order:
            self.copy(i, m).wait_send()
        self.own(i).wait()

    def start(self, i):
        if i >= self.turns:
            self.left(i - self.turns)
        picks, tokens = self.jobs[i][:2]
        for m in self.order + [0]:
            self.send[i % self.turns, m] = dot32(picks[m], tokens[...]).astype(self.send.dtype)
            if m:
                self.copy(i, m).start()
            else:
                self.own(i).start()

    def landed(self, i):
        for m in self.order:
            self.copy(i, m).wait_recv()
        if i >= len(self.jobs) - self.turns:
            self.left(i)

    def finish(self):
        for i in range(len(self.jobs)):
            self.landed(i)


def row_groups(ns):
    return [(2, 6), (6, ns), (0, 2)]


def moe_forward(pick, pick_next, tokens, gates, gate_w, up_w, down_w, nc, ns):
    cap, count = pick.shape[1:]
    width, hidden = gate_w.shape
    low, f32 = jnp.bfloat16, jnp.float32
    groups = row_groups(ns)
    most = max(end - start for start, end in groups) * cap

    def kernel(p_in, n_in, t_in, s_in, g_hbm, u_hbm, d_hbm, r_out, y_out, t_all, s_all, n_out, kg_out, ku_out,
               wg, wu, wd, send, yield_, nsend, inner, keep_g, keep_u, ks, ws, ss, rs, ys, yr, ts, tr, ls, ns_, nr):
        me = Place(nc, ns)
        loads = [
            pltpu.make_async_copy(source, target, ws.at[i])
            for i, (source, target) in enumerate(((g_hbm, wg), (u_hbm, wu), (d_hbm, wd)))
        ]
        for load in loads:
            load.start()
        keep = [
            pltpu.make_async_copy(t_in, t_all.at[me.c], ls.at[0]),
            pltpu.make_async_copy(s_in, s_all.at[me.c], ls.at[1]),
        ]
        for copy in keep:
            copy.start()
        greet_experts(me)

        def there(m):
            return (me.c, me.s ^ m)

        def out_copy(m):
            return remote(send.at[m], r_out.at[m], ss.at[m], rs.at[m], there(m))

        def back_copy(m):
            return remote(yield_.at[m], y_out.at[m], ys.at[m], yr.at[m], there(m))

        for m in list(range(2, 6)) + [1]:
            send[m] = dot32(p_in[m], t_in[...]).astype(low)
            out_copy(m).start()
        chain = Chain(me, ((t_in, t_all), (s_in, s_all)), ts, tr)
        chain.start(0)
        r_out[0] = dot32(p_in[0], t_in[...]).astype(low)
        for m in range(6, ns):
            send[m] = dot32(p_in[m], t_in[...]).astype(low)
        for load in loads:
            load.wait()
        for turn, (begin, end) in enumerate(groups):
            size = (end - begin) * cap
            here = pl.ds(begin * cap, size)
            for m in range(begin, end):
                if m:
                    out_copy(m).wait_recv()
            if turn == 0:
                for m in range(6, ns):
                    out_copy(m).start()

            def up(n, carry):
                rows = r_out[begin:end].reshape(size, width)
                at = pl.ds(pl.multiple_of(n * TILE, TILE), TILE)
                value, slope = gelu_parts(dot32(rows, wg[:, at]))
                linear = dot32(rows, wu[:, at])
                inner[:size, at] = (value * linear).astype(low)
                keep_g[here, at] = (slope * linear).astype(low)
                keep_u[here, at] = value.astype(low)
                return carry

            lax.fori_loop(0, hidden // TILE, up, 0)
            for i, (kept, target) in enumerate(((keep_g, kg_out), (keep_u, ku_out))):
                copy = pltpu.make_async_copy(kept.at[here], target.at[here], ks.at[turn, i])
                copy.start()
                keep.append(copy)
            chain.start(turn + 1)
            if turn == 0:
                spread = Spread(me, [(n_in, t_all.at[me.c ^ 1], n_out)], nsend, ns_, nr)
                spread.start(0)

            def down(n, carry):
                at = pl.ds(pl.multiple_of(n * TILE, TILE), TILE)
                value = dot32(inner[:size], wd[:, at]).astype(low)
                yield_[begin:end, :, at] = value.reshape(end - begin, cap, TILE)
                return carry

            lax.fori_loop(0, width // TILE, down, 0)
            for m in range(begin, end):
                if m:
                    back_copy(m).start()
        y_out[0] = yield_[0]
        for hop in range(len(groups) + 1, nc):
            chain.start(hop)
        for m in range(1, ns):
            back_copy(m).wait_recv()
        for copy in keep:
            copy.wait()
        for m in range(1, ns):
            out_copy(m).wait_send()
            back_copy(m).wait_send()
        spread.finish()
        chain.finish()

    exchange = (ns, cap, width)
    return pl.pallas_call(
        kernel,
        name="moe_forward",
        cost_estimate=pl.CostEstimate(flops=45 * 10**9, bytes_accessed=10**7, transcendentals=0),
        out_shape=(
            jax.ShapeDtypeStruct(exchange, low),
            jax.ShapeDtypeStruct(exchange, low),
            jax.ShapeDtypeStruct((nc,) + tokens.shape, low),
            jax.ShapeDtypeStruct((nc,) + gates.shape, f32),
            jax.ShapeDtypeStruct(exchange, low),
            jax.ShapeDtypeStruct((ns * cap, hidden), low),
            jax.ShapeDtypeStruct((ns * cap, hidden), low),
        ),
        in_specs=[pl.BlockSpec(memory_space=VMEM)] * 4 + [pl.BlockSpec(memory_space=ANY)] * 3,
        out_specs=[pl.BlockSpec(memory_space=VMEM)] * 4 + [pl.BlockSpec(memory_space=ANY)] * 3,
        scratch_shapes=[
            VMEM((width, hidden), low),
            VMEM((width, hidden), low),
            VMEM((hidden, width), low),
            VMEM(exchange, low),
            VMEM(exchange, low),
            VMEM((1,) + exchange, low),
            VMEM((most, hidden), low),
            VMEM((ns * cap, hidden), low),
            VMEM((ns * cap, hidden), low),
            SEM.DMA((3, 2)),
            SEM.DMA((3,)),
            SEM.DMA((ns,)),
            SEM.DMA((ns,)),
            SEM.DMA((ns,)),
            SEM.DMA((ns,)),
            SEM.DMA((2, nc, 2)),
            SEM.DMA((2, nc, 2)),
            SEM.DMA((2,)),
            SEM.DMA((1, ns)),
            SEM.DMA((1, ns)),
        ],
        compiler_params=pltpu.CompilerParams(
            collective_id=5, has_side_effects=True, vmem_limit_bytes=56 * 1024 * 1024
        ),
    )(pick, pick_next, tokens, gates, gate_w, up_w, down_w)


def combine(returned, pick_first, pick_second, gates, residual, teacher, valid, ratio):
    rows, width = returned.shape
    count = residual.shape[0]
    low, f32 = jnp.bfloat16, jnp.float32

    def kernel(r_in, p1, p2, s_in, x_in, t_in, v_in, k_in, y_out, g_out, gl_out, b_out, d_out, q_out):
        first, second = s_in[:, 0:1], s_in[:, 1:2]
        pulls = [jnp.zeros((count, 1), f32)] * 2
        squares = jnp.zeros((8, 128), f32)
        for n in range(0, width, TILE):
            at = slice(n, n + TILE)
            one, two = tn(p1[...], r_in[:, at]), tn(p2[...], r_in[:, at])
            value = x_in[:, at] + first * one + second * two
            y_out[:, at] = value.astype(low)
            off = value - t_in[:, at].astype(f32)
            kept = v_in[...] * off
            square = jnp.sum((kept * off).reshape(count // 8, 8, TILE), axis=0)
            for left in range(0, TILE, 128):
                squares = squares + square[:, left : left + 128]
            pull = k_in[...] * kept
            g_out[:, at] = pull
            gl_out[:, at] = pull.astype(low)
            pulls = [
                total + jnp.sum(pull * part, axis=1, keepdims=True)
                for total, part in zip(pulls, (one, two))
            ]
            back = dot32(p1[...], (first * pull).astype(low)) + dot32(p2[...], (second * pull).astype(low))
            b_out[:, at] = back.astype(low)
        d_out[:, 0:1] = pulls[0]
        d_out[:, 1:2] = pulls[1]
        q_out[...] = squares

    return pl.pallas_call(
        kernel,
        name="combine",
        out_shape=(
            jax.ShapeDtypeStruct((count, width), low),
            jax.ShapeDtypeStruct((count, width), f32),
            jax.ShapeDtypeStruct((count, width), low),
            jax.ShapeDtypeStruct((rows, width), low),
            jax.ShapeDtypeStruct((count, 2), f32),
            jax.ShapeDtypeStruct((8, 128), f32),
        ),
        in_specs=[pl.BlockSpec(memory_space=VMEM)] * 8,
        out_specs=[pl.BlockSpec(memory_space=VMEM)] * 6,
        compiler_params=pltpu.CompilerParams(vmem_limit_bytes=48 * 1024 * 1024),
    )(returned, pick_first, pick_second, gates, residual, teacher, valid, ratio)


def moe_backward(grads, kept_g, kept_u, cotangents, pick_next, tokens, gate_w, up_w, down_w, nc, ns):
    cap = grads.shape[1]
    width, hidden = gate_w.shape
    low, f32 = jnp.bfloat16, jnp.float32
    groups = row_groups(ns)
    most = max(end - start for start, end in groups) * cap
    more = pick_next.shape[0]

    def kernel(g_in, t_in, n_in, f_in, g_hbm, u_hbm, d_hbm, kg_hbm, ku_hbm, g_out, x_out, t_all, n_out,
               wg, wu, wd, yield_, nsend, slope_g, slope_u, dg, du, ws, ss, rs, ys, yr, ts, tr, ls, ns_, nr):
        me = Place(nc, ns)
        loads = [
            pltpu.make_async_copy(source, target, ws.at[i])
            for i, (source, target) in enumerate(
                ((d_hbm, wd), (kg_hbm, slope_g), (ku_hbm, slope_u), (g_hbm, wg), (u_hbm, wu))
            )
        ]
        for load in loads:
            load.start()
        keep = pltpu.make_async_copy(t_in, t_all.at[me.c], ls.at[0])
        keep.start()
        greet_experts(me)

        def there(m):
            return (me.c, me.s ^ m)

        def out_copy(m):
            return remote(g_in.at[m], g_out.at[m], ss.at[m], rs.at[m], there(m))

        def back_copy(m):
            return remote(yield_.at[m], x_out.at[m], ys.at[m], yr.at[m], there(m))

        for m in list(range(2, 6)) + [1]:
            out_copy(m).start()
        chain = Chain(me, ((t_in, t_all),), ts, tr)
        chain.start(0)
        g_out[0] = g_in[0]
        for load in loads:
            load.wait()

        jobs = [(n_in.at[i], f_in.at[me.c ^ (i + 2)], n_out.at[i]) for i in range(more)]
        spread = Spread(me, jobs, nsend, ns_, nr)
        for turn, (begin, end) in enumerate(groups):
            size = (end - begin) * cap
            for m in range(begin, end):
                if m:
                    out_copy(m).wait_recv()
            if turn == 0:
                for m in range(6, ns):
                    out_copy(m).start()
            here = slice(begin * cap, end * cap)

            def up(n, carry):
                taken = g_out[begin:end].reshape(size, width)
                at = pl.ds(pl.multiple_of(n * TILE, TILE), TILE)
                value = nt(taken, wd[at])
                dg[:size, at] = (value * slope_g[here, at].astype(f32)).astype(low)
                du[:size, at] = (value * slope_u[here, at].astype(f32)).astype(low)
                return carry

            lax.fori_loop(0, hidden // TILE, up, 0)
            chain.start(turn + 1)
            if turn == 0:
                for i in range(more):
                    spread.start(i)

            def down(n, carry):
                at = pl.ds(pl.multiple_of(n * TILE, TILE), TILE)
                value = nt(dg[:size], wg[at]) + nt(du[:size], wu[at])
                yield_[begin:end, :, at] = value.astype(low).reshape(end - begin, cap, TILE)
                return carry

            lax.fori_loop(0, width // TILE, down, 0)
            for m in range(begin, end):
                if m:
                    back_copy(m).start()
        x_out[0] = yield_[0]
        for hop in range(len(groups) + 1, nc):
            chain.start(hop)
        for m in range(1, ns):
            back_copy(m).wait_recv()
        keep.wait()
        for m in range(1, ns):
            out_copy(m).wait_send()
            back_copy(m).wait_send()
        spread.finish()
        chain.finish()

    exchange = (ns, cap, width)
    return pl.pallas_call(
        kernel,
        name="moe_backward",
        cost_estimate=pl.CostEstimate(flops=45 * 10**9, bytes_accessed=10**7, transcendentals=0),
        out_shape=(
            jax.ShapeDtypeStruct(exchange, low),
            jax.ShapeDtypeStruct(exchange, low),
            jax.ShapeDtypeStruct((nc,) + cotangents.shape, low),
            jax.ShapeDtypeStruct((more,) + exchange, low),
        ),
        in_specs=[pl.BlockSpec(memory_space=VMEM)] * 4 + [pl.BlockSpec(memory_space=ANY)] * 5,
        out_specs=[pl.BlockSpec(memory_space=VMEM)] * 2 + [pl.BlockSpec(memory_space=ANY)] * 2,
        scratch_shapes=[
            VMEM((width, hidden), low),
            VMEM((width, hidden), low),
            VMEM((hidden, width), low),
            VMEM(exchange, low),
            VMEM((1,) + exchange, low),
            VMEM((ns * cap, hidden), low),
            VMEM((ns * cap, hidden), low),
            VMEM((most, hidden), low),
            VMEM((most, hidden), low),
            SEM.DMA((5,)),
            SEM.DMA((ns,)),
            SEM.DMA((ns,)),
            SEM.DMA((ns,)),
            SEM.DMA((ns,)),
            SEM.DMA((2, nc, 1)),
            SEM.DMA((2, nc, 1)),
            SEM.DMA((1,)),
            SEM.DMA((more, ns)),
            SEM.DMA((more, ns)),
        ],
        compiler_params=pltpu.CompilerParams(
            collective_id=6, has_side_effects=True, vmem_limit_bytes=60 * 1024 * 1024
        ),
    )(grads, cotangents, pick_next, tokens, gate_w, up_w, down_w, kept_g, kept_u)


def slice_plan(hidden, nc):
    exact, tiles = hidden // nc, hidden // 128
    wide = max(-(-((c + 1) * exact) // 128) - (c * exact) // 128 for c in range(nc))
    return [min((c * exact) // 128, tiles - wide) * 128 for c in range(nc)], wide * 128


def finish_all(
    grads, small, squares, terms, own_terms, dh, inputs, gain, picks, normed, rows, row_grads, gate_w, up_w, down_w, nc, ns, kept
):
    nj = ns // 2
    parts, piece, width = grads.shape[0], grads.shape[4], grads.shape[5]
    low, f32 = jnp.bfloat16, jnp.float32
    tile = squares.shape
    features, hidden = gate_w.shape
    band, half, exact = features // nc, hidden // 2, hidden // nc
    wide = slice_plan(half, nc // 2)[1]
    more = picks.shape[0]
    exchange = picks.shape[1:3] + (features,)
    row_at = [(i, n) for i, x in enumerate(rows) for n in range(x.shape[0])]
    row_at = row_at + [(None, n) for n in range(more)]
    grad_at = [(len(rows) + i, n) for i, x in enumerate(row_grads) for n in range(x.shape[0])]
    count, block = len(rows) + len(row_grads), rows[0].shape[1]
    blocks = len(row_at)
    positions = own_terms.shape[0]
    rest = half - wide
    widths = [wide] + ([rest - 128, 128] if nc == 4 else [128] * (rest // 128))

    def kernel(g_in, e_in, q_in, f_in, fo_in, dh_in, t_in, gain_in, p_in, n_in, *refs):
        (g_hbm, u_hbm, d_hbm, k0_out, k1_out, k2_out, k3_out, e_out, q_out, wg_out, wu_out, wd_out, x_out, n_out,
         gt, et, gc, ec, gx, ex, gz, ez, g_sum, qz, qx, qc, qa, qb,
         cs, cr, xs, xr, zs, zr, q1s, q1r, q2s, q2r, q3s, q3r,
         xb, yb, wg, wu, wd, inner, dg, du, ag, au, ad, pair_send, down_send, ws, rs, ps, pr, ds, dr,
         fland, fs, fr, nsend, ns_, nr) = refs[count:]
        me = Place(nc, ns)
        k_out = (k0_out, k1_out, k2_out, k3_out)
        high, lower = me.c // 2, me.c % 2
        begin = pl.multiple_of(lower * half, 128)
        place = lower * (nc // 2) + high
        source = (me.c % (nc // 2)) * 2 + me.c // (nc // 2)
        offset = high * exact
        cut = pl.multiple_of(jnp.minimum(offset // 128, (half - wide) // 128) * 128, 128)
        begins = [cut] + [lax.rem(cut + sum(widths[:n]), half) for n in range(1, len(widths))]

        def fetch(i):
            (a, n), (b, k) = row_at[i % blocks], grad_at[i % blocks]
            if a is None:
                return [
                    pltpu.make_async_copy(
                        n_out.at[n, m], xb.at[i % 2, pl.ds(m * cap, cap)], rs.at[i % 2, 2 + m]
                    )
                    for m in range(ns)
                ] + [pltpu.make_async_copy(refs[b].at[k], yb.at[i % 2], rs.at[i % 2, 1])]
            return [
                pltpu.make_async_copy(refs[a].at[n], xb.at[i % 2], rs.at[i % 2, 0]),
                pltpu.make_async_copy(refs[b].at[k], yb.at[i % 2], rs.at[i % 2, 1]),
            ]

        loads = fetch(0) + [
            pltpu.make_async_copy(g_hbm.at[:, pl.ds(begin, half)], wg, ws.at[0]),
            pltpu.make_async_copy(u_hbm.at[:, pl.ds(begin, half)], wu, ws.at[1]),
            pltpu.make_async_copy(d_hbm.at[pl.ds(begin, half)], wd, ws.at[2]),
        ]
        for load in loads:
            load.start()
        barrier = pltpu.get_barrier_semaphore()
        partners = [me.along(d) for d in range(1, nc)] + [(me.c, me.s ^ m) for m in range(1, ns)]
        for partner in partners:
            pl.semaphore_signal(barrier, inc=1, device_id=partner, device_id_type=MESH)
        pl.semaphore_wait(barrier, len(partners))

        def pass_terms(step):
            for side, direction in enumerate((-1, 1)):
                here = me.c if direction < 0 else nc - 1 - me.c
                ahead = step - (nc - 1 - here)
                number = ahead if direction < 0 else nc - 1 - ahead
                sends = (ahead >= 0) & (ahead < here)

                @pl.when(sends & (here < nc - 1))
                def _():
                    term_copy(side, direction, number, True).wait_recv()
                    for i in range(0, positions, 64):
                        at = pl.ds(i, 64)
                        fland[number, at] = (
                            fland[number, at].astype(f32) + f_in[number, at].astype(f32)
                        ).astype(low)

                @pl.when(sends & (here == nc - 1))
                def _():
                    fland[number] = f_in[number]

                @pl.when(sends)
                def _():
                    term_copy(side, direction, number, False).start()

        def term_copy(side, direction, number, landing):
            target = me.c if landing else lax.rem(me.c + direction + nc, nc)
            place = jnp.where(number == target, nc, number) if direction > 0 else number
            source = place if landing else number
            return remote(
                fland.at[source], fland.at[place], fs.at[side, number], fr.at[side, number],
                (lax.rem(me.c + direction + nc, nc), me.s),
            )

        def end_terms():
            x_out[...] = fo_in[...]
            for side, direction in enumerate((-1, 1)):
                here = me.c if direction < 0 else nc - 1 - me.c

                @pl.when(here < nc - 1)
                def _():
                    term_copy(side, direction, me.c, True).wait_recv()
                    x_out[...] += fland[nc if direction > 0 else me.c].astype(f32)

            x = t_in[...].astype(f32)
            rate = lax.rsqrt(jnp.mean(x * x, axis=-1, keepdims=True) + epsilon)
            scaled = x_out[...] * gain_in[...]
            pull = jnp.mean(scaled * x, axis=-1, keepdims=True)
            x_out[...] = dh_in[...] + rate * scaled - x * (rate * rate * rate * pull)

        def sent_terms():
            for side, direction in enumerate((-1, 1)):
                here = me.c if direction < 0 else nc - 1 - me.c
                for ahead in range(nc - 1):

                    @pl.when(ahead < here)
                    def _():
                        number = ahead if direction < 0 else nc - 1 - ahead
                        term_copy(side, direction, number, False).wait_send()

        cap = exchange[1]
        jobs = [(p_in.at[i], n_in.at[me.c ^ (nc - more + i)], n_out.at[i]) for i in range(more)]
        spread = Spread(me, jobs, nsend, ns_, nr)
        pass_terms(0)
        for i in range(more):
            spread.start(i)

        def both(pairs, send, recv, device):
            return [
                remote(one, target, send.at[i], recv.at[i], device)
                for i, (one, target) in enumerate(pairs)
            ]

        def core_copy(d):
            row = lax.rem(me.c + d, nc)
            other = 1 - me.core
            return both(
                ((g_in.at[:, row, :, other], gc.at[d]), (e_in.at[row, :, other], ec.at[d])),
                cs.at[d], cr.at[d], me.twin(),
            )

        def cross_copy(d, k):
            return both(
                ((gt.at[d, :, me.j ^ k], gx.at[d, k - 1]), (et.at[d, me.j ^ k], ex.at[d, k - 1])),
                xs.at[d, k], xr.at[d, k], me.across(k),
            )

        def along_copy(d):
            return both(
                ((gt.at[d, :, me.j], gz.at[d - 1]), (et.at[d, me.j], ez.at[d - 1])),
                zs.at[d], zr.at[d], me.along(d),
            )

        def start(copies):
            for copy in copies:
                copy.start()

        def landed(copies):
            for copy in copies:
                copy.wait_recv()

        def q_along(d):
            return remote(q_in, qz.at[d - 1], q1s.at[d], q1r.at[d], me.along(d))

        def q_across(k):
            return remote(qa, qx.at[k - 1], q2s.at[k], q2r.at[k], me.across(k))

        q_twin = remote(qb, qc, q3s.at[0], q3r.at[0], me.twin())
        order = list(range(1, nc)) + [0]

        def core_stage():
            for d in order:
                landed(core_copy(d))
                row = lax.rem(me.c + d, nc)

                def add_core(i, carry):
                    for k in range(nj):
                        gt[d, i, k] = (
                            g_in[i, row, k, me.core].astype(f32) + gc[d, i, k].astype(f32)
                        ).astype(low)
                    return carry

                lax.fori_loop(0, parts, add_core, 0)
                for k in range(nj):
                    et[d, k] = (
                        e_in[row, k, me.core].astype(f32) + ec[d, k].astype(f32)
                    ).astype(low)
                for k in range(1, nj):
                    start(cross_copy(d, k))
            for d in range(1, nc):
                q_along(d).wait_recv()
            value = q_in[...]
            for d in range(1, nc):
                value = value + qz[d - 1]
            qa[...] = value
            for k in range(1, nj):
                q_across(k).start()

        def cross_stage():
            for d in order:
                for k in range(1, nj):
                    landed(cross_copy(d, k))

                def add_cross(i, carry):
                    value = gt[d, i, me.j].astype(f32)
                    for k in range(1, nj):
                        value = value + gx[d, k - 1, i].astype(f32)
                    if d == 0:
                        g_sum[i] = value
                    else:
                        gt[d, i, me.j] = value.astype(low)
                    return carry

                lax.fori_loop(0, parts, add_cross, 0)
                value = et[d, me.j].astype(f32)
                for k in range(1, nj):
                    value = value + ex[d, k - 1].astype(f32)
                if d:
                    et[d, me.j] = value.astype(low)
                    start(along_copy(d))
                else:
                    e_out[...] = value
            for k in range(1, nj):
                q_across(k).wait_recv()
            value = qa[...]
            for k in range(1, nj):
                value = value + qx[k - 1]
            qb[...] = value
            q_twin.start()

        def along_stage():
            for i in range(kept):
                k_out[i][:, pl.ds(pl.multiple_of(me.c * width, width), width)] = g_sum[i]
            for d in range(1, nc):
                landed(along_copy(d))
                row = lax.rem(me.c - d + nc, nc)
                for i in range(kept):
                    at = pl.ds(pl.multiple_of(row * width, width), width)
                    k_out[i][:, at] = gz[d - 1, i].astype(f32)
                e_out[...] = e_out[...] + ez[d - 1].astype(f32)
            for i in range(kept, parts):
                value = g_sum[i]
                for d in range(1, nc):
                    value = value + gz[d - 1, i].astype(f32)
                k_out[kept][:, (i - kept) * width : (i - kept + 1) * width] = value
            q_twin.wait()
            q_out[...] = qb[...] + qc[...]

        def pair_copy(i, p):
            at = pl.multiple_of(begins[p], 128)
            return remote(
                pair_send.at[i, :, pl.ds(at, widths[p])],
                (wg_out, wu_out)[i].at[:, pl.ds(pl.multiple_of(begin + at, 128), widths[p])],
                ps.at[i, p], pr.at[i, p], (me.c + 1 - 2 * lower, me.s),
            )

        def pair_landing(i, p):
            at = pl.multiple_of(half - begin + begins[p], 128)
            landing = (wg_out, wu_out)[i].at[:, pl.ds(at, widths[p])]
            return remote(landing, landing, ps.at[i, p], pr.at[i, p], me.along(1))

        down_copy = remote(down_send, wd_out, ds.at[0], dr.at[0], (place, me.s))

        def give(i, p, total):
            at = pl.multiple_of(begins[p], 128)
            other = total[pl.ds(pl.multiple_of((1 - lower) * band, band), band), : widths[p]]
            pair_send[i, :, pl.ds(at, widths[p])] = other.astype(low)
            pair_copy(i, p).start()
            own = total[pl.ds(pl.multiple_of(lower * band, band), band), : widths[p]]
            at = pl.multiple_of(begin + at, 128)
            (wg_out, wu_out)[i][:, pl.ds(at, widths[p])] = own.astype(low)

        for d in order:
            start(core_copy(d))
        for d in range(1, nc):
            q_along(d).start()
        for load in loads:
            load.wait()
        steps = [[core_stage], [], [], [], [], [], [cross_stage], [], [], [along_stage]]
        places = [2 * n + 1 for n in range(nc - 2)]
        stages = [
            (steps[n] if n < len(steps) else [])
            + [lambda step=step + 1: pass_terms(step) for step, place_ in enumerate(places) if place_ == n]
            for n in range(max(len(steps), len(places) and places[-1] + 1))
        ]
        last = blocks - 1
        for p, size in enumerate(widths):
            cuts = [(n, min(n + TILE, size)) for n in range(0, size, TILE)]
            for i in range(blocks):
                turn = p * blocks + i
                if turn:
                    for load in fetch(turn):
                        load.wait()
                x, dy = xb.at[turn % 2], yb.at[turn % 2]
                for left, right in cuts:
                    at = pl.ds(pl.multiple_of(begins[p] + left, 128), right - left)
                    value, slope = gelu_parts(dot32(x[...], wg[:, at]))
                    linear = dot32(x[...], wu[:, at])
                    down = nt(dy[...], wd[at])
                    inner[:, left:right] = (value * linear).astype(low)
                    dg[:, left:right] = (down * linear * slope).astype(low)
                    du[:, left:right] = (down * value).astype(low)
                if turn + 1 < blocks * len(widths):
                    if turn + 1 < blocks and row_at[turn + 1][0] is None:
                        spread.landed(row_at[turn + 1][1])
                    for load in fetch(turn + 1):
                        load.start()
                mine = x[:, pl.ds(pl.multiple_of(high * 2 * band, 2 * band), 2 * band)]
                for n, (total, grad) in enumerate(((ag, dg), (au, du))):
                    if i:
                        total[:, :size] += tn(mine, grad[:, :size])
                    else:
                        total[:, :size] = tn(mine, grad[:, :size])
                    if i == last:
                        give(n, p, total)
                if p == 0:
                    if i:
                        ad[...] += tn(inner[...], dy[...])
                    else:
                        ad[...] = tn(inner[...], dy[...])
                    if i == last:
                        at = pl.ds(pl.multiple_of(offset - cut, 16), exact)
                        down_send[...] = ad[at].astype(low)

                        @pl.when(place != me.c)
                        def _():
                            down_copy.start()

                        @pl.when(place == me.c)
                        def _():
                            wd_out[...] = down_send[...]

                if stages and turn + 1 < blocks * len(widths):
                    for stage in stages.pop(0):
                        stage()
        for group in stages:
            for stage in group:
                stage()
        end_terms()
        for i in range(2):
            for p in range(len(widths)):
                pair_landing(i, p).wait_recv()

        @pl.when(source != me.c)
        def _():
            down_copy.wait_recv()

        @pl.when(place != me.c)
        def _():
            down_copy.wait_send()

        for d in order:
            started = core_copy(d) + [copy for k in range(1, nj) for copy in cross_copy(d, k)]
            if d:
                started = started + along_copy(d) + [q_along(d)]
            for copy in started:
                copy.wait_send()
        for k in range(1, nj):
            q_across(k).wait_send()
        for i in range(2):
            for p in range(len(widths)):
                pair_copy(i, p).wait_send()
        sent_terms()

    one, extra = (parts, piece, width), small.shape[3:]
    return pl.pallas_call(
        kernel,
        name="finish_all",
        cost_estimate=pl.CostEstimate(flops=80 * 10**9, bytes_accessed=10**7, transcendentals=0),
        out_shape=(
            *[jax.ShapeDtypeStruct((piece, nc * width), f32)] * 4,
            jax.ShapeDtypeStruct(extra, f32),
            jax.ShapeDtypeStruct(tile, f32),
            jax.ShapeDtypeStruct((band, hidden), low),
            jax.ShapeDtypeStruct((band, hidden), low),
            jax.ShapeDtypeStruct((exact, features), low),
            jax.ShapeDtypeStruct(own_terms.shape, f32),
            jax.ShapeDtypeStruct((more,) + exchange, low),
        ),
        in_specs=[pl.BlockSpec(memory_space=VMEM)] * 10 + [pl.BlockSpec(memory_space=ANY)] * (count + 3),
        out_specs=[pl.BlockSpec(memory_space=VMEM)] * 10 + [pl.BlockSpec(memory_space=ANY)],
        scratch_shapes=[
            VMEM((nc, parts, nj, piece, width), low),
            VMEM((nc, nj) + extra, low),
            VMEM((nc, parts, nj, piece, width), low),
            VMEM((nc, nj) + extra, low),
            VMEM((nc, nj - 1) + one, low),
            VMEM((nc, nj - 1) + extra, low),
            VMEM((nc - 1,) + one, low),
            VMEM((nc - 1,) + extra, low),
            VMEM(one, f32),
            VMEM((nc - 1,) + tile, f32),
            VMEM((nj - 1,) + tile, f32),
            VMEM(tile, f32),
            VMEM(tile, f32),
            VMEM(tile, f32),
            SEM.DMA((nc, 2)),
            SEM.DMA((nc, 2)),
            SEM.DMA((nc, nj, 2)),
            SEM.DMA((nc, nj, 2)),
            SEM.DMA((nc, 2)),
            SEM.DMA((nc, 2)),
            SEM.DMA((nc,)),
            SEM.DMA((nc,)),
            SEM.DMA((nj,)),
            SEM.DMA((nj,)),
            SEM.DMA((1,)),
            SEM.DMA((1,)),
            VMEM((2, block, features), low),
            VMEM((2, block, features), low),
            VMEM((features, half), low),
            VMEM((features, half), low),
            VMEM((half, features), low),
            VMEM((block, wide), low),
            VMEM((block, wide), low),
            VMEM((block, wide), low),
            VMEM((2 * band, wide), f32),
            VMEM((2 * band, wide), f32),
            VMEM((wide, features), f32),
            VMEM((2, band, half), low),
            VMEM((exact, features), low),
            SEM.DMA((3,)),
            SEM.DMA((2, 2 + ns)),
            SEM.DMA((2, len(widths))),
            SEM.DMA((2, len(widths))),
            SEM.DMA((1,)),
            SEM.DMA((1,)),
            VMEM((nc + 1,) + own_terms.shape, low),
            SEM.DMA((2, nc)),
            SEM.DMA((2, nc)),
            VMEM((1,) + exchange, low),
            SEM.DMA((more, ns)),
            SEM.DMA((more, ns)),
        ],
        compiler_params=pltpu.CompilerParams(
            collective_id=2, has_side_effects=True, vmem_limit_bytes=60 * 1024 * 1024
        ),
    )(grads, small, squares, terms, own_terms, dh, inputs, gain, picks, normed, *rows, *row_grads, gate_w, up_w, down_w)


def per_device(
    tokens,
    segments,
    valid,
    routes,
    teacher,
    norm_attn,
    w_query,
    w_key,
    w_value,
    output_weight,
    rel_bias,
    norm_ffn,
    w_router,
    w_gate,
    w_up,
    w_down,
):
    nc = lax.axis_size("ctx")
    ns = lax.axis_size("shard")
    c, s = lax.axis_index("ctx"), lax.axis_index("shard")
    n_dev, nj = nc * ns, ns // 2
    row_count, width = tokens.shape[1:]
    top_count = routes.shape[2]
    experts = w_router.shape[1]
    capacity = (5 * row_count * top_count + 4 * experts - 1) // (4 * experts)
    length = row_count * nc
    low = jnp.bfloat16
    f32 = jnp.float32
    piece = w_query.shape[0]
    band = 2 * row_count

    route_local = routes[0]
    expert_ids = jnp.arange(experts, dtype=jnp.int32)
    route_hot = route_local[:, :, None] == expert_ids[None, None, :]
    flat_routes = route_local.reshape(row_count * top_count)
    route_hits = (flat_routes[:, None] == expert_ids[None, :]).astype(jnp.int32)
    before = jnp.cumsum(route_hits, axis=0) - route_hits
    slot_rank = jnp.sum(before * route_hits, axis=1).reshape(row_count, top_count)

    part = width // nc
    smalls = (
        norm_attn, norm_ffn, rel_bias, w_router.reshape(-1), segments[0].astype(low), valid[0].astype(low),
        route_local.astype(low).T.reshape(-1), slot_rank.astype(low).T.reshape(-1),
    )
    sizes = [x.shape[0] for x in smalls]
    starts = [sum(sizes[:i]) for i in range(len(sizes))]
    extra = jnp.concatenate(smalls + (jnp.zeros((EXTRA * part - sum(sizes),), low),))
    shares = [w.reshape(piece, nc, part).transpose(1, 0, 2) for w in (w_query, w_key, w_value, output_weight)]
    shares = jnp.concatenate(
        [x[:, None] for x in shares[:3]] + [jnp.broadcast_to(shares[3][None], (nc, nc, piece, part))], axis=1
    )
    weights, extras, tokens_all = gather_all(
        shares, extra.reshape(EXTRA, part), tokens[0], nc, ns
    )
    extras = extras.reshape(nc, ns, EXTRA * part)
    gain_attn, gain_ffn, full_bias, full_router = (
        extras[:, :, begin : begin + size].reshape(-1)
        for begin, size in zip(starts[:4], sizes[:4])
    )
    full_router = full_router.reshape(width, experts)
    table = full_bias.reshape(BUCKETS, HEADS).astype(f32)
    line = lax.dynamic_slice_in_dim(extras, s, 1, 1)[:, 0]
    line_seg = line[:, starts[4] : starts[4] + row_count].reshape(length).astype(jnp.int32)
    line_valid = line[:, starts[5] : starts[5] + row_count].reshape(length) > 0
    key_code = jnp.where(line_valid, line_seg, -1)[None]
    query_code = line_seg[:, None]
    valid_count = jnp.sum(extras[:, :, starts[5] : starts[5] + row_count].astype(f32))

    spot = (jnp.arange(band)[None, :] - jnp.arange(CHUNK)[:, None]) % band
    distance = jnp.where(spot <= row_count, row_count - spot, 3 * row_count - spot)
    level = bucket_of(distance, BUCKETS)
    level_hot = (level[:, :, None] == jnp.arange(BUCKETS)[None, None, :]).astype(f32)
    heads = HEADS // nc
    own_table = lax.dynamic_slice_in_dim(table, c * heads, heads, 1)
    slopes = jnp.einsum(
        "ixb,bh->hix", level_hot, own_table - own_table[BUCKETS - 1 :], precision=highest_precision
    )

    gain_one, gain_two = gain_attn.astype(f32), gain_ffn.astype(f32)
    first_all, queries, keys, values, mixed, log_total, residual, ffn_low = attend_forward(
        tokens_all, weights, gain_one[None], gain_two[None], query_code, key_code, slopes, nc, ns
    )
    ffn_in = ffn_low.astype(f32)
    router = full_router.astype(f32)
    logits = jnp.dot(ffn_in, router, precision=highest_precision)
    picked = jnp.sum(jnp.where(route_hot, logits[:, None, :], 0.0), axis=-1)
    gate_probs = jax.nn.softmax(picked, axis=-1)

    slots = -(-capacity // 16) * 16
    target = (route_local ^ s) * slots + slot_rank
    slot_ids = jnp.arange(experts * slots, dtype=jnp.int32)
    pick_first = (slot_ids[:, None] == target[None, :, 0]).astype(low)
    pick_second = (slot_ids[:, None] == target[None, :, 1]).astype(low)
    pick_both = pick_first + pick_second
    gate_w, up_w, down_w = w_gate[0], w_up[0], w_down[0]
    gate_rows = jnp.concatenate((gate_probs.T, jnp.zeros((8 - top_count, row_count), f32)), axis=0)
    other_line = line[c ^ jnp.arange(1, nc)]
    other_routes, other_slots = (
        other_line[:, starts[i] : starts[i] + top_count * row_count]
        .astype(jnp.int32)
        .reshape(nc - 1, top_count, row_count)
        for i in (6, 7)
    )
    other_target = (other_routes ^ s) * slots + other_slots
    other_first, other_second = (
        slot_ids[None, :, None] == other_target[:, m, None, :] for m in range(2)
    )
    other_picks = (other_first | other_second).astype(low).reshape(nc - 1, experts, slots, row_count)
    expert_rows, returned, ffn_all, gates_all, rows_next, kept_g, kept_u = moe_forward(
        pick_both.reshape(experts, slots, row_count), other_picks[0], ffn_low, gate_rows,
        gate_w, up_w, down_w, nc, ns,
    )
    everything = float(row_count * nc * ns)
    output, cotangent, cotangent_low, back_send, gate_grad, squares = combine(
        returned.reshape(experts * slots, width), pick_first, pick_second, gate_probs, residual, teacher[0],
        valid[0].astype(f32)[:, None], (everything / valid_count).reshape(1, 1),
    )
    other_gates = gates_all[c ^ jnp.arange(1, nc)].astype(low)
    other_weighted = (
        jnp.where(other_first, other_gates[:, 0, None, :], low(0))
        + jnp.where(other_second, other_gates[:, 1, None, :], low(0))
    ).reshape(other_picks.shape)
    out_grad, sent_back, cotangent_all, rows_later = moe_backward(
        back_send.reshape(experts, slots, width), kept_g, kept_u, cotangent_low,
        other_picks[1 : nc // 2], ffn_all, gate_w, up_w, down_w, nc, ns,
    )
    ffn_grad = tn(pick_both, sent_back.reshape(experts * slots, width))
    pick_grad = gate_probs * (gate_grad - jnp.sum(gate_probs * gate_grad, axis=-1, keepdims=True))
    logits_grad = jnp.sum(jnp.where(route_hot, pick_grad[:, :, None], 0.0), axis=1)
    router_grad = contract(ffn_in, logits_grad, 0, 0, highest_precision)
    ffn_grad = ffn_grad + contract(logits_grad, router, 1, 1, highest_precision)
    unused, norm_two_back = jax.vjp(rms_norm, residual, gain_two)
    residual_from_norm, gain_two_grad = norm_two_back(ffn_grad)
    residual_grad = cotangent + residual_from_norm
    attn_grad_low = residual_grad.astype(low)
    hidden_own, hidden_terms, w_grads, gain_one_grad, near_sum, far_sum, other_grads = attend_backward(
        attn_grad_low, mixed, tokens_all, first_all, queries, keys, values, log_total, weights,
        query_code, key_code, slopes, other_weighted, cotangent_all, nc, ns,
    )
    own_bias = jnp.einsum("hix,ixb->bh", near_sum, level_hot, precision=highest_precision)
    last_bucket = (jnp.arange(BUCKETS) == BUCKETS - 1).astype(f32)
    own_bias = own_bias + last_bucket[:, None] * jnp.sum(far_sum, axis=(1, 2))[None, :]
    bias_grad = lax.dynamic_update_slice_in_dim(
        jnp.zeros((BUCKETS, HEADS), f32), own_bias, c * heads, 1
    )
    small_grads = jnp.concatenate(
        [
            x.reshape(n_dev, -1).astype(low)
            for x in (gain_one_grad, gain_two_grad, bias_grad, router_grad)
        ],
        axis=1,
    )
    small_grads = jnp.pad(small_grads, ((0, 0), (0, EXTRA * part - small_grads.shape[1])))
    *attn_sums, small_sum, square_sum, gate_w_sum, up_w_sum, down_w_sum, input_grad, unused = finish_all(
        w_grads.reshape(3 + nc, nc, nj, 2, piece, part),
        small_grads.reshape(nc, nj, 2, EXTRA, part),
        squares,
        hidden_terms,
        hidden_own,
        residual_grad,
        tokens[0],
        gain_one[None],
        other_picks[nc // 2 :],
        ffn_all,
        [x.reshape(-1, experts * slots, width) for x in (expert_rows, rows_next, rows_later)],
        [x.reshape(-1, experts * slots, width) for x in (out_grad, other_grads)],
        gate_w,
        up_w,
        down_w,
        nc,
        ns,
        3,
    )
    loss_value = jnp.sum(square_sum) / (2.0 * width * valid_count)
    small_sum = small_sum.reshape(-1)
    tails = [small_sum[begin : begin + size] for begin, size in zip(starts[:4], sizes[:4])]
    return (
        output[None],
        loss_value,
        input_grad[None],
        tails[0],
        attn_sums[0],
        attn_sums[1],
        attn_sums[2],
        attn_sums[3],
        tails[2],
        tails[1],
        tails[3].reshape(w_router.shape),
        gate_w_sum[None].astype(f32),
        up_w_sum[None].astype(f32),
        down_w_sum[None].astype(f32),
    )


def solution(mesh):
    return jax.shard_map(
        per_device,
        mesh=mesh,
        in_specs=(
            P("shard", "ctx", None),
            P("shard", "ctx"),
            P("shard", "ctx"),
            P("shard", "ctx", None),
            P("shard", "ctx", None),
            P(("ctx", "shard")),
            P(("ctx", "shard"), None),
            P(("ctx", "shard"), None),
            P(("ctx", "shard"), None),
            P(("ctx", "shard"), None),
            P(("ctx", "shard")),
            P(("ctx", "shard")),
            P(("ctx", "shard"), None),
            P("shard", None, None),
            P("shard", None, None),
            P("shard", None, None),
        ),
        out_specs=(
            P("shard", "ctx", None),
            P(),
            P("shard", "ctx", None),
            P(("ctx", "shard")),
            P(("ctx", "shard"), None),
            P(("ctx", "shard"), None),
            P(("ctx", "shard"), None),
            P(("ctx", "shard"), None),
            P(("ctx", "shard")),
            P(("ctx", "shard")),
            P(("ctx", "shard"), None),
            P("shard", "ctx", None),
            P("shard", "ctx", None),
            P("shard", "ctx", None),
        ),
        check_vma=False,
    )
```
